32 devices in a mesh: groups: 2 (over y), facex: 4 (over z), facey: 2 (over x), lev: 2 (over core).
Axes of the slice: x: 2, y: 2, z: 4, core: 2. Of those that a mesh axis runs over, the one named last changes fastest.
Arguments:
- tracer: float32 [8, 48, 64, 256], P('lev', 'groups', 'facex', 'facey'), parts along dimension 1, may hold values from -6 to 6
- west_courant: float32 [48, 64, 256], P('groups', 'facex', 'facey'), parts along dimension 0, may hold values from -0.24 to 0.24
- south_courant: float32 [48, 64, 256], P('groups', 'facex', 'facey'), parts along dimension 0, may hold values from -0.24 to 0.24
- mixing: float32 [46, 64, 256], P('groups', 'facex', 'facey'), parts along dimension 0, may hold values from 0.05 to 5
- adjoint_later: float32 [8, 48, 64, 256], P('lev', 'groups', 'facex', 'facey'), parts along dimension 1, may hold values from -6 to 6
- emission_scale: float32 [64, 256], P('facex', 'facey'), may hold values from 0.3 to 3
- send_cells: int32 [4, 2, 16, 32], P('facex', 'facey', 'groups'), parts along dimension 2, may hold values from 0 to 2047
- send_counts: int32 [4, 2, 16], P('facex', 'facey', 'groups'), parts along dimension 2, may hold values from 0 to 32, as said below
- kernels: float32 [4, 2, 16, 24, 32], P('facex', 'facey', 'groups'), parts along dimension 2, may hold values from 0.02 to 0.2
- observed: float32 [4, 2, 16, 32], P('facex', 'facey', 'groups'), parts along dimension 2, may hold values from -8 to 8
- error_weight: float32 [4, 2, 16, 32], P('facex', 'facey', 'groups'), parts along dimension 2, may hold values from 1 to 4
- regrid_index: int32 [4, 2, 16, 128], P('facex', 'facey'), may hold values from 0 to 2047, as said below
- regrid_weight: float32 [4, 2, 16, 128], P('facex', 'facey'), may hold values from 0.02 to 0.12
Outputs:
- advanced: float32 [8, 48, 64, 256], P('lev', 'groups', 'facex', 'facey'), parts along dimension 1
- gradient_latlon: float32 [8, 4, 2, 256], P('lev', 'facex', 'facey', 'groups'), parts along dimension 3
The draws below stay inside these ranges and needn't reach their ends.
There are 2 independent parts, one for each index of `groups`. The reference program is written for one: setup_inputs(seed, part) draws one part's arguments, and reference() takes and returns one part's arrays. A program takes and returns all parts, laid end to end along the dimension named above; an argument that names none is the same for every part. Nothing has to cross between parts.
Inputs may be any that keep to these rules, and one draw needn't show every extreme that they name: `send_counts`: slots at and beyond the count are unused. In every draw one owner holds 32 soundings from every tile. `regrid_index`: x * 32 + r of a cell in the band of the lat-lon tile.
All inputs are finite; a program needn't handle non-finite values.
Results may differ from the reference program's by a relative error of at most 0.0003.
Values sent between devices are 32-bit elements; how exact they have to be, the bound alone decides.
No kernel may reach another device: no remote copies, remote signals or barrier semaphores. Data moves between devices by JAX's collectives and lax.ppermute only.
A program may use at most 128 MiB of HBM per device.

```python
import math
import jax
import jax.numpy as jnp
from jax import lax

TRACERS = 8
LEV = 24
CX = 16
CY = 128
CAP = 32
RATIO = 4
TAPS = 16
NX = 64
NY = 256
TILES = 8
SUB = 32
LL = 128
N_FACEX = 4
N_FACEY = 2


def draw_send_counts(key, part):
    key = jax.random.fold_in(key, 11)
    key_draw, key_busy, key_full = jax.random.split(key, 3)
    grid_shape = (N_FACEX, N_FACEY, N_FACEX * N_FACEY)
    drawn = jax.random.randint(key_draw, grid_shape, 0, CAP + 1)
    busy_level = jax.random.randint(key_busy, (N_FACEX, N_FACEY, 1), 1, 5)
    counts = jnp.minimum(CAP, drawn * busy_level // 2)
    full_owner = jax.random.randint(key_full, (), 0, N_FACEX * N_FACEY)
    owners = jnp.arange(N_FACEX * N_FACEY)[None, None, :]
    return jnp.where(owners == full_owner, CAP, counts).astype(jnp.int32)


def draw_regrid_index(key, part):
    key = jax.random.fold_in(key, 23)
    key_east, key_north = jax.random.split(key, 2)
    lon_count = NX // RATIO
    grid_shape = (N_FACEX, N_FACEY, TAPS, LL)
    tap_ids = jnp.arange(TAPS)[None, None, :, None]
    cell_ids = jnp.arange(LL)[None, None, None, :]
    pinned = (tap_ids == TAPS - 1) & (cell_ids == LL - 1) | (tap_ids == 0) & (cell_ids == 0)
    shift_east = jnp.where(pinned, 0, jax.random.randint(key_east, grid_shape, -1, 2))
    shift_north = jnp.where(pinned, 0, jax.random.randint(key_north, grid_shape, -1, 2))
    column = jnp.mod(RATIO * (cell_ids % lon_count) + tap_ids % RATIO + shift_east, NX)
    row_index = jnp.clip(RATIO * (cell_ids // lon_count) + tap_ids // RATIO + shift_north, 0, SUB - 1)
    return (column * SUB + row_index).astype(jnp.int32)


def plant(entries, rng, low, high):
    spot = [jax.random.randint(jax.random.fold_in(rng, axis), (), 0, length) for axis, length in enumerate(entries.shape)]
    main_axis = entries.shape.index(max(entries.shape))
    next_to = spot[:main_axis] + [(spot[main_axis] + 1) % entries.shape[main_axis]] + spot[main_axis + 1:]
    return entries.at[tuple(spot)].set(low).at[tuple(next_to)].set(high)


def steps_of(key, shape, shards, low, largest):
    loudness = 1.0
    for position, blocks in shards:
        heights = jax.random.uniform(jax.random.fold_in(jax.random.fold_in(key, 6), position), (blocks,), jnp.float32, low / len(shards), largest / len(shards))
        loudness = loudness * jnp.repeat(jnp.exp(heights), shape[position] // blocks).reshape((-1,) + (1,) * (len(shape) - 1 - position))
    return loudness


def normal_values(key, dims, deviation, bound, shards=(), kind=jnp.bfloat16):
    values = deviation * jax.random.normal(key, dims, jnp.float32)
    if shards:
        values = values * steps_of(key, dims, shards, -0.22, 0.18)
    return jnp.clip(values, -bound, bound).astype(kind)


def setup_inputs(seed: int = 0, part: int = 0) -> dict:
    keys = jax.random.split(jax.random.key(seed), 14)
    part_splits = jax.random.split(jax.random.fold_in(keys[13], part), 14)
    return {
        "tracer": normal_values(part_splits[0], (TRACERS, LEV, NX, NY), 1.0, 6.0, ((0, 2), (2, 4), (3, 2)), jnp.float32),
        "west_courant": jnp.clip(jax.random.uniform(part_splits[1], (LEV, NX, NY), jnp.float32, -0.24, 0.24) * steps_of(part_splits[1], (LEV, NX, NY), ((1, 4), (2, 2)), -0.4, 0.0), -0.24, 0.24),
        "south_courant": jnp.clip(jax.random.uniform(part_splits[2], (LEV, NX, NY), jnp.float32, -0.24, 0.24) * steps_of(part_splits[2], (LEV, NX, NY), ((1, 4), (2, 2)), -0.4, 0.0), -0.24, 0.24),
        "mixing": jnp.clip(jnp.exp(math.log(5.0) - 4.6051702 * jax.random.uniform(part_splits[3], (LEV - 1, NX, NY), jnp.float32) ** steps_of(part_splits[3], (LEV - 1, NX, NY), ((1, 4), (2, 2)), -0.2, 0.2)), 0.05, 5.0),
        "adjoint_later": normal_values(part_splits[4], (TRACERS, LEV, NX, NY), 1.0, 6.0, ((0, 2), (2, 4), (3, 2)), jnp.float32),
        "emission_scale": jnp.clip(jnp.exp(math.log(3.0) - 2.3025851 * jax.random.uniform(keys[5], (NX, NY), jnp.float32) ** steps_of(keys[5], (NX, NY), ((0, 4), (1, 2)), -0.2, 0.2)), 0.3, 3.0),
        "send_cells": plant(jax.random.randint(part_splits[6], (N_FACEX, N_FACEY, TILES, CAP), 0, CX * CY), jax.random.fold_in(part_splits[6], 1), 0, (CX * CY) - 1).astype(jnp.int32),
        "send_counts": draw_send_counts(jax.random.fold_in(jax.random.fold_in(keys[13], part), 71), part),
        "kernels": jnp.clip(jnp.exp(math.log(0.2) - 2.3025851 * jax.random.uniform(part_splits[8], (N_FACEX, N_FACEY, TILES, LEV, CAP), jnp.float32) ** steps_of(part_splits[8], (N_FACEX, N_FACEY, TILES, LEV, CAP), ((0, 4), (1, 2)), -0.2, 0.2)), 0.02, 0.2),
        "observed": normal_values(part_splits[9], (N_FACEX, N_FACEY, TILES, CAP), 2.0, 8.0, ((0, 4), (1, 2)), jnp.float32),
        "error_weight": jnp.clip(jnp.exp(math.log(4.0) - 1.3862944 * jax.random.uniform(part_splits[10], (N_FACEX, N_FACEY, TILES, CAP), jnp.float32) ** steps_of(part_splits[10], (N_FACEX, N_FACEY, TILES, CAP), ((0, 4), (1, 2)), -0.2, 0.2)), 1.0, 4.0),
        "regrid_index": draw_regrid_index(jax.random.fold_in(keys[13], 71), part),
        "regrid_weight": jnp.clip(jnp.exp(math.log(0.12) - 1.7917595 * jax.random.uniform(keys[12], (N_FACEX, N_FACEY, TAPS, LL), jnp.float32) ** steps_of(keys[12], (N_FACEX, N_FACEY, TAPS, LL), ((0, 4), (1, 2)), -0.2, 0.2)), 0.02, 0.12),
    }


def factor(mixing):
    levels = mixing.shape[0] + 1
    inverse = []
    upper_ratio = []
    for level_index in range(levels):
        diagonal = 1.0 + jnp.zeros_like(mixing[0])
        if level_index > 0:
            diagonal = diagonal + mixing[level_index - 1]
        if level_index < levels - 1:
            diagonal = diagonal + mixing[level_index]
        if level_index > 0:
            diagonal = diagonal - mixing[level_index - 1] * mixing[level_index - 1] * inverse[level_index - 1]
        inverse.append(1.0 / diagonal)
        if level_index < levels - 1:
            upper_ratio.append(-mixing[level_index] * inverse[level_index])
    return inverse, upper_ratio


def solve_column(source, mixing, inverse, upper_ratio):
    levels = len(inverse)
    forward = []
    for level_index in range(levels):
        running = source[:, level_index]
        if level_index > 0:
            running = running + mixing[level_index - 1] * forward[level_index - 1]
        forward.append(running * inverse[level_index])
    result = list(forward)
    for level_index in range(levels - 2, -1, -1):
        result[level_index] = forward[level_index] - upper_ratio[level_index] * result[level_index + 1]
    return jnp.stack(result, axis=1)


def advance(middle, west_side, east_side, south_side, north_side, west_courant, courant_east, south_courant, courant_north):
    flux_west = jnp.maximum(west_courant, 0.0) * west_side + jnp.minimum(west_courant, 0.0) * middle
    flux_east = jnp.maximum(courant_east, 0.0) * middle + jnp.minimum(courant_east, 0.0) * east_side
    flux_south = jnp.maximum(south_courant, 0.0) * south_side + jnp.minimum(south_courant, 0.0) * middle
    flux_north = jnp.maximum(courant_north, 0.0) * middle + jnp.minimum(courant_north, 0.0) * north_side
    return middle + flux_west - flux_east + flux_south - flux_north


def retreat(middle, west_side, east_side, south_side, north_side, west_courant, courant_east, south_courant, courant_north):
    along_x = (jnp.minimum(west_courant, 0.0) - jnp.maximum(courant_east, 0.0)) * middle + jnp.maximum(courant_east, 0.0) * east_side - jnp.minimum(west_courant, 0.0) * west_side
    along_y = (jnp.minimum(south_courant, 0.0) - jnp.maximum(courant_north, 0.0)) * middle + jnp.maximum(courant_north, 0.0) * north_side - jnp.minimum(south_courant, 0.0) * south_side
    return middle + along_x + along_y


def neighbours(field):
    west_side = jnp.roll(field, 1, axis=2)
    east_side = jnp.roll(field, -1, axis=2)
    zero_row = jnp.zeros_like(field[..., :1])
    south_side = jnp.concatenate([zero_row, field[..., :-1]], axis=-1)
    north_side = jnp.concatenate([field[..., 1:], zero_row], axis=-1)
    return field, west_side, east_side, south_side, north_side


def weigh_residual(modeled, counts, observed, weights, slot_count):
    live = jnp.arange(slot_count)[None, :] < counts[:, None]
    return jnp.where(live, weights * (modeled - observed), 0.0)


def take_band(band_flat, tap_ids):
    return jnp.take(band_flat, tap_ids, axis=1)


def reference(tracer, west_courant, south_courant, mixing, adjoint_later, emission_scale, send_cells, send_counts, kernels, observed, error_weight, regrid_index, regrid_weight):
    tile_count = N_FACEX * N_FACEY
    inverse, upper_ratio = factor(mixing)
    courant_east = jnp.roll(west_courant, -1, axis=1)
    courant_north = jnp.concatenate([south_courant[..., 1:], jnp.zeros_like(south_courant[..., :1])], axis=-1)
    middle, west_side, east_side, south_side, north_side = neighbours(tracer)
    upwinded = advance(middle, west_side, east_side, south_side, north_side, west_courant, courant_east, south_courant, courant_north)
    advanced = solve_column(upwinded, mixing, inverse, upper_ratio)
    tile_fields = advanced.reshape(TRACERS, LEV, N_FACEX, CX, N_FACEY, CY).transpose(2, 4, 0, 1, 3, 5).reshape(tile_count, TRACERS, LEV, CX * CY)
    cell_table = send_cells.reshape(tile_count, tile_count, CAP)
    count_table = send_counts.reshape(tile_count, tile_count)
    kernel_table = kernels.reshape(tile_count, tile_count, LEV, CAP)
    observed_table = observed.reshape(tile_count, tile_count, CAP)
    weight_table = error_weight.reshape(tile_count, tile_count, CAP)

    def per_source(source_id):
        cell_ids = cell_table[source_id].reshape(-1)
        picked = jnp.take(tile_fields[source_id], cell_ids, axis=2).reshape(TRACERS, LEV, tile_count, CAP)
        column_total = jnp.sum(picked, axis=0).transpose(1, 0, 2)
        kernel_here = kernel_table[:, source_id]
        modeled = jnp.sum(kernel_here * column_total, axis=1)
        weighted = weigh_residual(modeled, count_table[source_id], observed_table[:, source_id], weight_table[:, source_id], CAP)
        returned = (kernel_here * weighted[:, None, :]).transpose(1, 0, 2).reshape(LEV, -1)
        return jnp.zeros((LEV, CX * CY), jnp.float32).at[:, cell_ids].add(returned)

    forcing = lax.map(per_source, jnp.arange(tile_count))
    forcing = forcing.reshape(N_FACEX, N_FACEY, LEV, CX, CY).transpose(2, 0, 3, 1, 4).reshape(LEV, NX, NY)
    forced = adjoint_later + forcing[None]
    smoothed = solve_column(forced, mixing, inverse, upper_ratio)
    middle, west_side, east_side, south_side, north_side = neighbours(smoothed)
    swept_back = retreat(middle, west_side, east_side, south_side, north_side, west_courant, courant_east, south_courant, courant_north)
    surface = swept_back[:, 0] * emission_scale
    band_slabs = surface.reshape(TRACERS, NX, N_FACEY, N_FACEX, SUB).transpose(3, 2, 0, 1, 4).reshape(tile_count, TRACERS, NX * SUB)
    tap_table = regrid_index.reshape(tile_count, TAPS * LL)
    gathered = jax.vmap(take_band)(band_slabs, tap_table).reshape(tile_count, TRACERS, TAPS, LL)
    latlon = jnp.sum(gathered * regrid_weight.reshape(tile_count, 1, TAPS, LL), axis=2)
    latlon = latlon.reshape(N_FACEX, N_FACEY, TRACERS, LL).transpose(2, 0, 1, 3)
    return advanced, latlon
```

```python
import functools

import jax
import jax.numpy as jnp
from jax import lax
from jax.experimental import pallas as pl
from jax.experimental.pallas import tpu as pltpu
from jax.sharding import PartitionSpec as P

F32 = jnp.float32
BF16 = jnp.bfloat16
LANES = 128


def call(body, outs, ins, name, flops, smem=()):
    moved = sum(4 * a.size for a in ins) + sum(4 * o.size for o in outs)
    return pl.pallas_call(
        body,
        out_shape=outs,
        in_specs=[
            pl.BlockSpec(memory_space=pltpu.SMEM if i in smem else pltpu.VMEM)
            for i in range(len(ins))
        ],
        out_specs=[pl.BlockSpec(memory_space=pltpu.VMEM)] * len(outs),
        compiler_params=pltpu.CompilerParams(vmem_limit_bytes=40 << 20),
        cost_estimate=pl.CostEstimate(flops=flops, bytes_accessed=moved, transcendentals=0),
        name=name,
    )(*ins)


def shape(*dims, dtype=F32):
    return jax.ShapeDtypeStruct(dims, dtype)


def iota(dims, axis):
    return lax.broadcasted_iota(jnp.int32, dims, axis)


def halves(values):
    high = values.astype(BF16)
    return high, (values - high.astype(F32)).astype(BF16)


def tile_of(sizes):
    return lax.axis_index("facex") * sizes[1] + lax.axis_index("facey")


def is_even(axis):
    return lax.rem(lax.axis_index(axis), 2) == 0


def down(values):
    rolled = pltpu.roll(values, 1, 0)
    return jnp.where(iota(values.shape, 0) == 0, 0.0, rolled)


def up(values):
    rows = values.shape[0]
    rolled = pltpu.roll(values, rows - 1, 0)
    return jnp.where(iota(values.shape, 0) == rows - 1, 0.0, rolled)


def right(values):
    rolled = pltpu.roll(values, 1, 1)
    return jnp.where(iota(values.shape, 1) == 0, 0.0, rolled)


def left(values):
    lanes = values.shape[1]
    rolled = pltpu.roll(values, lanes - 1, 1)
    return jnp.where(iota(values.shape, 1) == lanes - 1, 0.0, rolled)


def inner_step(cells, west, south):
    flux_x = jnp.maximum(west, 0.0) * down(cells) + jnp.minimum(west, 0.0) * cells
    flux_y = jnp.maximum(south, 0.0) * right(cells) + jnp.minimum(south, 0.0) * cells
    return cells + flux_x - up(flux_x) + flux_y - left(flux_y)


def pack_kernel(sizes, plan, *refs):
    tracer, west, south, scale, kernels, observed, weights = refs[:7]
    rows_out = refs[7:9]
    lanes_out = refs[9 : 9 + plan["y_ops"]]
    own_out = refs[9 + plan["y_ops"]]
    block_outs = refs[10 + plan["y_ops"] :]
    carried, levels, cx, cy = tracer.shape
    me = tile_of(sizes)

    def block(offset):
        where_to = jnp.bitwise_xor(me, offset)
        mine = kernels[where_to]
        last = jnp.concatenate(
            [
                observed[pl.ds(where_to, 1), :],
                weights[pl.ds(where_to, 1), :],
                jnp.zeros((6, mine.shape[1]), F32),
            ],
            axis=0,
        )
        return jnp.concatenate([mine[8 * g : 8 * g + 8] for g in range(levels // 8)] + [last], axis=1)

    even_x = is_even("facex")
    head = (carried + 1) * levels
    for number, out in enumerate(rows_out):
        sends_last = even_x if number == 0 else jnp.logical_not(even_x)
        row = jnp.where(sends_last, cx - 1, 0)
        for level in range(levels):
            for t in range(carried):
                out[t * levels + level : t * levels + level + 1, :] = tracer[
                    t, level, pl.ds(row, 1), :
                ]
            out[carried * levels + level : carried * levels + level + 1, :] = west[
                level, pl.ds(row, 1), :
            ]
        out[head : head + 8, :] = jnp.broadcast_to(scale[pl.ds(row, 1), :], (8, cy))
        if plan["x_blocks"][number]:
            out[head + 8 : head + 16, :] = block(plan["x_blocks"][number])
    even_y = is_even("facey")
    lane = iota((cx, cy), 1)
    for number, out in enumerate(lanes_out):
        sends_last = even_y if number == 0 else jnp.logical_not(even_y)
        edge = jnp.where(sends_last, cy - 1, 0)
        packed = jnp.zeros((cx, cy), F32)
        for f in range(carried + 1):
            for level in range(levels):
                values = tracer[f, level] if f < carried else south[level]
                spot = f * levels + level
                moved = pltpu.roll(values, lax.rem(spot + cy - edge, cy), 1)
                packed = jnp.where(lane == spot, moved, packed)
        out[0:cx, :] = packed
        if number == 0:
            out[cx : cx + 8, :] = block(plan["y_block"])
    own_out[...] = block(0)
    first_core = lax.axis_index("lev") == 0
    for out, (for_first, for_second) in zip(block_outs, plan["pairs"]):
        out[...] = block(jnp.where(first_core, for_first, for_second))


def factor_kernel(sizes, *refs):
    (tracer, west, south, mixing, adjoint, cells, counts) = refs[:7]
    inverse_out, ratio_out, base_out, inner_out, columns_out, rows_out, picks_out, live_out = refs[7:]
    carried, levels, cx, cy = tracer.shape
    owners, cap = cells.shape
    slots = owners * cap
    me = tile_of(sizes)
    first = []
    before = None
    for level in range(levels):
        diagonal = jnp.ones((cx, cy), F32)
        if level > 0:
            diagonal = diagonal + mixing[level - 1]
        if level < levels - 1:
            diagonal = diagonal + mixing[level]
        if level > 0:
            diagonal = diagonal - mixing[level - 1] * mixing[level - 1] * before
        inverse = 1.0 / diagonal
        inverse_out[level] = inverse
        if level < levels - 1:
            ratio_out[level] = mixing[level] * inverse
        first.append(inverse if level == 0 else mixing[level - 1] * first[-1] * inverse)
        before = inverse
    weight = first
    for level in range(levels - 2, -1, -1):
        weight[level] = first[level] + ratio_out[level] * weight[level + 1]
    for t in range(carried):
        total = weight[0] * adjoint[t, 0]
        for level in range(1, levels):
            total = total + weight[level] * adjoint[t, level]
        base_out[t] = total
    for level in range(levels):
        total = tracer[0, level]
        for t in range(1, carried):
            total = total + tracer[t, level]
        inner_out[level] = inner_step(total, west[level], south[level])
    cell_parts = []
    live_parts = []
    slot = iota((1, cap), 1)
    for offset in range(owners):
        owner = jnp.bitwise_xor(me, offset)
        cell_parts.append(cells[pl.ds(owner, 1), :])
        live_parts.append(jnp.where(slot < counts[owner], 1.0, 0.0))
    cell = jnp.concatenate(cell_parts, axis=1)
    live_out[...] = jnp.concatenate(live_parts, axis=1)
    x_of = lax.div(cell, cy)
    y_of = lax.rem(cell, cy)
    in_row = jnp.where(iota((cx, slots), 0) == x_of, 1.0, 0.0)
    in_lane = jnp.where(iota((cy, slots), 0) == y_of, 1.0, 0.0).astype(BF16)
    rows_out[...] = in_row
    picks_out[...] = in_lane
    high, low = halves(jnp.concatenate(weight, axis=0))
    picked = jnp.dot(high, in_lane, preferred_element_type=F32)
    picked = picked + jnp.dot(low, in_lane, preferred_element_type=F32)
    for level in range(levels):
        part = picked[level * cx : (level + 1) * cx] * in_row
        columns_out[level : level + 1, :] = jnp.sum(part, axis=0, keepdims=True)


def sides(first, second):
    even_x = is_even("facex")
    return jnp.where(even_x, second, first), jnp.where(even_x, first, second)


def seam_lanes(number, sent, got, carried, levels):
    cy = sent.shape[1]
    spot = carried * levels
    lane = iota(sent.shape, 1)

    def spread(values):
        result = jnp.zeros_like(values)
        for t in range(carried):
            moved = pltpu.roll(values, (t * levels - spot) % cy, 1)
            inside = jnp.logical_and(lane >= t * levels, lane < (t + 1) * levels)
            result = jnp.where(inside, moved, result)
        return result

    even_y = is_even("facey")
    north = even_y if number == 0 else jnp.logical_not(even_y)
    beyond = spread(got)
    inside = spread(sent)
    to_north = -(jnp.maximum(beyond, 0.0) * sent + jnp.minimum(beyond, 0.0) * got)
    to_south = jnp.maximum(inside, 0.0) * got
    return jnp.where(north, to_north, to_south), jnp.where(north, cy - 1, 0)


def observe_kernel(sizes, plan, carried, *refs):
    refs = list(refs)
    inner, mixing, inverse, ratio, columns, in_row, in_lane, live = refs[:8]
    sent = refs[8:10]
    got = refs[10:12]
    refs = refs[12:]
    y_sent = refs[: plan["y_ops"]]
    y_got = refs[plan["y_ops"] : 2 * plan["y_ops"]]
    refs = refs[2 * plan["y_ops"] :]
    own = refs[0]
    n_pairs = len(plan["pairs"])
    pair_got = refs[1 : 1 + n_pairs]
    swapped = refs[1 + n_pairs] if n_pairs else None
    modeled_out, state_out = refs[-2:]
    levels, cx, cy = inner.shape
    slots = in_row.shape[1]
    head = (carried + 1) * levels

    def summed(rows):
        total = rows[0:levels]
        for t in range(1, carried):
            total = total + rows[t * levels : (t + 1) * levels]
        return total

    beyond_west, beyond_east = sides(got[0][0:head], got[1][0:head])
    at_west, at_east = sides(sent[0][0:head], sent[1][0:head])
    spot = carried * levels
    face_west = at_west[spot:head]
    face_east = beyond_east[spot:head]
    from_west = jnp.maximum(face_west, 0.0) * summed(beyond_west)
    from_east = -(
        jnp.maximum(face_east, 0.0) * summed(at_east) + jnp.minimum(face_east, 0.0) * summed(beyond_east)
    )
    lane_parts = []
    for number in range(plan["y_ops"]):
        part, spot_y = seam_lanes(number, y_sent[number][0:cx, :], y_got[number][0:cx, :], carried, levels)
        total = part
        for t in range(1, carried):
            total = total + pltpu.roll(part, (-t * levels) % cy, 1)
        lane_parts.append((total, spot_y))
    lane = iota((cx, cy), 1)
    row = iota((cx, cy), 0)
    forward = []
    for level in range(levels):
        value = inner[level]
        value = value + jnp.where(row == 0, from_west[level : level + 1], 0.0)
        value = value + jnp.where(row == cx - 1, from_east[level : level + 1], 0.0)
        for total, spot_y in lane_parts:
            moved = pltpu.roll(total, lax.rem(spot_y - level + cy, cy), 1)
            value = value + jnp.where(lane == spot_y, moved, 0.0)
        if level > 0:
            value = value + mixing[level - 1] * forward[-1]
        forward.append(value * inverse[level])
    result = forward
    for level in range(levels - 2, -1, -1):
        result[level] = forward[level] + ratio[level] * result[level + 1]
    high, low = halves(jnp.concatenate(result, axis=0))
    picks = in_lane[...]
    picked = jnp.dot(high, picks, preferred_element_type=F32)
    picked = picked + jnp.dot(low, picks, preferred_element_type=F32)

    blocks = {0: own[...], plan["y_block"]: y_got[0][cx : cx + 8, :]}
    for number in range(2):
        if plan["x_blocks"][number]:
            blocks[plan["x_blocks"][number]] = got[number][head + 8 : head + 16, :]
    first_core = lax.axis_index("lev") == 0
    for number, (for_first, for_second) in enumerate(plan["pairs"]):
        mine = pair_got[number][...]
        other = swapped[8 * number : 8 * number + 8, :]
        if for_first == for_second:
            blocks[for_first] = mine
        else:
            blocks[for_first] = jnp.where(first_core, mine, other)
            blocks[for_second] = jnp.where(first_core, other, mine)
    cap = slots // len(blocks)
    per_tile = LANES // cap
    group_of_lane = lax.div(iota((8, LANES), 1), cap)

    def gathered(group):
        tiles = []
        for start in range(0, len(blocks), per_tile):
            tile = jnp.zeros((8, LANES), F32)
            for a in range(per_tile):
                moved = pltpu.roll(blocks[start + a], (cap * (a - group)) % LANES, 1)
                tile = jnp.where(group_of_lane == a, moved, tile)
            tiles.append(tile)
        return jnp.concatenate(tiles, axis=1)

    groups = [gathered(g) for g in range(levels // 8)]
    last = gathered(levels // 8)
    total = jnp.zeros((cx, slots), F32)
    sensitivity = jnp.zeros((8, slots), F32)
    for g, kernel in enumerate(groups):
        sensitivity = sensitivity + kernel * columns[8 * g : 8 * g + 8, :]
        for l in range(8):
            level = 8 * g + l
            total = total + kernel[l : l + 1] * picked[level * cx : (level + 1) * cx]
    modeled_out[...] = jnp.sum(total * in_row[...], axis=0, keepdims=True)
    gain = jnp.sum(sensitivity, axis=0, keepdims=True) * last[1:2] * live[...]
    state_out[...] = jnp.concatenate([gain, last[0:1]], axis=0)


def force_kernel(plan, *refs):
    modeled, modeled_other, state, in_row, in_lane, base, base_other = refs[:7]
    near_out = refs[7]
    rim_outs = refs[8:]
    carried, cx, cy = base.shape
    misfit = modeled[...] + modeled_other[...] - state[1:2, :]
    force = state[0:1, :] * misfit
    high, low = halves(in_row[...] * force)
    picks = in_lane[...]
    dims = (((1,), (1,)), ((), ()))
    scattered = lax.dot_general(high, picks, dims, preferred_element_type=F32)
    scattered = scattered + lax.dot_general(low, picks, dims, preferred_element_type=F32)
    lane = iota((cx, cy), 1)
    even_y = is_even("facey")
    edges = []
    for number in range(len(rim_outs)):
        sends_last = even_y if number == 0 else jnp.logical_not(even_y)
        edges.append(jnp.where(sends_last, cy - 1, 0))
    rims = [jnp.zeros((cx, cy), F32) for _ in rim_outs]
    for t in range(2 * carried):
        values = scattered + (base[t] if t < carried else base_other[t - carried])
        near_out[t] = values
        for number, edge in enumerate(edges):
            moved = pltpu.roll(values, lax.rem(t + cy - edge, cy), 1)
            rims[number] = jnp.where(lane == t, moved, rims[number])
    for rim, out in zip(rims, rim_outs):
        out[...] = rim


def surface_kernel(sizes, plan, carried, levels, *refs):
    near, west, south, scale = refs[:4]
    got = refs[4:6]
    y_got = refs[6 : 6 + plan["y_ops"]]
    rims = refs[6 + plan["y_ops"] : 6 + 2 * plan["y_ops"]]
    outs = refs[6 + 2 * plan["y_ops"] :]
    tracers, cx, cy = near.shape
    band = cy // sizes[0]
    per_tile = min(tracers, LANES // band)
    spot = carried * levels
    head = (carried + 1) * levels
    lane = iota((cx, cy), 1)
    row = iota((cx, cy), 0)
    even_y = is_even("facey")
    face_west = west[...]
    face_south = south[...]
    scales = scale[...]
    beyond_west, beyond_east = sides(got[0][head : head + 1], got[1][head : head + 1])
    _, east_wind = sides(got[0][spot : spot + 1], got[1][spot : spot + 1])
    face_east = jnp.where(row == cx - 1, east_wind, pltpu.roll(face_west, cx - 1, 0))
    face_north = left(face_south)
    norths = []
    for number in range(plan["y_ops"]):
        norths.append(even_y if number == 0 else jnp.logical_not(even_y))
        moved = pltpu.roll(y_got[number][0:cx, :], cy - 1 - spot, 1)
        keep = jnp.logical_and(lane == cy - 1, norths[number])
        face_north = jnp.where(keep, moved, face_north)
    to_middle = 1.0 + jnp.minimum(face_west, 0.0) - jnp.maximum(face_east, 0.0)
    to_middle = scales * (to_middle + jnp.minimum(face_south, 0.0) - jnp.maximum(face_north, 0.0))
    to_east = jnp.where(row == cx - 1, 0.0, scales * jnp.maximum(face_east, 0.0))
    to_west = jnp.where(row == 0, 0.0, scales * jnp.minimum(face_west, 0.0))
    to_north = scales * jnp.maximum(face_north, 0.0)
    to_south = scales * jnp.minimum(face_south, 0.0)
    west_gain = beyond_west * jnp.maximum(face_west[0:1], 0.0)
    east_gain = -beyond_east * jnp.minimum(face_east[cx - 1 : cx], 0.0)
    filler = jnp.zeros((6, cy), F32)
    grown = []
    for t in range(tracers):
        values = near[t]
        north_side = left(values)
        south_side = right(values)
        for number in range(plan["y_ops"]):
            rim = rims[number][...]
            at_north = jnp.logical_and(lane == cy - 1, norths[number])
            at_south = jnp.logical_and(lane == 0, jnp.logical_not(norths[number]))
            north_side = jnp.where(at_north, pltpu.roll(rim, (cy - 1 - t) % cy, 1), north_side)
            south_side = jnp.where(at_south, pltpu.roll(rim, (-t) % cy, 1), south_side)
        swept = to_middle * values + to_east * pltpu.roll(values, cx - 1, 0) - to_west * pltpu.roll(values, 1, 0)
        swept = swept + to_north * north_side - to_south * south_side
        grown.append(
            jnp.concatenate(
                [swept, west_gain * values[0:1], east_gain * values[cx - 1 : cx], filler], axis=0
            )
        )
    rows = cx + 8
    group_of_lane = lax.div(iota((rows, cy), 1), band)
    first_core = lax.axis_index("lev") == 0
    place = lax.axis_index("facex")
    for out, (for_first, for_second) in zip(outs, plan["bands"]):
        offset = for_first if for_first == for_second else jnp.where(first_core, for_first, for_second)
        target = jnp.bitwise_xor(place, offset)
        count = carried if for_first == for_second else tracers
        for start in range(0, count, per_tile):
            tile = jnp.zeros((rows, cy), F32)
            for a in range(min(per_tile, count - start)):
                moved = pltpu.roll(grown[start + a], lax.rem(band * a + cy - band * target, cy), 1)
                tile = jnp.where(group_of_lane == a, moved, tile)
            out[start // per_tile * rows : (start // per_tile + 1) * rows, :] = tile


def regrid_kernel(sizes, plan, carried, cx, band, *refs):
    index, weight = refs[:2]
    blocks = refs[2:-1]
    out = refs[-1]
    taps, cells = index.shape
    tracers = 2 * carried
    rows = cx + 8
    per_tile = min(tracers, LANES // band)
    lane = iota((rows, LANES), 1)
    row = iota((rows, cells), 0)
    first_core = lax.axis_index("lev") == 0
    place = lax.axis_index("facex")
    around = sizes[0] * cx
    parts = []
    row_places = []
    for block, (for_first, for_second) in zip(blocks, plan["bands"]):
        offset = for_first if for_first == for_second else jnp.where(first_core, for_first, for_second)
        start = jnp.bitwise_xor(place, offset) * cx
        places = start + row
        places = jnp.where(row == cx, lax.rem(start + around - 1, around), places)
        places = jnp.where(row == cx + 1, lax.rem(start + cx, around), places)
        row_places.append(places)
        count = carried if for_first == for_second else tracers
        mine = []
        for t in range(count):
            tile = block[t // per_tile * rows : (t // per_tile + 1) * rows, :]
            a = t % per_tile
            values = tile if a == 0 else pltpu.roll(tile, (-band * a) % LANES, 1)
            high = values.astype(BF16).astype(F32)
            low = pltpu.roll(values - high, band, 1)
            both = jnp.where(lane < band, high, jnp.where(lane < 2 * band, low, 0.0))
            mine.append(both.astype(BF16))
        parts.append(mine)
    left_side = jnp.concatenate([jnp.concatenate(mine, axis=0) for mine in parts], axis=0)
    spread = iota((LANES, cells), 0)
    in_band = lax.rem(spread, band)
    used = spread < 2 * band
    totals = [[jnp.zeros((rows, cells), F32) for _ in mine] for mine in parts]
    for tap in range(taps):
        place_of = index[tap : tap + 1, :]
        column = lax.div(place_of, band)
        in_lane = lax.rem(place_of, band)
        picks = jnp.where(jnp.logical_and(in_band == in_lane, used), 1.0, 0.0).astype(BF16)
        picked = jnp.dot(left_side, picks, preferred_element_type=F32)
        at = 0
        for number, mine in enumerate(parts):
            chosen = jnp.where(row_places[number] == column, weight[tap : tap + 1, :], 0.0)
            for t in range(len(mine)):
                totals[number][t] = totals[number][t] + chosen * picked[at : at + rows]
                at += rows
    sums = [jnp.zeros((1, cells), F32) for _ in range(tracers)]
    for mine in totals:
        for t, total in enumerate(mine):
            sums[t] = sums[t] + jnp.sum(total, axis=0, keepdims=True)
    out[...] = jnp.concatenate(sums, axis=0)


def advance_kernel(plan, *refs):
    tracer, west, south, mixing, inverse, ratio = refs[:6]
    sent = refs[6:8]
    got = refs[8:10]
    y_sent = refs[10 : 10 + plan["y_ops"]]
    y_got = refs[10 + plan["y_ops"] : 10 + 2 * plan["y_ops"]]
    out = refs[-1]
    carried, levels, cx, cy = tracer.shape
    head = (carried + 1) * levels
    spot = carried * levels
    beyond_west, beyond_east = sides(got[0][0:head], got[1][0:head])
    at_west, at_east = sides(sent[0][0:head], sent[1][0:head])
    face_west = at_west[spot:head]
    face_east = beyond_east[spot:head]
    lane = iota((cx, cy), 1)
    row = iota((cx, cy), 0)
    seams = [
        seam_lanes(n, y_sent[n][0:cx, :], y_got[n][0:cx, :], carried, levels) for n in range(plan["y_ops"])
    ]
    for t in range(carried):
        part = slice(t * levels, (t + 1) * levels)
        from_west = jnp.maximum(face_west, 0.0) * beyond_west[part]
        from_east = -(
            jnp.maximum(face_east, 0.0) * at_east[part] + jnp.minimum(face_east, 0.0) * beyond_east[part]
        )
        result = []
        for level in range(levels):
            value = inner_step(tracer[t, level], west[level], south[level])
            value = value + jnp.where(row == 0, from_west[level : level + 1], 0.0)
            value = value + jnp.where(row == cx - 1, from_east[level : level + 1], 0.0)
            for packed, spot_y in seams:
                moved = pltpu.roll(packed, lax.rem(spot_y - (t * levels + level) + 2 * cy, cy), 1)
                value = value + jnp.where(lane == spot_y, moved, 0.0)
            if level > 0:
                value = value + mixing[level - 1] * result[-1]
            result.append(value * inverse[level])
        out[t, levels - 1] = result[-1]
        for level in range(levels - 2, -1, -1):
            result[level] = result[level] + ratio[level] * result[level + 1]
            out[t, level] = result[level]


GROUP = ("facex", "facey", "lev")


def exchange(values, sizes, rule):
    many_x, many_y, cores = sizes
    pairs = []
    for x in range(many_x):
        for y in range(many_y):
            for c in range(cores):
                to = rule(x, y, c)
                if to is not None:
                    pairs.append(((x * many_y + y) * cores + c, (to[0] * many_y + to[1]) * cores + to[2]))
    return lax.ppermute(values, GROUP, pairs)


def make_plan(sizes):
    many_x, many_y, _ = sizes
    tiles = many_x * many_y
    x_blocks = [many_y, (many_x - 1) * many_y if many_x == 4 else 0]
    taken = {0, 1, *x_blocks}
    rest = [d for d in range(tiles) if d not in taken]
    rest.sort(key=lambda d: (d // many_y != many_x // 2, d))
    pairs = [(rest[n], rest[min(n + 1, len(rest) - 1)]) for n in range(0, len(rest), 2)]
    others = list(range(many_x - 1, 1, -1))
    bands = [(0, 0), (1, 1)] + [(others[n], others[n + 1]) for n in range(0, len(others), 2)]
    return {
        "x_blocks": x_blocks,
        "y_block": 1,
        "y_ops": 1 if many_y == 2 else 2,
        "pairs": pairs,
        "bands": bands,
    }


def local(
    sizes,
    tracer,
    west_courant,
    south_courant,
    mixing,
    adjoint_later,
    emission_scale,
    send_cells,
    send_counts,
    kernels,
    observed,
    error_weight,
    regrid_index,
    regrid_weight,
):
    plan = make_plan(sizes)
    many_x, many_y, _ = sizes
    carried, levels, cx, cy = tracer.shape
    owners, cap = send_cells.shape[2:]
    slots = owners * cap
    taps, ll = regrid_index.shape[2:]
    head = (carried + 1) * levels
    y_ops = plan["y_ops"]
    band = cy // many_x

    def next_x(number):
        def rule(x, y, c):
            step = 1 if (x % 2 == 0) == (number == 0) else -1
            return ((x + step) % many_x, y, c)

        return rule

    def next_y(number):
        def rule(x, y, c):
            to = y + (1 if (y % 2 == 0) == (number == 0) else -1)
            return (x, to, c) if 0 <= to < many_y else None

        return rule

    def jump(for_first, for_second):
        def rule(x, y, c):
            d = for_first if c == 0 else for_second
            return (x ^ (d // many_y), y ^ (d % many_y), c)

        return rule

    def other_core(values):
        return exchange(values, sizes, lambda x, y, c: (x, y, 1 - c))

    row_shapes = [shape(head + (16 if plan["x_blocks"][n] else 8), cy) for n in range(2)]
    lane_shapes = [shape(cx + (8 if n == 0 else 0), cy) for n in range(y_ops)]
    packed = call(
        functools.partial(pack_kernel, sizes, plan),
        row_shapes + lane_shapes + [shape(8, LANES)] * (1 + len(plan["pairs"])),
        [
            tracer,
            west_courant,
            south_courant,
            emission_scale,
            kernels.reshape(owners, levels, cap),
            observed.reshape(owners, cap),
            error_weight.reshape(owners, cap),
        ],
        "pack",
        100000,
    )
    rows_sent = packed[:2]
    lanes_sent = packed[2 : 2 + y_ops]
    own_block = packed[2 + y_ops]
    pair_sent = packed[3 + y_ops :]
    rows_got = [exchange(rows_sent[n], sizes, next_x(n)) for n in range(2)]
    lanes_got = [exchange(lanes_sent[n], sizes, next_y(n)) for n in range(y_ops)]
    pair_got = [exchange(s, sizes, jump(*p)) for s, p in zip(pair_sent, plan["pairs"])]
    inverse, ratio, base, inner, columns, in_row, in_lane, live = call(
        functools.partial(factor_kernel, sizes),
        [
            shape(levels, cx, cy),
            shape(levels - 1, cx, cy),
            shape(carried, cx, cy),
            shape(levels, cx, cy),
            shape(levels, slots),
            shape(cx, slots),
            shape(cy, slots, dtype=BF16),
            shape(1, slots),
        ],
        [
            tracer,
            west_courant,
            south_courant,
            mixing,
            adjoint_later,
            send_cells.reshape(owners, cap),
            send_counts.reshape(owners),
        ],
        "factor",
        3000000,
        smem=(6,),
    )
    base_other = other_core(base)
    swapped = [other_core(jnp.concatenate(pair_got, axis=0))] if pair_got else []
    modeled, state = call(
        functools.partial(observe_kernel, sizes, plan, carried),
        [shape(1, slots), shape(2, slots)],
        [inner, mixing, inverse, ratio, columns, in_row, in_lane, live]
        + list(rows_sent)
        + rows_got
        + list(lanes_sent)
        + lanes_got
        + [own_block]
        + pair_got
        + swapped,
        "observe",
        2000000,
    )
    modeled_other = other_core(modeled)
    (advanced,) = call(
        functools.partial(advance_kernel, plan),
        [shape(*tracer.shape)],
        [tracer, west_courant, south_courant, mixing, inverse, ratio]
        + list(rows_sent)
        + rows_got
        + list(lanes_sent)
        + lanes_got,
        "advance",
        6000000,
    )
    near, *rims_sent = call(
        functools.partial(force_kernel, plan),
        [shape(2 * carried, cx, cy)] + [shape(cx, cy)] * y_ops,
        [modeled, modeled_other, state, in_row, in_lane, base, base_other],
        "force",
        200000,
    )
    rims_got = [exchange(rims_sent[n], sizes, next_y(n)) for n in range(y_ops)]
    per_tile = min(2 * carried, LANES // band)

    def band_shape(first, second):
        count = carried if first == second else 2 * carried
        return shape(-(-count // per_tile) * (cx + 8), cy)

    band_sent = call(
        functools.partial(surface_kernel, sizes, plan, carried, levels),
        [band_shape(*b) for b in plan["bands"]],
        [near, west_courant[0], south_courant[0], emission_scale] + rows_got + lanes_got + rims_got,
        "surface",
        400000,
    )
    band_got = [
        s if first == second == 0 else exchange(s, sizes, jump(first * many_y, second * many_y))
        for s, (first, second) in zip(band_sent, plan["bands"])
    ]
    (sums,) = call(
        functools.partial(regrid_kernel, sizes, plan, carried, cx, band),
        [shape(2 * carried, ll)],
        [regrid_index.reshape(taps, ll), regrid_weight.reshape(taps, ll)] + band_got,
        "regrid",
        1000000,
    )
    sums_other = other_core(sums[carried:])
    latlon = sums[:carried] + sums_other
    return (advanced, latlon[:, None, None, :])


def solution(mesh):
    in_specs = (
        P("lev", "groups", "facex", "facey"),
        P("groups", "facex", "facey"),
        P("groups", "facex", "facey"),
        P("groups", "facex", "facey"),
        P("lev", "groups", "facex", "facey"),
        P("facex", "facey"),
        P("facex", "facey", "groups", None),
        P("facex", "facey", "groups"),
        P("facex", "facey", "groups", None, None),
        P("facex", "facey", "groups", None),
        P("facex", "facey", "groups", None),
        P("facex", "facey", None, None),
        P("facex", "facey", None, None),
    )
    out_specs = (P("lev", "groups", "facex", "facey"), P("lev", "facex", "facey", "groups"))
    sizes = tuple(mesh.shape[axis] for axis in GROUP)
    return jax.shard_map(
        functools.partial(local, sizes), mesh=mesh, in_specs=in_specs, out_specs=out_specs, check_vma=False
    )
```

```python
import functools

import jax
import jax.numpy as jnp
from jax import lax
from jax.experimental import pallas as pl
from jax.experimental.pallas import tpu as pltpu
from jax.sharding import PartitionSpec as P

F32 = jnp.float32
BF16 = jnp.bfloat16
LANES = 128


def call(body, outs, ins, name, flops, smem=(), hbm=(), scratch=(), out_hbm=()):
    moved = sum(4 * a.size for a in ins) + sum(4 * o.size for o in outs)
    ins = [pltpu.with_memory_space_constraint(a, pltpu.HBM) if i in hbm else a for i, a in enumerate(ins)]

    def space(number):
        return pltpu.SMEM if number in smem else pltpu.HBM if number in hbm else pltpu.VMEM

    return pl.pallas_call(
        body,
        out_shape=outs,
        in_specs=[pl.BlockSpec(memory_space=space(i)) for i in range(len(ins))],
        out_specs=[
            pl.BlockSpec(memory_space=pltpu.HBM if i in out_hbm else pltpu.VMEM) for i in range(len(outs))
        ],
        scratch_shapes=scratch,
        compiler_params=pltpu.CompilerParams(vmem_limit_bytes=40 << 20),
        cost_estimate=pl.CostEstimate(flops=flops, bytes_accessed=moved, transcendentals=0),
        name=name,
    )(*ins)


def shape(*dims, dtype=F32):
    return jax.ShapeDtypeStruct(dims, dtype)


def iota(dims, axis):
    return lax.broadcasted_iota(jnp.int32, dims, axis)


def halves(values):
    high = values.astype(BF16)
    return high, (values - high.astype(F32)).astype(BF16)


def tile_of(sizes):
    return lax.axis_index("facex") * sizes[1] + lax.axis_index("facey")


def is_even(axis):
    return lax.rem(lax.axis_index(axis), 2) == 0


def up(values):
    rows = values.shape[0]
    rolled = pltpu.roll(values, rows - 1, 0)
    return jnp.where(iota(values.shape, 0) == rows - 1, 0.0, rolled)


def right(values):
    rolled = pltpu.roll(values, 1, 1)
    return jnp.where(iota(values.shape, 1) == 0, 0.0, rolled)


def left(values):
    lanes = values.shape[1]
    rolled = pltpu.roll(values, lanes - 1, 1)
    return jnp.where(iota(values.shape, 1) == lanes - 1, 0.0, rolled)


def shares(west, south):
    east, north = up(west), left(south)
    middle = 1.0 + jnp.minimum(west, 0.0) - jnp.maximum(east, 0.0)
    middle = middle + jnp.minimum(south, 0.0) - jnp.maximum(north, 0.0)
    row, lane = iota(west.shape, 0), iota(west.shape, 1)
    return (
        middle,
        jnp.where(row == 0, 0.0, jnp.maximum(west, 0.0)),
        -jnp.minimum(east, 0.0),
        jnp.where(lane == 0, 0.0, jnp.maximum(south, 0.0)),
        -jnp.minimum(north, 0.0),
    )


def mix(parts, cells):
    rows, lanes = cells.shape
    middle, west, east, south, north = parts
    total = middle * cells + west * pltpu.roll(cells, 1, 0) + east * pltpu.roll(cells, rows - 1, 0)
    return total + south * pltpu.roll(cells, 1, 1) + north * pltpu.roll(cells, lanes - 1, 1)


def pack_kernel(sizes, plan, *refs):
    sources, refs = refs[:9], refs[9:]
    rows_out, refs = refs[:2], refs[2:]
    lanes_out, refs = refs[: plan["y_ops"]], refs[plan["y_ops"] :]
    own_out, refs = refs[0], refs[1:]
    block_outs, refs = refs[: len(plan["pairs"])], refs[len(plan["pairs"]) :]
    cell_out, live_out, tracer, west, south, scale, kernels, observed, weights, cells, counts, done = refs
    carried, levels, cx, cy = tracer.shape
    me = tile_of(sizes)
    copies = [
        pltpu.make_async_copy(source, target, done.at[number])
        for number, (source, target) in enumerate(
            zip(sources[1:], (west, south, scale, kernels, observed, weights, cells, counts))
        )
    ]
    copies += [
        pltpu.make_async_copy(sources[0].at[t], tracer.at[t], done.at[8 + t]) for t in range(carried)
    ]
    for number in (3, 4, 5, 6, 7, 0, 2, *range(8, 8 + carried), 1):
        copies[number].start()

    def block(offset):
        where_to = jnp.bitwise_xor(me, offset)
        mine = kernels[where_to]
        last = jnp.concatenate(
            [
                observed[pl.ds(where_to, 1), :],
                weights[pl.ds(where_to, 1), :],
                jnp.zeros((6, mine.shape[1]), F32),
            ],
            axis=0,
        )
        return jnp.concatenate([mine[8 * g : 8 * g + 8] for g in range(levels // 8)] + [last], axis=1)

    for number in (3, 4, 5):
        copies[number].wait()
    head = (carried + 1) * levels
    for number, out in enumerate(rows_out):
        if plan["x_blocks"][number]:
            out[head + 8 : head + 16, :] = block(plan["x_blocks"][number])
    lanes_out[0][cx : cx + 8, :] = block(plan["y_block"])
    own_out[...] = block(0)
    first_core = lax.axis_index("lev") == 0
    for out, (for_first, for_second) in zip(block_outs, plan["pairs"]):
        out[...] = block(jnp.where(first_core, for_first, for_second))

    owners, cap = cells.shape
    slot = iota((1, cap), 1)
    copies[6].wait()
    copies[7].wait()
    cell_parts = []
    live_parts = []
    for offset in range(owners):
        owner = jnp.bitwise_xor(me, offset)
        cell_parts.append(cells[pl.ds(owner, 1), :])
        live_parts.append(jnp.where(slot < counts[owner], 1.0, 0.0))
    cell_out[...] = jnp.concatenate(cell_parts, axis=1)
    live_out[...] = jnp.concatenate(live_parts, axis=1)

    even_x = is_even("facex")
    even_y = is_even("facey")
    last_row = [
        jnp.where(even_x if number == 0 else jnp.logical_not(even_x), cx - 1, 0)
        for number in range(len(rows_out))
    ]
    edge = [
        jnp.where(even_y if number == 0 else jnp.logical_not(even_y), cy - 1, 0)
        for number in range(len(lanes_out))
    ]
    lane = iota((cx, cy), 1)
    copies[0].wait()
    copies[2].wait()
    for row, out in zip(last_row, rows_out):
        for level in range(levels):
            spot = carried * levels + level
            out[spot : spot + 1, :] = west[level, pl.ds(row, 1), :]
        out[head : head + 8, :] = jnp.broadcast_to(scale[pl.ds(row, 1), :], (8, cy))
    packed = [jnp.zeros((cx, cy), F32) for _ in lanes_out]
    for f in range(carried + 1):
        copies[8 + f if f < carried else 1].wait()
        for level in range(levels):
            spot = f * levels + level
            values = tracer[f, level] if f < carried else south[level]
            for number, at in enumerate(edge):
                moved = pltpu.roll(values, lax.rem(spot + cy - at, cy), 1)
                packed[number] = jnp.where(lane == spot, moved, packed[number])
            if f < carried:
                for row, out in zip(last_row, rows_out):
                    out[spot : spot + 1, :] = tracer[f, level, pl.ds(row, 1), :]
    for values, out in zip(packed, lanes_out):
        out[0:cx, :] = values


def factor_kernel(sizes, *refs):
    (tracer, west, south, mixing, adjoint, cells) = refs[:6]
    inverse_out, ratio_out, base_out, inner_out, shares_out, columns_out, rows_out, picks_out = refs[6:]
    carried, levels, cx, cy = tracer.shape
    slots = cells.shape[1]
    first = []
    before = None
    for level in range(levels):
        diagonal = jnp.ones((cx, cy), F32)
        if level > 0:
            diagonal = diagonal + mixing[level - 1]
        if level < levels - 1:
            diagonal = diagonal + mixing[level]
        if level > 0:
            diagonal = diagonal - mixing[level - 1] * mixing[level - 1] * before
        inverse = 1.0 / diagonal
        inverse_out[level] = inverse
        if level < levels - 1:
            ratio_out[level] = mixing[level] * inverse
        first.append(inverse if level == 0 else mixing[level - 1] * first[-1] * inverse)
        before = inverse
    ratio_out[levels - 1] = jnp.zeros((cx, cy), F32)
    weight = first
    for level in range(levels - 2, -1, -1):
        weight[level] = first[level] + ratio_out[level] * weight[level + 1]
    for t in range(carried):
        total = weight[0] * adjoint[t, 0]
        for level in range(1, levels):
            total = total + weight[level] * adjoint[t, level]
        base_out[t] = total
    for level in range(levels):
        total = tracer[0, level]
        for t in range(1, carried):
            total = total + tracer[t, level]
        parts = shares(west[level], south[level])
        for number, part in enumerate(parts):
            shares_out[number, level] = part
        inner_out[level] = mix(parts, total)
    cell = cells[...]
    x_of = lax.div(cell, cy)
    y_of = lax.rem(cell, cy)
    in_row = jnp.where(iota((cx, slots), 0) == x_of, 1.0, 0.0)
    in_lane = jnp.where(iota((cy, slots), 0) == y_of, 1.0, 0.0).astype(BF16)
    rows_out[...] = in_row
    picks_out[...] = in_lane
    high, low = halves(jnp.concatenate(weight, axis=0))
    picked = jnp.dot(high, in_lane, preferred_element_type=F32)
    picked = picked + jnp.dot(low, in_lane, preferred_element_type=F32)
    for level in range(levels):
        part = picked[level * cx : (level + 1) * cx] * in_row
        columns_out[level : level + 1, :] = jnp.sum(part, axis=0, keepdims=True)


def sides(first, second):
    even_x = is_even("facex")
    return jnp.where(even_x, second, first), jnp.where(even_x, first, second)


def seam_lanes(number, sent, got, carried, levels):
    cy = sent.shape[1]
    spot = carried * levels
    lane = iota(sent.shape, 1)

    def spread(values):
        result = jnp.zeros_like(values)
        for t in range(carried):
            moved = pltpu.roll(values, (t * levels - spot) % cy, 1)
            inside = jnp.logical_and(lane >= t * levels, lane < (t + 1) * levels)
            result = jnp.where(inside, moved, result)
        return result

    even_y = is_even("facey")
    north = even_y if number == 0 else jnp.logical_not(even_y)
    beyond = spread(got)
    inside = spread(sent)
    to_north = -(jnp.maximum(beyond, 0.0) * sent + jnp.minimum(beyond, 0.0) * got)
    to_south = jnp.maximum(inside, 0.0) * got
    return jnp.where(north, to_north, to_south), jnp.where(north, cy - 1, 0)


def observe_kernel(sizes, plan, carried, *refs):
    refs = list(refs)
    inner, mixing, inverse, ratio, columns, in_row, in_lane, live = refs[:8]
    sent = refs[8:10]
    got = refs[10:12]
    refs = refs[12:]
    y_sent = refs[: plan["y_ops"]]
    y_got = refs[plan["y_ops"] : 2 * plan["y_ops"]]
    refs = refs[2 * plan["y_ops"] :]
    own = refs[0]
    n_pairs = len(plan["pairs"])
    pair_got = refs[1 : 1 + n_pairs]
    swapped = refs[1 + n_pairs] if n_pairs else None
    modeled_out, state_out = refs[-2:]
    levels, cx, cy = inner.shape
    slots = in_row.shape[1]
    head = (carried + 1) * levels

    def summed(rows):
        total = rows[0:levels]
        for t in range(1, carried):
            total = total + rows[t * levels : (t + 1) * levels]
        return total

    beyond_west, beyond_east = sides(got[0][0:head], got[1][0:head])
    at_west, at_east = sides(sent[0][0:head], sent[1][0:head])
    spot = carried * levels
    face_west = at_west[spot:head]
    face_east = beyond_east[spot:head]
    from_west = jnp.maximum(face_west, 0.0) * summed(beyond_west)
    from_east = -(
        jnp.maximum(face_east, 0.0) * summed(at_east) + jnp.minimum(face_east, 0.0) * summed(beyond_east)
    )
    lane_parts = []
    for number in range(plan["y_ops"]):
        part, spot_y = seam_lanes(number, y_sent[number][0:cx, :], y_got[number][0:cx, :], carried, levels)
        total = part
        for t in range(1, carried):
            total = total + pltpu.roll(part, (-t * levels) % cy, 1)
        lane_parts.append((total, spot_y))
    lane = iota((cx, cy), 1)
    row = iota((cx, cy), 0)
    forward = []
    for level in range(levels):
        value = inner[level]
        value = value + jnp.where(row == 0, from_west[level : level + 1], 0.0)
        value = value + jnp.where(row == cx - 1, from_east[level : level + 1], 0.0)
        for total, spot_y in lane_parts:
            moved = pltpu.roll(total, lax.rem(spot_y - level + cy, cy), 1)
            value = value + jnp.where(lane == spot_y, moved, 0.0)
        if level > 0:
            value = value + mixing[level - 1] * forward[-1]
        forward.append(value * inverse[level])
    result = forward
    for level in range(levels - 2, -1, -1):
        result[level] = forward[level] + ratio[level] * result[level + 1]
    high, low = halves(jnp.concatenate(result, axis=0))
    picks = in_lane[...]
    picked = jnp.dot(high, picks, preferred_element_type=F32)
    picked = picked + jnp.dot(low, picks, preferred_element_type=F32)

    blocks = {0: own[...], plan["y_block"]: y_got[0][cx : cx + 8, :]}
    for number in range(2):
        if plan["x_blocks"][number]:
            blocks[plan["x_blocks"][number]] = got[number][head + 8 : head + 16, :]
    first_core = lax.axis_index("lev") == 0
    for number, (for_first, for_second) in enumerate(plan["pairs"]):
        mine = pair_got[number][...]
        other = swapped[8 * number : 8 * number + 8, :]
        if for_first == for_second:
            blocks[for_first] = mine
        else:
            blocks[for_first] = jnp.where(first_core, mine, other)
            blocks[for_second] = jnp.where(first_core, other, mine)
    cap = slots // len(blocks)
    per_tile = LANES // cap
    group_of_lane = lax.div(iota((8, LANES), 1), cap)

    def gathered(group):
        tiles = []
        for start in range(0, len(blocks), per_tile):
            tile = jnp.zeros((8, LANES), F32)
            for a in range(per_tile):
                moved = pltpu.roll(blocks[start + a], (cap * (a - group)) % LANES, 1)
                tile = jnp.where(group_of_lane == a, moved, tile)
            tiles.append(tile)
        return jnp.concatenate(tiles, axis=1)

    groups = [gathered(g) for g in range(levels // 8)]
    last = gathered(levels // 8)
    total = jnp.zeros((cx, slots), F32)
    sensitivity = jnp.zeros((8, slots), F32)
    for g, kernel in enumerate(groups):
        sensitivity = sensitivity + kernel * columns[8 * g : 8 * g + 8, :]
        for l in range(8):
            level = 8 * g + l
            total = total + kernel[l : l + 1] * picked[level * cx : (level + 1) * cx]
    modeled_out[...] = jnp.sum(total * in_row[...], axis=0, keepdims=True)
    gain = jnp.sum(sensitivity, axis=0, keepdims=True) * last[1:2] * live[...]
    state_out[...] = jnp.concatenate([gain, last[0:1]], axis=0)


def force_kernel(plan, *refs):
    modeled, modeled_other, state, in_row, in_lane, base, base_other = refs[:7]
    near_out = refs[7]
    rim_outs = refs[8:]
    carried, cx, cy = base.shape
    misfit = modeled[...] + modeled_other[...] - state[1:2, :]
    force = state[0:1, :] * misfit
    high, low = halves(in_row[...] * force)
    picks = in_lane[...]
    dims = (((1,), (1,)), ((), ()))
    scattered = lax.dot_general(high, picks, dims, preferred_element_type=F32)
    scattered = scattered + lax.dot_general(low, picks, dims, preferred_element_type=F32)
    lane = iota((cx, cy), 1)
    even_y = is_even("facey")
    edges = []
    for number in range(len(rim_outs)):
        sends_last = even_y if number == 0 else jnp.logical_not(even_y)
        edges.append(jnp.where(sends_last, cy - 1, 0))
    rims = [jnp.zeros((cx, cy), F32) for _ in rim_outs]
    for t in range(2 * carried):
        values = scattered + (base[t] if t < carried else base_other[t - carried])
        near_out[t] = values
        for number, edge in enumerate(edges):
            moved = pltpu.roll(values, lax.rem(t + cy - edge, cy), 1)
            rims[number] = jnp.where(lane == t, moved, rims[number])
    for rim, out in zip(rims, rim_outs):
        out[...] = rim


def surface_kernel(sizes, plan, carried, levels, *refs):
    near, west, south, scale = refs[:4]
    got = refs[4:6]
    y_got = refs[6 : 6 + plan["y_ops"]]
    rims = refs[6 + plan["y_ops"] : 6 + 2 * plan["y_ops"]]
    outs = refs[6 + 2 * plan["y_ops"] :]
    tracers, cx, cy = near.shape
    band = cy // sizes[0]
    per_tile = min(tracers, LANES // band)
    spot = carried * levels
    head = (carried + 1) * levels
    lane = iota((cx, cy), 1)
    row = iota((cx, cy), 0)
    even_y = is_even("facey")
    face_west = west[...]
    face_south = south[...]
    scales = scale[...]
    beyond_west, beyond_east = sides(got[0][head : head + 1], got[1][head : head + 1])
    _, east_wind = sides(got[0][spot : spot + 1], got[1][spot : spot + 1])
    face_east = jnp.where(row == cx - 1, east_wind, pltpu.roll(face_west, cx - 1, 0))
    face_north = left(face_south)
    norths = []
    for number in range(plan["y_ops"]):
        norths.append(even_y if number == 0 else jnp.logical_not(even_y))
        moved = pltpu.roll(y_got[number][0:cx, :], cy - 1 - spot, 1)
        keep = jnp.logical_and(lane == cy - 1, norths[number])
        face_north = jnp.where(keep, moved, face_north)
    to_middle = 1.0 + jnp.minimum(face_west, 0.0) - jnp.maximum(face_east, 0.0)
    to_middle = scales * (to_middle + jnp.minimum(face_south, 0.0) - jnp.maximum(face_north, 0.0))
    to_east = jnp.where(row == cx - 1, 0.0, scales * jnp.maximum(face_east, 0.0))
    to_west = jnp.where(row == 0, 0.0, scales * jnp.minimum(face_west, 0.0))
    to_north = scales * jnp.maximum(face_north, 0.0)
    to_south = scales * jnp.minimum(face_south, 0.0)
    west_gain = beyond_west * jnp.maximum(face_west[0:1], 0.0)
    east_gain = -beyond_east * jnp.minimum(face_east[cx - 1 : cx], 0.0)
    filler = jnp.zeros((6, cy), F32)
    grown = []
    for t in range(tracers):
        values = near[t]
        north_side = left(values)
        south_side = right(values)
        for number in range(plan["y_ops"]):
            rim = rims[number][...]
            at_north = jnp.logical_and(lane == cy - 1, norths[number])
            at_south = jnp.logical_and(lane == 0, jnp.logical_not(norths[number]))
            north_side = jnp.where(at_north, pltpu.roll(rim, (cy - 1 - t) % cy, 1), north_side)
            south_side = jnp.where(at_south, pltpu.roll(rim, (-t) % cy, 1), south_side)
        swept = to_middle * values + to_east * pltpu.roll(values, cx - 1, 0) - to_west * pltpu.roll(values, 1, 0)
        swept = swept + to_north * north_side - to_south * south_side
        grown.append(
            jnp.concatenate(
                [swept, west_gain * values[0:1], east_gain * values[cx - 1 : cx], filler], axis=0
            )
        )
    rows = cx + 8
    group_of_lane = lax.div(iota((rows, cy), 1), band)
    first_core = lax.axis_index("lev") == 0
    place = lax.axis_index("facex")
    for out, (for_first, for_second) in zip(outs, plan["bands"]):
        offset = for_first if for_first == for_second else jnp.where(first_core, for_first, for_second)
        target = jnp.bitwise_xor(place, offset)
        count = carried if for_first == for_second else tracers
        for start in range(0, count, per_tile):
            tile = jnp.zeros((rows, cy), F32)
            for a in range(min(per_tile, count - start)):
                moved = pltpu.roll(grown[start + a], lax.rem(band * a + cy - band * target, cy), 1)
                tile = jnp.where(group_of_lane == a, moved, tile)
            out[start // per_tile * rows : (start // per_tile + 1) * rows, :] = tile


def regrid_kernel(sizes, plan, carried, cx, band, *refs):
    index, weight = refs[:2]
    blocks = refs[2:-1]
    out = refs[-1]
    taps, cells = index.shape
    tracers = 2 * carried
    rows = cx + 8
    per_tile = min(tracers, LANES // band)
    lane = iota((rows, LANES), 1)
    row = iota((rows, cells), 0)
    first_core = lax.axis_index("lev") == 0
    place = lax.axis_index("facex")
    around = sizes[0] * cx
    parts = []
    row_places = []
    for block, (for_first, for_second) in zip(blocks, plan["bands"]):
        offset = for_first if for_first == for_second else jnp.where(first_core, for_first, for_second)
        start = jnp.bitwise_xor(place, offset) * cx
        places = start + row
        places = jnp.where(row == cx, lax.rem(start + around - 1, around), places)
        places = jnp.where(row == cx + 1, lax.rem(start + cx, around), places)
        row_places.append(places)
        count = carried if for_first == for_second else tracers
        mine = []
        for t in range(count):
            tile = block[t // per_tile * rows : (t // per_tile + 1) * rows, :]
            a = t % per_tile
            values = tile if a == 0 else pltpu.roll(tile, (-band * a) % LANES, 1)
            high = values.astype(BF16).astype(F32)
            low = pltpu.roll(values - high, band, 1)
            both = jnp.where(lane < band, high, jnp.where(lane < 2 * band, low, 0.0))
            mine.append(both.astype(BF16))
        parts.append(mine)
    left_side = jnp.concatenate([jnp.concatenate(mine, axis=0) for mine in parts], axis=0)
    spread = iota((LANES, cells), 0)
    in_band = lax.rem(spread, band)
    used = spread < 2 * band
    totals = [[jnp.zeros((rows, cells), F32) for _ in mine] for mine in parts]
    for tap in range(taps):
        place_of = index[tap : tap + 1, :]
        column = lax.div(place_of, band)
        in_lane = lax.rem(place_of, band)
        picks = jnp.where(jnp.logical_and(in_band == in_lane, used), 1.0, 0.0).astype(BF16)
        picked = jnp.dot(left_side, picks, preferred_element_type=F32)
        at = 0
        for number, mine in enumerate(parts):
            chosen = jnp.where(row_places[number] == column, weight[tap : tap + 1, :], 0.0)
            for t in range(len(mine)):
                totals[number][t] = totals[number][t] + chosen * picked[at : at + rows]
                at += rows
    sums = [jnp.zeros((1, cells), F32) for _ in range(tracers)]
    for mine in totals:
        for t, total in enumerate(mine):
            sums[t] = sums[t] + jnp.sum(total, axis=0, keepdims=True)
    out[...] = jnp.concatenate(sums, axis=0)


def advance_kernel(plan, *refs):
    tracer, parts, mixing, inverse, ratio = refs[:5]
    sent = refs[5:7]
    got = refs[7:9]
    y_sent = refs[9 : 9 + plan["y_ops"]]
    y_got = refs[9 + plan["y_ops"] : 9 + 2 * plan["y_ops"]]
    target, out, west_rows, east_rows, done = refs[-5:]
    carried, levels, cx, cy = tracer.shape
    head = (carried + 1) * levels
    spot = carried * levels
    beyond_west, beyond_east = sides(got[0][0:head], got[1][0:head])
    at_west, at_east = sides(sent[0][0:head], sent[1][0:head])
    face_west = at_west[spot:head]
    face_east = beyond_east[spot:head]
    for t in range(carried):
        part = slice(t * levels, (t + 1) * levels)
        west_rows[part, :] = jnp.maximum(face_west, 0.0) * beyond_west[part]
        east_rows[part, :] = -(
            jnp.maximum(face_east, 0.0) * at_east[part] + jnp.minimum(face_east, 0.0) * beyond_east[part]
        )
    lane = iota((cx, cy), 1)
    row = iota((cx, cy), 0)
    seams = [
        seam_lanes(n, y_sent[n][0:cx, :], y_got[n][0:cx, :], carried, levels) for n in range(plan["y_ops"])
    ]
    stride = 4

    def forward(step, before):
        mixed = []
        for k in range(stride):
            level = step * stride + k
            weights = [parts[n, level] for n in range(5)]
            mixed.append([])
            for t in range(carried):
                value = mix(weights, tracer[t, level])
                value = value + jnp.where(row == 0, west_rows[pl.ds(t * levels + level, 1), :], 0.0)
                value = value + jnp.where(row == cx - 1, east_rows[pl.ds(t * levels + level, 1), :], 0.0)
                for packed, spot_y in seams:
                    moved = pltpu.roll(packed, lax.rem(spot_y - (t * levels + level) + 2 * cy, cy), 1)
                    value = value + jnp.where(lane == spot_y, moved, 0.0)
                mixed[k].append(value)
        for k in range(stride):
            level = step * stride + k
            from_below = mixing[jnp.maximum(level - 1, 0)]
            scaled = inverse[level]
            after = []
            for t in range(carried):
                value = (mixed[k][t] + from_below * before[t]) * scaled
                out[t, level] = value
                after.append(value)
            before = after
        return tuple(before)

    def copy(step):
        part = pl.ds(levels - (step + 1) * stride, stride)
        return pltpu.make_async_copy(out.at[:, part], target.at[:, part], done.at[step])

    start = tuple(jnp.zeros((cx, cy), F32) for _ in range(carried))
    lax.fori_loop(0, levels // stride, forward, start)
    above = list(start)
    for step in range(levels // stride):
        for k in range(stride):
            level = levels - 1 - step * stride - k
            factor = ratio[level]
            for t in range(carried):
                above[t] = out[t, level] + factor * above[t]
                out[t, level] = above[t]
        copy(step).start()
    for step in range(levels // stride):
        copy(step).wait()


GROUP = ("facex", "facey", "lev")


def exchange(values, sizes, rule):
    many_x, many_y, cores = sizes
    pairs = []
    for x in range(many_x):
        for y in range(many_y):
            for c in range(cores):
                to = rule(x, y, c)
                if to is not None:
                    pairs.append(((x * many_y + y) * cores + c, (to[0] * many_y + to[1]) * cores + to[2]))
    return lax.ppermute(values, GROUP, pairs)


def make_plan(sizes):
    many_x, many_y, _ = sizes
    tiles = many_x * many_y
    x_blocks = [many_y, (many_x - 1) * many_y if many_x == 4 else 0]
    taken = {0, 1, *x_blocks}
    rest = [d for d in range(tiles) if d not in taken]
    rest.sort(key=lambda d: (d // many_y != many_x // 2, d))
    pairs = [(rest[n], rest[min(n + 1, len(rest) - 1)]) for n in range(0, len(rest), 2)]
    others = list(range(many_x - 1, 1, -1))
    bands = [(0, 0), (1, 1)] + [(others[n], others[n + 1]) for n in range(0, len(others), 2)]
    return {
        "x_blocks": x_blocks,
        "y_block": 1,
        "y_ops": 1 if many_y == 2 else 2,
        "pairs": pairs,
        "bands": bands,
    }


def local(
    sizes,
    tracer,
    west_courant,
    south_courant,
    mixing,
    adjoint_later,
    emission_scale,
    send_cells,
    send_counts,
    kernels,
    observed,
    error_weight,
    regrid_index,
    regrid_weight,
):
    plan = make_plan(sizes)
    many_x, many_y, _ = sizes
    carried, levels, cx, cy = tracer.shape
    owners, cap = send_cells.shape[2:]
    slots = owners * cap
    taps, ll = regrid_index.shape[2:]
    head = (carried + 1) * levels
    y_ops = plan["y_ops"]
    band = cy // many_x

    def next_x(number):
        def rule(x, y, c):
            step = 1 if (x % 2 == 0) == (number == 0) else -1
            return ((x + step) % many_x, y, c)

        return rule

    def next_y(number):
        def rule(x, y, c):
            to = y + (1 if (y % 2 == 0) == (number == 0) else -1)
            return (x, to, c) if 0 <= to < many_y else None

        return rule

    def jump(for_first, for_second):
        def rule(x, y, c):
            d = for_first if c == 0 else for_second
            return (x ^ (d // many_y), y ^ (d % many_y), c)

        return rule

    def other_core(values):
        return exchange(values, sizes, lambda x, y, c: (x, y, 1 - c))

    row_shapes = [shape(head + (16 if plan["x_blocks"][n] else 8), cy) for n in range(2)]
    lane_shapes = [shape(cx + (8 if n == 0 else 0), cy) for n in range(y_ops)]
    packed = call(
        functools.partial(pack_kernel, sizes, plan),
        row_shapes
        + lane_shapes
        + [shape(8, LANES)] * (1 + len(plan["pairs"]))
        + [shape(1, slots, dtype=jnp.int32), shape(1, slots)]
        + [shape(*tracer.shape), shape(*west_courant.shape), shape(*south_courant.shape)],
        [
            tracer,
            west_courant,
            south_courant,
            emission_scale,
            kernels.reshape(owners, levels, cap),
            observed.reshape(owners, cap),
            error_weight.reshape(owners, cap),
            send_cells.reshape(owners, cap),
            send_counts.reshape(owners),
        ],
        "pack",
        100000,
        hbm=range(9),
        scratch=[
            pltpu.VMEM((cx, cy), F32),
            pltpu.VMEM((owners, levels, cap), F32),
            pltpu.VMEM((owners, cap), F32),
            pltpu.VMEM((owners, cap), F32),
            pltpu.VMEM((owners, cap), jnp.int32),
            pltpu.SMEM((owners,), jnp.int32),
            pltpu.SemaphoreType.DMA((8 + carried,)),
        ],
    )
    rows_sent = packed[:2]
    lanes_sent = packed[2 : 2 + y_ops]
    own_block = packed[2 + y_ops]
    pair_sent = packed[3 + y_ops : -5]
    cell, live, tracer, west_courant, south_courant = packed[-5:]
    rows_got = [exchange(rows_sent[n], sizes, next_x(n)) for n in range(2)]
    lanes_got = [exchange(lanes_sent[n], sizes, next_y(n)) for n in range(y_ops)]
    pair_got = [exchange(s, sizes, jump(*p)) for s, p in zip(pair_sent, plan["pairs"])]
    inverse, ratio, base, inner, parts, columns, in_row, in_lane = call(
        functools.partial(factor_kernel, sizes),
        [
            shape(levels, cx, cy),
            shape(levels, cx, cy),
            shape(carried, cx, cy),
            shape(levels, cx, cy),
            shape(5, levels, cx, cy),
            shape(levels, slots),
            shape(cx, slots),
            shape(cy, slots, dtype=BF16),
        ],
        [
            tracer,
            west_courant,
            south_courant,
            mixing,
            adjoint_later,
            cell,
        ],
        "factor",
        3000000,
    )
    base_other = other_core(base)
    swapped = [other_core(jnp.concatenate(pair_got, axis=0))] if pair_got else []
    modeled, state = call(
        functools.partial(observe_kernel, sizes, plan, carried),
        [shape(1, slots), shape(2, slots)],
        [inner, mixing, inverse, ratio, columns, in_row, in_lane, live]
        + list(rows_sent)
        + rows_got
        + list(lanes_sent)
        + lanes_got
        + [own_block]
        + pair_got
        + swapped,
        "observe",
        2000000,
    )
    modeled_other = other_core(modeled)
    near, *rims_sent = call(
        functools.partial(force_kernel, plan),
        [shape(2 * carried, cx, cy)] + [shape(cx, cy)] * y_ops,
        [modeled, modeled_other, state, in_row, in_lane, base, base_other],
        "force",
        200000,
    )
    rims_got = [exchange(rims_sent[n], sizes, next_y(n)) for n in range(y_ops)]
    held, *_ = lax.optimization_barrier((tracer, *rims_sent))
    (advanced,) = call(
        functools.partial(advance_kernel, plan),
        [shape(*tracer.shape)],
        [held, parts, mixing, inverse, ratio]
        + list(rows_sent)
        + rows_got
        + list(lanes_sent)
        + lanes_got,
        "advance",
        6000000,
        scratch=[pltpu.VMEM(tracer.shape, F32)]
        + [pltpu.VMEM((carried * levels, cy), F32)] * 2
        + [pltpu.SemaphoreType.DMA((levels // 4,))],
        out_hbm=(0,),
    )
    advanced, *rims_got = lax.optimization_barrier((advanced, *rims_got))
    per_tile = min(2 * carried, LANES // band)

    def band_shape(first, second):
        count = carried if first == second else 2 * carried
        return shape(-(-count // per_tile) * (cx + 8), cy)

    band_sent = call(
        functools.partial(surface_kernel, sizes, plan, carried, levels),
        [band_shape(*b) for b in plan["bands"]],
        [near, west_courant[0], south_courant[0], emission_scale] + rows_got + lanes_got + rims_got,
        "surface",
        400000,
    )
    band_got = [
        s if first == second == 0 else exchange(s, sizes, jump(first * many_y, second * many_y))
        for s, (first, second) in zip(band_sent, plan["bands"])
    ]
    (sums,) = call(
        functools.partial(regrid_kernel, sizes, plan, carried, cx, band),
        [shape(2 * carried, ll)],
        [regrid_index.reshape(taps, ll), regrid_weight.reshape(taps, ll)] + band_got,
        "regrid",
        1000000,
    )
    sums_other = other_core(sums[carried:])
    latlon = sums[:carried] + sums_other
    return (advanced, latlon[:, None, None, :])


def solution(mesh):
    in_specs = (
        P("lev", "groups", "facex", "facey"),
        P("groups", "facex", "facey"),
        P("groups", "facex", "facey"),
        P("groups", "facex", "facey"),
        P("lev", "groups", "facex", "facey"),
        P("facex", "facey"),
        P("facex", "facey", "groups", None),
        P("facex", "facey", "groups"),
        P("facex", "facey", "groups", None, None),
        P("facex", "facey", "groups", None),
        P("facex", "facey", "groups", None),
        P("facex", "facey", None, None),
        P("facex", "facey", None, None),
    )
    out_specs = (P("lev", "groups", "facex", "facey"), P("lev", "facex", "facey", "groups"))
    sizes = tuple(mesh.shape[axis] for axis in GROUP)
    return jax.shard_map(
        functools.partial(local, sizes), mesh=mesh, in_specs=in_specs, out_specs=out_specs, check_vma=False
    )
```

```python
import functools

import jax
import jax.numpy as jnp
from jax import lax
from jax.experimental import pallas as pl
from jax.experimental.pallas import tpu as pltpu
from jax.sharding import PartitionSpec as P

F32 = jnp.float32
BF16 = jnp.bfloat16
LANES = 128


def call(body, outs, ins, name, flops, smem=(), hbm=(), scratch=(), out_hbm=()):
    moved = sum(4 * a.size for a in ins) + sum(4 * o.size for o in outs)
    ins = [pltpu.with_memory_space_constraint(a, pltpu.HBM) if i in hbm else a for i, a in enumerate(ins)]

    def space(number):
        return pltpu.SMEM if number in smem else pltpu.HBM if number in hbm else pltpu.VMEM

    return pl.pallas_call(
        body,
        out_shape=outs,
        in_specs=[pl.BlockSpec(memory_space=space(i)) for i in range(len(ins))],
        out_specs=[
            pl.BlockSpec(memory_space=pltpu.HBM if i in out_hbm else pltpu.VMEM) for i in range(len(outs))
        ],
        scratch_shapes=scratch,
        compiler_params=pltpu.CompilerParams(vmem_limit_bytes=40 << 20),
        cost_estimate=pl.CostEstimate(flops=flops, bytes_accessed=moved, transcendentals=0),
        name=name,
    )(*ins)


def shape(*dims, dtype=F32):
    return jax.ShapeDtypeStruct(dims, dtype)


def iota(dims, axis):
    return lax.broadcasted_iota(jnp.int32, dims, axis)


def halves(values):
    high = values.astype(BF16)
    return high, (values - high.astype(F32)).astype(BF16)


def tile_of(sizes):
    return lax.axis_index("facex") * sizes[1] + lax.axis_index("facey")


def is_even(axis):
    return lax.rem(lax.axis_index(axis), 2) == 0


def up(values):
    rows = values.shape[0]
    rolled = pltpu.roll(values, rows - 1, 0)
    return jnp.where(iota(values.shape, 0) == rows - 1, 0.0, rolled)


def right(values):
    rolled = pltpu.roll(values, 1, 1)
    return jnp.where(iota(values.shape, 1) == 0, 0.0, rolled)


def left(values):
    lanes = values.shape[1]
    rolled = pltpu.roll(values, lanes - 1, 1)
    return jnp.where(iota(values.shape, 1) == lanes - 1, 0.0, rolled)


def shares(west, south):
    east, north = up(west), left(south)
    middle = 1.0 + jnp.minimum(west, 0.0) - jnp.maximum(east, 0.0)
    middle = middle + jnp.minimum(south, 0.0) - jnp.maximum(north, 0.0)
    row, lane = iota(west.shape, 0), iota(west.shape, 1)
    return (
        middle,
        jnp.where(row == 0, 0.0, jnp.maximum(west, 0.0)),
        -jnp.minimum(east, 0.0),
        jnp.where(lane == 0, 0.0, jnp.maximum(south, 0.0)),
        -jnp.minimum(north, 0.0),
    )


def mix(parts, cells):
    rows, lanes = cells.shape
    middle, west, east, south, north = parts
    total = middle * cells + west * pltpu.roll(cells, 1, 0) + east * pltpu.roll(cells, rows - 1, 0)
    return total + south * pltpu.roll(cells, 1, 1) + north * pltpu.roll(cells, lanes - 1, 1)


def pack_kernel(sizes, plan, *refs):
    sources, refs = refs[:10], refs[10:]
    lanes_out, refs = refs[: plan["y_ops"]], refs[plan["y_ops"] :]
    own_out, refs = refs[0], refs[1:]
    block_outs, refs = refs[: len(plan["pairs"])], refs[len(plan["pairs"]) :]
    cell_out, live_out, tracer, west, south, scale, mixing, *refs = refs
    kernels, observed, weights, cells, counts, done = refs
    carried, levels, cx, cy = tracer.shape
    me = tile_of(sizes)
    copies = [
        pltpu.make_async_copy(source, target, done.at[number])
        for number, (source, target) in enumerate(
            zip(sources[1:], (west, south, scale, kernels, observed, weights, cells, counts, mixing))
        )
    ]
    copies += [
        pltpu.make_async_copy(sources[0].at[t], tracer.at[t], done.at[9 + t]) for t in range(carried)
    ]
    for number in (3, 4, 5, 6, 7, 1, 0, 8, *range(9, 9 + carried), 2):
        copies[number].start()

    def block(offset):
        where_to = jnp.bitwise_xor(me, offset)
        mine = kernels[where_to]
        last = jnp.concatenate(
            [
                observed[pl.ds(where_to, 1), :],
                weights[pl.ds(where_to, 1), :],
                jnp.zeros((6, mine.shape[1]), F32),
            ],
            axis=0,
        )
        return jnp.concatenate([mine[8 * g : 8 * g + 8] for g in range(levels // 8)] + [last], axis=1)

    for number in (3, 4, 5):
        copies[number].wait()
    for number, offset in enumerate(plan["y_blocks"]):
        at = plan["y_tiles"] * cx + 8 * number
        lanes_out[0][at : at + 8, :] = block(offset)
    for number, offset in enumerate(plan["own_blocks"]):
        own_out[8 * number : 8 * number + 8, :] = block(offset)
    first_core = lax.axis_index("lev") == 0
    for out, (for_first, for_second) in zip(block_outs, plan["pairs"]):
        out[...] = block(jnp.where(first_core, for_first, for_second))

    owners, cap = cells.shape
    slot = iota((1, cap), 1)
    copies[6].wait()
    copies[7].wait()
    cell_parts = []
    live_parts = []
    for offset in range(owners):
        owner = jnp.bitwise_xor(me, offset)
        cell_parts.append(cells[pl.ds(owner, 1), :])
        live_parts.append(jnp.where(slot < counts[owner], 1.0, 0.0))
    cell = jnp.concatenate(cell_parts, axis=1)
    live = jnp.concatenate(live_parts, axis=1)
    cell_out[...] = cell
    live_out[...] = live
    if plan["relay"]:
        at = plan["y_tiles"] * cx + 8 * len(plan["y_blocks"])
        strips = owners * cap // LANES
        for number in range(strips):
            part = slice(number * LANES, (number + 1) * LANES)
            lanes_out[0][at + number : at + number + 1, :] = cell[:, part].astype(F32)
            lanes_out[0][at + strips + number : at + strips + number + 1, :] = live[:, part]

    even_y = is_even("facey")
    edge = [
        jnp.where(even_y if number == 0 else jnp.logical_not(even_y), cy - 1, 0)
        for number in range(len(lanes_out))
    ]
    lane = iota((cx, cy), 1)
    packed = [jnp.zeros((cx, cy), F32) for _ in lanes_out]
    behind = jnp.zeros((cx, cy), F32)
    inner_edge = jnp.where(edge[0] == 0, 1, cy - 2)
    for number in (1, 0, 8):
        copies[number].wait()
    for level in range(levels):
        spot = carried * levels + level
        for number, at in enumerate(edge):
            moved = pltpu.roll(south[level], lax.rem(spot + cy - at, cy), 1)
            packed[number] = jnp.where(lane == spot, moved, packed[number])
        if plan["relay"]:
            for number, (values, at) in enumerate(
                ((west[level], edge[0]), (south[level], inner_edge), (mixing[min(level, levels - 2)], edge[0]))
            ):
                spot = (number + 1) * levels + level
                if number < 2 or level < levels - 1:
                    moved = pltpu.roll(values, lax.rem(spot + cy - at, cy), 1)
                    behind = jnp.where(lane == spot, moved, behind)
    for t in range(carried):
        copies[9 + t].wait()
        for level in range(levels):
            spot = t * levels + level
            values = tracer[t, level]
            for number, at in enumerate(edge):
                moved = pltpu.roll(values, lax.rem(spot + cy - at, cy), 1)
                packed[number] = jnp.where(lane == spot, moved, packed[number])
    for values, out in zip(packed, lanes_out):
        out[0:cx, :] = values
    if plan["relay"]:
        for level in range(levels):
            total = tracer[0, level]
            for t in range(1, carried):
                total = total + tracer[t, level]
            moved = pltpu.roll(total, lax.rem(level + cy - inner_edge, cy), 1)
            behind = jnp.where(lane == level, moved, behind)
        lanes_out[0][cx : 2 * cx, :] = behind
    copies[2].wait()


def rows_kernel(plan, tracer, west, scale, blocks, *outs):
    carried, levels, cx, cy = tracer.shape
    head = (carried + 1) * levels
    even_x = is_even("facex")
    for number, out in enumerate(outs):
        row = jnp.where(even_x if number == 0 else jnp.logical_not(even_x), cx - 1, 0)
        for level in range(levels):
            for t in range(carried):
                spot = t * levels + level
                out[spot : spot + 1, :] = tracer[t, level, pl.ds(row, 1), :]
            spot = carried * levels + level
            out[spot : spot + 1, :] = west[level, pl.ds(row, 1), :]
        out[head : head + 8, :] = jnp.broadcast_to(scale[pl.ds(row, 1), :], (8, cy))
        if plan["x_blocks"][number] and not plan["relay"]:
            at = 8 * plan["own_blocks"].index(plan["x_blocks"][number])
            out[head + 8 : head + 16, :] = blocks[at : at + 8, :]


def relay_kernel(plan, head, cx, *refs):
    rows, blocks, y_got = refs[:2], refs[2], refs[3]
    outs = refs[4:6]
    x_outs = refs[6:]
    base = plan["y_tiles"] * cx

    def fill(out, start, offset):
        out[start : start + 16, :] = blocks[8 * offset : 8 * offset + 16, :]
        out[start + 16 : start + 32, :] = y_got[base + 8 * offset : base + 8 * offset + 16, :]

    even_x = is_even("facex")
    for number, out in enumerate(outs):
        out[0 : head + 8, :] = rows[number][0 : head + 8, :]
        row = jnp.where(even_x if number == 0 else jnp.logical_not(even_x), cx - 1, 0)
        for tile in range(2):
            out[head + 8 + tile : head + 9 + tile, :] = y_got[pl.ds(tile * cx + row, 1), :]
        out[head + 10 : head + 16, :] = jnp.zeros((6, out.shape[1]), F32)
        if plan["x_blocks"][number]:
            fill(out, head + 16, plan["x_blocks"][number])
    for out, offset in zip(x_outs, plan["x_ops"]):
        fill(out, 0, offset)


def rim_kernel(plan, carried, levels, cx, y_sent, y_got, *refs):
    inverse_out, ratio_out, mixing_out, pieces_out, columns_out, rows_out, picks_out, live_out, square = refs
    cy = y_got.shape[1]
    slots = live_out.shape[1]

    def turned(values):
        square[...] = jnp.zeros((LANES, LANES), F32)
        square[0:cx, :] = values
        return jnp.transpose(square[...])

    def summed(values):
        total = values[0:levels]
        for t in range(1, carried):
            total = total + values[t * levels : (t + 1) * levels]
        return total

    spot = carried * levels
    beyond = turned(y_got[0:cx, :])
    behind = turned(y_got[cx : 2 * cx, :])
    mine = turned(y_sent[0:cx, :])
    north = is_even("facey")
    second, inner_face = behind[0:levels], behind[2 * levels : 3 * levels]
    edge_face, own_face = beyond[spot : spot + levels], mine[spot : spot + levels]
    own_edge = summed(mine)
    pieces_out[0] = summed(beyond)
    pieces_out[1] = behind[levels : 2 * levels]
    pieces_out[2] = edge_face
    pieces_out[3] = jnp.where(north, inner_face, own_face)
    pieces_out[4] = jnp.where(north, own_edge, second)
    pieces_out[5] = jnp.where(north, second, own_edge)
    mixing_out[...] = behind[3 * levels : 4 * levels]

    def level_of(ref, level):
        return jnp.broadcast_to(ref[level : level + 1, :], (8, LANES))

    first = []
    ratios = []
    before = None
    for level in range(levels):
        diagonal = jnp.ones((8, LANES), F32)
        if level > 0:
            below = level_of(mixing_out, level - 1)
            diagonal = diagonal + below
        if level < levels - 1:
            diagonal = diagonal + level_of(mixing_out, level)
        if level > 0:
            diagonal = diagonal - below * below * before
        inverse = 1.0 / diagonal
        ratios.append(level_of(mixing_out, level) * inverse if level < levels - 1 else jnp.zeros((8, LANES), F32))
        inverse_out[level : level + 1, :] = inverse[0:1]
        ratio_out[level : level + 1, :] = ratios[-1][0:1]
        first.append(inverse if level == 0 else below * first[-1] * inverse)
        before = inverse
    weight = first
    for level in range(levels - 2, -1, -1):
        weight[level] = first[level] + ratios[level] * weight[level + 1]
    for level in range(levels):
        square[level : level + 1, :] = weight[level][0:1]
    at = plan["y_tiles"] * cx + 8 * len(plan["y_blocks"])
    strips = slots // LANES
    cell = jnp.concatenate([y_got[at + n : at + n + 1, :] for n in range(strips)], axis=1).astype(jnp.int32)
    live_out[...] = jnp.concatenate([y_got[at + strips + n : at + strips + n + 1, :] for n in range(strips)], axis=1)
    on_edge = lax.rem(cell, cy) == jnp.where(north, 0, cy - 1)
    x_of = jnp.where(on_edge, lax.div(cell, cy), LANES)
    picks = jnp.where(iota((LANES, slots), 0) == x_of, 1.0, 0.0)
    rows_out[...] = picks[0:cx]
    picks = picks.astype(BF16)
    picks_out[...] = picks
    high, low = halves(square[0:levels, :])
    columns_out[...] = jnp.dot(high, picks, preferred_element_type=F32) + jnp.dot(
        low, picks, preferred_element_type=F32
    )


def factor_kernel(sizes, *refs):
    (tracer, west, south, mixing, adjoint, cells) = refs[:6]
    inverse_out, ratio_out, base_out, inner_out, shares_out, columns_out, rows_out, picks_out, rim_out = refs[6:]
    carried, levels, cx, cy = tracer.shape
    slots = cells.shape[1]
    first = []
    before = None
    for level in range(levels):
        diagonal = jnp.ones((cx, cy), F32)
        if level > 0:
            diagonal = diagonal + mixing[level - 1]
        if level < levels - 1:
            diagonal = diagonal + mixing[level]
        if level > 0:
            diagonal = diagonal - mixing[level - 1] * mixing[level - 1] * before
        inverse = 1.0 / diagonal
        inverse_out[level] = inverse
        if level < levels - 1:
            ratio_out[level] = mixing[level] * inverse
        first.append(inverse if level == 0 else mixing[level - 1] * first[-1] * inverse)
        before = inverse
    ratio_out[levels - 1] = jnp.zeros((cx, cy), F32)
    weight = first
    for level in range(levels - 2, -1, -1):
        weight[level] = first[level] + ratio_out[level] * weight[level + 1]
    for t in range(carried):
        total = weight[0] * adjoint[t, 0]
        for level in range(1, levels):
            total = total + weight[level] * adjoint[t, level]
        base_out[t] = total
        edge = jnp.where(is_even("facey"), cy - 1, 0)
        moved = pltpu.roll(total, lax.rem(t + cy - edge, cy), 1)
        rim = jnp.where(iota((cx, cy), 1) == t, moved, jnp.zeros((cx, cy), F32) if t == 0 else rim)
    rim_out[...] = rim
    for level in range(levels):
        total = tracer[0, level]
        for t in range(1, carried):
            total = total + tracer[t, level]
        parts = shares(west[level], south[level])
        for number, part in enumerate(parts):
            shares_out[number, level] = part
        inner_out[level] = mix(parts, total)
    cell = cells[...]
    x_of = lax.div(cell, cy)
    y_of = lax.rem(cell, cy)
    in_row = jnp.where(iota((cx, slots), 0) == x_of, 1.0, 0.0)
    in_lane = jnp.where(iota((cy, slots), 0) == y_of, 1.0, 0.0).astype(BF16)
    rows_out[...] = in_row
    picks_out[...] = in_lane
    high, low = halves(jnp.concatenate(weight, axis=0))
    picked = jnp.dot(high, in_lane, preferred_element_type=F32)
    picked = picked + jnp.dot(low, in_lane, preferred_element_type=F32)
    for level in range(levels):
        part = picked[level * cx : (level + 1) * cx] * in_row
        columns_out[level : level + 1, :] = jnp.sum(part, axis=0, keepdims=True)


def sides(first, second):
    even_x = is_even("facex")
    return jnp.where(even_x, second, first), jnp.where(even_x, first, second)


def seam_lanes(number, sent, got, carried, levels):
    cy = sent.shape[1]
    spot = carried * levels
    lane = iota(sent.shape, 1)

    def spread(values):
        result = jnp.zeros_like(values)
        for t in range(carried):
            moved = pltpu.roll(values, (t * levels - spot) % cy, 1)
            inside = jnp.logical_and(lane >= t * levels, lane < (t + 1) * levels)
            result = jnp.where(inside, moved, result)
        return result

    even_y = is_even("facey")
    north = even_y if number == 0 else jnp.logical_not(even_y)
    beyond = spread(got)
    inside = spread(sent)
    to_north = -(jnp.maximum(beyond, 0.0) * sent + jnp.minimum(beyond, 0.0) * got)
    to_south = jnp.maximum(inside, 0.0) * got
    return jnp.where(north, to_north, to_south), jnp.where(north, cy - 1, 0)


def observe_kernel(sizes, plan, carried, *refs):
    refs = list(refs)
    inner, mixing, inverse, ratio, columns, in_row, in_lane, live = refs[:8]
    sent = refs[8:10]
    got = refs[10:12]
    refs = refs[12:]
    y_sent = refs[: plan["y_ops"]]
    y_got = refs[plan["y_ops"] : 2 * plan["y_ops"]]
    refs = refs[2 * plan["y_ops"] :]
    own = refs[0]
    n_pairs = len(plan["pairs"])
    pair_got = refs[1 : 1 + n_pairs]
    swapped = refs[1 + n_pairs] if n_pairs else None
    if plan["relay"]:
        x_got = refs[1 : 1 + len(plan["x_ops"])]
        refs = refs[1 + len(plan["x_ops"]) :]
        base, rim_base, *rim = refs[:10]
        parcel, state_out, turn, rise = refs[10:]
    else:
        modeled_out, state_out = refs[-2:]
    levels, cx, cy = inner.shape
    slots = in_row.shape[1]
    head = (carried + 1) * levels

    def summed(rows):
        total = rows[0:levels]
        for t in range(1, carried):
            total = total + rows[t * levels : (t + 1) * levels]
        return total

    beyond_west, beyond_east = sides(got[0][0:head], got[1][0:head])
    at_west, at_east = sides(sent[0][0:head], sent[1][0:head])
    spot = carried * levels
    face_west = at_west[spot:head]
    face_east = beyond_east[spot:head]
    from_west = jnp.maximum(face_west, 0.0) * summed(beyond_west)
    from_east = -(
        jnp.maximum(face_east, 0.0) * summed(at_east) + jnp.minimum(face_east, 0.0) * summed(beyond_east)
    )
    lane_parts = []
    for number in range(plan["y_ops"]):
        part, spot_y = seam_lanes(number, y_sent[number][0:cx, :], y_got[number][0:cx, :], carried, levels)
        total = part
        for t in range(1, carried):
            total = total + pltpu.roll(part, (-t * levels) % cy, 1)
        lane_parts.append((total, spot_y))
    lane = iota((cx, cy), 1)
    row = iota((cx, cy), 0)
    forward = []
    for level in range(levels):
        value = inner[level]
        value = value + jnp.where(row == 0, from_west[level : level + 1], 0.0)
        value = value + jnp.where(row == cx - 1, from_east[level : level + 1], 0.0)
        for total, spot_y in lane_parts:
            moved = pltpu.roll(total, lax.rem(spot_y - level + cy, cy), 1)
            value = value + jnp.where(lane == spot_y, moved, 0.0)
        if level > 0:
            value = value + mixing[level - 1] * forward[-1]
        forward.append(value * inverse[level])
    result = forward
    for level in range(levels - 2, -1, -1):
        result[level] = forward[level] + ratio[level] * result[level + 1]
    high, low = halves(jnp.concatenate(result, axis=0))
    picks = in_lane[...]
    picked = jnp.dot(high, picks, preferred_element_type=F32)
    picked = picked + jnp.dot(low, picks, preferred_element_type=F32)

    start = plan["y_tiles"] * cx
    if plan["relay"]:

        def block_at(ref, row):
            return ref[row : row + 8, :]

        blocks = {0: block_at(own, 0), 1: block_at(y_got[0], start + 8)}
        rim_blocks = {0: block_at(y_got[0], start), 1: block_at(own, 8)}
        carriers = [(offset, got[n], head + 16) for n, offset in enumerate(plan["x_blocks"]) if offset]
        carriers += [(offset, ref, 0) for offset, ref in zip(plan["x_ops"], x_got)]
        for offset, ref, row in carriers:
            blocks[offset], rim_blocks[offset + 1] = block_at(ref, row), block_at(ref, row + 8)
            rim_blocks[offset], blocks[offset + 1] = block_at(ref, row + 16), block_at(ref, row + 24)
    else:
        blocks = {0: own[0:8, :], plan["y_blocks"][0]: y_got[0][start : start + 8, :]}
        for number in range(2):
            offset = plan["x_blocks"][number]
            if offset:
                blocks[offset] = got[number][head + 8 : head + 16, :]
    first_core = lax.axis_index("lev") == 0
    for number, (for_first, for_second) in enumerate(plan["pairs"]):
        mine = pair_got[number][...]
        other = swapped[8 * number : 8 * number + 8, :]
        if for_first == for_second:
            blocks[for_first] = mine
        else:
            blocks[for_first] = jnp.where(first_core, mine, other)
            blocks[for_second] = jnp.where(first_core, other, mine)
    cap = slots // len(blocks)
    per_tile = LANES // cap
    group_of_lane = lax.div(iota((8, LANES), 1), cap)

    def gathered(group, blocks):
        tiles = []
        for start in range(0, len(blocks), per_tile):
            tile = jnp.zeros((8, LANES), F32)
            for a in range(per_tile):
                moved = pltpu.roll(blocks[start + a], (cap * (a - group)) % LANES, 1)
                tile = jnp.where(group_of_lane == a, moved, tile)
            tiles.append(tile)
        return jnp.concatenate(tiles, axis=1)

    groups = [gathered(g, blocks) for g in range(levels // 8)]
    last = gathered(levels // 8, blocks)
    total = jnp.zeros((cx, slots), F32)
    sensitivity = jnp.zeros((8, slots), F32)
    for g, kernel in enumerate(groups):
        sensitivity = sensitivity + kernel * columns[8 * g : 8 * g + 8, :]
        for l in range(8):
            level = 8 * g + l
            total = total + kernel[l : l + 1] * picked[level * cx : (level + 1) * cx]
    modeled = jnp.sum(total * in_row[...], axis=0, keepdims=True)
    gain = jnp.sum(sensitivity, axis=0, keepdims=True) * last[1:2] * live[...]
    if not plan["relay"]:
        modeled_out[...] = modeled
        state_out[...] = jnp.concatenate([gain, last[0:1]], axis=0)
        return

    rim_inverse, rim_ratio, rim_mixing, pieces, rim_columns, rim_rows, rim_picks, rim_live = rim
    corners_west, corners_east = sides(got[0][head + 8 : head + 16, :], got[1][head + 8 : head + 16, :])
    turn[...] = jnp.zeros((LANES, LANES), F32)
    turn[0:1, :] = corners_west[0:1]
    turn[cx - 1 : cx, :] = corners_east[0:1]
    turn[2 * cx - 1 : 2 * cx, :] = corners_east[1:2]
    turned = jnp.transpose(turn[...])
    ends = turned[0:levels]
    for t in range(1, carried):
        ends = ends + turned[t * levels : (t + 1) * levels]
    end_face = pltpu.roll(turned[levels : 2 * levels], LANES - cx, 1)
    place = iota((levels, LANES), 1)
    cells, face_w, face_s, face_n, south_cells, north_cells = (pieces[n] for n in range(6))
    west_cells = jnp.where(place == 0, ends, pltpu.roll(cells, 1, 1))
    east_cells = jnp.where(place == cx - 1, ends, pltpu.roll(cells, LANES - 1, 1))
    face_e = jnp.where(place == cx - 1, end_face, pltpu.roll(face_w, LANES - 1, 1))
    rise[0:levels, :] = advance_cells(
        cells, west_cells, east_cells, south_cells, north_cells, face_w, face_e, face_s, face_n
    )

    def level_of(ref, level):
        return jnp.broadcast_to(ref[level : level + 1, :], (8, LANES))

    climbed = []
    for level in range(levels):
        value = level_of(rise, level)
        if level > 0:
            value = value + level_of(rim_mixing, level - 1) * climbed[-1]
        climbed.append(value * level_of(rim_inverse, level))
    for level in range(levels - 2, -1, -1):
        climbed[level] = climbed[level] + level_of(rim_ratio, level) * climbed[level + 1]
    for level in range(levels):
        rise[level : level + 1, :] = climbed[level][0:1]
    high, low = halves(rise[0:levels, :])
    picks = rim_picks[...]
    picked = jnp.dot(high, picks, preferred_element_type=F32)
    picked = picked + jnp.dot(low, picks, preferred_element_type=F32)
    rim_total = jnp.zeros((8, slots), F32)
    sensitivity = jnp.zeros((8, slots), F32)
    for g in range(levels // 8):
        kernel = gathered(g, rim_blocks)
        rim_total = rim_total + kernel * picked[8 * g : 8 * g + 8]
        sensitivity = sensitivity + kernel * rim_columns[8 * g : 8 * g + 8, :]
    rim_modeled = jnp.sum(rim_total, axis=0, keepdims=True)
    rim_last = gathered(levels // 8, rim_blocks)
    rim_gain = jnp.sum(sensitivity, axis=0, keepdims=True) * rim_last[1:2] * rim_live[...]
    state_out[...] = jnp.concatenate([gain, last[0:1], rim_gain, rim_last[0:1]], axis=0)
    strips = slots // LANES
    for number in range(strips):
        part = slice(number * LANES, (number + 1) * LANES)
        parcel[number : number + 1, :] = modeled[:, part]
        parcel[strips + number : strips + number + 1, :] = rim_modeled[:, part]
    at = plan["parcel"]
    for t in range(carried):
        parcel[at + t * cx : at + (t + 1) * cx, :] = base[t]
    at = at + carried * cx
    parcel[at : at + cx, :] = rim_base[...]
    parcel[at + cx : at + 2 * cx, :] = y_got[0][0:cx, :]


def advance_cells(cells, west, east, south, north, face_w, face_e, face_s, face_n):
    flux_w = jnp.maximum(face_w, 0.0) * west + jnp.minimum(face_w, 0.0) * cells
    flux_e = jnp.maximum(face_e, 0.0) * cells + jnp.minimum(face_e, 0.0) * east
    flux_s = jnp.maximum(face_s, 0.0) * south + jnp.minimum(face_s, 0.0) * cells
    flux_n = jnp.maximum(face_n, 0.0) * cells + jnp.minimum(face_n, 0.0) * north
    return cells + flux_w - flux_e + flux_s - flux_n


def scatter(force, in_row, in_lane):
    high, low = halves(in_row * force)
    dims = (((1,), (1,)), ((), ()))
    scattered = lax.dot_general(high, in_lane, dims, preferred_element_type=F32)
    return scattered + lax.dot_general(low, in_lane, dims, preferred_element_type=F32)


def force_kernel(plan, *refs):
    modeled, modeled_other, state, in_row, in_lane, base, base_other = refs[:7]
    near_out = refs[7]
    rim_outs = refs[8:]
    carried, cx, cy = base.shape
    misfit = modeled[...] + modeled_other[...] - state[1:2, :]
    force = state[0:1, :] * misfit
    scattered = scatter(force, in_row[...], in_lane[...])
    lane = iota((cx, cy), 1)
    even_y = is_even("facey")
    edges = []
    for number in range(len(rim_outs)):
        sends_last = even_y if number == 0 else jnp.logical_not(even_y)
        edges.append(jnp.where(sends_last, cy - 1, 0))
    rims = [jnp.zeros((cx, cy), F32) for _ in rim_outs]
    for t in range(2 * carried):
        values = scattered + (base[t] if t < carried else base_other[t - carried])
        near_out[t] = values
        for number, edge in enumerate(edges):
            moved = pltpu.roll(values, lax.rem(t + cy - edge, cy), 1)
            rims[number] = jnp.where(lane == t, moved, rims[number])
    for rim, out in zip(rims, rim_outs):
        out[...] = rim


def surface_kernel(sizes, plan, carried, levels, *refs):
    y_ops = plan["y_ops"]
    near = refs[0]
    rims = refs[6 + y_ops : 6 + 2 * y_ops]
    rim_values = [[rim[...] for rim in rims] for _ in range(near.shape[0])]
    values = [near[t] for t in range(near.shape[0])]
    spread_surface(
        sizes, plan, carried, levels, values, rim_values, refs[1:4], refs[4:6], refs[6 : 6 + y_ops], refs[6 + 2 * y_ops :]
    )


def weigh_kernel(sizes, plan, carried, levels, *refs):
    parcel, other, state, in_row, in_lane, base, rim_rows, rim_base = refs[:8]
    cx, cy = base.shape[1:]
    strips = state.shape[1] // LANES

    def misfit(kind):
        both = parcel[kind * strips : (kind + 1) * strips, :] + other[kind * strips : (kind + 1) * strips, :]
        flat = jnp.concatenate([both[n : n + 1] for n in range(strips)], axis=1)
        return state[2 * kind : 2 * kind + 1, :] * (flat - state[2 * kind + 1 : 2 * kind + 2, :])

    scattered = scatter(misfit(0), in_row[...], in_lane[...])
    on_rim = jnp.sum(rim_rows[...] * misfit(1), axis=1, keepdims=True)
    at = plan["parcel"]
    near = [scattered + base[t] for t in range(carried)]
    near += [scattered + other[at + t * cx : at + (t + 1) * cx, :] for t in range(carried)]
    at = at + carried * cx
    mine, others = other[at : at + cx, :] + on_rim, rim_base[...] + on_rim
    rims = [[mine if t < carried else others] for t in range(2 * carried)]
    spread_surface(sizes, plan, carried, levels, near, rims, refs[8:11], refs[11:13], refs[13:14], refs[14:])


def spread_surface(sizes, plan, carried, levels, near, rim_values, fields, got, y_got, outs):
    west, south, scale = fields
    tracers = len(near)
    cx, cy = near[0].shape
    band = cy // sizes[0]
    per_tile = min(tracers, LANES // band)
    spot = carried * levels
    head = (carried + 1) * levels
    lane = iota((cx, cy), 1)
    row = iota((cx, cy), 0)
    even_y = is_even("facey")
    face_west = west[...]
    face_south = south[...]
    scales = scale[...]
    beyond_west, beyond_east = sides(got[0][head : head + 1], got[1][head : head + 1])
    _, east_wind = sides(got[0][spot : spot + 1], got[1][spot : spot + 1])
    face_east = jnp.where(row == cx - 1, east_wind, pltpu.roll(face_west, cx - 1, 0))
    face_north = left(face_south)
    norths = []
    for number in range(plan["y_ops"]):
        norths.append(even_y if number == 0 else jnp.logical_not(even_y))
        moved = pltpu.roll(y_got[number][0:cx, :], cy - 1 - spot, 1)
        keep = jnp.logical_and(lane == cy - 1, norths[number])
        face_north = jnp.where(keep, moved, face_north)
    to_middle = 1.0 + jnp.minimum(face_west, 0.0) - jnp.maximum(face_east, 0.0)
    to_middle = scales * (to_middle + jnp.minimum(face_south, 0.0) - jnp.maximum(face_north, 0.0))
    to_east = jnp.where(row == cx - 1, 0.0, scales * jnp.maximum(face_east, 0.0))
    to_west = jnp.where(row == 0, 0.0, scales * jnp.minimum(face_west, 0.0))
    to_north = scales * jnp.maximum(face_north, 0.0)
    to_south = scales * jnp.minimum(face_south, 0.0)
    west_gain = beyond_west * jnp.maximum(face_west[0:1], 0.0)
    east_gain = -beyond_east * jnp.minimum(face_east[cx - 1 : cx], 0.0)
    filler = jnp.zeros((6, cy), F32)
    grown = []
    for t in range(tracers):
        values = near[t]
        north_side = left(values)
        south_side = right(values)
        for number in range(plan["y_ops"]):
            rim = rim_values[t][number]
            spot_t = t % carried if plan["relay"] else t
            at_north = jnp.logical_and(lane == cy - 1, norths[number])
            at_south = jnp.logical_and(lane == 0, jnp.logical_not(norths[number]))
            north_side = jnp.where(at_north, pltpu.roll(rim, (cy - 1 - spot_t) % cy, 1), north_side)
            south_side = jnp.where(at_south, pltpu.roll(rim, (-spot_t) % cy, 1), south_side)
        swept = to_middle * values + to_east * pltpu.roll(values, cx - 1, 0) - to_west * pltpu.roll(values, 1, 0)
        swept = swept + to_north * north_side - to_south * south_side
        grown.append(
            jnp.concatenate(
                [swept, west_gain * values[0:1], east_gain * values[cx - 1 : cx], filler], axis=0
            )
        )
    rows = cx + 8
    group_of_lane = lax.div(iota((rows, cy), 1), band)
    first_core = lax.axis_index("lev") == 0
    place = lax.axis_index("facex")
    for out, (for_first, for_second) in zip(outs, plan["bands"]):
        offset = for_first if for_first == for_second else jnp.where(first_core, for_first, for_second)
        target = jnp.bitwise_xor(place, offset)
        count = carried if for_first == for_second else tracers
        skip = carried if for_first == for_second != 0 and plan["cross"] else 0
        for start in range(0, count, per_tile):
            tile = jnp.zeros((rows, cy), F32)
            for a in range(min(per_tile, count - start)):
                moved = pltpu.roll(grown[skip + start + a], lax.rem(band * a + cy - band * target, cy), 1)
                tile = jnp.where(group_of_lane == a, moved, tile)
            out[start // per_tile * rows : (start // per_tile + 1) * rows, :] = tile


def regrid_kernel(sizes, plan, carried, cx, band, *refs):
    index, weight = refs[:2]
    blocks = refs[2:-1]
    out = refs[-1]
    taps, cells = index.shape
    tracers = 2 * carried
    rows = cx + 8
    per_tile = min(tracers, LANES // band)
    lane = iota((rows, LANES), 1)
    row = iota((rows, cells), 0)
    first_core = lax.axis_index("lev") == 0
    place = lax.axis_index("facex")
    around = sizes[0] * cx
    parts = []
    row_places = []
    for block, (for_first, for_second) in zip(blocks, plan["bands"]):
        from_first, from_second = (for_second, for_first) if plan["cross"] else (for_first, for_second)
        offset = for_first if for_first == for_second else jnp.where(first_core, from_first, from_second)
        start = jnp.bitwise_xor(place, offset) * cx
        places = start + row
        places = jnp.where(row == cx, lax.rem(start + around - 1, around), places)
        places = jnp.where(row == cx + 1, lax.rem(start + cx, around), places)
        row_places.append(places)
        count = carried if for_first == for_second else tracers
        mine = []
        for t in range(count):
            tile = block[t // per_tile * rows : (t // per_tile + 1) * rows, :]
            a = t % per_tile
            values = tile if a == 0 else pltpu.roll(tile, (-band * a) % LANES, 1)
            high = values.astype(BF16).astype(F32)
            low = pltpu.roll(values - high, band, 1)
            both = jnp.where(lane < band, high, jnp.where(lane < 2 * band, low, 0.0))
            mine.append(both.astype(BF16))
        parts.append(mine)
    left_side = jnp.concatenate([jnp.concatenate(mine, axis=0) for mine in parts], axis=0)
    spread = iota((LANES, cells), 0)
    in_band = lax.rem(spread, band)
    used = spread < 2 * band
    totals = [[jnp.zeros((rows, cells), F32) for _ in mine] for mine in parts]
    for tap in range(taps):
        place_of = index[tap : tap + 1, :]
        column = lax.div(place_of, band)
        in_lane = lax.rem(place_of, band)
        picks = jnp.where(jnp.logical_and(in_band == in_lane, used), 1.0, 0.0).astype(BF16)
        picked = jnp.dot(left_side, picks, preferred_element_type=F32)
        at = 0
        for number, mine in enumerate(parts):
            chosen = jnp.where(row_places[number] == column, weight[tap : tap + 1, :], 0.0)
            for t in range(len(mine)):
                totals[number][t] = totals[number][t] + chosen * picked[at : at + rows]
                at += rows
    sums = [jnp.zeros((1, cells), F32) for _ in range(tracers)]
    for mine in totals:
        skip = carried if len(mine) == tracers and plan["cross"] else 0
        for t, total in enumerate(mine):
            to = (t + skip) % tracers
            sums[to] = sums[to] + jnp.sum(total, axis=0, keepdims=True)
    out[...] = jnp.concatenate(sums, axis=0)


def advance_kernel(plan, *refs):
    tracer, parts, mixing, inverse, ratio = refs[:5]
    sent = refs[5:7]
    got = refs[7:9]
    y_sent = refs[9 : 9 + plan["y_ops"]]
    y_got = refs[9 + plan["y_ops"] : 9 + 2 * plan["y_ops"]]
    target, out, west_rows, east_rows, done = refs[-5:]
    carried, levels, cx, cy = tracer.shape
    head = (carried + 1) * levels
    spot = carried * levels
    beyond_west, beyond_east = sides(got[0][0:head], got[1][0:head])
    at_west, at_east = sides(sent[0][0:head], sent[1][0:head])
    face_west = at_west[spot:head]
    face_east = beyond_east[spot:head]
    for t in range(carried):
        part = slice(t * levels, (t + 1) * levels)
        west_rows[part, :] = jnp.maximum(face_west, 0.0) * beyond_west[part]
        east_rows[part, :] = -(
            jnp.maximum(face_east, 0.0) * at_east[part] + jnp.minimum(face_east, 0.0) * beyond_east[part]
        )
    lane = iota((cx, cy), 1)
    row = iota((cx, cy), 0)
    seams = [
        seam_lanes(n, y_sent[n][0:cx, :], y_got[n][0:cx, :], carried, levels) for n in range(plan["y_ops"])
    ]
    stride = 4

    def forward(step, before):
        mixed = []
        for k in range(stride):
            level = step * stride + k
            weights = [parts[n, level] for n in range(5)]
            mixed.append([])
            for t in range(carried):
                value = mix(weights, tracer[t, level])
                value = value + jnp.where(row == 0, west_rows[pl.ds(t * levels + level, 1), :], 0.0)
                value = value + jnp.where(row == cx - 1, east_rows[pl.ds(t * levels + level, 1), :], 0.0)
                for packed, spot_y in seams:
                    moved = pltpu.roll(packed, lax.rem(spot_y - (t * levels + level) + 2 * cy, cy), 1)
                    value = value + jnp.where(lane == spot_y, moved, 0.0)
                mixed[k].append(value)
        for k in range(stride):
            level = step * stride + k
            from_below = mixing[jnp.maximum(level - 1, 0)]
            scaled = inverse[level]
            after = []
            for t in range(carried):
                value = (mixed[k][t] + from_below * before[t]) * scaled
                out[t, level] = value
                after.append(value)
            before = after
        return tuple(before)

    def copy(step):
        part = pl.ds(levels - (step + 1) * stride, stride)
        return pltpu.make_async_copy(out.at[:, part], target.at[:, part], done.at[step])

    start = tuple(jnp.zeros((cx, cy), F32) for _ in range(carried))
    lax.fori_loop(0, levels // stride, forward, start)
    above = list(start)
    for step in range(levels // stride):
        for k in range(stride):
            level = levels - 1 - step * stride - k
            factor = ratio[level]
            for t in range(carried):
                above[t] = out[t, level] + factor * above[t]
                out[t, level] = above[t]
        copy(step).start()
    for step in range(levels // stride):
        copy(step).wait()


GROUP = ("facex", "facey", "lev")


def exchange(values, sizes, rule):
    many_x, many_y, cores = sizes
    pairs = []
    for x in range(many_x):
        for y in range(many_y):
            for c in range(cores):
                to = rule(x, y, c)
                if to is not None:
                    pairs.append(((x * many_y + y) * cores + c, (to[0] * many_y + to[1]) * cores + to[2]))
    return lax.ppermute(values, GROUP, pairs)


def make_plan(sizes):
    many_x, many_y, _ = sizes
    tiles = many_x * many_y
    x_blocks = [many_y, (many_x - 1) * many_y if many_x == 4 else 0]
    relay = many_y == 2
    if relay:
        own_blocks = list(range(tiles))
        y_blocks = own_blocks
        x_ops = [offset for offset in own_blocks[2::2] if offset not in x_blocks]
        pairs = []
    else:
        own_blocks = [0] + [offset for offset in x_blocks if offset]
        y_blocks = [1]
        x_ops = []
        rest = [d for d in range(tiles) if d not in {1, *own_blocks}]
        rest.sort(key=lambda d: (d // many_y != many_x // 2, d))
        pairs = [(rest[n], rest[min(n + 1, len(rest) - 1)]) for n in range(0, len(rest), 2)]
    others = list(range(many_x - 1, 1, -1))
    bands = [(0, 0), (1, 1)] + [(others[n], others[n + 1]) for n in range(0, len(others), 2)]
    return {
        "relay": relay,
        "cross": 1 if relay else 0,
        "x_blocks": x_blocks,
        "x_ops": x_ops,
        "own_blocks": own_blocks,
        "y_blocks": y_blocks,
        "y_ops": 1 if many_y == 2 else 2,
        "y_tiles": 2 if relay else 1,
        "pairs": pairs,
        "bands": bands,
    }


def local(
    sizes,
    tracer,
    west_courant,
    south_courant,
    mixing,
    adjoint_later,
    emission_scale,
    send_cells,
    send_counts,
    kernels,
    observed,
    error_weight,
    regrid_index,
    regrid_weight,
):
    plan = make_plan(sizes)
    many_x, many_y, _ = sizes
    carried, levels, cx, cy = tracer.shape
    owners, cap = send_cells.shape[2:]
    slots = owners * cap
    taps, ll = regrid_index.shape[2:]
    head = (carried + 1) * levels
    y_ops = plan["y_ops"]
    band = cy // many_x

    def next_x(number):
        def rule(x, y, c):
            step = 1 if (x % 2 == 0) == (number == 0) else -1
            return ((x + step) % many_x, y, c)

        return rule

    def next_y(number):
        def rule(x, y, c):
            to = y + (1 if (y % 2 == 0) == (number == 0) else -1)
            return (x, to, c ^ plan["cross"]) if 0 <= to < many_y else None

        return rule

    def jump(for_first, for_second, cross=0):
        def rule(x, y, c):
            d = for_first if c == 0 else for_second
            return (x ^ (d // many_y), y ^ (d % many_y), c ^ cross)

        return rule

    def other_core(values):
        return exchange(values, sizes, lambda x, y, c: (x, y, 1 - c))

    strips = slots // LANES
    plan["parcel"] = -(-2 * strips // 8) * 8
    extra = 48 if plan["relay"] else 16
    row_shapes = [shape(head + extra, cy)] * 2
    y_rows = plan["y_tiles"] * cx + 8 * len(plan["y_blocks"]) + (plan["parcel"] if plan["relay"] else 0)
    lane_shapes = [shape(y_rows if n == 0 else cx, cy) for n in range(y_ops)]
    packed = call(
        functools.partial(pack_kernel, sizes, plan),
        lane_shapes
        + [shape(8 * len(plan["own_blocks"]), LANES)]
        + [shape(8, LANES)] * len(plan["pairs"])
        + [shape(1, slots, dtype=jnp.int32), shape(1, slots)]
        + [shape(*a.shape) for a in (tracer, west_courant, south_courant, emission_scale, mixing)],
        [
            tracer,
            west_courant,
            south_courant,
            emission_scale,
            kernels.reshape(owners, levels, cap),
            observed.reshape(owners, cap),
            error_weight.reshape(owners, cap),
            send_cells.reshape(owners, cap),
            send_counts.reshape(owners),
            mixing,
        ],
        "pack",
        100000,
        hbm=range(10),
        scratch=[
            pltpu.VMEM((owners, levels, cap), F32),
            pltpu.VMEM((owners, cap), F32),
            pltpu.VMEM((owners, cap), F32),
            pltpu.VMEM((owners, cap), jnp.int32),
            pltpu.SMEM((owners,), jnp.int32),
            pltpu.SemaphoreType.DMA((9 + carried,)),
        ],
    )
    lanes_sent = packed[:y_ops]
    own_blocks = packed[y_ops]
    pair_sent = packed[1 + y_ops : -7]
    cell, live, tracer, west_courant, south_courant, emission_scale, mixing = packed[-7:]
    lanes_got = [exchange(lanes_sent[n], sizes, next_y(n)) for n in range(y_ops)]
    held, *_ = lax.optimization_barrier((tracer, *lanes_sent))
    inverse, ratio, base, inner, parts, columns, in_row, in_lane, base_rim = call(
        functools.partial(factor_kernel, sizes),
        [
            shape(levels, cx, cy),
            shape(levels, cx, cy),
            shape(carried, cx, cy),
            shape(levels, cx, cy),
            shape(5, levels, cx, cy),
            shape(levels, slots),
            shape(cx, slots),
            shape(cy, slots, dtype=BF16),
            shape(cx, cy),
        ],
        [held, west_courant, south_courant, mixing, adjoint_later, cell],
        "factor",
        3000000,
    )
    rows_sent = call(
        functools.partial(rows_kernel, plan),
        row_shapes,
        [tracer, west_courant, emission_scale, own_blocks],
        "rows",
        100000,
    )
    per_tile = min(2 * carried, LANES // band)

    def band_shape(first, second):
        count = carried if first == second else 2 * carried
        return shape(-(-count // per_tile) * (cx + 8), cy)

    band_shapes = [band_shape(*b) for b in plan["bands"]]
    fields = [west_courant[0], south_courant[0], emission_scale]
    observe = functools.partial(
        call, functools.partial(observe_kernel, sizes, plan, carried), name="observe", flops=2000000
    )
    if plan["relay"]:
        base, *lanes_got = lax.optimization_barrier((base, *lanes_got))
        relayed = call(
            functools.partial(relay_kernel, plan, head, cx),
            row_shapes + [shape(32, LANES)] * len(plan["x_ops"]),
            [*rows_sent, own_blocks, lanes_got[0]],
            "relay",
            10000,
        )
        rows_sent, x_sent = relayed[:2], relayed[2:]
        second_got = exchange(rows_sent[1], sizes, next_x(1))
        x_got = [exchange(s, sizes, jump(d, d, 1)) for s, d in zip(x_sent, plan["x_ops"])]
        rows_got = [exchange(rows_sent[0], sizes, next_x(0)), second_got]
        held_y, *_ = lax.optimization_barrier((lanes_got[0], *rows_sent, *x_sent))
        rim = call(
            functools.partial(rim_kernel, plan, carried, levels, cx),
            [
                shape(levels, LANES),
                shape(levels, LANES),
                shape(levels, LANES),
                shape(6, levels, LANES),
                shape(levels, slots),
                shape(cx, slots),
                shape(LANES, slots, dtype=BF16),
                shape(1, slots),
            ],
            [lanes_sent[0], held_y],
            "rim",
            400000,
            scratch=[pltpu.VMEM((LANES, LANES), F32)],
        )
        base_rim, _ = lax.optimization_barrier((base_rim, rim[0]))
        rim_base = exchange(base_rim, sizes, next_y(0))
        parcel_rows = plan["parcel"] + (carried + 2) * cx
        parcel, state = observe(
            [shape(parcel_rows, cy), shape(4, slots)],
            [inner, mixing, inverse, ratio, columns, in_row, in_lane, live, *rows_sent, *rows_got]
            + [*lanes_sent, *lanes_got, own_blocks, *x_got, base, rim_base, *rim],
            scratch=[pltpu.VMEM((LANES, LANES), F32), pltpu.VMEM((levels, LANES), F32)],
        )
        parcel_other = other_core(parcel)
        band_sent = call(
            functools.partial(weigh_kernel, sizes, plan, carried, levels),
            band_shapes,
            [parcel, parcel_other, state, in_row, in_lane, base, rim[5], rim_base, *fields, *rows_got, *lanes_got],
            "weigh",
            500000,
        )
        lanes_own = [parcel_other[parcel_rows - cx :]]
        held, *_ = lax.optimization_barrier((tracer, *band_sent))
    else:
        rows_got = [exchange(rows_sent[n], sizes, next_x(n)) for n in range(2)]
        pair_got = [exchange(s, sizes, jump(*p)) for s, p in zip(pair_sent, plan["pairs"])]
        base_other = other_core(base)
        modeled, state = observe(
            [shape(1, slots), shape(2, slots)],
            [inner, mixing, inverse, ratio, columns, in_row, in_lane, live, *rows_sent, *rows_got]
            + [*lanes_sent, *lanes_got, own_blocks, *pair_got]
            + [other_core(jnp.concatenate(pair_got, axis=0))],
        )
        near, *rims_sent = call(
            functools.partial(force_kernel, plan),
            [shape(2 * carried, cx, cy)] + [shape(cx, cy)] * y_ops,
            [modeled, other_core(modeled), state, in_row, in_lane, base, base_other],
            "force",
            200000,
        )
        rims_got = [exchange(rims_sent[n], sizes, next_y(n)) for n in range(y_ops)]
        band_sent = call(
            functools.partial(surface_kernel, sizes, plan, carried, levels),
            band_shapes,
            [near, *fields, *rows_got, *lanes_got, *rims_got],
            "surface",
            400000,
        )
        lanes_own = lanes_got
        held = tracer
    (advanced,) = call(
        functools.partial(advance_kernel, plan),
        [shape(*tracer.shape)],
        [held, parts, mixing, inverse, ratio]
        + list(rows_sent)
        + rows_got
        + list(lanes_sent)
        + lanes_own,
        "advance",
        6000000,
        scratch=[pltpu.VMEM(tracer.shape, F32)]
        + [pltpu.VMEM((carried * levels, cy), F32)] * 2
        + [pltpu.SemaphoreType.DMA((levels // 4,))],
        out_hbm=(0,),
    )
    band_got = [
        s
        if first == second == 0
        else exchange(s, sizes, jump(first * many_y, second * many_y, plan["cross"]))
        for s, (first, second) in zip(band_sent, plan["bands"])
    ]
    advanced, *band_got = lax.optimization_barrier((advanced, *band_got))
    (sums,) = call(
        functools.partial(regrid_kernel, sizes, plan, carried, cx, band),
        [shape(2 * carried, ll)],
        [regrid_index.reshape(taps, ll), regrid_weight.reshape(taps, ll)] + band_got,
        "regrid",
        1000000,
    )
    sums_other = other_core(sums[carried:])
    latlon = sums[:carried] + sums_other
    return (advanced, latlon[:, None, None, :])


def solution(mesh):
    in_specs = (
        P("lev", "groups", "facex", "facey"),
        P("groups", "facex", "facey"),
        P("groups", "facex", "facey"),
        P("groups", "facex", "facey"),
        P("lev", "groups", "facex", "facey"),
        P("facex", "facey"),
        P("facex", "facey", "groups", None),
        P("facex", "facey", "groups"),
        P("facex", "facey", "groups", None, None),
        P("facex", "facey", "groups", None),
        P("facex", "facey", "groups", None),
        P("facex", "facey", None, None),
        P("facex", "facey", None, None),
    )
    out_specs = (P("lev", "groups", "facex", "facey"), P("lev", "facex", "facey", "groups"))
    sizes = tuple(mesh.shape[axis] for axis in GROUP)
    return jax.shard_map(
        functools.partial(local, sizes), mesh=mesh, in_specs=in_specs, out_specs=out_specs, check_vma=False
    )
```

```python
import functools

import jax
import jax.numpy as jnp
from jax import lax
from jax.experimental import pallas as pl
from jax.experimental.pallas import tpu as pltpu
from jax.sharding import PartitionSpec as P

F32 = jnp.float32
BF16 = jnp.bfloat16
LANES = 128


def call(body, outs, ins, name, flops, smem=(), hbm=(), scratch=(), out_hbm=()):
    moved = sum(4 * a.size for a in ins) + sum(4 * o.size for o in outs)
    ins = [pltpu.with_memory_space_constraint(a, pltpu.HBM) if i in hbm else a for i, a in enumerate(ins)]

    def space(number):
        return pltpu.SMEM if number in smem else pltpu.HBM if number in hbm else pltpu.VMEM

    return pl.pallas_call(
        body,
        out_shape=outs,
        in_specs=[pl.BlockSpec(memory_space=space(i)) for i in range(len(ins))],
        out_specs=[
            pl.BlockSpec(memory_space=pltpu.HBM if i in out_hbm else pltpu.VMEM) for i in range(len(outs))
        ],
        scratch_shapes=scratch,
        compiler_params=pltpu.CompilerParams(vmem_limit_bytes=40 << 20),
        cost_estimate=pl.CostEstimate(flops=flops, bytes_accessed=moved, transcendentals=0),
        name=name,
    )(*ins)


def shape(*dims, dtype=F32):
    return jax.ShapeDtypeStruct(dims, dtype)


def iota(dims, axis):
    return lax.broadcasted_iota(jnp.int32, dims, axis)


def halves(values):
    high = values.astype(BF16)
    return high, (values - high.astype(F32)).astype(BF16)


def tile_of(sizes):
    return lax.axis_index("facex") * sizes[1] + lax.axis_index("facey")


def is_even(axis):
    return lax.rem(lax.axis_index(axis), 2) == 0


def up(values):
    rows = values.shape[0]
    rolled = pltpu.roll(values, rows - 1, 0)
    return jnp.where(iota(values.shape, 0) == rows - 1, 0.0, rolled)


def right(values):
    rolled = pltpu.roll(values, 1, 1)
    return jnp.where(iota(values.shape, 1) == 0, 0.0, rolled)


def left(values):
    lanes = values.shape[1]
    rolled = pltpu.roll(values, lanes - 1, 1)
    return jnp.where(iota(values.shape, 1) == lanes - 1, 0.0, rolled)


def shares(west, south):
    east, north = up(west), left(south)
    middle = 1.0 + jnp.minimum(west, 0.0) - jnp.maximum(east, 0.0)
    middle = middle + jnp.minimum(south, 0.0) - jnp.maximum(north, 0.0)
    row, lane = iota(west.shape, 0), iota(west.shape, 1)
    return (
        middle,
        jnp.where(row == 0, 0.0, jnp.maximum(west, 0.0)),
        -jnp.minimum(east, 0.0),
        jnp.where(lane == 0, 0.0, jnp.maximum(south, 0.0)),
        -jnp.minimum(north, 0.0),
    )


def mix(parts, cells):
    rows, lanes = cells.shape
    middle, west, east, south, north = parts
    total = middle * cells + west * pltpu.roll(cells, 1, 0) + east * pltpu.roll(cells, rows - 1, 0)
    return total + south * pltpu.roll(cells, 1, 1) + north * pltpu.roll(cells, lanes - 1, 1)


def pack_kernel(sizes, plan, *refs):
    sources, refs = refs[:10], refs[10:]
    lanes_out, refs = refs[: plan["y_ops"]], refs[plan["y_ops"] :]
    own_out, refs = refs[0], refs[1:]
    block_outs, refs = refs[: len(plan["pairs"])], refs[len(plan["pairs"]) :]
    cell_out, live_out, tracer, west, south, scale, mixing, *refs = refs
    kernels, observed, weights, cells, counts, done = refs
    carried, levels, cx, cy = tracer.shape
    me = tile_of(sizes)
    copies = [
        pltpu.make_async_copy(source, target, done.at[number])
        for number, (source, target) in enumerate(
            zip(sources[1:], (west, south, scale, kernels, observed, weights, cells, counts, mixing))
        )
    ]
    copies += [
        pltpu.make_async_copy(sources[0].at[t], tracer.at[t], done.at[9 + t]) for t in range(carried)
    ]
    for number in (3, 4, 5, 6, 7, 1, 0, 8, *range(9, 9 + carried), 2):
        copies[number].start()

    def block(offset):
        where_to = jnp.bitwise_xor(me, offset)
        mine = kernels[where_to]
        last = jnp.concatenate(
            [
                observed[pl.ds(where_to, 1), :],
                weights[pl.ds(where_to, 1), :],
                jnp.zeros((6, mine.shape[1]), F32),
            ],
            axis=0,
        )
        return jnp.concatenate([mine[8 * g : 8 * g + 8] for g in range(levels // 8)] + [last], axis=1)

    for number in (3, 4, 5):
        copies[number].wait()
    for number, offset in enumerate(plan["y_blocks"]):
        at = plan["y_tiles"] * cx + 8 * number
        lanes_out[0][at : at + 8, :] = block(offset)
    for number, offset in enumerate(plan["own_blocks"]):
        own_out[8 * number : 8 * number + 8, :] = block(offset)
    first_core = lax.axis_index("lev") == 0
    for out, (for_first, for_second) in zip(block_outs, plan["pairs"]):
        out[...] = block(jnp.where(first_core, for_first, for_second))

    owners, cap = cells.shape
    slot = iota((1, cap), 1)
    copies[6].wait()
    copies[7].wait()
    cell_parts = []
    live_parts = []
    for offset in range(owners):
        owner = jnp.bitwise_xor(me, offset)
        cell_parts.append(cells[pl.ds(owner, 1), :])
        live_parts.append(jnp.where(slot < counts[owner], 1.0, 0.0))
    cell = jnp.concatenate(cell_parts, axis=1)
    live = jnp.concatenate(live_parts, axis=1)
    cell_out[...] = cell
    live_out[...] = live
    if plan["relay"]:
        at = plan["y_tiles"] * cx + 8 * len(plan["y_blocks"])
        strips = owners * cap // LANES
        for number in range(strips):
            part = slice(number * LANES, (number + 1) * LANES)
            lanes_out[0][at + number : at + number + 1, :] = cell[:, part].astype(F32)
            lanes_out[0][at + strips + number : at + strips + number + 1, :] = live[:, part]

    for number in (1, 0, 8):
        copies[number].wait()
    lane = iota((cx, cy), 1)
    if plan["relay"]:
        edge = edge_of(0, cy)
        inner = jnp.where(edge == 0, 1, cy - 2)
        tiles = {name: LanePacker(lane, at) for name, at in zip("cdvwuk", (edge, inner, edge, inner, edge, edge))}
        for level in range(levels):
            turned = pltpu.roll(south[level], level, 1) if level else south[level]
            tiles["v"].put(level, turned)
            tiles["w"].put(level, turned)
            tiles["u"].put(level, pltpu.roll(west[level], level, 1) if level else west[level])
            if level < levels - 1:
                tiles["k"].put(level, pltpu.roll(mixing[level], level, 1) if level else mixing[level])
        totals = None
        for t in range(carried):
            copies[9 + t].wait()
            totals = [tracer[t, level] + (totals[level] if t else 0.0) for level in range(levels)]
        for level in range(levels):
            turned = pltpu.roll(totals[level], level, 1) if level else totals[level]
            tiles["c"].put(level, turned)
            tiles["d"].put(level, turned)
        packed = jnp.zeros((cx, cy), F32)
        for name in "cdvwu":
            packed = packed + tiles[name].packed(plan["lane_" + name])
        lanes_out[0][0:cx, :] = packed
        lanes_out[0][cx : 2 * cx, :] = tiles["k"].packed(0)
    else:
        edges = [LanePacker(lane, edge_of(number, cy)) for number in range(len(lanes_out))]
        for t in range(carried):
            copies[9 + t].wait()
        for f in range(carried + 1):
            for level in range(levels):
                spot = f * levels + level
                values = tracer[f, level] if f < carried else south[level]
                for tile in edges:
                    tile.put(spot, pltpu.roll(values, spot, 1) if spot else values)
        for tile, out in zip(edges, lanes_out):
            out[0:cx, :] = tile.packed(0)
    copies[2].wait()


class LanePacker:
    def __init__(self, lane, edge):
        self.lanes = lane.shape[1]
        self.back = lax.rem(2 * self.lanes - edge, self.lanes)
        self.place = lax.rem(lane + self.back, self.lanes)
        self.tile = jnp.zeros(lane.shape, F32)

    def put(self, spot, turned):
        self.tile = jnp.where(self.place == spot, turned, self.tile)

    def packed(self, start):
        return pltpu.roll(self.tile, lax.rem(self.back + start, self.lanes), 1)


def edge_of(number, lanes):
    even_y = is_even("facey")
    return jnp.where(even_y if number == 0 else jnp.logical_not(even_y), lanes - 1, 0)


def rows_kernel(plan, tracer, west, scale, blocks, *outs):
    carried, levels, cx, cy = tracer.shape
    head = (carried + 1) * levels
    even_x = is_even("facex")
    if plan["relay"]:
        tile = LanePacker(iota((cx, cy), 1), edge_of(0, cy))
        for t in range(carried):
            for level in range(levels):
                spot = t * levels + level
                tile.put(spot, pltpu.roll(tracer[t, level], spot, 1) if spot else tracer[t, level])
        outs[2][...] = tile.packed(0)
    for number, out in enumerate(outs[:2]):
        row = jnp.where(even_x if number == 0 else jnp.logical_not(even_x), cx - 1, 0)
        for level in range(levels):
            for t in range(carried):
                spot = t * levels + level
                out[spot : spot + 1, :] = tracer[t, level, pl.ds(row, 1), :]
            spot = carried * levels + level
            out[spot : spot + 1, :] = west[level, pl.ds(row, 1), :]
        out[head : head + 8, :] = jnp.broadcast_to(scale[pl.ds(row, 1), :], (8, cy))
        if plan["x_blocks"][number] and not plan["relay"]:
            at = 8 * plan["own_blocks"].index(plan["x_blocks"][number])
            out[head + 8 : head + 16, :] = blocks[at : at + 8, :]


def relay_kernel(plan, head, cx, number, rows, blocks, y_got, out):
    even_x = is_even("facex")
    out[0 : head + 8, :] = rows[0 : head + 8, :]
    row = jnp.where(even_x if number == 0 else jnp.logical_not(even_x), cx - 1, 0)
    out[head + 8 : head + 16, :] = jnp.broadcast_to(y_got[pl.ds(row, 1), :], (8, out.shape[1]))
    offset = plan["x_blocks"][number]
    if offset:
        at = plan["y_tiles"] * cx + 8 * offset
        out[head + 16 : head + 32, :] = blocks[8 * offset : 8 * offset + 16, :]
        out[head + 32 : head + 48, :] = y_got[at : at + 16, :]


def beyond_kernel(plan, cx, blocks, y_got, *outs):
    for out, offset in zip(outs, plan["x_ops"]):
        at = plan["y_tiles"] * cx + 8 * offset
        out[0:16, :] = blocks[8 * offset : 8 * offset + 16, :]
        out[16:32, :] = y_got[at : at + 16, :]


def rim_kernel(plan, carried, levels, cx, y_sent, y_got, base, base_other, lanes, *refs):
    inverse_out, ratio_out, mixing_out, pieces_out, columns_out, rows_out, picks_out, live_out, base_out, square = refs
    cy = y_got.shape[1]
    slots = live_out.shape[1]

    def turned(values):
        square[...] = jnp.zeros((LANES, LANES), F32)
        square[0:cx, :] = values
        return jnp.transpose(square[...])

    def part(values, name):
        return values[plan["lane_" + name] : plan["lane_" + name] + levels]

    beyond = turned(y_got[0:cx, :])
    mine = turned(y_sent[0:cx, :])
    mixing_out[...] = turned(y_got[cx : 2 * cx, :])[0:levels]
    north = is_even("facey")
    pieces_out[0] = part(beyond, "c")
    pieces_out[1] = part(beyond, "u")
    pieces_out[2] = part(beyond, "v")
    pieces_out[3] = jnp.where(north, part(beyond, "w"), part(mine, "v"))
    pieces_out[4] = jnp.where(north, part(mine, "c"), part(beyond, "d"))
    pieces_out[5] = jnp.where(north, part(beyond, "d"), part(mine, "c"))

    def level_of(ref, level):
        return jnp.broadcast_to(ref[level : level + 1, :], (8, LANES))

    first = []
    ratios = []
    before = None
    for level in range(levels):
        diagonal = jnp.ones((8, LANES), F32)
        if level > 0:
            below = level_of(mixing_out, level - 1)
            diagonal = diagonal + below
        if level < levels - 1:
            diagonal = diagonal + level_of(mixing_out, level)
        if level > 0:
            diagonal = diagonal - below * below * before
        inverse = 1.0 / diagonal
        ratios.append(level_of(mixing_out, level) * inverse if level < levels - 1 else jnp.zeros((8, LANES), F32))
        inverse_out[level : level + 1, :] = inverse[0:1]
        ratio_out[level : level + 1, :] = ratios[-1][0:1]
        first.append(inverse if level == 0 else below * first[-1] * inverse)
        before = inverse
    weight = first
    for level in range(levels - 2, -1, -1):
        weight[level] = first[level] + ratios[level] * weight[level + 1]
    for level in range(levels):
        square[level : level + 1, :] = weight[level][0:1]
    weights = square[0:levels, :]
    tile = LanePacker(iota((cx, cy), 1), edge_of(0, cy))
    for t in range(2 * carried):
        values = base[t] if t < carried else base_other[t - carried]
        tile.put(t, pltpu.roll(values, t, 1) if t else values)
    base_out[0:cx, :] = tile.packed(0)
    base_out[cx : 2 * cx, :] = lanes[...]
    at = plan["y_tiles"] * cx + 8 * len(plan["y_blocks"])
    strips = slots // LANES
    cell = jnp.concatenate([y_got[at + n : at + n + 1, :] for n in range(strips)], axis=1).astype(jnp.int32)
    live_out[...] = jnp.concatenate([y_got[at + strips + n : at + strips + n + 1, :] for n in range(strips)], axis=1)
    on_edge = lax.rem(cell, cy) == jnp.where(north, 0, cy - 1)
    x_of = jnp.where(on_edge, lax.div(cell, cy), LANES)
    picks = jnp.where(iota((LANES, slots), 0) == x_of, 1.0, 0.0)
    rows_out[...] = picks[0:cx]
    picks = picks.astype(BF16)
    picks_out[...] = picks
    high, low = halves(weights)
    columns_out[...] = jnp.dot(high, picks, preferred_element_type=F32) + jnp.dot(
        low, picks, preferred_element_type=F32
    )


def factor_kernel(sizes, *refs):
    (tracer, west, south, mixing, adjoint, cells) = refs[:6]
    inverse_out, ratio_out, base_out, inner_out, shares_out, columns_out, rows_out, picks_out = refs[6:]
    carried, levels, cx, cy = tracer.shape
    slots = cells.shape[1]
    first = []
    before = None
    for level in range(levels):
        diagonal = jnp.ones((cx, cy), F32)
        if level > 0:
            diagonal = diagonal + mixing[level - 1]
        if level < levels - 1:
            diagonal = diagonal + mixing[level]
        if level > 0:
            diagonal = diagonal - mixing[level - 1] * mixing[level - 1] * before
        inverse = 1.0 / diagonal
        inverse_out[level] = inverse
        if level < levels - 1:
            ratio_out[level] = mixing[level] * inverse
        first.append(inverse if level == 0 else mixing[level - 1] * first[-1] * inverse)
        before = inverse
    ratio_out[levels - 1] = jnp.zeros((cx, cy), F32)
    weight = first
    for level in range(levels - 2, -1, -1):
        weight[level] = first[level] + ratio_out[level] * weight[level + 1]
    for t in range(carried):
        total = weight[0] * adjoint[t, 0]
        for level in range(1, levels):
            total = total + weight[level] * adjoint[t, level]
        base_out[t] = total
    for level in range(levels):
        total = tracer[0, level]
        for t in range(1, carried):
            total = total + tracer[t, level]
        parts = shares(west[level], south[level])
        for number, part in enumerate(parts):
            shares_out[number, level] = part
        inner_out[level] = mix(parts, total)
    cell = cells[...]
    x_of = lax.div(cell, cy)
    y_of = lax.rem(cell, cy)
    in_row = jnp.where(iota((cx, slots), 0) == x_of, 1.0, 0.0)
    in_lane = jnp.where(iota((cy, slots), 0) == y_of, 1.0, 0.0).astype(BF16)
    rows_out[...] = in_row
    picks_out[...] = in_lane
    high, low = halves(jnp.concatenate(weight, axis=0))
    picked = jnp.dot(high, in_lane, preferred_element_type=F32)
    picked = picked + jnp.dot(low, in_lane, preferred_element_type=F32)
    for level in range(levels):
        part = picked[level * cx : (level + 1) * cx] * in_row
        columns_out[level : level + 1, :] = jnp.sum(part, axis=0, keepdims=True)


def sides(first, second):
    even_x = is_even("facex")
    return jnp.where(even_x, second, first), jnp.where(even_x, first, second)


def seam(number, sent, got, sent_face, got_face):
    even_y = is_even("facey")
    north = even_y if number == 0 else jnp.logical_not(even_y)
    to_north = -(jnp.maximum(got_face, 0.0) * sent + jnp.minimum(got_face, 0.0) * got)
    to_south = jnp.maximum(sent_face, 0.0) * got
    return jnp.where(north, to_north, to_south), jnp.where(north, sent.shape[1] - 1, 0)


def spread_wind(values, start, carried, levels):
    lane = iota(values.shape, 1)
    result = jnp.zeros_like(values)
    for t in range(carried):
        moved = pltpu.roll(values, (t * levels - start) % values.shape[1], 1)
        inside = jnp.logical_and(lane >= t * levels, lane < (t + 1) * levels)
        result = jnp.where(inside, moved, result)
    return result


def seam_lanes(number, plan, sent, got, sent_wind, got_wind, carried, levels):
    start = plan["lane_v"]
    faces = [spread_wind(wind, start, carried, levels) for wind in (sent_wind, got_wind)]
    return seam(number, sent, got, *faces)


def observe_kernel(sizes, plan, carried, *refs):
    refs = list(refs)
    got = refs[1::-1]
    inner, mixing, inverse, ratio, columns, in_row, in_lane, live = refs[2:10]
    sent = refs[10:12]
    refs = refs[12:]
    y_sent = refs[: plan["y_ops"]]
    y_got = refs[plan["y_ops"] : 2 * plan["y_ops"]]
    refs = refs[2 * plan["y_ops"] :]
    own = refs[0]
    n_pairs = len(plan["pairs"])
    pair_got = refs[1 : 1 + n_pairs]
    swapped = refs[1 + n_pairs] if n_pairs else None
    if plan["relay"]:
        x_got = refs[1 : 1 + len(plan["x_ops"])]
        refs = refs[1 + len(plan["x_ops"]) :]
        rim = refs[:8]
        parcel, state_out, turn, rise = refs[8:]
    else:
        modeled_out, state_out = refs[-2:]
    levels, cx, cy = inner.shape
    slots = in_row.shape[1]
    head = (carried + 1) * levels

    def summed(rows):
        total = rows[0:levels]
        for t in range(1, carried):
            total = total + rows[t * levels : (t + 1) * levels]
        return total

    beyond_west, beyond_east = sides(got[0][0:head], got[1][0:head])
    at_west, at_east = sides(sent[0][0:head], sent[1][0:head])
    spot = carried * levels
    face_west = at_west[spot:head]
    face_east = beyond_east[spot:head]
    from_west = jnp.maximum(face_west, 0.0) * summed(beyond_west)
    from_east = -(
        jnp.maximum(face_east, 0.0) * summed(at_east) + jnp.minimum(face_east, 0.0) * summed(beyond_east)
    )
    lane_parts = []
    for number in range(plan["y_ops"]):
        mine, beyond = y_sent[number][0:cx, :], y_got[number][0:cx, :]
        if plan["relay"]:
            faces = [pltpu.roll(values, cy - plan["lane_v"], 1) for values in (mine, beyond)]
            total, spot_y = seam(number, mine, beyond, *faces)
        else:
            part, spot_y = seam_lanes(number, plan, mine, beyond, mine, beyond, carried, levels)
            total = part
            for t in range(1, carried):
                total = total + pltpu.roll(part, (-t * levels) % cy, 1)
        lane_parts.append((pltpu.roll(total, spot_y, 1), spot_y))
    lane = iota((cx, cy), 1)
    row = iota((cx, cy), 0)
    forward = []
    for level in range(levels):
        value = inner[level]
        value = value + jnp.where(row == 0, from_west[level : level + 1], 0.0)
        value = value + jnp.where(row == cx - 1, from_east[level : level + 1], 0.0)
        for total, spot_y in lane_parts:
            moved = pltpu.roll(total, cy - level, 1) if level else total
            value = value + jnp.where(lane == spot_y, moved, 0.0)
        if level > 0:
            value = value + mixing[level - 1] * forward[-1]
        forward.append(value * inverse[level])
    result = forward
    for level in range(levels - 2, -1, -1):
        result[level] = forward[level] + ratio[level] * result[level + 1]
    high, low = halves(jnp.concatenate(result, axis=0))
    picks = in_lane[...]
    picked = jnp.dot(high, picks, preferred_element_type=F32)
    picked = picked + jnp.dot(low, picks, preferred_element_type=F32)

    start = plan["y_tiles"] * cx
    if plan["relay"]:

        def block_at(ref, row):
            return ref[row : row + 8, :]

        blocks = {0: block_at(own, 0), 1: block_at(y_got[0], start + 8)}
        rim_blocks = {0: block_at(y_got[0], start), 1: block_at(own, 8)}
        carriers = [(offset, got[n], head + 16) for n, offset in enumerate(plan["x_blocks"]) if offset]
        carriers += [(offset, ref, 0) for offset, ref in zip(plan["x_ops"], x_got)]
        for offset, ref, row in carriers:
            blocks[offset], rim_blocks[offset + 1] = block_at(ref, row), block_at(ref, row + 8)
            rim_blocks[offset], blocks[offset + 1] = block_at(ref, row + 16), block_at(ref, row + 24)
    else:
        blocks = {0: own[0:8, :], plan["y_blocks"][0]: y_got[0][start : start + 8, :]}
        for number in range(2):
            offset = plan["x_blocks"][number]
            if offset:
                blocks[offset] = got[number][head + 8 : head + 16, :]
    first_core = lax.axis_index("lev") == 0
    for number, (for_first, for_second) in enumerate(plan["pairs"]):
        mine = pair_got[number][...]
        other = swapped[8 * number : 8 * number + 8, :]
        if for_first == for_second:
            blocks[for_first] = mine
        else:
            blocks[for_first] = jnp.where(first_core, mine, other)
            blocks[for_second] = jnp.where(first_core, other, mine)
    cap = slots // len(blocks)
    per_tile = LANES // cap
    group_of_lane = lax.div(iota((8, LANES), 1), cap)

    def gathered(group, blocks):
        tiles = []
        for start in range(0, len(blocks), per_tile):
            tile = jnp.zeros((8, LANES), F32)
            for a in range(per_tile):
                moved = pltpu.roll(blocks[start + a], (cap * (a - group)) % LANES, 1)
                tile = jnp.where(group_of_lane == a, moved, tile)
            tiles.append(tile)
        return jnp.concatenate(tiles, axis=1)

    groups = [gathered(g, blocks) for g in range(levels // 8)]
    last = gathered(levels // 8, blocks)
    total = jnp.zeros((cx, slots), F32)
    sensitivity = jnp.zeros((8, slots), F32)
    for g, kernel in enumerate(groups):
        sensitivity = sensitivity + kernel * columns[8 * g : 8 * g + 8, :]
        for l in range(8):
            level = 8 * g + l
            total = total + kernel[l : l + 1] * picked[level * cx : (level + 1) * cx]
    modeled = jnp.sum(total * in_row[...], axis=0, keepdims=True)
    gain = jnp.sum(sensitivity, axis=0, keepdims=True) * last[1:2] * live[...]
    if not plan["relay"]:
        modeled_out[...] = modeled
        state_out[...] = jnp.concatenate([gain, last[0:1]], axis=0)
        return

    rim_inverse, rim_ratio, rim_mixing, pieces, rim_columns, rim_rows, rim_picks, rim_live = rim
    corners_west, corners_east = sides(got[0][head + 8 : head + 16, :], got[1][head + 8 : head + 16, :])
    turn[...] = jnp.zeros((LANES, LANES), F32)
    turn[0:1, :] = corners_west[0:1]
    turn[cx - 1 : cx, :] = corners_east[0:1]
    turned = jnp.transpose(turn[...])
    ends = turned[plan["lane_c"] : plan["lane_c"] + levels]
    end_face = turned[plan["lane_u"] : plan["lane_u"] + levels]
    place = iota((levels, LANES), 1)
    cells, face_w, face_s, face_n, south_cells, north_cells = (pieces[n] for n in range(6))
    west_cells = jnp.where(place == 0, ends, pltpu.roll(cells, 1, 1))
    east_cells = jnp.where(place == cx - 1, ends, pltpu.roll(cells, LANES - 1, 1))
    face_e = jnp.where(place == cx - 1, end_face, pltpu.roll(face_w, LANES - 1, 1))
    rise[0:levels, :] = advance_cells(
        cells, west_cells, east_cells, south_cells, north_cells, face_w, face_e, face_s, face_n
    )

    def level_of(ref, level):
        return jnp.broadcast_to(ref[level : level + 1, :], (8, LANES))

    climbed = []
    for level in range(levels):
        value = level_of(rise, level)
        if level > 0:
            value = value + level_of(rim_mixing, level - 1) * climbed[-1]
        climbed.append(value * level_of(rim_inverse, level))
    for level in range(levels - 2, -1, -1):
        climbed[level] = climbed[level] + level_of(rim_ratio, level) * climbed[level + 1]
    for level in range(levels):
        rise[level : level + 1, :] = climbed[level][0:1]
    high, low = halves(rise[0:levels, :])
    picks = rim_picks[...]
    picked = jnp.dot(high, picks, preferred_element_type=F32)
    picked = picked + jnp.dot(low, picks, preferred_element_type=F32)
    rim_total = jnp.zeros((8, slots), F32)
    sensitivity = jnp.zeros((8, slots), F32)
    for g in range(levels // 8):
        kernel = gathered(g, rim_blocks)
        rim_total = rim_total + kernel * picked[8 * g : 8 * g + 8]
        sensitivity = sensitivity + kernel * rim_columns[8 * g : 8 * g + 8, :]
    rim_modeled = jnp.sum(rim_total, axis=0, keepdims=True)
    rim_last = gathered(levels // 8, rim_blocks)
    rim_gain = jnp.sum(sensitivity, axis=0, keepdims=True) * rim_last[1:2] * rim_live[...]
    state_out[...] = jnp.concatenate([gain, last[0:1], rim_gain, rim_last[0:1]], axis=0)
    strips = slots // LANES
    for number in range(strips):
        part = slice(number * LANES, (number + 1) * LANES)
        parcel[number : number + 1, :] = modeled[:, part]
        parcel[strips + number : strips + number + 1, :] = rim_modeled[:, part]


def advance_cells(cells, west, east, south, north, face_w, face_e, face_s, face_n):
    flux_w = jnp.maximum(face_w, 0.0) * west + jnp.minimum(face_w, 0.0) * cells
    flux_e = jnp.maximum(face_e, 0.0) * cells + jnp.minimum(face_e, 0.0) * east
    flux_s = jnp.maximum(face_s, 0.0) * south + jnp.minimum(face_s, 0.0) * cells
    flux_n = jnp.maximum(face_n, 0.0) * cells + jnp.minimum(face_n, 0.0) * north
    return cells + flux_w - flux_e + flux_s - flux_n


def scatter(force, in_row, in_lane):
    high, low = halves(in_row * force)
    dims = (((1,), (1,)), ((), ()))
    scattered = lax.dot_general(high, in_lane, dims, preferred_element_type=F32)
    return scattered + lax.dot_general(low, in_lane, dims, preferred_element_type=F32)


def force_kernel(plan, *refs):
    modeled, modeled_other, state, in_row, in_lane, base, base_other = refs[:7]
    near_out = refs[7]
    rim_outs = refs[8:]
    carried, cx, cy = base.shape
    misfit = modeled[...] + modeled_other[...] - state[1:2, :]
    force = state[0:1, :] * misfit
    scattered = scatter(force, in_row[...], in_lane[...])
    lane = iota((cx, cy), 1)
    even_y = is_even("facey")
    edges = []
    for number in range(len(rim_outs)):
        sends_last = even_y if number == 0 else jnp.logical_not(even_y)
        edges.append(jnp.where(sends_last, cy - 1, 0))
    rims = [jnp.zeros((cx, cy), F32) for _ in rim_outs]
    for t in range(2 * carried):
        values = scattered + (base[t] if t < carried else base_other[t - carried])
        near_out[t] = values
        for number, edge in enumerate(edges):
            moved = pltpu.roll(values, lax.rem(t + cy - edge, cy), 1)
            rims[number] = jnp.where(lane == t, moved, rims[number])
    for rim, out in zip(rims, rim_outs):
        out[...] = rim


def surface_kernel(sizes, plan, carried, levels, *refs):
    y_ops = plan["y_ops"]
    near = refs[0]
    rims = refs[6 + y_ops : 6 + 2 * y_ops]
    rim_values = [[rim[...] for rim in rims] for _ in range(near.shape[0])]
    values = [near[t] for t in range(near.shape[0])]
    spread_surface(
        sizes, plan, carried, levels, values, rim_values, refs[1:4], refs[4:6], refs[6 : 6 + y_ops], refs[6 + 2 * y_ops :]
    )


def weigh_kernel(sizes, plan, carried, levels, *refs):
    parcel, other, state, in_row, in_lane, base, base_other, rim_rows, rim_base = refs[:9]
    cx, cy = base.shape[1:]
    strips = state.shape[1] // LANES

    def misfit(kind):
        both = parcel[kind * strips : (kind + 1) * strips, :] + other[kind * strips : (kind + 1) * strips, :]
        flat = jnp.concatenate([both[n : n + 1] for n in range(strips)], axis=1)
        return state[2 * kind : 2 * kind + 1, :] * (flat - state[2 * kind + 1 : 2 * kind + 2, :])

    scattered = scatter(misfit(0), in_row[...], in_lane[...])
    on_rim = jnp.sum(rim_rows[...] * misfit(1), axis=1, keepdims=True)
    near = [scattered + base[t] for t in range(carried)]
    near += [scattered + base_other[t] for t in range(carried)]
    rims = [[rim_base[0:cx, :] + on_rim] for _ in near]
    spread_surface(sizes, plan, carried, levels, near, rims, refs[9:12], refs[12:14], refs[14:15], refs[15:])


def spread_surface(sizes, plan, carried, levels, near, rim_values, fields, got, y_got, outs):
    west, south, scale = fields
    tracers = len(near)
    cx, cy = near[0].shape
    spot_v = plan["lane_v"]
    band = cy // sizes[0]
    per_tile = min(tracers, LANES // band)
    spot = carried * levels
    head = (carried + 1) * levels
    lane = iota((cx, cy), 1)
    row = iota((cx, cy), 0)
    even_y = is_even("facey")
    face_west = west[...]
    face_south = south[...]
    scales = scale[...]
    beyond_west, beyond_east = sides(got[0][head : head + 1], got[1][head : head + 1])
    _, east_wind = sides(got[0][spot : spot + 1], got[1][spot : spot + 1])
    face_east = jnp.where(row == cx - 1, east_wind, pltpu.roll(face_west, cx - 1, 0))
    face_north = left(face_south)
    norths = []
    for number in range(plan["y_ops"]):
        norths.append(even_y if number == 0 else jnp.logical_not(even_y))
        moved = pltpu.roll(y_got[number][0:cx, :], cy - 1 - spot_v, 1)
        keep = jnp.logical_and(lane == cy - 1, norths[number])
        face_north = jnp.where(keep, moved, face_north)
    to_middle = 1.0 + jnp.minimum(face_west, 0.0) - jnp.maximum(face_east, 0.0)
    to_middle = scales * (to_middle + jnp.minimum(face_south, 0.0) - jnp.maximum(face_north, 0.0))
    to_east = jnp.where(row == cx - 1, 0.0, scales * jnp.maximum(face_east, 0.0))
    to_west = jnp.where(row == 0, 0.0, scales * jnp.minimum(face_west, 0.0))
    to_north = scales * jnp.maximum(face_north, 0.0)
    to_south = scales * jnp.minimum(face_south, 0.0)
    west_gain = beyond_west * jnp.maximum(face_west[0:1], 0.0)
    east_gain = -beyond_east * jnp.minimum(face_east[cx - 1 : cx], 0.0)
    filler = jnp.zeros((6, cy), F32)
    grown = []
    for t in range(tracers):
        values = near[t]
        north_side = left(values)
        south_side = right(values)
        for number in range(plan["y_ops"]):
            rim = rim_values[t][number]
            at_north = jnp.logical_and(lane == cy - 1, norths[number])
            at_south = jnp.logical_and(lane == 0, jnp.logical_not(norths[number]))
            north_side = jnp.where(at_north, pltpu.roll(rim, (cy - 1 - t) % cy, 1), north_side)
            south_side = jnp.where(at_south, pltpu.roll(rim, (-t) % cy, 1), south_side)
        swept = to_middle * values + to_east * pltpu.roll(values, cx - 1, 0) - to_west * pltpu.roll(values, 1, 0)
        swept = swept + to_north * north_side - to_south * south_side
        grown.append(
            jnp.concatenate(
                [swept, west_gain * values[0:1], east_gain * values[cx - 1 : cx], filler], axis=0
            )
        )
    rows = cx + 8
    group_of_lane = lax.div(iota((rows, cy), 1), band)
    first_core = lax.axis_index("lev") == 0
    place = lax.axis_index("facex")
    for out, (for_first, for_second) in zip(outs, plan["bands"]):
        offset = for_first if for_first == for_second else jnp.where(first_core, for_first, for_second)
        target = jnp.bitwise_xor(place, offset)
        count = carried if for_first == for_second else tracers
        skip = carried if for_first == for_second != 0 and plan["cross"] else 0
        for start in range(0, count, per_tile):
            tile = jnp.zeros((rows, cy), F32)
            for a in range(min(per_tile, count - start)):
                moved = pltpu.roll(grown[skip + start + a], lax.rem(band * a + cy - band * target, cy), 1)
                tile = jnp.where(group_of_lane == a, moved, tile)
            out[start // per_tile * rows : (start // per_tile + 1) * rows, :] = tile


def regrid_kernel(sizes, plan, carried, cx, band, *refs):
    index, weight = refs[:2]
    blocks = refs[2:-1]
    out = refs[-1]
    taps, cells = index.shape
    tracers = 2 * carried
    rows = cx + 8
    per_tile = min(tracers, LANES // band)
    lane = iota((rows, LANES), 1)
    row = iota((rows, cells), 0)
    first_core = lax.axis_index("lev") == 0
    place = lax.axis_index("facex")
    around = sizes[0] * cx
    parts = []
    row_places = []
    for block, (for_first, for_second) in zip(blocks, plan["bands"]):
        from_first, from_second = (for_second, for_first) if plan["cross"] else (for_first, for_second)
        offset = for_first if for_first == for_second else jnp.where(first_core, from_first, from_second)
        start = jnp.bitwise_xor(place, offset) * cx
        places = start + row
        places = jnp.where(row == cx, lax.rem(start + around - 1, around), places)
        places = jnp.where(row == cx + 1, lax.rem(start + cx, around), places)
        row_places.append(places)
        count = carried if for_first == for_second else tracers
        mine = []
        for t in range(count):
            tile = block[t // per_tile * rows : (t // per_tile + 1) * rows, :]
            a = t % per_tile
            values = tile if a == 0 else pltpu.roll(tile, (-band * a) % LANES, 1)
            high = values.astype(BF16).astype(F32)
            low = pltpu.roll(values - high, band, 1)
            both = jnp.where(lane < band, high, jnp.where(lane < 2 * band, low, 0.0))
            mine.append(both.astype(BF16))
        parts.append(mine)
    left_side = jnp.concatenate([jnp.concatenate(mine, axis=0) for mine in parts], axis=0)
    spread = iota((LANES, cells), 0)
    in_band = lax.rem(spread, band)
    used = spread < 2 * band
    totals = [[jnp.zeros((rows, cells), F32) for _ in mine] for mine in parts]
    for tap in range(taps):
        place_of = index[tap : tap + 1, :]
        column = lax.div(place_of, band)
        in_lane = lax.rem(place_of, band)
        picks = jnp.where(jnp.logical_and(in_band == in_lane, used), 1.0, 0.0).astype(BF16)
        picked = jnp.dot(left_side, picks, preferred_element_type=F32)
        at = 0
        for number, mine in enumerate(parts):
            chosen = jnp.where(row_places[number] == column, weight[tap : tap + 1, :], 0.0)
            for t in range(len(mine)):
                totals[number][t] = totals[number][t] + chosen * picked[at : at + rows]
                at += rows
    sums = [jnp.zeros((1, cells), F32) for _ in range(tracers)]
    for mine in totals:
        skip = carried if len(mine) == tracers and plan["cross"] else 0
        for t, total in enumerate(mine):
            to = (t + skip) % tracers
            sums[to] = sums[to] + jnp.sum(total, axis=0, keepdims=True)
    out[...] = jnp.concatenate(sums, axis=0)


def advance_kernel(plan, *refs):
    tracer, parts, mixing, inverse, ratio = refs[:5]
    sent = refs[5:7]
    got = refs[7:9]
    y_ops = plan["y_ops"]
    y_sent, y_got, winds_sent, winds_got = (refs[9 + n * y_ops : 9 + (n + 1) * y_ops] for n in range(4))
    target, out, west_rows, east_rows, done = refs[-5:]
    carried, levels, cx, cy = tracer.shape
    head = (carried + 1) * levels
    spot = carried * levels
    beyond_west, beyond_east = sides(got[0][0:head], got[1][0:head])
    at_west, at_east = sides(sent[0][0:head], sent[1][0:head])
    face_west = at_west[spot:head]
    face_east = beyond_east[spot:head]
    for t in range(carried):
        part = slice(t * levels, (t + 1) * levels)
        west_rows[part, :] = jnp.maximum(face_west, 0.0) * beyond_west[part]
        east_rows[part, :] = -(
            jnp.maximum(face_east, 0.0) * at_east[part] + jnp.minimum(face_east, 0.0) * beyond_east[part]
        )
    lane = iota((cx, cy), 1)
    row = iota((cx, cy), 0)
    seams = [
        seam_lanes(
            n,
            plan,
            y_sent[n][0:cx, :],
            y_got[n][-cx:, :] if plan["relay"] else y_got[n][0:cx, :],
            winds_sent[n][0:cx, :],
            winds_got[n][0:cx, :],
            carried,
            levels,
        )
        for n in range(y_ops)
    ]
    stride = 4

    def forward(step, before):
        mixed = []
        for k in range(stride):
            level = step * stride + k
            weights = [parts[n, level] for n in range(5)]
            mixed.append([])
            for t in range(carried):
                value = mix(weights, tracer[t, level])
                value = value + jnp.where(row == 0, west_rows[pl.ds(t * levels + level, 1), :], 0.0)
                value = value + jnp.where(row == cx - 1, east_rows[pl.ds(t * levels + level, 1), :], 0.0)
                for packed, spot_y in seams:
                    moved = pltpu.roll(packed, lax.rem(spot_y - (t * levels + level) + 2 * cy, cy), 1)
                    value = value + jnp.where(lane == spot_y, moved, 0.0)
                mixed[k].append(value)
        for k in range(stride):
            level = step * stride + k
            from_below = mixing[jnp.maximum(level - 1, 0)]
            scaled = inverse[level]
            after = []
            for t in range(carried):
                value = (mixed[k][t] + from_below * before[t]) * scaled
                out[t, level] = value
                after.append(value)
            before = after
        return tuple(before)

    def copy(step):
        part = pl.ds(levels - (step + 1) * stride, stride)
        return pltpu.make_async_copy(out.at[:, part], target.at[:, part], done.at[step])

    start = tuple(jnp.zeros((cx, cy), F32) for _ in range(carried))
    lax.fori_loop(0, levels // stride, forward, start)
    above = list(start)
    for step in range(levels // stride):
        for k in range(stride):
            level = levels - 1 - step * stride - k
            factor = ratio[level]
            for t in range(carried):
                above[t] = out[t, level] + factor * above[t]
                out[t, level] = above[t]
        copy(step).start()
    for step in range(levels // stride):
        copy(step).wait()


GROUP = ("facex", "facey", "lev")


def exchange(values, sizes, rule):
    many_x, many_y, cores = sizes
    pairs = []
    for x in range(many_x):
        for y in range(many_y):
            for c in range(cores):
                to = rule(x, y, c)
                if to is not None:
                    pairs.append(((x * many_y + y) * cores + c, (to[0] * many_y + to[1]) * cores + to[2]))
    return lax.ppermute(values, GROUP, pairs)


def make_plan(sizes):
    many_x, many_y, _ = sizes
    tiles = many_x * many_y
    x_blocks = [many_y, (many_x - 1) * many_y if many_x == 4 else 0]
    relay = many_y == 2
    if relay:
        own_blocks = list(range(tiles))
        y_blocks = own_blocks
        x_ops = [offset for offset in own_blocks[2::2] if offset not in x_blocks]
        pairs = []
    else:
        own_blocks = [0] + [offset for offset in x_blocks if offset]
        y_blocks = [1]
        x_ops = []
        rest = [d for d in range(tiles) if d not in {1, *own_blocks}]
        rest.sort(key=lambda d: (d // many_y != many_x // 2, d))
        pairs = [(rest[n], rest[min(n + 1, len(rest) - 1)]) for n in range(0, len(rest), 2)]
    others = list(range(many_x - 1, 1, -1))
    bands = [(0, 0), (1, 1)] + [(others[n], others[n + 1]) for n in range(0, len(others), 2)]
    return {
        "relay": relay,
        "cross": 1 if relay else 0,
        "x_blocks": x_blocks,
        "x_ops": x_ops,
        "own_blocks": own_blocks,
        "y_blocks": y_blocks,
        "y_ops": 1 if many_y == 2 else 2,
        "y_tiles": 2 if relay else 1,
        "pairs": pairs,
        "bands": bands,
    }


def lane_plan(plan, carried, levels):
    starts = {"c": 0, "d": levels, "v": 2 * levels, "w": 3 * levels, "u": 4 * levels}
    if not plan["relay"]:
        starts = {"v": carried * levels}
    return {"lane_" + name: start for name, start in starts.items()}


def local(
    sizes,
    tracer,
    west_courant,
    south_courant,
    mixing,
    adjoint_later,
    emission_scale,
    send_cells,
    send_counts,
    kernels,
    observed,
    error_weight,
    regrid_index,
    regrid_weight,
):
    plan = make_plan(sizes)
    many_x, many_y, _ = sizes
    carried, levels, cx, cy = tracer.shape
    owners, cap = send_cells.shape[2:]
    slots = owners * cap
    taps, ll = regrid_index.shape[2:]
    plan.update(lane_plan(plan, carried, levels))
    head = (carried + 1) * levels
    y_ops = plan["y_ops"]
    band = cy // many_x

    def next_x(number):
        def rule(x, y, c):
            step = 1 if (x % 2 == 0) == (number == 0) else -1
            return ((x + step) % many_x, y, c)

        return rule

    def next_y(number, cross):
        def rule(x, y, c):
            to = y + (1 if (y % 2 == 0) == (number == 0) else -1)
            return (x, to, c ^ cross) if 0 <= to < many_y else None

        return rule

    def jump(for_first, for_second, cross=0):
        def rule(x, y, c):
            d = for_first if c == 0 else for_second
            return (x ^ (d // many_y), y ^ (d % many_y), c ^ cross)

        return rule

    def other_core(values):
        return exchange(values, sizes, lambda x, y, c: (x, y, 1 - c))

    strips = slots // LANES
    plan["parcel"] = -(-2 * strips // 8) * 8
    extra = 48 if plan["relay"] else 16
    row_shapes = [shape(head + extra, cy)] * 2
    y_rows = plan["y_tiles"] * cx + 8 * len(plan["y_blocks"]) + (plan["parcel"] if plan["relay"] else 0)
    lane_shapes = [shape(y_rows if n == 0 else cx, cy) for n in range(y_ops)]
    packed = call(
        functools.partial(pack_kernel, sizes, plan),
        lane_shapes
        + [shape(8 * len(plan["own_blocks"]), LANES)]
        + [shape(8, LANES)] * len(plan["pairs"])
        + [shape(1, slots, dtype=jnp.int32), shape(1, slots)]
        + [shape(*a.shape) for a in (tracer, west_courant, south_courant, emission_scale, mixing)],
        [
            tracer,
            west_courant,
            south_courant,
            emission_scale,
            kernels.reshape(owners, levels, cap),
            observed.reshape(owners, cap),
            error_weight.reshape(owners, cap),
            send_cells.reshape(owners, cap),
            send_counts.reshape(owners),
            mixing,
        ],
        "pack",
        100000,
        hbm=range(10),
        scratch=[
            pltpu.VMEM((owners, levels, cap), F32),
            pltpu.VMEM((owners, cap), F32),
            pltpu.VMEM((owners, cap), F32),
            pltpu.VMEM((owners, cap), jnp.int32),
            pltpu.SMEM((owners,), jnp.int32),
            pltpu.SemaphoreType.DMA((9 + carried,)),
        ],
    )
    lanes_sent = packed[:y_ops]
    own_blocks = packed[y_ops]
    pair_sent = packed[1 + y_ops : -7]
    cell, live, tracer, west_courant, south_courant, emission_scale, mixing = packed[-7:]
    lanes_got = [exchange(lanes_sent[n], sizes, next_y(n, plan["cross"])) for n in range(y_ops)]
    held, *_ = lax.optimization_barrier((tracer, *lanes_sent))
    inverse, ratio, base, inner, parts, columns, in_row, in_lane = call(
        functools.partial(factor_kernel, sizes),
        [
            shape(levels, cx, cy),
            shape(levels, cx, cy),
            shape(carried, cx, cy),
            shape(levels, cx, cy),
            shape(5, levels, cx, cy),
            shape(levels, slots),
            shape(cx, slots),
            shape(cy, slots, dtype=BF16),
        ],
        [held, west_courant, south_courant, mixing, adjoint_later, cell],
        "factor",
        3000000,
    )
    rows_sent = list(
        call(
            functools.partial(rows_kernel, plan),
            row_shapes + ([shape(cx, cy)] if plan["relay"] else []),
            [tracer, west_courant, emission_scale, own_blocks],
            "rows",
            100000,
        )
    )
    per_tile = min(2 * carried, LANES // band)

    def band_shape(first, second):
        count = carried if first == second else 2 * carried
        return shape(-(-count // per_tile) * (cx + 8), cy)

    band_shapes = [band_shape(*b) for b in plan["bands"]]
    fields = [west_courant[0], south_courant[0], emission_scale]
    observe = functools.partial(
        call, functools.partial(observe_kernel, sizes, plan, carried), name="observe", flops=2000000
    )
    if plan["relay"]:
        base, *lanes_got = lax.optimization_barrier((base, *lanes_got))
        lanes_each = rows_sent.pop()
        base_other = other_core(base)

        def relay(number, *after):
            held, *_ = lax.optimization_barrier((rows_sent[number], *after))
            return call(
                functools.partial(relay_kernel, plan, head, cx, number),
                [row_shapes[number]],
                [held, own_blocks, lanes_got[0]],
                "relay",
                10000,
            )[0]

        rows_sent = [relay(0), relay(1)]
        x_sent = call(
            functools.partial(beyond_kernel, plan, cx),
            [shape(32, LANES)] * len(plan["x_ops"]),
            [own_blocks, lanes_got[0]],
            "beyond",
            10000,
        )
        x_got = [exchange(s, sizes, jump(d, d, 1)) for s, d in zip(x_sent, plan["x_ops"])]
        rows_got = [exchange(rows_sent[n], sizes, next_x(n)) for n in range(2)]
        held_y, *_ = lax.optimization_barrier((lanes_got[0], *rows_sent))
        rim = call(
            functools.partial(rim_kernel, plan, carried, levels, cx),
            [
                shape(levels, LANES),
                shape(levels, LANES),
                shape(levels, LANES),
                shape(6, levels, LANES),
                shape(levels, slots),
                shape(cx, slots),
                shape(LANES, slots, dtype=BF16),
                shape(1, slots),
                shape(2 * cx, cy),
            ],
            [lanes_sent[0], held_y, base, base_other, lanes_each],
            "rim",
            400000,
            scratch=[pltpu.VMEM((LANES, LANES), F32)],
        )
        *rim, rim_sent = rim
        rim_got = exchange(rim_sent, sizes, next_y(0, 0))
        parcel, state = observe(
            [shape(plan["parcel"], cy), shape(4, slots)],
            [rows_got[1], rows_got[0], inner, mixing, inverse, ratio, columns, in_row, in_lane, live, *rows_sent]
            + [*lanes_sent, *lanes_got, own_blocks, *x_got, *rim],
            scratch=[pltpu.VMEM((LANES, LANES), F32), pltpu.VMEM((levels, LANES), F32)],
        )
        parcel_other = other_core(parcel)
        parcel_other, rim_got = lax.optimization_barrier((parcel_other, rim_got))
        band_sent = call(
            functools.partial(weigh_kernel, sizes, plan, carried, levels),
            band_shapes,
            [parcel, parcel_other, state, in_row, in_lane, base, base_other, rim[5], rim_got, *fields]
            + [*rows_got, *lanes_got],
            "weigh",
            500000,
        )
        lanes_own = [lanes_each, rim_got]
        held, *_ = lax.optimization_barrier((tracer, *band_sent))
    else:
        rows_got = [exchange(rows_sent[n], sizes, next_x(n)) for n in range(2)]
        pair_got = [exchange(s, sizes, jump(*p)) for s, p in zip(pair_sent, plan["pairs"])]
        base_other = other_core(base)
        modeled, state = observe(
            [shape(1, slots), shape(2, slots)],
            [rows_got[1], rows_got[0], inner, mixing, inverse, ratio, columns, in_row, in_lane, live, *rows_sent]
            + [*lanes_sent, *lanes_got, own_blocks, *pair_got]
            + [other_core(jnp.concatenate(pair_got, axis=0))],
        )
        near, *rims_sent = call(
            functools.partial(force_kernel, plan),
            [shape(2 * carried, cx, cy)] + [shape(cx, cy)] * y_ops,
            [modeled, other_core(modeled), state, in_row, in_lane, base, base_other],
            "force",
            200000,
        )
        rims_got = [exchange(rims_sent[n], sizes, next_y(n, 0)) for n in range(y_ops)]
        band_sent = call(
            functools.partial(surface_kernel, sizes, plan, carried, levels),
            band_shapes,
            [near, *fields, *rows_got, *lanes_got, *rims_got],
            "surface",
            400000,
        )
        lanes_own = [*lanes_sent, *lanes_got]
        held = tracer
    (advanced,) = call(
        functools.partial(advance_kernel, plan),
        [shape(*tracer.shape)],
        [held, parts, mixing, inverse, ratio]
        + list(rows_sent)
        + rows_got
        + lanes_own
        + list(lanes_sent)
        + lanes_got,
        "advance",
        6000000,
        scratch=[pltpu.VMEM(tracer.shape, F32)]
        + [pltpu.VMEM((carried * levels, cy), F32)] * 2
        + [pltpu.SemaphoreType.DMA((levels // 4,))],
        out_hbm=(0,),
    )
    band_got = [
        s
        if first == second == 0
        else exchange(s, sizes, jump(first * many_y, second * many_y, plan["cross"]))
        for s, (first, second) in zip(band_sent, plan["bands"])
    ]
    advanced, *band_got = lax.optimization_barrier((advanced, *band_got))
    (sums,) = call(
        functools.partial(regrid_kernel, sizes, plan, carried, cx, band),
        [shape(2 * carried, ll)],
        [regrid_index.reshape(taps, ll), regrid_weight.reshape(taps, ll)] + band_got,
        "regrid",
        1000000,
    )
    sums_other = other_core(sums[carried:])
    latlon = sums[:carried] + sums_other
    return (advanced, latlon[:, None, None, :])


def solution(mesh):
    in_specs = (
        P("lev", "groups", "facex", "facey"),
        P("groups", "facex", "facey"),
        P("groups", "facex", "facey"),
        P("groups", "facex", "facey"),
        P("lev", "groups", "facex", "facey"),
        P("facex", "facey"),
        P("facex", "facey", "groups", None),
        P("facex", "facey", "groups"),
        P("facex", "facey", "groups", None, None),
        P("facex", "facey", "groups", None),
        P("facex", "facey", "groups", None),
        P("facex", "facey", None, None),
        P("facex", "facey", None, None),
    )
    out_specs = (P("lev", "groups", "facex", "facey"), P("lev", "facex", "facey", "groups"))
    sizes = tuple(mesh.shape[axis] for axis in GROUP)
    return jax.shard_map(
        functools.partial(local, sizes), mesh=mesh, in_specs=in_specs, out_specs=out_specs, check_vma=False
    )
```

```python
import functools

import jax
import jax.numpy as jnp
from jax import lax
from jax.experimental import pallas as pl
from jax.experimental.pallas import tpu as pltpu
from jax.sharding import PartitionSpec as P

F32 = jnp.float32
BF16 = jnp.bfloat16
LANES = 128


def call(body, outs, ins, name, flops, smem=(), hbm=(), scratch=(), out_hbm=()):
    moved = sum(4 * a.size for a in ins) + sum(4 * o.size for o in outs)
    ins = [pltpu.with_memory_space_constraint(a, pltpu.HBM) if i in hbm else a for i, a in enumerate(ins)]

    def space(number):
        return pltpu.SMEM if number in smem else pltpu.HBM if number in hbm else pltpu.VMEM

    return pl.pallas_call(
        body,
        out_shape=outs,
        in_specs=[pl.BlockSpec(memory_space=space(i)) for i in range(len(ins))],
        out_specs=[
            pl.BlockSpec(memory_space=pltpu.HBM if i in out_hbm else pltpu.VMEM) for i in range(len(outs))
        ],
        scratch_shapes=scratch,
        compiler_params=pltpu.CompilerParams(vmem_limit_bytes=40 << 20),
        cost_estimate=pl.CostEstimate(flops=flops, bytes_accessed=moved, transcendentals=0),
        name=name,
    )(*ins)


def shape(*dims, dtype=F32):
    return jax.ShapeDtypeStruct(dims, dtype)


def iota(dims, axis):
    return lax.broadcasted_iota(jnp.int32, dims, axis)


def halves(values):
    high = values.astype(BF16)
    return high, (values - high.astype(F32)).astype(BF16)


def tile_of(sizes):
    return lax.axis_index("facex") * sizes[1] + lax.axis_index("facey")


def is_even(axis):
    return lax.rem(lax.axis_index(axis), 2) == 0


def up(values):
    rows = values.shape[0]
    rolled = pltpu.roll(values, rows - 1, 0)
    return jnp.where(iota(values.shape, 0) == rows - 1, 0.0, rolled)


def right(values):
    rolled = pltpu.roll(values, 1, 1)
    return jnp.where(iota(values.shape, 1) == 0, 0.0, rolled)


def left(values):
    lanes = values.shape[1]
    rolled = pltpu.roll(values, lanes - 1, 1)
    return jnp.where(iota(values.shape, 1) == lanes - 1, 0.0, rolled)


def shares(west, south):
    east, north = up(west), left(south)
    middle = 1.0 + jnp.minimum(west, 0.0) - jnp.maximum(east, 0.0)
    middle = middle + jnp.minimum(south, 0.0) - jnp.maximum(north, 0.0)
    row, lane = iota(west.shape, 0), iota(west.shape, 1)
    return (
        middle,
        jnp.where(row == 0, 0.0, jnp.maximum(west, 0.0)),
        -jnp.minimum(east, 0.0),
        jnp.where(lane == 0, 0.0, jnp.maximum(south, 0.0)),
        -jnp.minimum(north, 0.0),
    )


def mix(parts, cells):
    rows, lanes = cells.shape
    middle, west, east, south, north = parts
    total = middle * cells + west * pltpu.roll(cells, 1, 0) + east * pltpu.roll(cells, rows - 1, 0)
    return total + south * pltpu.roll(cells, 1, 1) + north * pltpu.roll(cells, lanes - 1, 1)


def pack_kernel(sizes, plan, *refs):
    sources, refs = refs[:10], refs[10:]
    lanes_out, refs = refs[: plan["y_ops"]], refs[plan["y_ops"] :]
    own_out, refs = refs[0], refs[1:]
    block_outs, refs = refs[: len(plan["pairs"])], refs[len(plan["pairs"]) :]
    cell_out, live_out, tracer, west, south, scale, mixing, *refs = refs
    kernels, observed, weights, cells, counts, done = refs
    carried, levels, cx, cy = tracer.shape
    me = tile_of(sizes)
    copies = [
        pltpu.make_async_copy(source, target, done.at[number])
        for number, (source, target) in enumerate(
            zip(sources[1:], (west, south, scale, kernels, observed, weights, cells, counts, mixing))
        )
    ]
    copies += [
        pltpu.make_async_copy(sources[0].at[t], tracer.at[t], done.at[9 + t]) for t in range(carried)
    ]
    for number in (3, 4, 5, 6, 7, 1, 0, 8, *range(9, 9 + carried), 2):
        copies[number].start()

    def block(offset):
        where_to = jnp.bitwise_xor(me, offset)
        mine = kernels[where_to]
        last = jnp.concatenate(
            [
                observed[pl.ds(where_to, 1), :],
                weights[pl.ds(where_to, 1), :],
                jnp.zeros((6, mine.shape[1]), F32),
            ],
            axis=0,
        )
        return jnp.concatenate([mine[8 * g : 8 * g + 8] for g in range(levels // 8)] + [last], axis=1)

    for number in (3, 4, 5):
        copies[number].wait()
    for number, offset in enumerate(plan["y_blocks"]):
        at = plan["y_tiles"] * cx + 8 * number
        lanes_out[0][at : at + 8, :] = block(offset)
    for number, offset in enumerate(plan["own_blocks"]):
        own_out[8 * number : 8 * number + 8, :] = block(offset)
    first_core = lax.axis_index("lev") == 0
    for out, (for_first, for_second) in zip(block_outs, plan["pairs"]):
        out[...] = block(jnp.where(first_core, for_first, for_second))

    owners, cap = cells.shape
    slot = iota((1, cap), 1)
    copies[6].wait()
    copies[7].wait()
    cell_parts = []
    live_parts = []
    for offset in range(owners):
        owner = jnp.bitwise_xor(me, offset)
        cell_parts.append(cells[pl.ds(owner, 1), :])
        live_parts.append(jnp.where(slot < counts[owner], 1.0, 0.0))
    cell = jnp.concatenate(cell_parts, axis=1)
    live = jnp.concatenate(live_parts, axis=1)
    cell_out[...] = cell
    live_out[...] = live
    if plan["relay"]:
        at = plan["y_tiles"] * cx + 8 * len(plan["y_blocks"])
        strips = owners * cap // LANES
        for number in range(strips):
            part = slice(number * LANES, (number + 1) * LANES)
            lanes_out[0][at + number : at + number + 1, :] = cell[:, part].astype(F32)
            lanes_out[0][at + strips + number : at + strips + number + 1, :] = live[:, part]

    for number in (1, 0, 8):
        copies[number].wait()
    lane = iota((cx, cy), 1)
    if plan["relay"]:
        edge = edge_of(0, cy)
        inner = jnp.where(edge == 0, 1, cy - 2)
        tiles = {name: LanePacker(lane, at) for name, at in zip("cdvwuk", (edge, inner, edge, inner, edge, edge))}
        for level in range(levels):
            turned = pltpu.roll(south[level], level, 1) if level else south[level]
            tiles["v"].put(level, turned)
            tiles["w"].put(level, turned)
            tiles["u"].put(level, pltpu.roll(west[level], level, 1) if level else west[level])
            if level < levels - 1:
                tiles["k"].put(level, pltpu.roll(mixing[level], level, 1) if level else mixing[level])
        totals = None
        for t in range(carried):
            copies[9 + t].wait()
            totals = [tracer[t, level] + (totals[level] if t else 0.0) for level in range(levels)]
        for level in range(levels):
            turned = pltpu.roll(totals[level], level, 1) if level else totals[level]
            tiles["c"].put(level, turned)
            tiles["d"].put(level, turned)
        packed = jnp.zeros((cx, cy), F32)
        for name in "cdvwu":
            packed = packed + tiles[name].packed(plan["lane_" + name])
        lanes_out[0][0:cx, :] = packed
        lanes_out[0][cx : 2 * cx, :] = tiles["k"].packed(0)
    else:
        edges = [LanePacker(lane, edge_of(number, cy)) for number in range(len(lanes_out))]
        for t in range(carried):
            copies[9 + t].wait()
        for f in range(carried + 1):
            for level in range(levels):
                spot = f * levels + level
                values = tracer[f, level] if f < carried else south[level]
                for tile in edges:
                    tile.put(spot, pltpu.roll(values, spot, 1) if spot else values)
        for tile, out in zip(edges, lanes_out):
            out[0:cx, :] = tile.packed(0)
    copies[2].wait()


class LanePacker:
    def __init__(self, lane, edge):
        self.lanes = lane.shape[1]
        self.back = lax.rem(2 * self.lanes - edge, self.lanes)
        self.place = lax.rem(lane + self.back, self.lanes)
        self.tile = jnp.zeros(lane.shape, F32)

    def put(self, spot, turned):
        self.tile = jnp.where(self.place == spot, turned, self.tile)

    def packed(self, start):
        return pltpu.roll(self.tile, lax.rem(self.back + start, self.lanes), 1)


def edge_of(number, lanes):
    even_y = is_even("facey")
    return jnp.where(even_y if number == 0 else jnp.logical_not(even_y), lanes - 1, 0)


def rows_kernel(plan, tracer, west, scale, blocks, *outs):
    carried, levels, cx, cy = tracer.shape
    head = (carried + 1) * levels
    even_x = is_even("facex")
    if plan["relay"]:
        tile = LanePacker(iota((cx, cy), 1), edge_of(0, cy))
        for t in range(carried):
            for level in range(levels):
                spot = t * levels + level
                tile.put(spot, pltpu.roll(tracer[t, level], spot, 1) if spot else tracer[t, level])
        outs[2][...] = tile.packed(0)
    for number, out in enumerate(outs[:2]):
        row = jnp.where(even_x if number == 0 else jnp.logical_not(even_x), cx - 1, 0)
        for level in range(levels):
            for t in range(carried):
                spot = t * levels + level
                out[spot : spot + 1, :] = tracer[t, level, pl.ds(row, 1), :]
            spot = carried * levels + level
            out[spot : spot + 1, :] = west[level, pl.ds(row, 1), :]
        out[head : head + 8, :] = jnp.broadcast_to(scale[pl.ds(row, 1), :], (8, cy))
        if plan["x_blocks"][number] and not plan["relay"]:
            at = 8 * plan["own_blocks"].index(plan["x_blocks"][number])
            out[head + 8 : head + 16, :] = blocks[at : at + 8, :]


def relay_kernel(plan, head, cx, number, rows, blocks, y_got, out):
    even_x = is_even("facex")
    out[0 : head + 8, :] = rows[0 : head + 8, :]
    row = jnp.where(even_x if number == 0 else jnp.logical_not(even_x), cx - 1, 0)
    out[head + 8 : head + 16, :] = jnp.broadcast_to(y_got[pl.ds(row, 1), :], (8, out.shape[1]))
    offset = plan["x_blocks"][number]
    if offset:
        at = plan["y_tiles"] * cx + 8 * offset
        out[head + 16 : head + 32, :] = blocks[8 * offset : 8 * offset + 16, :]
        out[head + 32 : head + 48, :] = y_got[at : at + 16, :]


def beyond_kernel(plan, cx, blocks, y_got, *outs):
    for out, offset in zip(outs, plan["x_ops"]):
        at = plan["y_tiles"] * cx + 8 * offset
        out[0:16, :] = blocks[8 * offset : 8 * offset + 16, :]
        out[16:32, :] = y_got[at : at + 16, :]


def rim_kernel(plan, carried, levels, cx, y_sent, y_got, base, base_other, lanes, *refs):
    inverse_out, ratio_out, lower_out, pieces_out, columns_out, rows_out, picks_out, live_out, base_out, square = refs
    cy = y_got.shape[1]
    slots = live_out.shape[1]

    def turned(values):
        square[...] = jnp.zeros((LANES, LANES), F32)
        square[0:cx, :] = values
        return jnp.transpose(square[...])

    def part(values, name):
        return values[plan["lane_" + name] : plan["lane_" + name] + levels]

    beyond = turned(y_got[0:cx, :])
    mine = turned(y_sent[0:cx, :])
    coupling = turned(y_got[cx : 2 * cx, :])
    north = is_even("facey")
    pieces_out[0] = part(beyond, "c")
    pieces_out[1] = part(beyond, "u")
    pieces_out[2] = part(beyond, "v")
    pieces_out[3] = jnp.where(north, part(beyond, "w"), part(mine, "v"))
    pieces_out[4] = jnp.where(north, part(mine, "c"), part(beyond, "d"))
    pieces_out[5] = jnp.where(north, part(beyond, "d"), part(mine, "c"))

    def level_of(ref, level):
        return jnp.broadcast_to(ref[level : level + 1, :], (8, LANES))

    square[...] = coupling
    first = []
    ratios = []
    before = None
    for level in range(levels):
        diagonal = jnp.ones((8, LANES), F32)
        if level > 0:
            below = level_of(square, level - 1)
            diagonal = diagonal + below
        if level < levels - 1:
            diagonal = diagonal + level_of(square, level)
        if level > 0:
            diagonal = diagonal - below * below * before
        inverse = 1.0 / diagonal
        ratios.append(level_of(square, level) * inverse if level < levels - 1 else jnp.zeros((8, LANES), F32))
        lower = below * inverse if level > 0 else jnp.zeros((8, LANES), F32)
        lower_out[level : level + 1, :] = lower[0:1]
        inverse_out[level : level + 1, :] = inverse[0:1]
        ratio_out[level : level + 1, :] = ratios[-1][0:1]
        first.append(inverse if level == 0 else lower * first[-1])
        before = inverse
    weight = first
    for level in range(levels - 2, -1, -1):
        weight[level] = first[level] + ratios[level] * weight[level + 1]
    for level in range(levels):
        square[level : level + 1, :] = weight[level][0:1]
    weights = square[0:levels, :]
    tile = LanePacker(iota((cx, cy), 1), edge_of(0, cy))
    for t in range(2 * carried):
        values = base[t] if t < carried else base_other[t - carried]
        tile.put(t, pltpu.roll(values, t, 1) if t else values)
    base_out[0:cx, :] = tile.packed(0)
    base_out[cx : 2 * cx, :] = lanes[...]
    at = plan["y_tiles"] * cx + 8 * len(plan["y_blocks"])
    strips = slots // LANES
    cell = jnp.concatenate([y_got[at + n : at + n + 1, :] for n in range(strips)], axis=1).astype(jnp.int32)
    live_out[...] = jnp.concatenate([y_got[at + strips + n : at + strips + n + 1, :] for n in range(strips)], axis=1)
    on_edge = lax.rem(cell, cy) == jnp.where(north, 0, cy - 1)
    x_of = jnp.where(on_edge, lax.div(cell, cy), LANES)
    picks = jnp.where(iota((LANES, slots), 0) == x_of, 1.0, 0.0)
    rows_out[...] = picks[0:cx]
    picks = picks.astype(BF16)
    picks_out[...] = picks
    high, low = halves(weights)
    columns_out[...] = jnp.dot(high, picks, preferred_element_type=F32) + jnp.dot(
        low, picks, preferred_element_type=F32
    )


def factor_kernel(sizes, *refs):
    (tracer, west, south, mixing, adjoint, cells) = refs[:6]
    inverse_out, lower_out, ratio_out, base_out, inner_out, shares_out, columns_out, rows_out, picks_out = refs[6:]
    carried, levels, cx, cy = tracer.shape
    slots = cells.shape[1]
    first = []
    before = None
    for level in range(levels):
        diagonal = jnp.ones((cx, cy), F32)
        if level > 0:
            diagonal = diagonal + mixing[level - 1]
        if level < levels - 1:
            diagonal = diagonal + mixing[level]
        if level > 0:
            diagonal = diagonal - mixing[level - 1] * mixing[level - 1] * before
        inverse = 1.0 / diagonal
        inverse_out[level] = inverse
        if level < levels - 1:
            ratio_out[level] = mixing[level] * inverse
        lower = mixing[level - 1] * inverse if level > 0 else jnp.zeros((cx, cy), F32)
        lower_out[level] = lower
        first.append(inverse if level == 0 else lower * first[-1])
        before = inverse
    ratio_out[levels - 1] = jnp.zeros((cx, cy), F32)
    weight = first
    for level in range(levels - 2, -1, -1):
        weight[level] = first[level] + ratio_out[level] * weight[level + 1]
    for t in range(carried):
        total = weight[0] * adjoint[t, 0]
        for level in range(1, levels):
            total = total + weight[level] * adjoint[t, level]
        base_out[t] = total
    for level in range(levels):
        total = tracer[0, level]
        for t in range(1, carried):
            total = total + tracer[t, level]
        parts = shares(west[level], south[level])
        for number, part in enumerate(parts):
            shares_out[number, level] = part
        inner_out[level] = mix(parts, total)
    cell = cells[...]
    x_of = lax.div(cell, cy)
    y_of = lax.rem(cell, cy)
    in_row = jnp.where(iota((cx, slots), 0) == x_of, 1.0, 0.0)
    in_lane = jnp.where(iota((cy, slots), 0) == y_of, 1.0, 0.0).astype(BF16)
    rows_out[...] = in_row
    picks_out[...] = in_lane
    high, low = halves(jnp.concatenate(weight, axis=0))
    picked = jnp.dot(high, in_lane, preferred_element_type=F32)
    picked = picked + jnp.dot(low, in_lane, preferred_element_type=F32)
    for level in range(levels):
        part = picked[level * cx : (level + 1) * cx] * in_row
        columns_out[level : level + 1, :] = jnp.sum(part, axis=0, keepdims=True)


def sides(first, second):
    even_x = is_even("facex")
    return jnp.where(even_x, second, first), jnp.where(even_x, first, second)


def seam(number, sent, got, sent_face, got_face):
    even_y = is_even("facey")
    north = even_y if number == 0 else jnp.logical_not(even_y)
    to_north = -(jnp.maximum(got_face, 0.0) * sent + jnp.minimum(got_face, 0.0) * got)
    to_south = jnp.maximum(sent_face, 0.0) * got
    return jnp.where(north, to_north, to_south), jnp.where(north, sent.shape[1] - 1, 0)


def spread_wind(values, start, carried, levels):
    lane = iota(values.shape, 1)
    result = jnp.zeros_like(values)
    for t in range(carried):
        moved = pltpu.roll(values, (t * levels - start) % values.shape[1], 1)
        inside = jnp.logical_and(lane >= t * levels, lane < (t + 1) * levels)
        result = jnp.where(inside, moved, result)
    return result


def seam_lanes(number, plan, sent, got, sent_wind, got_wind, carried, levels):
    start = plan["lane_v"]
    faces = [spread_wind(wind, start, carried, levels) for wind in (sent_wind, got_wind)]
    return seam(number, sent, got, *faces)


def observe_kernel(sizes, plan, carried, *refs):
    refs = list(refs)
    got = refs[1::-1]
    inner, lower, inverse, ratio, columns, in_row, in_lane, live = refs[2:10]
    sent = refs[10:12]
    refs = refs[12:]
    y_sent = refs[: plan["y_ops"]]
    y_got = refs[plan["y_ops"] : 2 * plan["y_ops"]]
    refs = refs[2 * plan["y_ops"] :]
    own = refs[0]
    n_pairs = len(plan["pairs"])
    pair_got = refs[1 : 1 + n_pairs]
    swapped = refs[1 + n_pairs] if n_pairs else None
    if plan["relay"]:
        x_got = refs[1 : 1 + len(plan["x_ops"])]
        refs = refs[1 + len(plan["x_ops"]) :]
        rim = refs[:8]
        parcel, state_out, turn, rise = refs[8:]
    else:
        modeled_out, state_out = refs[-2:]
    levels, cx, cy = inner.shape
    slots = in_row.shape[1]
    head = (carried + 1) * levels

    def summed(rows):
        total = rows[0:levels]
        for t in range(1, carried):
            total = total + rows[t * levels : (t + 1) * levels]
        return total

    beyond_west, beyond_east = sides(got[0][0:head], got[1][0:head])
    at_west, at_east = sides(sent[0][0:head], sent[1][0:head])
    spot = carried * levels
    face_west = at_west[spot:head]
    face_east = beyond_east[spot:head]
    from_west = jnp.maximum(face_west, 0.0) * summed(beyond_west)
    from_east = -(
        jnp.maximum(face_east, 0.0) * summed(at_east) + jnp.minimum(face_east, 0.0) * summed(beyond_east)
    )
    lane_parts = []
    for number in range(plan["y_ops"]):
        mine, beyond = y_sent[number][0:cx, :], y_got[number][0:cx, :]
        if plan["relay"]:
            faces = [pltpu.roll(values, cy - plan["lane_v"], 1) for values in (mine, beyond)]
            total, spot_y = seam(number, mine, beyond, *faces)
        else:
            part, spot_y = seam_lanes(number, plan, mine, beyond, mine, beyond, carried, levels)
            total = part
            for t in range(1, carried):
                total = total + pltpu.roll(part, (-t * levels) % cy, 1)
        lane_parts.append((pltpu.roll(total, spot_y, 1), spot_y))
    lane = iota((cx, cy), 1)
    row = iota((cx, cy), 0)
    forward = []
    for level in range(levels):
        value = inner[level]
        value = value + jnp.where(row == 0, from_west[level : level + 1], 0.0)
        value = value + jnp.where(row == cx - 1, from_east[level : level + 1], 0.0)
        for total, spot_y in lane_parts:
            moved = pltpu.roll(total, cy - level, 1) if level else total
            value = value + jnp.where(lane == spot_y, moved, 0.0)
        value = value * inverse[level]
        forward.append(value + lower[level] * forward[-1] if level else value)
    result = forward
    for level in range(levels - 2, -1, -1):
        result[level] = forward[level] + ratio[level] * result[level + 1]
    high, low = halves(jnp.concatenate(result, axis=0))
    picks = in_lane[...]
    picked = jnp.dot(high, picks, preferred_element_type=F32)
    picked = picked + jnp.dot(low, picks, preferred_element_type=F32)

    start = plan["y_tiles"] * cx
    if plan["relay"]:

        def block_at(ref, row):
            return ref[row : row + 8, :]

        blocks = {0: block_at(own, 0), 1: block_at(y_got[0], start + 8)}
        rim_blocks = {0: block_at(y_got[0], start), 1: block_at(own, 8)}
        carriers = [(offset, got[n], head + 16) for n, offset in enumerate(plan["x_blocks"]) if offset]
        carriers += [(offset, ref, 0) for offset, ref in zip(plan["x_ops"], x_got)]
        for offset, ref, row in carriers:
            blocks[offset], rim_blocks[offset + 1] = block_at(ref, row), block_at(ref, row + 8)
            rim_blocks[offset], blocks[offset + 1] = block_at(ref, row + 16), block_at(ref, row + 24)
    else:
        blocks = {0: own[0:8, :], plan["y_blocks"][0]: y_got[0][start : start + 8, :]}
        for number in range(2):
            offset = plan["x_blocks"][number]
            if offset:
                blocks[offset] = got[number][head + 8 : head + 16, :]
    first_core = lax.axis_index("lev") == 0
    for number, (for_first, for_second) in enumerate(plan["pairs"]):
        mine = pair_got[number][...]
        other = swapped[8 * number : 8 * number + 8, :]
        if for_first == for_second:
            blocks[for_first] = mine
        else:
            blocks[for_first] = jnp.where(first_core, mine, other)
            blocks[for_second] = jnp.where(first_core, other, mine)
    cap = slots // len(blocks)
    per_tile = LANES // cap
    group_of_lane = lax.div(iota((8, LANES), 1), cap)

    def gathered(group, blocks):
        tiles = []
        for start in range(0, len(blocks), per_tile):
            tile = jnp.zeros((8, LANES), F32)
            for a in range(per_tile):
                moved = pltpu.roll(blocks[start + a], (cap * (a - group)) % LANES, 1)
                tile = jnp.where(group_of_lane == a, moved, tile)
            tiles.append(tile)
        return jnp.concatenate(tiles, axis=1)

    groups = [gathered(g, blocks) for g in range(levels // 8)]
    last = gathered(levels // 8, blocks)
    total = jnp.zeros((cx, slots), F32)
    sensitivity = jnp.zeros((8, slots), F32)
    for g, kernel in enumerate(groups):
        sensitivity = sensitivity + kernel * columns[8 * g : 8 * g + 8, :]
        for l in range(8):
            level = 8 * g + l
            total = total + kernel[l : l + 1] * picked[level * cx : (level + 1) * cx]
    modeled = jnp.sum(total * in_row[...], axis=0, keepdims=True)
    gain = jnp.sum(sensitivity, axis=0, keepdims=True) * last[1:2] * live[...]
    if not plan["relay"]:
        modeled_out[...] = modeled
        state_out[...] = jnp.concatenate([gain, last[0:1]], axis=0)
        return

    rim_inverse, rim_ratio, rim_lower, pieces, rim_columns, rim_rows, rim_picks, rim_live = rim
    corners_west, corners_east = sides(got[0][head + 8 : head + 16, :], got[1][head + 8 : head + 16, :])
    turn[...] = jnp.zeros((LANES, LANES), F32)
    turn[0:1, :] = corners_west[0:1]
    turn[cx - 1 : cx, :] = corners_east[0:1]
    turned = jnp.transpose(turn[...])
    ends = turned[plan["lane_c"] : plan["lane_c"] + levels]
    end_face = turned[plan["lane_u"] : plan["lane_u"] + levels]
    place = iota((levels, LANES), 1)
    cells, face_w, face_s, face_n, south_cells, north_cells = (pieces[n] for n in range(6))
    west_cells = jnp.where(place == 0, ends, pltpu.roll(cells, 1, 1))
    east_cells = jnp.where(place == cx - 1, ends, pltpu.roll(cells, LANES - 1, 1))
    face_e = jnp.where(place == cx - 1, end_face, pltpu.roll(face_w, LANES - 1, 1))
    rise[0:levels, :] = advance_cells(
        cells, west_cells, east_cells, south_cells, north_cells, face_w, face_e, face_s, face_n
    )

    def level_of(ref, level):
        return jnp.broadcast_to(ref[level : level + 1, :], (8, LANES))

    climbed = []
    for level in range(levels):
        value = level_of(rise, level) * level_of(rim_inverse, level)
        climbed.append(value + level_of(rim_lower, level) * climbed[-1] if level else value)
    for level in range(levels - 2, -1, -1):
        climbed[level] = climbed[level] + level_of(rim_ratio, level) * climbed[level + 1]
    for level in range(levels):
        rise[level : level + 1, :] = climbed[level][0:1]
    high, low = halves(rise[0:levels, :])
    picks = rim_picks[...]
    picked = jnp.dot(high, picks, preferred_element_type=F32)
    picked = picked + jnp.dot(low, picks, preferred_element_type=F32)
    rim_total = jnp.zeros((8, slots), F32)
    sensitivity = jnp.zeros((8, slots), F32)
    for g in range(levels // 8):
        kernel = gathered(g, rim_blocks)
        rim_total = rim_total + kernel * picked[8 * g : 8 * g + 8]
        sensitivity = sensitivity + kernel * rim_columns[8 * g : 8 * g + 8, :]
    rim_modeled = jnp.sum(rim_total, axis=0, keepdims=True)
    rim_last = gathered(levels // 8, rim_blocks)
    rim_gain = jnp.sum(sensitivity, axis=0, keepdims=True) * rim_last[1:2] * rim_live[...]
    state_out[...] = jnp.concatenate([gain, last[0:1], rim_gain, rim_last[0:1]], axis=0)
    strips = slots // LANES
    for number in range(strips):
        part = slice(number * LANES, (number + 1) * LANES)
        parcel[number : number + 1, :] = modeled[:, part]
        parcel[strips + number : strips + number + 1, :] = rim_modeled[:, part]


def advance_cells(cells, west, east, south, north, face_w, face_e, face_s, face_n):
    flux_w = jnp.maximum(face_w, 0.0) * west + jnp.minimum(face_w, 0.0) * cells
    flux_e = jnp.maximum(face_e, 0.0) * cells + jnp.minimum(face_e, 0.0) * east
    flux_s = jnp.maximum(face_s, 0.0) * south + jnp.minimum(face_s, 0.0) * cells
    flux_n = jnp.maximum(face_n, 0.0) * cells + jnp.minimum(face_n, 0.0) * north
    return cells + flux_w - flux_e + flux_s - flux_n


def scatter(force, in_row, in_lane):
    high, low = halves(in_row * force)
    dims = (((1,), (1,)), ((), ()))
    scattered = lax.dot_general(high, in_lane, dims, preferred_element_type=F32)
    return scattered + lax.dot_general(low, in_lane, dims, preferred_element_type=F32)


def force_kernel(plan, *refs):
    modeled, modeled_other, state, in_row, in_lane, base, base_other = refs[:7]
    near_out = refs[7]
    rim_outs = refs[8:]
    carried, cx, cy = base.shape
    misfit = modeled[...] + modeled_other[...] - state[1:2, :]
    force = state[0:1, :] * misfit
    scattered = scatter(force, in_row[...], in_lane[...])
    lane = iota((cx, cy), 1)
    even_y = is_even("facey")
    edges = []
    for number in range(len(rim_outs)):
        sends_last = even_y if number == 0 else jnp.logical_not(even_y)
        edges.append(jnp.where(sends_last, cy - 1, 0))
    rims = [jnp.zeros((cx, cy), F32) for _ in rim_outs]
    for t in range(2 * carried):
        values = scattered + (base[t] if t < carried else base_other[t - carried])
        near_out[t] = values
        for number, edge in enumerate(edges):
            moved = pltpu.roll(values, lax.rem(t + cy - edge, cy), 1)
            rims[number] = jnp.where(lane == t, moved, rims[number])
    for rim, out in zip(rims, rim_outs):
        out[...] = rim


def surface_kernel(sizes, plan, carried, levels, *refs):
    y_ops = plan["y_ops"]
    near = refs[0]
    rims = refs[6 + y_ops : 6 + 2 * y_ops]
    rim_values = [[rim[...] for rim in rims] for _ in range(near.shape[0])]
    values = [near[t] for t in range(near.shape[0])]
    spread_surface(
        sizes, plan, carried, levels, values, rim_values, refs[1:4], refs[4:6], refs[6 : 6 + y_ops], refs[6 + 2 * y_ops :]
    )


def weigh_kernel(sizes, plan, carried, levels, *refs):
    parcel, other, state, in_row, in_lane, base, base_other, rim_rows, rim_base = refs[:9]
    cx, cy = base.shape[1:]
    strips = state.shape[1] // LANES

    def misfit(kind):
        both = parcel[kind * strips : (kind + 1) * strips, :] + other[kind * strips : (kind + 1) * strips, :]
        flat = jnp.concatenate([both[n : n + 1] for n in range(strips)], axis=1)
        return state[2 * kind : 2 * kind + 1, :] * (flat - state[2 * kind + 1 : 2 * kind + 2, :])

    scattered = scatter(misfit(0), in_row[...], in_lane[...])
    on_rim = jnp.sum(rim_rows[...] * misfit(1), axis=1, keepdims=True)
    near = [scattered + base[t] for t in range(carried)]
    near += [scattered + base_other[t] for t in range(carried)]
    rims = [[rim_base[0:cx, :] + on_rim] for _ in near]
    spread_surface(sizes, plan, carried, levels, near, rims, refs[9:12], refs[12:14], refs[14:15], refs[15:])


def spread_surface(sizes, plan, carried, levels, near, rim_values, fields, got, y_got, outs):
    west, south, scale = fields
    tracers = len(near)
    cx, cy = near[0].shape
    spot_v = plan["lane_v"]
    band = cy // sizes[0]
    per_tile = min(tracers, LANES // band)
    spot = carried * levels
    head = (carried + 1) * levels
    lane = iota((cx, cy), 1)
    row = iota((cx, cy), 0)
    even_y = is_even("facey")
    face_west = west[...]
    face_south = south[...]
    scales = scale[...]
    beyond_west, beyond_east = sides(got[0][head : head + 1], got[1][head : head + 1])
    _, east_wind = sides(got[0][spot : spot + 1], got[1][spot : spot + 1])
    face_east = jnp.where(row == cx - 1, east_wind, pltpu.roll(face_west, cx - 1, 0))
    face_north = left(face_south)
    norths = []
    for number in range(plan["y_ops"]):
        norths.append(even_y if number == 0 else jnp.logical_not(even_y))
        moved = pltpu.roll(y_got[number][0:cx, :], cy - 1 - spot_v, 1)
        keep = jnp.logical_and(lane == cy - 1, norths[number])
        face_north = jnp.where(keep, moved, face_north)
    to_middle = 1.0 + jnp.minimum(face_west, 0.0) - jnp.maximum(face_east, 0.0)
    to_middle = scales * (to_middle + jnp.minimum(face_south, 0.0) - jnp.maximum(face_north, 0.0))
    to_east = jnp.where(row == cx - 1, 0.0, scales * jnp.maximum(face_east, 0.0))
    to_west = jnp.where(row == 0, 0.0, scales * jnp.minimum(face_west, 0.0))
    to_north = scales * jnp.maximum(face_north, 0.0)
    to_south = scales * jnp.minimum(face_south, 0.0)
    west_gain = beyond_west * jnp.maximum(face_west[0:1], 0.0)
    east_gain = -beyond_east * jnp.minimum(face_east[cx - 1 : cx], 0.0)
    filler = jnp.zeros((6, cy), F32)
    grown = []
    for t in range(tracers):
        values = near[t]
        north_side = left(values)
        south_side = right(values)
        for number in range(plan["y_ops"]):
            rim = rim_values[t][number]
            at_north = jnp.logical_and(lane == cy - 1, norths[number])
            at_south = jnp.logical_and(lane == 0, jnp.logical_not(norths[number]))
            north_side = jnp.where(at_north, pltpu.roll(rim, (cy - 1 - t) % cy, 1), north_side)
            south_side = jnp.where(at_south, pltpu.roll(rim, (-t) % cy, 1), south_side)
        swept = to_middle * values + to_east * pltpu.roll(values, cx - 1, 0) - to_west * pltpu.roll(values, 1, 0)
        swept = swept + to_north * north_side - to_south * south_side
        grown.append(
            jnp.concatenate(
                [swept, west_gain * values[0:1], east_gain * values[cx - 1 : cx], filler], axis=0
            )
        )
    rows = cx + 8
    group_of_lane = lax.div(iota((rows, cy), 1), band)
    first_core = lax.axis_index("lev") == 0
    place = lax.axis_index("facex")
    for out, (for_first, for_second) in zip(outs, plan["bands"]):
        offset = for_first if for_first == for_second else jnp.where(first_core, for_first, for_second)
        target = jnp.bitwise_xor(place, offset)
        count = carried if for_first == for_second else tracers
        skip = carried if for_first == for_second != 0 and plan["cross"] else 0
        for start in range(0, count, per_tile):
            tile = jnp.zeros((rows, cy), F32)
            for a in range(min(per_tile, count - start)):
                moved = pltpu.roll(grown[skip + start + a], lax.rem(band * a + cy - band * target, cy), 1)
                tile = jnp.where(group_of_lane == a, moved, tile)
            out[start // per_tile * rows : (start // per_tile + 1) * rows, :] = tile


def regrid_kernel(sizes, plan, bands, carried, cx, band, *refs):
    index, weight = refs[:2]
    blocks = refs[2:-1]
    out = refs[-1]
    taps, cells = index.shape
    tracers = 2 * carried
    rows = cx + 8
    per_tile = min(tracers, LANES // band)
    lane = iota((rows, LANES), 1)
    row = iota((rows, cells), 0)
    first_core = lax.axis_index("lev") == 0
    place = lax.axis_index("facex")
    around = sizes[0] * cx
    parts = []
    row_places = []
    for block, (for_first, for_second) in zip(blocks, bands):
        from_first, from_second = (for_second, for_first) if plan["cross"] else (for_first, for_second)
        offset = for_first if for_first == for_second else jnp.where(first_core, from_first, from_second)
        start = jnp.bitwise_xor(place, offset) * cx
        places = start + row
        places = jnp.where(row == cx, lax.rem(start + around - 1, around), places)
        places = jnp.where(row == cx + 1, lax.rem(start + cx, around), places)
        row_places.append(places)
        count = carried if for_first == for_second else tracers
        mine = []
        for t in range(count):
            tile = block[t // per_tile * rows : (t // per_tile + 1) * rows, :]
            a = t % per_tile
            values = tile if a == 0 else pltpu.roll(tile, (-band * a) % LANES, 1)
            high = values.astype(BF16).astype(F32)
            low = pltpu.roll(values - high, band, 1)
            both = jnp.where(lane < band, high, jnp.where(lane < 2 * band, low, 0.0))
            mine.append(both.astype(BF16))
        parts.append(mine)
    left_side = jnp.concatenate([jnp.concatenate(mine, axis=0) for mine in parts], axis=0)
    spread = iota((LANES, cells), 0)
    in_band = lax.rem(spread, band)
    used = spread < 2 * band
    totals = [[jnp.zeros((rows, cells), F32) for _ in mine] for mine in parts]
    for tap in range(taps):
        place_of = index[tap : tap + 1, :]
        column = lax.div(place_of, band)
        in_lane = lax.rem(place_of, band)
        picks = jnp.where(jnp.logical_and(in_band == in_lane, used), 1.0, 0.0).astype(BF16)
        picked = jnp.dot(left_side, picks, preferred_element_type=F32)
        at = 0
        for number, mine in enumerate(parts):
            chosen = jnp.where(row_places[number] == column, weight[tap : tap + 1, :], 0.0)
            for t in range(len(mine)):
                totals[number][t] = totals[number][t] + chosen * picked[at : at + rows]
                at += rows
    sums = [jnp.zeros((1, cells), F32) for _ in range(out.shape[0])]
    for mine in totals:
        skip = carried if len(mine) == tracers and plan["cross"] else 0
        for t, total in enumerate(mine):
            to = (t + skip) % tracers
            sums[to] = sums[to] + jnp.sum(total, axis=0, keepdims=True)
    out[...] = jnp.concatenate(sums, axis=0)


def advance_kernel(plan, *refs):
    tracer, parts, lower, inverse, ratio = refs[:5]
    sent = refs[5:7]
    got = refs[7:9]
    y_ops = plan["y_ops"]
    y_sent, y_got, winds_sent, winds_got = (refs[9 + n * y_ops : 9 + (n + 1) * y_ops] for n in range(4))
    target, out, west_rows, east_rows, done = refs[-5:]
    carried, levels, cx, cy = tracer.shape
    head = (carried + 1) * levels
    spot = carried * levels
    beyond_west, beyond_east = sides(got[0][0:head], got[1][0:head])
    at_west, at_east = sides(sent[0][0:head], sent[1][0:head])
    face_west = at_west[spot:head]
    face_east = beyond_east[spot:head]
    for t in range(carried):
        part = slice(t * levels, (t + 1) * levels)
        west_rows[part, :] = jnp.maximum(face_west, 0.0) * beyond_west[part]
        east_rows[part, :] = -(
            jnp.maximum(face_east, 0.0) * at_east[part] + jnp.minimum(face_east, 0.0) * beyond_east[part]
        )
    lane = iota((cx, cy), 1)
    row = iota((cx, cy), 0)
    seams = [
        seam_lanes(
            n,
            plan,
            y_sent[n][0:cx, :],
            y_got[n][-cx:, :] if plan["relay"] else y_got[n][0:cx, :],
            winds_sent[n][0:cx, :],
            winds_got[n][0:cx, :],
            carried,
            levels,
        )
        for n in range(y_ops)
    ]
    stride = 4

    def forward(step, before):
        mixed = []
        for k in range(stride):
            level = step * stride + k
            weights = [parts[n, level] for n in range(5)]
            mixed.append([])
            for t in range(carried):
                value = mix(weights, tracer[t, level])
                value = value + jnp.where(row == 0, west_rows[pl.ds(t * levels + level, 1), :], 0.0)
                value = value + jnp.where(row == cx - 1, east_rows[pl.ds(t * levels + level, 1), :], 0.0)
                for packed, spot_y in seams:
                    moved = pltpu.roll(packed, lax.rem(spot_y - (t * levels + level) + 2 * cy, cy), 1)
                    value = value + jnp.where(lane == spot_y, moved, 0.0)
                mixed[k].append(value)
        for k in range(stride):
            level = step * stride + k
            from_below = lower[level]
            scaled = inverse[level]
            after = []
            for t in range(carried):
                value = mixed[k][t] * scaled + from_below * before[t]
                out[t, level] = value
                after.append(value)
            before = after
        return tuple(before)

    def copy(step):
        part = pl.ds(levels - (step + 1) * stride, stride)
        return pltpu.make_async_copy(out.at[:, part], target.at[:, part], done.at[step])

    start = tuple(jnp.zeros((cx, cy), F32) for _ in range(carried))
    lax.fori_loop(0, levels // stride, forward, start)
    above = list(start)
    for step in range(levels // stride):
        for k in range(stride):
            level = levels - 1 - step * stride - k
            factor = ratio[level]
            for t in range(carried):
                above[t] = out[t, level] + factor * above[t]
                out[t, level] = above[t]
        copy(step).start()
    for step in range(levels // stride):
        copy(step).wait()


GROUP = ("facex", "facey", "lev")


def exchange(values, sizes, rule):
    many_x, many_y, cores = sizes
    pairs = []
    for x in range(many_x):
        for y in range(many_y):
            for c in range(cores):
                to = rule(x, y, c)
                if to is not None:
                    pairs.append(((x * many_y + y) * cores + c, (to[0] * many_y + to[1]) * cores + to[2]))
    return lax.ppermute(values, GROUP, pairs)


def make_plan(sizes):
    many_x, many_y, _ = sizes
    tiles = many_x * many_y
    x_blocks = [many_y, (many_x - 1) * many_y if many_x == 4 else 0]
    relay = many_y == 2
    if relay:
        own_blocks = list(range(tiles))
        y_blocks = own_blocks
        x_ops = [offset for offset in own_blocks[2::2] if offset not in x_blocks]
        pairs = []
    else:
        own_blocks = [0] + [offset for offset in x_blocks if offset]
        y_blocks = [1]
        x_ops = []
        rest = [d for d in range(tiles) if d not in {1, *own_blocks}]
        rest.sort(key=lambda d: (d // many_y != many_x // 2, d))
        pairs = [(rest[n], rest[min(n + 1, len(rest) - 1)]) for n in range(0, len(rest), 2)]
    others = list(range(many_x - 1, 1, -1))
    bands = [(0, 0), (1, 1)] + [(others[n], others[n + 1]) for n in range(0, len(others), 2)]
    return {
        "relay": relay,
        "cross": 1 if relay else 0,
        "x_blocks": x_blocks,
        "x_ops": x_ops,
        "own_blocks": own_blocks,
        "y_blocks": y_blocks,
        "y_ops": 1 if many_y == 2 else 2,
        "y_tiles": 2 if relay else 1,
        "pairs": pairs,
        "bands": bands,
    }


def lane_plan(plan, carried, levels):
    starts = {"c": 0, "d": levels, "v": 2 * levels, "w": 3 * levels, "u": 4 * levels}
    if not plan["relay"]:
        starts = {"v": carried * levels}
    return {"lane_" + name: start for name, start in starts.items()}


def local(
    sizes,
    tracer,
    west_courant,
    south_courant,
    mixing,
    adjoint_later,
    emission_scale,
    send_cells,
    send_counts,
    kernels,
    observed,
    error_weight,
    regrid_index,
    regrid_weight,
):
    plan = make_plan(sizes)
    many_x, many_y, _ = sizes
    carried, levels, cx, cy = tracer.shape
    owners, cap = send_cells.shape[2:]
    slots = owners * cap
    taps, ll = regrid_index.shape[2:]
    plan.update(lane_plan(plan, carried, levels))
    head = (carried + 1) * levels
    y_ops = plan["y_ops"]
    band = cy // many_x

    def next_x(number):
        def rule(x, y, c):
            step = 1 if (x % 2 == 0) == (number == 0) else -1
            return ((x + step) % many_x, y, c)

        return rule

    def next_y(number, cross):
        def rule(x, y, c):
            to = y + (1 if (y % 2 == 0) == (number == 0) else -1)
            return (x, to, c ^ cross) if 0 <= to < many_y else None

        return rule

    def jump(for_first, for_second, cross=0):
        def rule(x, y, c):
            d = for_first if c == 0 else for_second
            return (x ^ (d // many_y), y ^ (d % many_y), c ^ cross)

        return rule

    def other_core(values):
        return exchange(values, sizes, lambda x, y, c: (x, y, 1 - c))

    strips = slots // LANES
    plan["parcel"] = -(-2 * strips // 8) * 8
    extra = 48 if plan["relay"] else 16
    row_shapes = [shape(head + extra, cy)] * 2
    y_rows = plan["y_tiles"] * cx + 8 * len(plan["y_blocks"]) + (plan["parcel"] if plan["relay"] else 0)
    lane_shapes = [shape(y_rows if n == 0 else cx, cy) for n in range(y_ops)]
    packed = call(
        functools.partial(pack_kernel, sizes, plan),
        lane_shapes
        + [shape(8 * len(plan["own_blocks"]), LANES)]
        + [shape(8, LANES)] * len(plan["pairs"])
        + [shape(1, slots, dtype=jnp.int32), shape(1, slots)]
        + [shape(*a.shape) for a in (tracer, west_courant, south_courant, emission_scale, mixing)],
        [
            tracer,
            west_courant,
            south_courant,
            emission_scale,
            kernels.reshape(owners, levels, cap),
            observed.reshape(owners, cap),
            error_weight.reshape(owners, cap),
            send_cells.reshape(owners, cap),
            send_counts.reshape(owners),
            mixing,
        ],
        "pack",
        100000,
        hbm=range(10),
        scratch=[
            pltpu.VMEM((owners, levels, cap), F32),
            pltpu.VMEM((owners, cap), F32),
            pltpu.VMEM((owners, cap), F32),
            pltpu.VMEM((owners, cap), jnp.int32),
            pltpu.SMEM((owners,), jnp.int32),
            pltpu.SemaphoreType.DMA((9 + carried,)),
        ],
    )
    lanes_sent = packed[:y_ops]
    own_blocks = packed[y_ops]
    pair_sent = packed[1 + y_ops : -7]
    cell, live, tracer, west_courant, south_courant, emission_scale, mixing = packed[-7:]
    lanes_got = [exchange(lanes_sent[n], sizes, next_y(n, plan["cross"])) for n in range(y_ops)]
    held, *_ = lax.optimization_barrier((tracer, *lanes_sent))
    inverse, lower, ratio, base, inner, parts, columns, in_row, in_lane = call(
        functools.partial(factor_kernel, sizes),
        [
            shape(levels, cx, cy),
            shape(levels, cx, cy),
            shape(levels, cx, cy),
            shape(carried, cx, cy),
            shape(levels, cx, cy),
            shape(5, levels, cx, cy),
            shape(levels, slots),
            shape(cx, slots),
            shape(cy, slots, dtype=BF16),
        ],
        [held, west_courant, south_courant, mixing, adjoint_later, cell],
        "factor",
        3000000,
    )
    rows_sent = list(
        call(
            functools.partial(rows_kernel, plan),
            row_shapes + ([shape(cx, cy)] if plan["relay"] else []),
            [tracer, west_courant, emission_scale, own_blocks],
            "rows",
            100000,
        )
    )
    per_tile = min(2 * carried, LANES // band)

    def band_shape(first, second):
        count = carried if first == second else 2 * carried
        return shape(-(-count // per_tile) * (cx + 8), cy)

    band_shapes = [band_shape(*b) for b in plan["bands"]]
    fields = [west_courant[0], south_courant[0], emission_scale]
    observe = functools.partial(
        call, functools.partial(observe_kernel, sizes, plan, carried), name="observe", flops=2000000
    )
    if plan["relay"]:
        base, *lanes_got = lax.optimization_barrier((base, *lanes_got))
        lanes_each = rows_sent.pop()
        base_other = other_core(base)

        def relay(number, *after):
            held, *_ = lax.optimization_barrier((rows_sent[number], *after))
            return call(
                functools.partial(relay_kernel, plan, head, cx, number),
                [row_shapes[number]],
                [held, own_blocks, lanes_got[0]],
                "relay",
                10000,
            )[0]

        rows_sent = [relay(0), relay(1)]
        x_sent = call(
            functools.partial(beyond_kernel, plan, cx),
            [shape(32, LANES)] * len(plan["x_ops"]),
            [own_blocks, lanes_got[0]],
            "beyond",
            10000,
        )
        x_got = [exchange(s, sizes, jump(d, d, 1)) for s, d in zip(x_sent, plan["x_ops"])]
        rows_got = [exchange(rows_sent[n], sizes, next_x(n)) for n in range(2)]
        held_y, *_ = lax.optimization_barrier((lanes_got[0], *rows_sent))
        rim = call(
            functools.partial(rim_kernel, plan, carried, levels, cx),
            [
                shape(levels, LANES),
                shape(levels, LANES),
                shape(levels, LANES),
                shape(6, levels, LANES),
                shape(levels, slots),
                shape(cx, slots),
                shape(LANES, slots, dtype=BF16),
                shape(1, slots),
                shape(2 * cx, cy),
            ],
            [lanes_sent[0], held_y, base, base_other, lanes_each],
            "rim",
            400000,
            scratch=[pltpu.VMEM((LANES, LANES), F32)],
        )
        *rim, rim_sent = rim
        rim_got = exchange(rim_sent, sizes, next_y(0, 0))
        parcel, state = observe(
            [shape(plan["parcel"], cy), shape(4, slots)],
            [rows_got[1], rows_got[0], inner, lower, inverse, ratio, columns, in_row, in_lane, live, *rows_sent]
            + [*lanes_sent, *lanes_got, own_blocks, *x_got, *rim],
            scratch=[pltpu.VMEM((LANES, LANES), F32), pltpu.VMEM((levels, LANES), F32)],
        )
        parcel_other = other_core(parcel)
        parcel_other, rim_got = lax.optimization_barrier((parcel_other, rim_got))
        band_sent = call(
            functools.partial(weigh_kernel, sizes, plan, carried, levels),
            band_shapes,
            [parcel, parcel_other, state, in_row, in_lane, base, base_other, rim[5], rim_got, *fields]
            + [*rows_got, *lanes_got],
            "weigh",
            500000,
        )
        lanes_own = [lanes_each, rim_got]
        held, *_ = lax.optimization_barrier((tracer, *band_sent))
    else:
        rows_got = [exchange(rows_sent[n], sizes, next_x(n)) for n in range(2)]
        pair_got = [exchange(s, sizes, jump(*p)) for s, p in zip(pair_sent, plan["pairs"])]
        base_other = other_core(base)
        modeled, state = observe(
            [shape(1, slots), shape(2, slots)],
            [rows_got[1], rows_got[0], inner, lower, inverse, ratio, columns, in_row, in_lane, live, *rows_sent]
            + [*lanes_sent, *lanes_got, own_blocks, *pair_got]
            + [other_core(jnp.concatenate(pair_got, axis=0))],
        )
        near, *rims_sent = call(
            functools.partial(force_kernel, plan),
            [shape(2 * carried, cx, cy)] + [shape(cx, cy)] * y_ops,
            [modeled, other_core(modeled), state, in_row, in_lane, base, base_other],
            "force",
            200000,
        )
        rims_got = [exchange(rims_sent[n], sizes, next_y(n, 0)) for n in range(y_ops)]
        band_sent = call(
            functools.partial(surface_kernel, sizes, plan, carried, levels),
            band_shapes,
            [near, *fields, *rows_got, *lanes_got, *rims_got],
            "surface",
            400000,
        )
        lanes_own = [*lanes_sent, *lanes_got]
        held = tracer
    (advanced,) = call(
        functools.partial(advance_kernel, plan),
        [shape(*tracer.shape)],
        [held, parts, lower, inverse, ratio]
        + list(rows_sent)
        + rows_got
        + lanes_own
        + list(lanes_sent)
        + lanes_got,
        "advance",
        6000000,
        scratch=[pltpu.VMEM(tracer.shape, F32)]
        + [pltpu.VMEM((carried * levels, cy), F32)] * 2
        + [pltpu.SemaphoreType.DMA((levels // 4,))],
        out_hbm=(0,),
    )
    band_got = [
        s
        if first == second == 0
        else exchange(s, sizes, jump(first * many_y, second * many_y, plan["cross"]))
        for s, (first, second) in zip(band_sent, plan["bands"])
    ]
    tables = [regrid_index.reshape(taps, ll), regrid_weight.reshape(taps, ll)]
    kinds = [first == second for first, second in plan["bands"]]

    def regridded(near, blocks):
        bands = [pair for pair, kind in zip(plan["bands"], kinds) if kind == near]
        return call(
            functools.partial(regrid_kernel, sizes, plan, bands, carried, cx, band),
            [shape(carried if near else 2 * carried, ll)],
            [*tables, *blocks],
            "regrid",
            1000000,
        )[0]

    near_got = [got for got, kind in zip(band_got, kinds) if kind]
    far_got = [got for got, kind in zip(band_got, kinds) if not kind]
    advanced, *far_got = lax.optimization_barrier((advanced, *far_got))
    far = regridded(False, far_got)
    far_other = other_core(far[carried:])
    *near_got, _ = lax.optimization_barrier((*near_got, far))
    latlon = far[:carried] + far_other + regridded(True, near_got)
    return (advanced, latlon[:, None, None, :])


def solution(mesh):
    in_specs = (
        P("lev", "groups", "facex", "facey"),
        P("groups", "facex", "facey"),
        P("groups", "facex", "facey"),
        P("groups", "facex", "facey"),
        P("lev", "groups", "facex", "facey"),
        P("facex", "facey"),
        P("facex", "facey", "groups", None),
        P("facex", "facey", "groups"),
        P("facex", "facey", "groups", None, None),
        P("facex", "facey", "groups", None),
        P("facex", "facey", "groups", None),
        P("facex", "facey", None, None),
        P("facex", "facey", None, None),
    )
    out_specs = (P("lev", "groups", "facex", "facey"), P("lev", "facex", "facey", "groups"))
    sizes = tuple(mesh.shape[axis] for axis in GROUP)
    return jax.shard_map(
        functools.partial(local, sizes), mesh=mesh, in_specs=in_specs, out_specs=out_specs, check_vma=False
    )
```

```python
import functools

import jax
import jax.numpy as jnp
from jax import lax
from jax.experimental import pallas as pl
from jax.experimental.pallas import tpu as pltpu
from jax.sharding import PartitionSpec as P

F32 = jnp.float32
BF16 = jnp.bfloat16
LANES = 128


def call(body, outs, ins, name, flops, smem=(), hbm=(), scratch=(), out_hbm=()):
    moved = sum(4 * a.size for a in ins) + sum(4 * o.size for o in outs)
    ins = [pltpu.with_memory_space_constraint(a, pltpu.HBM) if i in hbm else a for i, a in enumerate(ins)]

    def space(number):
        return pltpu.SMEM if number in smem else pltpu.HBM if number in hbm else pltpu.VMEM

    return pl.pallas_call(
        body,
        out_shape=outs,
        in_specs=[pl.BlockSpec(memory_space=space(i)) for i in range(len(ins))],
        out_specs=[
            pl.BlockSpec(memory_space=pltpu.HBM if i in out_hbm else pltpu.VMEM) for i in range(len(outs))
        ],
        scratch_shapes=scratch,
        compiler_params=pltpu.CompilerParams(vmem_limit_bytes=40 << 20),
        cost_estimate=pl.CostEstimate(flops=flops, bytes_accessed=moved, transcendentals=0),
        name=name,
    )(*ins)


def shape(*dims, dtype=F32):
    return jax.ShapeDtypeStruct(dims, dtype)


def iota(dims, axis):
    return lax.broadcasted_iota(jnp.int32, dims, axis)


def halves(values):
    high = values.astype(BF16)
    return high, (values - high.astype(F32)).astype(BF16)


def tile_of(sizes):
    return lax.axis_index("facex") * sizes[1] + lax.axis_index("facey")


def is_even(axis):
    return lax.rem(lax.axis_index(axis), 2) == 0


def up(values):
    rows = values.shape[0]
    rolled = pltpu.roll(values, rows - 1, 0)
    return jnp.where(iota(values.shape, 0) == rows - 1, 0.0, rolled)


def right(values):
    rolled = pltpu.roll(values, 1, 1)
    return jnp.where(iota(values.shape, 1) == 0, 0.0, rolled)


def left(values):
    lanes = values.shape[1]
    rolled = pltpu.roll(values, lanes - 1, 1)
    return jnp.where(iota(values.shape, 1) == lanes - 1, 0.0, rolled)


def shares(west, south):
    east, north = up(west), left(south)
    middle = 1.0 + jnp.minimum(west, 0.0) - jnp.maximum(east, 0.0)
    middle = middle + jnp.minimum(south, 0.0) - jnp.maximum(north, 0.0)
    row, lane = iota(west.shape, 0), iota(west.shape, 1)
    return (
        middle,
        jnp.where(row == 0, 0.0, jnp.maximum(west, 0.0)),
        -jnp.minimum(east, 0.0),
        jnp.where(lane == 0, 0.0, jnp.maximum(south, 0.0)),
        -jnp.minimum(north, 0.0),
    )


def mix(parts, cells):
    rows, lanes = cells.shape
    middle, west, east, south, north = parts
    total = middle * cells + west * pltpu.roll(cells, 1, 0) + east * pltpu.roll(cells, rows - 1, 0)
    return total + south * pltpu.roll(cells, 1, 1) + north * pltpu.roll(cells, lanes - 1, 1)


def pack_kernel(sizes, plan, *refs):
    sources, refs = refs[:10], refs[10:]
    lanes_out, refs = refs[: plan["y_ops"]], refs[plan["y_ops"] :]
    own_out, refs = refs[0], refs[1:]
    block_outs, refs = refs[: len(plan["pairs"])], refs[len(plan["pairs"]) :]
    cell_out, live_out, tracer, west, south, scale, mixing, *refs = refs
    kernels, observed, weights, cells, counts, done = refs
    carried, levels, cx, cy = tracer.shape
    me = tile_of(sizes)
    copies = [
        pltpu.make_async_copy(source, target, done.at[number])
        for number, (source, target) in enumerate(
            zip(sources[1:], (west, south, scale, kernels, observed, weights, cells, counts, mixing))
        )
    ]
    copies += [
        pltpu.make_async_copy(sources[0].at[t], tracer.at[t], done.at[9 + t]) for t in range(carried)
    ]
    for number in (3, 4, 5, 6, 7, 1, 0, 8, *range(9, 9 + carried), 2):
        copies[number].start()

    def block(offset):
        where_to = jnp.bitwise_xor(me, offset)
        mine = kernels[where_to]
        last = jnp.concatenate(
            [
                observed[pl.ds(where_to, 1), :],
                weights[pl.ds(where_to, 1), :],
                jnp.zeros((6, mine.shape[1]), F32),
            ],
            axis=0,
        )
        return jnp.concatenate([mine[8 * g : 8 * g + 8] for g in range(levels // 8)] + [last], axis=1)

    for number in (3, 4, 5):
        copies[number].wait()
    for number, offset in enumerate(plan["y_blocks"]):
        at = plan["y_tiles"] * cx + 8 * number
        lanes_out[0][at : at + 8, :] = block(offset)
    for number, offset in enumerate(plan["own_blocks"]):
        own_out[8 * number : 8 * number + 8, :] = block(offset)
    first_core = lax.axis_index("lev") == 0
    for out, (for_first, for_second) in zip(block_outs, plan["pairs"]):
        out[...] = block(jnp.where(first_core, for_first, for_second))

    owners, cap = cells.shape
    slot = iota((1, cap), 1)
    copies[6].wait()
    copies[7].wait()
    cell_parts = []
    live_parts = []
    for offset in range(owners):
        owner = jnp.bitwise_xor(me, offset)
        cell_parts.append(cells[pl.ds(owner, 1), :])
        live_parts.append(jnp.where(slot < counts[owner], 1.0, 0.0))
    cell = jnp.concatenate(cell_parts, axis=1)
    live = jnp.concatenate(live_parts, axis=1)
    cell_out[...] = cell
    live_out[...] = live
    if plan["relay"]:
        at = plan["y_tiles"] * cx + 8 * len(plan["y_blocks"])
        strips = owners * cap // LANES
        for number in range(strips):
            part = slice(number * LANES, (number + 1) * LANES)
            lanes_out[0][at + number : at + number + 1, :] = cell[:, part].astype(F32)
            lanes_out[0][at + strips + number : at + strips + number + 1, :] = live[:, part]

    for number in (1, 0, 8):
        copies[number].wait()
    lane = iota((cx, cy), 1)
    if plan["relay"]:
        edge = edge_of(0, cy)
        inner = jnp.where(edge == 0, 1, cy - 2)
        tiles = {name: LanePacker(lane, at) for name, at in zip("cdvwuk", (edge, inner, edge, inner, edge, edge))}
        for level in range(levels):
            turned = pltpu.roll(south[level], level, 1) if level else south[level]
            tiles["v"].put(level, turned)
            tiles["w"].put(level, turned)
            tiles["u"].put(level, pltpu.roll(west[level], level, 1) if level else west[level])
            if level < levels - 1:
                tiles["k"].put(level, pltpu.roll(mixing[level], level, 1) if level else mixing[level])
        totals = None
        for t in range(carried):
            copies[9 + t].wait()
            totals = [tracer[t, level] + (totals[level] if t else 0.0) for level in range(levels)]
        for level in range(levels):
            turned = pltpu.roll(totals[level], level, 1) if level else totals[level]
            tiles["c"].put(level, turned)
            tiles["d"].put(level, turned)
        packed = jnp.zeros((cx, cy), F32)
        for name in "cdvwu":
            packed = packed + tiles[name].packed(plan["lane_" + name])
        lanes_out[0][0:cx, :] = packed
        lanes_out[0][cx : 2 * cx, :] = tiles["k"].packed(0)
    else:
        edges = [LanePacker(lane, edge_of(number, cy)) for number in range(len(lanes_out))]
        for t in range(carried):
            copies[9 + t].wait()
        for f in range(carried + 1):
            for level in range(levels):
                spot = f * levels + level
                values = tracer[f, level] if f < carried else south[level]
                for tile in edges:
                    tile.put(spot, pltpu.roll(values, spot, 1) if spot else values)
        for tile, out in zip(edges, lanes_out):
            out[0:cx, :] = tile.packed(0)
    copies[2].wait()


class LanePacker:
    def __init__(self, lane, edge):
        self.lanes = lane.shape[1]
        self.back = lax.rem(2 * self.lanes - edge, self.lanes)
        self.place = lax.rem(lane + self.back, self.lanes)
        self.tile = jnp.zeros(lane.shape, F32)

    def put(self, spot, turned):
        self.tile = jnp.where(self.place == spot, turned, self.tile)

    def packed(self, start):
        return pltpu.roll(self.tile, lax.rem(self.back + start, self.lanes), 1)


def edge_of(number, lanes):
    even_y = is_even("facey")
    return jnp.where(even_y if number == 0 else jnp.logical_not(even_y), lanes - 1, 0)


def rows_kernel(plan, tracer, west, scale, blocks, *outs):
    carried, levels, cx, cy = tracer.shape
    head = (carried + 1) * levels
    if plan["relay"]:
        tile = LanePacker(iota((cx, cy), 1), edge_of(0, cy))
        for t in range(carried):
            for level in range(levels):
                spot = t * levels + level
                tile.put(spot, pltpu.roll(tracer[t, level], spot, 1) if spot else tracer[t, level])
        outs[2][...] = tile.packed(0)
    for number, out in enumerate(outs[:2]):
        row = sent_row(plan, number, cx)
        for level in range(levels):
            for t in range(carried):
                spot = t * levels + level
                out[spot : spot + 1, :] = tracer[t, level, pl.ds(row, 1), :]
            spot = carried * levels + level
            out[spot : spot + 1, :] = west[level, pl.ds(row, 1), :]
        out[head : head + 8, :] = jnp.broadcast_to(scale[pl.ds(row, 1), :], (8, cy))
        if plan["x_blocks"][number] and not plan["relay"]:
            at = 8 * plan["own_blocks"].index(plan["x_blocks"][number])
            out[head + 8 : head + 16, :] = blocks[at : at + 8, :]


def relay_kernel(plan, head, cx, number, rows, blocks, y_got, out):
    out[0 : head + 8, :] = rows[0 : head + 8, :]
    row = sent_row(plan, number, cx)
    out[head + 1 : head + 2, :] = y_got[pl.ds(row, 1), :]
    near, far = plan["x_blocks"]
    even_x = is_even("facex")
    offset = jnp.where(even_x if number == 0 else jnp.logical_not(even_x), near, far)
    at = plan["y_tiles"] * cx + 8 * offset
    out[head + 8 : head + 24, :] = blocks[pl.ds(pl.multiple_of(8 * offset, 8), 16), :]
    out[head + 24 : head + 40, :] = y_got[pl.ds(pl.multiple_of(at, 8), 16), :]


def beyond_kernel(plan, cx, blocks, y_got, *outs):
    for out, offset in zip(outs, plan["x_ops"]):
        at = plan["y_tiles"] * cx + 8 * offset
        out[0:16, :] = blocks[8 * offset : 8 * offset + 16, :]
        out[16:32, :] = y_got[at : at + 16, :]


def rim_kernel(plan, carried, levels, cx, y_sent, y_got, base, base_other, lanes, *refs):
    inverse_out, ratio_out, lower_out, pieces_out, columns_out, rows_out, picks_out, live_out, base_out, square = refs
    cy = y_got.shape[1]
    slots = live_out.shape[1]

    def turned(values):
        square[...] = jnp.zeros((LANES, LANES), F32)
        square[0:cx, :] = values
        return jnp.transpose(square[...])

    def part(values, name):
        return values[plan["lane_" + name] : plan["lane_" + name] + levels]

    beyond = turned(y_got[0:cx, :])
    mine = turned(y_sent[0:cx, :])
    coupling = turned(y_got[cx : 2 * cx, :])
    north = is_even("facey")
    pieces_out[0] = part(beyond, "c")
    pieces_out[1] = part(beyond, "u")
    pieces_out[2] = part(beyond, "v")
    pieces_out[3] = jnp.where(north, part(beyond, "w"), part(mine, "v"))
    pieces_out[4] = jnp.where(north, part(mine, "c"), part(beyond, "d"))
    pieces_out[5] = jnp.where(north, part(beyond, "d"), part(mine, "c"))

    def level_of(ref, level):
        return jnp.broadcast_to(ref[level : level + 1, :], (8, LANES))

    square[...] = coupling
    first = []
    ratios = []
    before = None
    for level in range(levels):
        diagonal = jnp.ones((8, LANES), F32)
        if level > 0:
            below = level_of(square, level - 1)
            diagonal = diagonal + below
        if level < levels - 1:
            diagonal = diagonal + level_of(square, level)
        if level > 0:
            diagonal = diagonal - below * below * before
        inverse = 1.0 / diagonal
        ratios.append(level_of(square, level) * inverse if level < levels - 1 else jnp.zeros((8, LANES), F32))
        lower = below * inverse if level > 0 else jnp.zeros((8, LANES), F32)
        lower_out[level : level + 1, :] = lower[0:1]
        inverse_out[level : level + 1, :] = inverse[0:1]
        ratio_out[level : level + 1, :] = ratios[-1][0:1]
        first.append(inverse if level == 0 else lower * first[-1])
        before = inverse
    weight = first
    for level in range(levels - 2, -1, -1):
        weight[level] = first[level] + ratios[level] * weight[level + 1]
    for level in range(levels):
        square[level : level + 1, :] = weight[level][0:1]
    weights = square[0:levels, :]
    tile = LanePacker(iota((cx, cy), 1), edge_of(0, cy))
    for t in range(2 * carried):
        values = base[t] if t < carried else base_other[t - carried]
        tile.put(t, pltpu.roll(values, t, 1) if t else values)
    base_out[0:cx, :] = tile.packed(0)
    base_out[cx : 2 * cx, :] = lanes[...]
    at = plan["y_tiles"] * cx + 8 * len(plan["y_blocks"])
    strips = slots // LANES
    cell = jnp.concatenate([y_got[at + n : at + n + 1, :] for n in range(strips)], axis=1).astype(jnp.int32)
    live_out[...] = jnp.concatenate([y_got[at + strips + n : at + strips + n + 1, :] for n in range(strips)], axis=1)
    on_edge = lax.rem(cell, cy) == jnp.where(north, 0, cy - 1)
    x_of = jnp.where(on_edge, lax.div(cell, cy), LANES)
    picks = jnp.where(iota((LANES, slots), 0) == x_of, 1.0, 0.0)
    rows_out[...] = picks[0:cx]
    picks = picks.astype(BF16)
    picks_out[...] = picks
    high, low = halves(weights)
    columns_out[...] = jnp.dot(high, picks, preferred_element_type=F32) + jnp.dot(
        low, picks, preferred_element_type=F32
    )


def factor_kernel(sizes, *refs):
    (tracer, west, south, mixing, adjoint, cells) = refs[:6]
    inverse_out, lower_out, ratio_out, base_out, inner_out, shares_out, columns_out, rows_out, picks_out = refs[6:]
    carried, levels, cx, cy = tracer.shape
    slots = cells.shape[1]
    first = []
    before = None
    for level in range(levels):
        diagonal = jnp.ones((cx, cy), F32)
        if level > 0:
            diagonal = diagonal + mixing[level - 1]
        if level < levels - 1:
            diagonal = diagonal + mixing[level]
        if level > 0:
            diagonal = diagonal - mixing[level - 1] * mixing[level - 1] * before
        inverse = 1.0 / diagonal
        inverse_out[level] = inverse
        if level < levels - 1:
            ratio_out[level] = mixing[level] * inverse
        lower = mixing[level - 1] * inverse if level > 0 else jnp.zeros((cx, cy), F32)
        lower_out[level] = lower
        first.append(inverse if level == 0 else lower * first[-1])
        before = inverse
    ratio_out[levels - 1] = jnp.zeros((cx, cy), F32)
    weight = first
    for level in range(levels - 2, -1, -1):
        weight[level] = first[level] + ratio_out[level] * weight[level + 1]
    for t in range(carried):
        total = weight[0] * adjoint[t, 0]
        for level in range(1, levels):
            total = total + weight[level] * adjoint[t, level]
        base_out[t] = total
    for level in range(levels):
        total = tracer[0, level]
        for t in range(1, carried):
            total = total + tracer[t, level]
        parts = shares(west[level], south[level])
        for number, part in enumerate(parts):
            shares_out[number, level] = part
        inner_out[level] = mix(parts, total)
    cell = cells[...]
    x_of = lax.div(cell, cy)
    y_of = lax.rem(cell, cy)
    in_row = jnp.where(iota((cx, slots), 0) == x_of, 1.0, 0.0)
    in_lane = jnp.where(iota((cy, slots), 0) == y_of, 1.0, 0.0).astype(BF16)
    rows_out[...] = in_row
    picks_out[...] = in_lane
    high, low = halves(jnp.concatenate(weight, axis=0))
    picked = jnp.dot(high, in_lane, preferred_element_type=F32)
    picked = picked + jnp.dot(low, in_lane, preferred_element_type=F32)
    for level in range(levels):
        part = picked[level * cx : (level + 1) * cx] * in_row
        columns_out[level : level + 1, :] = jnp.sum(part, axis=0, keepdims=True)


def sides(plan, first, second):
    if plan["relay"]:
        return first, second
    even_x = is_even("facex")
    return jnp.where(even_x, second, first), jnp.where(even_x, first, second)


def own_sides(plan, first, second):
    return (second, first) if plan["relay"] else sides(plan, first, second)


def sent_row(plan, number, rows):
    if plan["relay"]:
        return rows - 1 if number == 0 else 0
    even_x = is_even("facex")
    return jnp.where(even_x if number == 0 else jnp.logical_not(even_x), rows - 1, 0)


def seam(number, sent, got, sent_face, got_face):
    even_y = is_even("facey")
    north = even_y if number == 0 else jnp.logical_not(even_y)
    to_north = -(jnp.maximum(got_face, 0.0) * sent + jnp.minimum(got_face, 0.0) * got)
    to_south = jnp.maximum(sent_face, 0.0) * got
    return jnp.where(north, to_north, to_south), jnp.where(north, sent.shape[1] - 1, 0)


def spread_wind(values, start, carried, levels):
    lane = iota(values.shape, 1)
    result = jnp.zeros_like(values)
    for t in range(carried):
        moved = pltpu.roll(values, (t * levels - start) % values.shape[1], 1)
        inside = jnp.logical_and(lane >= t * levels, lane < (t + 1) * levels)
        result = jnp.where(inside, moved, result)
    return result


def seam_lanes(number, plan, sent, got, sent_wind, got_wind, carried, levels):
    start = plan["lane_v"]
    faces = [spread_wind(wind, start, carried, levels) for wind in (sent_wind, got_wind)]
    return seam(number, sent, got, *faces)


def observe_kernel(sizes, plan, carried, *refs):
    refs = list(refs)
    got = refs[0:2]
    inner, lower, inverse, ratio, columns, in_row, in_lane, live = refs[2:10]
    sent = refs[10:12]
    refs = refs[12:]
    y_sent = refs[: plan["y_ops"]]
    y_got = refs[plan["y_ops"] : 2 * plan["y_ops"]]
    refs = refs[2 * plan["y_ops"] :]
    own = refs[0]
    n_pairs = len(plan["pairs"])
    pair_got = refs[1 : 1 + n_pairs]
    swapped = refs[1 + n_pairs] if n_pairs else None
    if plan["relay"]:
        x_got = refs[1 : 1 + len(plan["x_ops"])]
        refs = refs[1 + len(plan["x_ops"]) :]
        rim = refs[:8]
        parcel, state_out, turn, rise = refs[8:]
    else:
        modeled_out, state_out = refs[-2:]
    levels, cx, cy = inner.shape
    slots = in_row.shape[1]
    head = (carried + 1) * levels

    def summed(rows):
        total = rows[0:levels]
        for t in range(1, carried):
            total = total + rows[t * levels : (t + 1) * levels]
        return total

    beyond_west, beyond_east = sides(plan, got[0][0:head], got[1][0:head])
    at_west, at_east = own_sides(plan, sent[0][0:head], sent[1][0:head])
    spot = carried * levels
    face_west = at_west[spot:head]
    face_east = beyond_east[spot:head]
    from_west = jnp.maximum(face_west, 0.0) * summed(beyond_west)
    from_east = -(
        jnp.maximum(face_east, 0.0) * summed(at_east) + jnp.minimum(face_east, 0.0) * summed(beyond_east)
    )
    lane_parts = []
    for number in range(plan["y_ops"]):
        mine, beyond = y_sent[number][0:cx, :], y_got[number][0:cx, :]
        if plan["relay"]:
            faces = [pltpu.roll(values, cy - plan["lane_v"], 1) for values in (mine, beyond)]
            total, spot_y = seam(number, mine, beyond, *faces)
        else:
            part, spot_y = seam_lanes(number, plan, mine, beyond, mine, beyond, carried, levels)
            total = part
            for t in range(1, carried):
                total = total + pltpu.roll(part, (-t * levels) % cy, 1)
        lane_parts.append((pltpu.roll(total, spot_y, 1), spot_y))
    lane = iota((cx, cy), 1)
    row = iota((cx, cy), 0)
    forward = []
    for level in range(levels):
        value = inner[level]
        value = value + jnp.where(row == 0, from_west[level : level + 1], 0.0)
        value = value + jnp.where(row == cx - 1, from_east[level : level + 1], 0.0)
        for total, spot_y in lane_parts:
            moved = pltpu.roll(total, cy - level, 1) if level else total
            value = value + jnp.where(lane == spot_y, moved, 0.0)
        value = value * inverse[level]
        forward.append(value + lower[level] * forward[-1] if level else value)
    result = forward
    for level in range(levels - 2, -1, -1):
        result[level] = forward[level] + ratio[level] * result[level + 1]
    high, low = halves(jnp.concatenate(result, axis=0))
    picks = in_lane[...]
    picked = jnp.dot(high, picks, preferred_element_type=F32)
    picked = picked + jnp.dot(low, picks, preferred_element_type=F32)

    start = plan["y_tiles"] * cx
    if plan["relay"]:

        def block_at(ref, row):
            return ref[row : row + 8, :]

        blocks = {0: block_at(own, 0), 1: block_at(y_got[0], start + 8)}
        rim_blocks = {0: block_at(y_got[0], start), 1: block_at(own, 8)}
        even_x = is_even("facex")
        from_west, from_east = (got[n][head + 8 : head + 40, :] for n in range(2))
        carriers = [
            (plan["x_blocks"][0], jnp.where(even_x, from_east, from_west), 0),
            (plan["x_blocks"][1], jnp.where(even_x, from_west, from_east), 0),
        ]
        carriers += [(offset, ref, 0) for offset, ref in zip(plan["x_ops"], x_got)]
        for offset, ref, row in carriers:
            blocks[offset], rim_blocks[offset + 1] = block_at(ref, row), block_at(ref, row + 8)
            rim_blocks[offset], blocks[offset + 1] = block_at(ref, row + 16), block_at(ref, row + 24)
    else:
        blocks = {0: own[0:8, :], plan["y_blocks"][0]: y_got[0][start : start + 8, :]}
        for number in range(2):
            offset = plan["x_blocks"][number]
            if offset:
                blocks[offset] = got[number][head + 8 : head + 16, :]
    first_core = lax.axis_index("lev") == 0
    for number, (for_first, for_second) in enumerate(plan["pairs"]):
        mine = pair_got[number][...]
        other = swapped[8 * number : 8 * number + 8, :]
        if for_first == for_second:
            blocks[for_first] = mine
        else:
            blocks[for_first] = jnp.where(first_core, mine, other)
            blocks[for_second] = jnp.where(first_core, other, mine)
    cap = slots // len(blocks)
    per_tile = LANES // cap
    group_of_lane = lax.div(iota((8, LANES), 1), cap)

    def gathered(group, blocks):
        tiles = []
        for start in range(0, len(blocks), per_tile):
            tile = jnp.zeros((8, LANES), F32)
            for a in range(per_tile):
                moved = pltpu.roll(blocks[start + a], (cap * (a - group)) % LANES, 1)
                tile = jnp.where(group_of_lane == a, moved, tile)
            tiles.append(tile)
        return jnp.concatenate(tiles, axis=1)

    groups = [gathered(g, blocks) for g in range(levels // 8)]
    last = gathered(levels // 8, blocks)
    total = jnp.zeros((cx, slots), F32)
    sensitivity = jnp.zeros((8, slots), F32)
    for g, kernel in enumerate(groups):
        sensitivity = sensitivity + kernel * columns[8 * g : 8 * g + 8, :]
        for l in range(8):
            level = 8 * g + l
            total = total + kernel[l : l + 1] * picked[level * cx : (level + 1) * cx]
    modeled = jnp.sum(total * in_row[...], axis=0, keepdims=True)
    gain = jnp.sum(sensitivity, axis=0, keepdims=True) * last[1:2] * live[...]
    if not plan["relay"]:
        modeled_out[...] = modeled
        state_out[...] = jnp.concatenate([gain, last[0:1]], axis=0)
        return

    rim_inverse, rim_ratio, rim_lower, pieces, rim_columns, rim_rows, rim_picks, rim_live = rim
    corners_west, corners_east = sides(plan, got[0][head + 1 : head + 2, :], got[1][head + 1 : head + 2, :])
    turn[...] = jnp.zeros((LANES, LANES), F32)
    turn[0:1, :] = corners_west
    turn[cx - 1 : cx, :] = corners_east
    turned = jnp.transpose(turn[...])
    ends = turned[plan["lane_c"] : plan["lane_c"] + levels]
    end_face = turned[plan["lane_u"] : plan["lane_u"] + levels]
    place = iota((levels, LANES), 1)
    cells, face_w, face_s, face_n, south_cells, north_cells = (pieces[n] for n in range(6))
    west_cells = jnp.where(place == 0, ends, pltpu.roll(cells, 1, 1))
    east_cells = jnp.where(place == cx - 1, ends, pltpu.roll(cells, LANES - 1, 1))
    face_e = jnp.where(place == cx - 1, end_face, pltpu.roll(face_w, LANES - 1, 1))
    rise[0:levels, :] = advance_cells(
        cells, west_cells, east_cells, south_cells, north_cells, face_w, face_e, face_s, face_n
    )

    def level_of(ref, level):
        return jnp.broadcast_to(ref[level : level + 1, :], (8, LANES))

    climbed = []
    for level in range(levels):
        value = level_of(rise, level) * level_of(rim_inverse, level)
        climbed.append(value + level_of(rim_lower, level) * climbed[-1] if level else value)
    for level in range(levels - 2, -1, -1):
        climbed[level] = climbed[level] + level_of(rim_ratio, level) * climbed[level + 1]
    for level in range(levels):
        rise[level : level + 1, :] = climbed[level][0:1]
    high, low = halves(rise[0:levels, :])
    picks = rim_picks[...]
    picked = jnp.dot(high, picks, preferred_element_type=F32)
    picked = picked + jnp.dot(low, picks, preferred_element_type=F32)
    rim_total = jnp.zeros((8, slots), F32)
    sensitivity = jnp.zeros((8, slots), F32)
    for g in range(levels // 8):
        kernel = gathered(g, rim_blocks)
        rim_total = rim_total + kernel * picked[8 * g : 8 * g + 8]
        sensitivity = sensitivity + kernel * rim_columns[8 * g : 8 * g + 8, :]
    rim_modeled = jnp.sum(rim_total, axis=0, keepdims=True)
    rim_last = gathered(levels // 8, rim_blocks)
    rim_gain = jnp.sum(sensitivity, axis=0, keepdims=True) * rim_last[1:2] * rim_live[...]
    state_out[...] = jnp.concatenate([gain, last[0:1], rim_gain, rim_last[0:1]], axis=0)
    strips = slots // LANES
    for number in range(strips):
        part = slice(number * LANES, (number + 1) * LANES)
        parcel[number : number + 1, :] = modeled[:, part]
        parcel[strips + number : strips + number + 1, :] = rim_modeled[:, part]


def advance_cells(cells, west, east, south, north, face_w, face_e, face_s, face_n):
    flux_w = jnp.maximum(face_w, 0.0) * west + jnp.minimum(face_w, 0.0) * cells
    flux_e = jnp.maximum(face_e, 0.0) * cells + jnp.minimum(face_e, 0.0) * east
    flux_s = jnp.maximum(face_s, 0.0) * south + jnp.minimum(face_s, 0.0) * cells
    flux_n = jnp.maximum(face_n, 0.0) * cells + jnp.minimum(face_n, 0.0) * north
    return cells + flux_w - flux_e + flux_s - flux_n


def scatter(force, in_row, in_lane):
    high, low = halves(in_row * force)
    dims = (((1,), (1,)), ((), ()))
    scattered = lax.dot_general(high, in_lane, dims, preferred_element_type=F32)
    return scattered + lax.dot_general(low, in_lane, dims, preferred_element_type=F32)


def force_kernel(plan, *refs):
    modeled, modeled_other, state, in_row, in_lane, base, base_other = refs[:7]
    near_out = refs[7]
    rim_outs = refs[8:]
    carried, cx, cy = base.shape
    misfit = modeled[...] + modeled_other[...] - state[1:2, :]
    force = state[0:1, :] * misfit
    scattered = scatter(force, in_row[...], in_lane[...])
    lane = iota((cx, cy), 1)
    even_y = is_even("facey")
    edges = []
    for number in range(len(rim_outs)):
        sends_last = even_y if number == 0 else jnp.logical_not(even_y)
        edges.append(jnp.where(sends_last, cy - 1, 0))
    rims = [jnp.zeros((cx, cy), F32) for _ in rim_outs]
    for t in range(2 * carried):
        values = scattered + (base[t] if t < carried else base_other[t - carried])
        near_out[t] = values
        for number, edge in enumerate(edges):
            moved = pltpu.roll(values, lax.rem(t + cy - edge, cy), 1)
            rims[number] = jnp.where(lane == t, moved, rims[number])
    for rim, out in zip(rims, rim_outs):
        out[...] = rim


def surface_kernel(sizes, plan, carried, levels, *refs):
    y_ops = plan["y_ops"]
    near = refs[0]
    rims = refs[6 + y_ops : 6 + 2 * y_ops]
    rim_values = [[rim[...] for rim in rims] for _ in range(near.shape[0])]
    values = [near[t] for t in range(near.shape[0])]
    spread_surface(
        sizes, plan, carried, levels, values, rim_values, refs[1:4], refs[4:6], refs[6 : 6 + y_ops], refs[6 + 2 * y_ops :]
    )


def weigh_kernel(sizes, plan, carried, levels, *refs):
    parcel, other, state, in_row, in_lane, base, base_other, rim_rows, rim_base = refs[:9]
    cx, cy = base.shape[1:]
    strips = state.shape[1] // LANES

    def misfit(kind):
        both = parcel[kind * strips : (kind + 1) * strips, :] + other[kind * strips : (kind + 1) * strips, :]
        flat = jnp.concatenate([both[n : n + 1] for n in range(strips)], axis=1)
        return state[2 * kind : 2 * kind + 1, :] * (flat - state[2 * kind + 1 : 2 * kind + 2, :])

    scattered = scatter(misfit(0), in_row[...], in_lane[...])
    on_rim = jnp.sum(rim_rows[...] * misfit(1), axis=1, keepdims=True)
    near = [scattered + base[t] for t in range(carried)]
    near += [scattered + base_other[t] for t in range(carried)]
    rims = [[rim_base[0:cx, :] + on_rim] for _ in near]
    spread_surface(sizes, plan, carried, levels, near, rims, refs[9:12], refs[12:14], refs[14:15], refs[15:])


def spread_surface(sizes, plan, carried, levels, near, rim_values, fields, got, y_got, outs):
    west, south, scale = fields
    tracers = len(near)
    cx, cy = near[0].shape
    spot_v = plan["lane_v"]
    band = cy // sizes[0]
    per_tile = min(tracers, LANES // band)
    spot = carried * levels
    head = (carried + 1) * levels
    lane = iota((cx, cy), 1)
    row = iota((cx, cy), 0)
    even_y = is_even("facey")
    face_west = west[...]
    face_south = south[...]
    scales = scale[...]
    beyond_west, beyond_east = sides(plan, got[0][head : head + 1], got[1][head : head + 1])
    _, east_wind = sides(plan, got[0][spot : spot + 1], got[1][spot : spot + 1])
    face_east = jnp.where(row == cx - 1, east_wind, pltpu.roll(face_west, cx - 1, 0))
    face_north = left(face_south)
    norths = []
    for number in range(plan["y_ops"]):
        norths.append(even_y if number == 0 else jnp.logical_not(even_y))
        moved = pltpu.roll(y_got[number][0:cx, :], cy - 1 - spot_v, 1)
        keep = jnp.logical_and(lane == cy - 1, norths[number])
        face_north = jnp.where(keep, moved, face_north)
    to_middle = 1.0 + jnp.minimum(face_west, 0.0) - jnp.maximum(face_east, 0.0)
    to_middle = scales * (to_middle + jnp.minimum(face_south, 0.0) - jnp.maximum(face_north, 0.0))
    to_east = jnp.where(row == cx - 1, 0.0, scales * jnp.maximum(face_east, 0.0))
    to_west = jnp.where(row == 0, 0.0, scales * jnp.minimum(face_west, 0.0))
    to_north = scales * jnp.maximum(face_north, 0.0)
    to_south = scales * jnp.minimum(face_south, 0.0)
    west_gain = beyond_west * jnp.maximum(face_west[0:1], 0.0)
    east_gain = -beyond_east * jnp.minimum(face_east[cx - 1 : cx], 0.0)
    filler = jnp.zeros((6, cy), F32)
    grown = []
    for t in range(tracers):
        values = near[t]
        north_side = left(values)
        south_side = right(values)
        for number in range(plan["y_ops"]):
            rim = rim_values[t][number]
            at_north = jnp.logical_and(lane == cy - 1, norths[number])
            at_south = jnp.logical_and(lane == 0, jnp.logical_not(norths[number]))
            north_side = jnp.where(at_north, pltpu.roll(rim, (cy - 1 - t) % cy, 1), north_side)
            south_side = jnp.where(at_south, pltpu.roll(rim, (-t) % cy, 1), south_side)
        swept = to_middle * values + to_east * pltpu.roll(values, cx - 1, 0) - to_west * pltpu.roll(values, 1, 0)
        swept = swept + to_north * north_side - to_south * south_side
        grown.append(
            jnp.concatenate(
                [swept, west_gain * values[0:1], east_gain * values[cx - 1 : cx], filler], axis=0
            )
        )
    rows = cx + 8
    group_of_lane = lax.div(iota((rows, cy), 1), band)
    first_core = lax.axis_index("lev") == 0
    place = lax.axis_index("facex")
    for out, (for_first, for_second) in zip(outs, plan["bands"]):
        offset = for_first if for_first == for_second else jnp.where(first_core, for_first, for_second)
        target = jnp.bitwise_xor(place, offset)
        count = carried if for_first == for_second else tracers
        skip = carried if for_first == for_second != 0 and plan["cross"] else 0
        for start in range(0, count, per_tile):
            tile = jnp.zeros((rows, cy), F32)
            for a in range(min(per_tile, count - start)):
                moved = pltpu.roll(grown[skip + start + a], lax.rem(band * a + cy - band * target, cy), 1)
                tile = jnp.where(group_of_lane == a, moved, tile)
            out[start // per_tile * rows : (start // per_tile + 1) * rows, :] = tile


def regrid_kernel(sizes, plan, bands, carried, cx, band, *refs):
    index, weight = refs[:2]
    blocks, more, out = refs[2 : 2 + len(bands)], refs[2 + len(bands) : -1], refs[-1]
    taps, cells = index.shape
    rows = cx + 8
    per_tile = min(2 * carried, LANES // band)
    lane = iota((rows, LANES), 1)
    row = iota((rows, cells), 0)
    first_core = lax.axis_index("lev") == 0
    place = lax.axis_index("facex")
    around = sizes[0] * cx
    parts = []
    row_places = []
    for block, ((for_first, for_second), fetched, first) in zip(blocks, bands):
        if plan["cross"] != fetched:
            for_first, for_second = for_second, for_first
        offset = for_first if for_first == for_second else jnp.where(first_core, for_first, for_second)
        start = jnp.bitwise_xor(place, offset) * cx
        places = start + row
        places = jnp.where(row == cx, lax.rem(start + around - 1, around), places)
        places = jnp.where(row == cx + 1, lax.rem(start + cx, around), places)
        row_places.append(places)
        for t in range(first, first + carried):
            tile = block[t // per_tile * rows : (t // per_tile + 1) * rows, :]
            a = t % per_tile
            values = tile if a == 0 else pltpu.roll(tile, (-band * a) % LANES, 1)
            high = values.astype(BF16).astype(F32)
            low = pltpu.roll(values - high, band, 1)
            both = jnp.where(lane < band, high, jnp.where(lane < 2 * band, low, 0.0))
            parts.append(both.astype(BF16))
    left_side = jnp.concatenate(parts, axis=0)
    spread = iota((LANES, cells), 0)
    in_band = lax.rem(spread, band)
    used = spread < 2 * band
    totals = [jnp.zeros((rows, cells), F32) for _ in range(carried)]
    for tap in range(taps):
        place_of = index[tap : tap + 1, :]
        column = lax.div(place_of, band)
        in_lane = lax.rem(place_of, band)
        picks = jnp.where(jnp.logical_and(in_band == in_lane, used), 1.0, 0.0).astype(BF16)
        picked = jnp.dot(left_side, picks, preferred_element_type=F32)
        at = 0
        for places in row_places:
            chosen = jnp.where(places == column, weight[tap : tap + 1, :], 0.0)
            for t in range(carried):
                totals[t] = totals[t] + chosen * picked[at : at + rows]
                at += rows
    sums = jnp.concatenate([jnp.sum(total, axis=0, keepdims=True) for total in totals], axis=0)
    for ref in more:
        sums = sums + ref[...]
    out[...] = sums


def advance_kernel(plan, *refs):
    tracer, parts, lower, inverse, ratio = refs[:5]
    sent = refs[5:7]
    got = refs[7:9]
    y_ops = plan["y_ops"]
    y_sent, y_got, winds_sent, winds_got = (refs[9 + n * y_ops : 9 + (n + 1) * y_ops] for n in range(4))
    target, out, west_rows, east_rows, done = refs[-5:]
    carried, levels, cx, cy = tracer.shape
    head = (carried + 1) * levels
    spot = carried * levels
    beyond_west, beyond_east = sides(plan, got[0][0:head], got[1][0:head])
    at_west, at_east = own_sides(plan, sent[0][0:head], sent[1][0:head])
    face_west = at_west[spot:head]
    face_east = beyond_east[spot:head]
    for t in range(carried):
        part = slice(t * levels, (t + 1) * levels)
        west_rows[part, :] = jnp.maximum(face_west, 0.0) * beyond_west[part]
        east_rows[part, :] = -(
            jnp.maximum(face_east, 0.0) * at_east[part] + jnp.minimum(face_east, 0.0) * beyond_east[part]
        )
    lane = iota((cx, cy), 1)
    row = iota((cx, cy), 0)
    seams = [
        seam_lanes(
            n,
            plan,
            y_sent[n][0:cx, :],
            y_got[n][-cx:, :] if plan["relay"] else y_got[n][0:cx, :],
            winds_sent[n][0:cx, :],
            winds_got[n][0:cx, :],
            carried,
            levels,
        )
        for n in range(y_ops)
    ]
    stride = 4

    def forward(step, before):
        mixed = []
        for k in range(stride):
            level = step * stride + k
            weights = [parts[n, level] for n in range(5)]
            mixed.append([])
            for t in range(carried):
                value = mix(weights, tracer[t, level])
                value = value + jnp.where(row == 0, west_rows[pl.ds(t * levels + level, 1), :], 0.0)
                value = value + jnp.where(row == cx - 1, east_rows[pl.ds(t * levels + level, 1), :], 0.0)
                for packed, spot_y in seams:
                    moved = pltpu.roll(packed, lax.rem(spot_y - (t * levels + level) + 2 * cy, cy), 1)
                    value = value + jnp.where(lane == spot_y, moved, 0.0)
                mixed[k].append(value)
        for k in range(stride):
            level = step * stride + k
            from_below = lower[level]
            scaled = inverse[level]
            after = []
            for t in range(carried):
                value = mixed[k][t] * scaled + from_below * before[t]
                out[t, level] = value
                after.append(value)
            before = after
        return tuple(before)

    def copy(step):
        part = pl.ds(levels - (step + 1) * stride, stride)
        return pltpu.make_async_copy(out.at[:, part], target.at[:, part], done.at[step])

    start = tuple(jnp.zeros((cx, cy), F32) for _ in range(carried))
    lax.fori_loop(0, levels // stride, forward, start)
    above = list(start)
    for step in range(levels // stride):
        for k in range(stride):
            level = levels - 1 - step * stride - k
            factor = ratio[level]
            for t in range(carried):
                above[t] = out[t, level] + factor * above[t]
                out[t, level] = above[t]
        copy(step).start()
    for step in range(levels // stride):
        copy(step).wait()


GROUP = ("facex", "facey", "lev")


def exchange(values, sizes, rule):
    many_x, many_y, cores = sizes
    pairs = []
    for x in range(many_x):
        for y in range(many_y):
            for c in range(cores):
                to = rule(x, y, c)
                if to is not None:
                    pairs.append(((x * many_y + y) * cores + c, (to[0] * many_y + to[1]) * cores + to[2]))
    return lax.ppermute(values, GROUP, pairs)


def make_plan(sizes):
    many_x, many_y, _ = sizes
    tiles = many_x * many_y
    x_blocks = [many_y, (many_x - 1) * many_y if many_x == 4 else 0]
    relay = many_y == 2 and many_x == 4
    if relay:
        own_blocks = list(range(tiles))
        y_blocks = own_blocks
        x_ops = [offset for offset in own_blocks[2::2] if offset not in x_blocks]
        pairs = []
    else:
        own_blocks = [0] + [offset for offset in x_blocks if offset]
        y_blocks = [1]
        x_ops = []
        rest = [d for d in range(tiles) if d not in {1, *own_blocks}]
        rest.sort(key=lambda d: (d // many_y != many_x // 2, d))
        pairs = [(rest[n], rest[min(n + 1, len(rest) - 1)]) for n in range(0, len(rest), 2)]
    others = list(range(many_x - 1, 1, -1))
    bands = [(0, 0), (1, 1)] + [(others[n], others[n + 1]) for n in range(0, len(others), 2)]
    return {
        "relay": relay,
        "cross": 1 if relay else 0,
        "x_blocks": x_blocks,
        "x_ops": x_ops,
        "own_blocks": own_blocks,
        "y_blocks": y_blocks,
        "y_ops": 1 if many_y == 2 else 2,
        "y_tiles": 2 if relay else 1,
        "pairs": pairs,
        "bands": bands,
    }


def lane_plan(plan, carried, levels):
    starts = {"c": 0, "d": levels, "v": 2 * levels, "w": 3 * levels, "u": 4 * levels}
    if not plan["relay"]:
        starts = {"v": carried * levels}
    return {"lane_" + name: start for name, start in starts.items()}


def local(
    sizes,
    tracer,
    west_courant,
    south_courant,
    mixing,
    adjoint_later,
    emission_scale,
    send_cells,
    send_counts,
    kernels,
    observed,
    error_weight,
    regrid_index,
    regrid_weight,
):
    plan = make_plan(sizes)
    many_x, many_y, _ = sizes
    carried, levels, cx, cy = tracer.shape
    owners, cap = send_cells.shape[2:]
    slots = owners * cap
    taps, ll = regrid_index.shape[2:]
    plan.update(lane_plan(plan, carried, levels))
    head = (carried + 1) * levels
    y_ops = plan["y_ops"]
    band = cy // many_x

    def next_x(number):
        def rule(x, y, c):
            step = 1 if (plan["relay"] or x % 2 == 0) == (number == 0) else -1
            return ((x + step) % many_x, y, c)

        return rule

    def next_y(number, cross):
        def rule(x, y, c):
            to = y + (1 if (y % 2 == 0) == (number == 0) else -1)
            return (x, to, c ^ cross) if 0 <= to < many_y else None

        return rule

    def jump(for_first, for_second, cross=0):
        def rule(x, y, c):
            d = for_first if c == 0 else for_second
            return (x ^ (d // many_y), y ^ (d % many_y), c ^ cross)

        return rule

    def other_core(values):
        return exchange(values, sizes, lambda x, y, c: (x, y, 1 - c))

    strips = slots // LANES
    plan["parcel"] = -(-2 * strips // 8) * 8
    extra = 40 if plan["relay"] else 16
    row_shapes = [shape(head + extra, cy)] * 2
    y_rows = plan["y_tiles"] * cx + 8 * len(plan["y_blocks"]) + (plan["parcel"] if plan["relay"] else 0)
    lane_shapes = [shape(y_rows if n == 0 else cx, cy) for n in range(y_ops)]
    packed = call(
        functools.partial(pack_kernel, sizes, plan),
        lane_shapes
        + [shape(8 * len(plan["own_blocks"]), LANES)]
        + [shape(8, LANES)] * len(plan["pairs"])
        + [shape(1, slots, dtype=jnp.int32), shape(1, slots)]
        + [shape(*a.shape) for a in (tracer, west_courant, south_courant, emission_scale, mixing)],
        [
            tracer,
            west_courant,
            south_courant,
            emission_scale,
            kernels.reshape(owners, levels, cap),
            observed.reshape(owners, cap),
            error_weight.reshape(owners, cap),
            send_cells.reshape(owners, cap),
            send_counts.reshape(owners),
            mixing,
        ],
        "pack",
        100000,
        hbm=range(10),
        scratch=[
            pltpu.VMEM((owners, levels, cap), F32),
            pltpu.VMEM((owners, cap), F32),
            pltpu.VMEM((owners, cap), F32),
            pltpu.VMEM((owners, cap), jnp.int32),
            pltpu.SMEM((owners,), jnp.int32),
            pltpu.SemaphoreType.DMA((9 + carried,)),
        ],
    )
    lanes_sent = packed[:y_ops]
    own_blocks = packed[y_ops]
    pair_sent = packed[1 + y_ops : -7]
    cell, live, tracer, west_courant, south_courant, emission_scale, mixing = packed[-7:]
    lanes_got = [exchange(lanes_sent[n], sizes, next_y(n, plan["cross"])) for n in range(y_ops)]
    held, *_ = lax.optimization_barrier((tracer, *lanes_sent))
    inverse, lower, ratio, base, inner, parts, columns, in_row, in_lane = call(
        functools.partial(factor_kernel, sizes),
        [
            shape(levels, cx, cy),
            shape(levels, cx, cy),
            shape(levels, cx, cy),
            shape(carried, cx, cy),
            shape(levels, cx, cy),
            shape(5, levels, cx, cy),
            shape(levels, slots),
            shape(cx, slots),
            shape(cy, slots, dtype=BF16),
        ],
        [held, west_courant, south_courant, mixing, adjoint_later, cell],
        "factor",
        3000000,
    )
    rows_sent = list(
        call(
            functools.partial(rows_kernel, plan),
            row_shapes + ([shape(cx, cy)] if plan["relay"] else []),
            [tracer, west_courant, emission_scale, own_blocks],
            "rows",
            100000,
        )
    )
    per_tile = min(2 * carried, LANES // band)

    def band_shape(first, second):
        count = carried if first == second else 2 * carried
        return shape(-(-count // per_tile) * (cx + 8), cy)

    band_shapes = [band_shape(*b) for b in plan["bands"]]
    fields = [west_courant[0], south_courant[0], emission_scale]
    observe = functools.partial(
        call, functools.partial(observe_kernel, sizes, plan, carried), name="observe", flops=2000000
    )
    if plan["relay"]:
        base, *lanes_got = lax.optimization_barrier((base, *lanes_got))
        lanes_each = rows_sent.pop()
        base_other = other_core(base)

        def relay(number, *after):
            held, *_ = lax.optimization_barrier((rows_sent[number], *after))
            return call(
                functools.partial(relay_kernel, plan, head, cx, number),
                [row_shapes[number]],
                [held, own_blocks, lanes_got[0]],
                "relay",
                10000,
            )[0]

        rows_sent = [relay(0), relay(1)]
        x_sent = call(
            functools.partial(beyond_kernel, plan, cx),
            [shape(32, LANES)] * len(plan["x_ops"]),
            [own_blocks, lanes_got[0]],
            "beyond",
            10000,
        )
        x_got = [exchange(s, sizes, jump(d, d, 1)) for s, d in zip(x_sent, plan["x_ops"])]
        rows_got = [exchange(rows_sent[n], sizes, next_x(n)) for n in range(2)]
        held_y, *_ = lax.optimization_barrier((lanes_got[0], *rows_sent))
        rim = call(
            functools.partial(rim_kernel, plan, carried, levels, cx),
            [
                shape(levels, LANES),
                shape(levels, LANES),
                shape(levels, LANES),
                shape(6, levels, LANES),
                shape(levels, slots),
                shape(cx, slots),
                shape(LANES, slots, dtype=BF16),
                shape(1, slots),
                shape(2 * cx, cy),
            ],
            [lanes_sent[0], held_y, base, base_other, lanes_each],
            "rim",
            400000,
            scratch=[pltpu.VMEM((LANES, LANES), F32)],
        )
        *rim, rim_sent = rim
        rim_got = exchange(rim_sent, sizes, next_y(0, 0))
        parcel, state = observe(
            [shape(plan["parcel"], cy), shape(4, slots)],
            [*rows_got, inner, lower, inverse, ratio, columns, in_row, in_lane, live, *rows_sent]
            + [*lanes_sent, *lanes_got, own_blocks, *x_got, *rim],
            scratch=[pltpu.VMEM((LANES, LANES), F32), pltpu.VMEM((levels, LANES), F32)],
        )
        parcel_other = other_core(parcel)
        parcel_other, rim_got = lax.optimization_barrier((parcel_other, rim_got))
        band_sent = call(
            functools.partial(weigh_kernel, sizes, plan, carried, levels),
            band_shapes,
            [parcel, parcel_other, state, in_row, in_lane, base, base_other, rim[5], rim_got, *fields]
            + [*rows_got, *lanes_got],
            "weigh",
            500000,
        )
        lanes_own = [lanes_each, rim_got]
        held, *_ = lax.optimization_barrier((tracer, *band_sent))
    else:
        rows_got = [exchange(rows_sent[n], sizes, next_x(n)) for n in range(2)]
        pair_got = [exchange(s, sizes, jump(*p)) for s, p in zip(pair_sent, plan["pairs"])]
        base_other = other_core(base)
        modeled, state = observe(
            [shape(1, slots), shape(2, slots)],
            [*rows_got, inner, lower, inverse, ratio, columns, in_row, in_lane, live, *rows_sent]
            + [*lanes_sent, *lanes_got, own_blocks, *pair_got]
            + [other_core(jnp.concatenate(pair_got, axis=0))],
        )
        near, *rims_sent = call(
            functools.partial(force_kernel, plan),
            [shape(2 * carried, cx, cy)] + [shape(cx, cy)] * y_ops,
            [modeled, other_core(modeled), state, in_row, in_lane, base, base_other],
            "force",
            200000,
        )
        rims_got = [exchange(rims_sent[n], sizes, next_y(n, 0)) for n in range(y_ops)]
        band_sent = call(
            functools.partial(surface_kernel, sizes, plan, carried, levels),
            band_shapes,
            [near, *fields, *rows_got, *lanes_got, *rims_got],
            "surface",
            400000,
        )
        lanes_own = [*lanes_sent, *lanes_got]
        held = tracer
    (advanced,) = call(
        functools.partial(advance_kernel, plan),
        [shape(*tracer.shape)],
        [held, parts, lower, inverse, ratio]
        + list(rows_sent)
        + rows_got
        + lanes_own
        + list(lanes_sent)
        + lanes_got,
        "advance",
        6000000,
        scratch=[pltpu.VMEM(tracer.shape, F32)]
        + [pltpu.VMEM((carried * levels, cy), F32)] * 2
        + [pltpu.SemaphoreType.DMA((levels // 4,))],
        out_hbm=(0,),
    )
    band_got = [
        s
        if first == second == 0
        else exchange(s, sizes, jump(first * many_y, second * many_y, plan["cross"]))
        for s, (first, second) in zip(band_sent, plan["bands"])
    ]
    tables = [regrid_index.reshape(taps, ll), regrid_weight.reshape(taps, ll)]
    kinds = [first == second for first, second in plan["bands"]]

    def regridded(bands, blocks, *more):
        return call(
            functools.partial(regrid_kernel, sizes, plan, bands, carried, cx, band),
            [shape(carried, ll)],
            [*tables, *blocks, *more],
            "regrid",
            1000000,
        )[0]

    near = [(pair, 0, 0) for pair, kind in zip(plan["bands"], kinds) if kind]
    far = [pair for pair, kind in zip(plan["bands"], kinds) if not kind]
    near_got = [got for got, kind in zip(band_got, kinds) if kind]
    far_got = [got for got, kind in zip(band_got, kinds) if not kind]
    advanced, near_got, far_got = lax.optimization_barrier((advanced, near_got, far_got))
    far_fetched = [other_core(got) for got in far_got]
    mine = carried if plan["cross"] else 0
    partial = regridded(near + [(pair, 0, mine) for pair in far], near_got + far_got)
    latlon = regridded([(pair, 1, carried - mine) for pair in far], far_fetched, partial)
    return (advanced, latlon[:, None, None, :])


def solution(mesh):
    in_specs = (
        P("lev", "groups", "facex", "facey"),
        P("groups", "facex", "facey"),
        P("groups", "facex", "facey"),
        P("groups", "facex", "facey"),
        P("lev", "groups", "facex", "facey"),
        P("facex", "facey"),
        P("facex", "facey", "groups", None),
        P("facex", "facey", "groups"),
        P("facex", "facey", "groups", None, None),
        P("facex", "facey", "groups", None),
        P("facex", "facey", "groups", None),
        P("facex", "facey", None, None),
        P("facex", "facey", None, None),
    )
    out_specs = (P("lev", "groups", "facex", "facey"), P("lev", "facex", "facey", "groups"))
    sizes = tuple(mesh.shape[axis] for axis in GROUP)
    return jax.shard_map(
        functools.partial(local, sizes), mesh=mesh, in_specs=in_specs, out_specs=out_specs, check_vma=False
    )
```

```python
import functools

import jax
import jax.numpy as jnp
from jax import lax
from jax.experimental import pallas as pl
from jax.experimental.pallas import tpu as pltpu
from jax.sharding import PartitionSpec as P

F32 = jnp.float32
BF16 = jnp.bfloat16
LANES = 128


def call(body, outs, ins, name, flops, smem=(), hbm=(), scratch=(), out_hbm=()):
    moved = sum(4 * a.size for a in ins) + sum(4 * o.size for o in outs)
    ins = [pltpu.with_memory_space_constraint(a, pltpu.HBM) if i in hbm else a for i, a in enumerate(ins)]

    def space(number):
        return pltpu.SMEM if number in smem else pltpu.HBM if number in hbm else pltpu.VMEM

    return pl.pallas_call(
        body,
        out_shape=outs,
        in_specs=[pl.BlockSpec(memory_space=space(i)) for i in range(len(ins))],
        out_specs=[
            pl.BlockSpec(memory_space=pltpu.HBM if i in out_hbm else pltpu.VMEM) for i in range(len(outs))
        ],
        scratch_shapes=scratch,
        compiler_params=pltpu.CompilerParams(vmem_limit_bytes=40 << 20),
        cost_estimate=pl.CostEstimate(flops=flops, bytes_accessed=moved, transcendentals=0),
        name=name,
    )(*ins)


def shape(*dims, dtype=F32):
    return jax.ShapeDtypeStruct(dims, dtype)


def iota(dims, axis):
    return lax.broadcasted_iota(jnp.int32, dims, axis)


def halves(values):
    high = values.astype(BF16)
    return high, (values - high.astype(F32)).astype(BF16)


def tile_of(sizes):
    return lax.axis_index("facex") * sizes[1] + lax.axis_index("facey")


def is_even(axis):
    return lax.rem(lax.axis_index(axis), 2) == 0


def up(values):
    rows = values.shape[0]
    rolled = pltpu.roll(values, rows - 1, 0)
    return jnp.where(iota(values.shape, 0) == rows - 1, 0.0, rolled)


def right(values):
    rolled = pltpu.roll(values, 1, 1)
    return jnp.where(iota(values.shape, 1) == 0, 0.0, rolled)


def left(values):
    lanes = values.shape[1]
    rolled = pltpu.roll(values, lanes - 1, 1)
    return jnp.where(iota(values.shape, 1) == lanes - 1, 0.0, rolled)


def shares(west, south):
    east, north = up(west), left(south)
    middle = 1.0 + jnp.minimum(west, 0.0) - jnp.maximum(east, 0.0)
    middle = middle + jnp.minimum(south, 0.0) - jnp.maximum(north, 0.0)
    row, lane = iota(west.shape, 0), iota(west.shape, 1)
    return (
        middle,
        jnp.where(row == 0, 0.0, jnp.maximum(west, 0.0)),
        -jnp.minimum(east, 0.0),
        jnp.where(lane == 0, 0.0, jnp.maximum(south, 0.0)),
        -jnp.minimum(north, 0.0),
    )


def mix(parts, cells):
    rows, lanes = cells.shape
    middle, west, east, south, north = parts
    total = middle * cells + west * pltpu.roll(cells, 1, 0) + east * pltpu.roll(cells, rows - 1, 0)
    return total + south * pltpu.roll(cells, 1, 1) + north * pltpu.roll(cells, lanes - 1, 1)


def pack_kernel(sizes, plan, *refs):
    sources, refs = refs[:10], refs[10:]
    lanes_out, refs = refs[: plan["y_ops"]], refs[plan["y_ops"] :]
    own_out, refs = refs[0], refs[1:]
    block_outs, refs = refs[: len(plan["pairs"])], refs[len(plan["pairs"]) :]
    cell_out, live_out, tracer, west, south, scale, mixing, *refs = refs
    kernels, observed, weights, cells, counts, done = refs
    carried, levels, cx, cy = tracer.shape
    me = tile_of(sizes)
    copies = [
        pltpu.make_async_copy(source, target, done.at[number])
        for number, (source, target) in enumerate(
            zip(sources[1:], (west, south, scale, kernels, observed, weights, cells, counts, mixing))
        )
    ]
    copies += [
        pltpu.make_async_copy(sources[0].at[t], tracer.at[t], done.at[9 + t]) for t in range(carried)
    ]
    for number in (3, 4, 5, 6, 7, 1, 0, 8, *range(9, 9 + carried), 2):
        copies[number].start()

    def block(offset):
        where_to = jnp.bitwise_xor(me, offset)
        mine = kernels[where_to]
        last = jnp.concatenate(
            [
                observed[pl.ds(where_to, 1), :],
                weights[pl.ds(where_to, 1), :],
                jnp.zeros((6, mine.shape[1]), F32),
            ],
            axis=0,
        )
        return jnp.concatenate([mine[8 * g : 8 * g + 8] for g in range(levels // 8)] + [last], axis=1)

    for number in (3, 4, 5):
        copies[number].wait()
    for number, offset in enumerate(plan["y_blocks"]):
        at = plan["y_tiles"] * cx + 8 * number
        lanes_out[0][at : at + 8, :] = block(offset)
    for number, offset in enumerate(plan["own_blocks"]):
        own_out[8 * number : 8 * number + 8, :] = block(offset)
    first_core = lax.axis_index("lev") == 0
    for out, (for_first, for_second) in zip(block_outs, plan["pairs"]):
        out[...] = block(jnp.where(first_core, for_first, for_second))

    owners, cap = cells.shape
    slot = iota((1, cap), 1)
    copies[6].wait()
    copies[7].wait()
    cell_parts = []
    live_parts = []
    for offset in range(owners):
        owner = jnp.bitwise_xor(me, offset)
        cell_parts.append(cells[pl.ds(owner, 1), :])
        live_parts.append(jnp.where(slot < counts[owner], 1.0, 0.0))
    cell = jnp.concatenate(cell_parts, axis=1)
    live = jnp.concatenate(live_parts, axis=1)
    cell_out[...] = cell
    live_out[...] = live
    if plan["relay"]:
        at = plan["y_tiles"] * cx + 8 * len(plan["y_blocks"])
        strips = owners * cap // LANES
        for number in range(strips):
            part = slice(number * LANES, (number + 1) * LANES)
            lanes_out[0][at + number : at + number + 1, :] = cell[:, part].astype(F32)
            lanes_out[0][at + strips + number : at + strips + number + 1, :] = live[:, part]

    for number in (1, 0, 8):
        copies[number].wait()
    lane = iota((cx, cy), 1)
    if plan["relay"]:
        edge = edge_of(0, cy)
        inner = jnp.where(edge == 0, 1, cy - 2)
        tiles = {name: LanePacker(lane, at) for name, at in zip("cdvwuk", (edge, inner, edge, inner, edge, edge))}
        for level in range(levels):
            turned = pltpu.roll(south[level], level, 1) if level else south[level]
            tiles["v"].put(level, turned)
            tiles["w"].put(level, turned)
            tiles["u"].put(level, pltpu.roll(west[level], level, 1) if level else west[level])
            if level < levels - 1:
                tiles["k"].put(level, pltpu.roll(mixing[level], level, 1) if level else mixing[level])
        totals = None
        for t in range(carried):
            copies[9 + t].wait()
            totals = [tracer[t, level] + (totals[level] if t else 0.0) for level in range(levels)]
        for level in range(levels):
            turned = pltpu.roll(totals[level], level, 1) if level else totals[level]
            tiles["c"].put(level, turned)
            tiles["d"].put(level, turned)
        packed = jnp.zeros((cx, cy), F32)
        for name in "cdvwu":
            packed = packed + tiles[name].packed(plan["lane_" + name])
        lanes_out[0][0:cx, :] = packed
        lanes_out[0][cx : 2 * cx, :] = tiles["k"].packed(0)
    else:
        edges = [LanePacker(lane, edge_of(number, cy)) for number in range(len(lanes_out))]
        for t in range(carried):
            copies[9 + t].wait()
        for f in range(carried + 1):
            for level in range(levels):
                spot = f * levels + level
                values = tracer[f, level] if f < carried else south[level]
                for tile in edges:
                    tile.put(spot, pltpu.roll(values, spot, 1) if spot else values)
        for tile, out in zip(edges, lanes_out):
            out[0:cx, :] = tile.packed(0)
    copies[2].wait()


class LanePacker:
    def __init__(self, lane, edge):
        self.lanes = lane.shape[1]
        self.back = lax.rem(2 * self.lanes - edge, self.lanes)
        self.place = lax.rem(lane + self.back, self.lanes)
        self.tile = jnp.zeros(lane.shape, F32)

    def put(self, spot, turned):
        self.tile = jnp.where(self.place == spot, turned, self.tile)

    def packed(self, start):
        return pltpu.roll(self.tile, lax.rem(self.back + start, self.lanes), 1)


def edge_of(number, lanes):
    even_y = is_even("facey")
    return jnp.where(even_y if number == 0 else jnp.logical_not(even_y), lanes - 1, 0)


def rows_kernel(plan, tracer, west, scale, blocks, *outs):
    carried, levels, cx, cy = tracer.shape
    head = (carried + 1) * levels
    if plan["relay"]:
        tile = LanePacker(iota((cx, cy), 1), edge_of(0, cy))
        for t in range(carried):
            for level in range(levels):
                spot = t * levels + level
                tile.put(spot, pltpu.roll(tracer[t, level], spot, 1) if spot else tracer[t, level])
        outs[2][...] = tile.packed(0)
    for number, out in enumerate(outs[:2]):
        row = sent_row(plan, number, cx)
        for level in range(levels):
            for t in range(carried):
                spot = t * levels + level
                out[spot : spot + 1, :] = tracer[t, level, pl.ds(row, 1), :]
            spot = carried * levels + level
            out[spot : spot + 1, :] = west[level, pl.ds(row, 1), :]
        out[head : head + 8, :] = jnp.broadcast_to(scale[pl.ds(row, 1), :], (8, cy))
        if plan["x_blocks"][number] and not plan["relay"]:
            at = 8 * plan["own_blocks"].index(plan["x_blocks"][number])
            out[head + 8 : head + 16, :] = blocks[at : at + 8, :]


def relay_kernel(plan, head, cx, number, rows, blocks, y_got, out):
    out[0 : head + 8, :] = rows[0 : head + 8, :]
    row = sent_row(plan, number, cx)
    out[head + 1 : head + 2, :] = y_got[pl.ds(row, 1), :]
    near, far = plan["x_blocks"]
    even_x = is_even("facex")
    offset = jnp.where(even_x if number == 0 else jnp.logical_not(even_x), near, far)
    at = plan["y_tiles"] * cx + 8 * offset
    out[head + 8 : head + 24, :] = blocks[pl.ds(pl.multiple_of(8 * offset, 8), 16), :]
    out[head + 24 : head + 40, :] = y_got[pl.ds(pl.multiple_of(at, 8), 16), :]


def beyond_kernel(plan, cx, blocks, y_got, *outs):
    for out, offset in zip(outs, plan["x_ops"]):
        at = plan["y_tiles"] * cx + 8 * offset
        out[0:16, :] = blocks[8 * offset : 8 * offset + 16, :]
        out[16:32, :] = y_got[at : at + 16, :]


def rim_kernel(plan, carried, levels, cx, y_sent, y_got, base, base_other, lanes, *refs):
    inverse_out, ratio_out, lower_out, pieces_out, columns_out, rows_out, picks_out, live_out, base_out, square = refs
    cy = y_got.shape[1]
    slots = live_out.shape[1]

    def turned(values):
        square[...] = jnp.zeros((LANES, LANES), F32)
        square[0:cx, :] = values
        return jnp.transpose(square[...])

    def part(values, name):
        return values[plan["lane_" + name] : plan["lane_" + name] + levels]

    beyond = turned(y_got[0:cx, :])
    mine = turned(y_sent[0:cx, :])
    coupling = turned(y_got[cx : 2 * cx, :])
    north = is_even("facey")
    pieces_out[0] = part(beyond, "c")
    pieces_out[1] = part(beyond, "u")
    pieces_out[2] = part(beyond, "v")
    pieces_out[3] = jnp.where(north, part(beyond, "w"), part(mine, "v"))
    pieces_out[4] = jnp.where(north, part(mine, "c"), part(beyond, "d"))
    pieces_out[5] = jnp.where(north, part(beyond, "d"), part(mine, "c"))

    def level_of(ref, level):
        return jnp.broadcast_to(ref[level : level + 1, :], (8, LANES))

    square[...] = coupling
    first = []
    ratios = []
    before = None
    for level in range(levels):
        diagonal = jnp.ones((8, LANES), F32)
        if level > 0:
            below = level_of(square, level - 1)
            diagonal = diagonal + below
        if level < levels - 1:
            diagonal = diagonal + level_of(square, level)
        if level > 0:
            diagonal = diagonal - below * below * before
        inverse = 1.0 / diagonal
        ratios.append(level_of(square, level) * inverse if level < levels - 1 else jnp.zeros((8, LANES), F32))
        lower = below * inverse if level > 0 else jnp.zeros((8, LANES), F32)
        lower_out[level : level + 1, :] = lower[0:1]
        inverse_out[level : level + 1, :] = inverse[0:1]
        ratio_out[level : level + 1, :] = ratios[-1][0:1]
        first.append(inverse if level == 0 else lower * first[-1])
        before = inverse
    weight = first
    for level in range(levels - 2, -1, -1):
        weight[level] = first[level] + ratios[level] * weight[level + 1]
    for level in range(levels):
        square[level : level + 1, :] = weight[level][0:1]
    weights = square[0:levels, :]
    tile = LanePacker(iota((cx, cy), 1), edge_of(0, cy))
    for t in range(2 * carried):
        values = base[t] if t < carried else base_other[t - carried]
        tile.put(t, pltpu.roll(values, t, 1) if t else values)
    base_out[0:cx, :] = tile.packed(0)
    base_out[cx : 2 * cx, :] = lanes[...]
    at = plan["y_tiles"] * cx + 8 * len(plan["y_blocks"])
    strips = slots // LANES
    cell = jnp.concatenate([y_got[at + n : at + n + 1, :] for n in range(strips)], axis=1).astype(jnp.int32)
    live_out[...] = jnp.concatenate([y_got[at + strips + n : at + strips + n + 1, :] for n in range(strips)], axis=1)
    on_edge = lax.rem(cell, cy) == jnp.where(north, 0, cy - 1)
    x_of = jnp.where(on_edge, lax.div(cell, cy), LANES)
    picks = jnp.where(iota((LANES, slots), 0) == x_of, 1.0, 0.0)
    rows_out[...] = picks[0:cx]
    picks = picks.astype(BF16)
    picks_out[...] = picks
    high, low = halves(weights)
    columns_out[...] = jnp.dot(high, picks, preferred_element_type=F32) + jnp.dot(
        low, picks, preferred_element_type=F32
    )


def factor_kernel(sizes, *refs):
    (tracer, west, south, mixing, adjoint, cells) = refs[:6]
    inverse_out, lower_out, ratio_out, base_out, inner_out, shares_out, columns_out, rows_out, picks_out = refs[6:]
    carried, levels, cx, cy = tracer.shape
    slots = cells.shape[1]
    first = []
    before = None
    for level in range(levels):
        diagonal = jnp.ones((cx, cy), F32)
        if level > 0:
            diagonal = diagonal + mixing[level - 1]
        if level < levels - 1:
            diagonal = diagonal + mixing[level]
        if level > 0:
            diagonal = diagonal - mixing[level - 1] * mixing[level - 1] * before
        inverse = 1.0 / diagonal
        inverse_out[level] = inverse
        if level < levels - 1:
            ratio_out[level] = mixing[level] * inverse
        lower = mixing[level - 1] * inverse if level > 0 else jnp.zeros((cx, cy), F32)
        lower_out[level] = lower
        first.append(inverse if level == 0 else lower * first[-1])
        before = inverse
    ratio_out[levels - 1] = jnp.zeros((cx, cy), F32)
    weight = first
    for level in range(levels - 2, -1, -1):
        weight[level] = first[level] + ratio_out[level] * weight[level + 1]
    for t in range(carried):
        total = weight[0] * adjoint[t, 0]
        for level in range(1, levels):
            total = total + weight[level] * adjoint[t, level]
        base_out[t] = total
    for level in range(levels):
        total = tracer[0, level]
        for t in range(1, carried):
            total = total + tracer[t, level]
        parts = shares(west[level], south[level])
        for number, part in enumerate(parts):
            shares_out[number, level] = part
        inner_out[level] = mix(parts, total)
    cell = cells[...]
    x_of = lax.div(cell, cy)
    y_of = lax.rem(cell, cy)
    in_row = jnp.where(iota((cx, slots), 0) == x_of, 1.0, 0.0)
    in_lane = jnp.where(iota((cy, slots), 0) == y_of, 1.0, 0.0).astype(BF16)
    rows_out[...] = in_row
    picks_out[...] = in_lane
    high, low = halves(jnp.concatenate(weight, axis=0))
    picked = jnp.dot(high, in_lane, preferred_element_type=F32)
    picked = picked + jnp.dot(low, in_lane, preferred_element_type=F32)
    for level in range(levels):
        part = picked[level * cx : (level + 1) * cx] * in_row
        columns_out[level : level + 1, :] = jnp.sum(part, axis=0, keepdims=True)


def sides(plan, first, second):
    if plan["relay"]:
        return first, second
    even_x = is_even("facex")
    return jnp.where(even_x, second, first), jnp.where(even_x, first, second)


def own_sides(plan, first, second):
    return (second, first) if plan["relay"] else sides(plan, first, second)


def sent_row(plan, number, rows):
    if plan["relay"]:
        return rows - 1 if number == 0 else 0
    even_x = is_even("facex")
    return jnp.where(even_x if number == 0 else jnp.logical_not(even_x), rows - 1, 0)


def seam(number, sent, got, sent_face, got_face):
    even_y = is_even("facey")
    north = even_y if number == 0 else jnp.logical_not(even_y)
    to_north = -(jnp.maximum(got_face, 0.0) * sent + jnp.minimum(got_face, 0.0) * got)
    to_south = jnp.maximum(sent_face, 0.0) * got
    return jnp.where(north, to_north, to_south), jnp.where(north, sent.shape[1] - 1, 0)


def spread_wind(values, start, carried, levels):
    lane = iota(values.shape, 1)
    result = jnp.zeros_like(values)
    for t in range(carried):
        moved = pltpu.roll(values, (t * levels - start) % values.shape[1], 1)
        inside = jnp.logical_and(lane >= t * levels, lane < (t + 1) * levels)
        result = jnp.where(inside, moved, result)
    return result


def seam_lanes(number, plan, sent, got, sent_wind, got_wind, carried, levels):
    start = plan["lane_v"]
    faces = [spread_wind(wind, start, carried, levels) for wind in (sent_wind, got_wind)]
    return seam(number, sent, got, *faces)


def block_groups(blocks, cap):
    per_tile = LANES // cap
    group_of_lane = lax.div(iota((8, LANES), 1), cap)
    groups = []
    for group in range(per_tile):
        tiles = []
        for start in range(0, len(blocks), per_tile):
            tile = jnp.zeros((8, LANES), F32)
            for a in range(per_tile):
                moved = pltpu.roll(blocks[start + a], (cap * (a - group)) % LANES, 1)
                tile = jnp.where(group_of_lane == a, moved, tile)
            tiles.append(tile)
        groups.append(jnp.concatenate(tiles, axis=1))
    return groups


def relayed_blocks(plan, head, cx, own, y_got, got, x_got):
    start = plan["y_tiles"] * cx

    def block_at(ref, row):
        return ref[row : row + 8, :]

    blocks = {0: block_at(own, 0), 1: block_at(y_got, start + 8)}
    rim_blocks = {0: block_at(y_got, start), 1: block_at(own, 8)}
    even_x = is_even("facex")
    from_west, from_east = (got[n][head + 8 : head + 40, :] for n in range(2))
    carriers = [
        (plan["x_blocks"][0], jnp.where(even_x, from_east, from_west)),
        (plan["x_blocks"][1], jnp.where(even_x, from_west, from_east)),
    ]
    carriers += [(offset, ref[...]) for offset, ref in zip(plan["x_ops"], x_got)]
    for offset, values in carriers:
        blocks[offset], rim_blocks[offset + 1] = block_at(values, 0), block_at(values, 8)
        rim_blocks[offset], blocks[offset + 1] = block_at(values, 16), block_at(values, 24)
    return blocks, rim_blocks


def observe_kernel(sizes, plan, carried, *refs):
    refs = list(refs)
    got = refs[0:2]
    inner, lower, inverse, ratio, in_row, in_lane = refs[2:8]
    sent = refs[8:10]
    refs = refs[10:]
    y_sent = refs[: plan["y_ops"]]
    y_got = refs[plan["y_ops"] : 2 * plan["y_ops"]]
    refs = refs[2 * plan["y_ops"] :]
    if plan["relay"]:
        rim_inverse, rim_ratio, rim_lower, pieces, rim_picks, parcel, turn, rise = refs
    else:
        columns, live, own, *refs = refs
        n_pairs = len(plan["pairs"])
        pair_got = refs[:n_pairs]
        swapped = refs[n_pairs] if n_pairs else None
        modeled_out, state_out = refs[-2:]
    levels, cx, cy = inner.shape
    slots = in_row.shape[1]
    head = (carried + 1) * levels

    def summed(rows):
        total = rows[0:levels]
        for t in range(1, carried):
            total = total + rows[t * levels : (t + 1) * levels]
        return total

    beyond_west, beyond_east = sides(plan, got[0][0:head], got[1][0:head])
    at_west, at_east = own_sides(plan, sent[0][0:head], sent[1][0:head])
    spot = carried * levels
    face_west = at_west[spot:head]
    face_east = beyond_east[spot:head]
    from_west = jnp.maximum(face_west, 0.0) * summed(beyond_west)
    from_east = -(
        jnp.maximum(face_east, 0.0) * summed(at_east) + jnp.minimum(face_east, 0.0) * summed(beyond_east)
    )
    lane_parts = []
    for number in range(plan["y_ops"]):
        mine, beyond = y_sent[number][0:cx, :], y_got[number][0:cx, :]
        if plan["relay"]:
            faces = [pltpu.roll(values, cy - plan["lane_v"], 1) for values in (mine, beyond)]
            total, spot_y = seam(number, mine, beyond, *faces)
        else:
            part, spot_y = seam_lanes(number, plan, mine, beyond, mine, beyond, carried, levels)
            total = part
            for t in range(1, carried):
                total = total + pltpu.roll(part, (-t * levels) % cy, 1)
        lane_parts.append((pltpu.roll(total, spot_y, 1), spot_y))
    lane = iota((cx, cy), 1)
    row = iota((cx, cy), 0)
    forward = []
    for level in range(levels):
        value = inner[level]
        value = value + jnp.where(row == 0, from_west[level : level + 1], 0.0)
        value = value + jnp.where(row == cx - 1, from_east[level : level + 1], 0.0)
        for total, spot_y in lane_parts:
            moved = pltpu.roll(total, cy - level, 1) if level else total
            value = value + jnp.where(lane == spot_y, moved, 0.0)
        value = value * inverse[level]
        forward.append(value + lower[level] * forward[-1] if level else value)
    result = forward
    for level in range(levels - 2, -1, -1):
        result[level] = forward[level] + ratio[level] * result[level + 1]
    high, low = halves(jnp.concatenate(result, axis=0))
    picks = in_lane[...]
    picked = jnp.dot(high, picks, preferred_element_type=F32)
    picked = picked + jnp.dot(low, picks, preferred_element_type=F32)

    if not plan["relay"]:
        start = plan["y_tiles"] * cx
        blocks = {0: own[0:8, :], plan["y_blocks"][0]: y_got[0][start : start + 8, :]}
        for number in range(2):
            offset = plan["x_blocks"][number]
            if offset:
                blocks[offset] = got[number][head + 8 : head + 16, :]
        first_core = lax.axis_index("lev") == 0
        for number, (for_first, for_second) in enumerate(plan["pairs"]):
            mine = pair_got[number][...]
            other = swapped[8 * number : 8 * number + 8, :]
            if for_first == for_second:
                blocks[for_first] = mine
            else:
                blocks[for_first] = jnp.where(first_core, mine, other)
                blocks[for_second] = jnp.where(first_core, other, mine)
        *groups, last = block_groups(blocks, slots // len(blocks))
        total = jnp.zeros((cx, slots), F32)
        sensitivity = jnp.zeros((8, slots), F32)
        for g, kernel in enumerate(groups):
            sensitivity = sensitivity + kernel * columns[8 * g : 8 * g + 8, :]
            for l in range(8):
                level = 8 * g + l
                total = total + kernel[l : l + 1] * picked[level * cx : (level + 1) * cx]
        modeled_out[...] = jnp.sum(total * in_row[...], axis=0, keepdims=True)
        gain = jnp.sum(sensitivity, axis=0, keepdims=True) * last[1:2] * live[...]
        state_out[...] = jnp.concatenate([gain, last[0:1]], axis=0)
        return

    chosen = in_row[...]
    for level in range(levels):
        part = picked[level * cx : (level + 1) * cx] * chosen
        parcel[level : level + 1, :] = jnp.sum(part, axis=0, keepdims=True)

    corners_west, corners_east = sides(plan, got[0][head + 1 : head + 2, :], got[1][head + 1 : head + 2, :])
    turn[...] = jnp.zeros((LANES, LANES), F32)
    turn[0:1, :] = corners_west
    turn[cx - 1 : cx, :] = corners_east
    turned = jnp.transpose(turn[...])
    ends = turned[plan["lane_c"] : plan["lane_c"] + levels]
    end_face = turned[plan["lane_u"] : plan["lane_u"] + levels]
    place = iota((levels, LANES), 1)
    cells, face_w, face_s, face_n, south_cells, north_cells = (pieces[n] for n in range(6))
    west_cells = jnp.where(place == 0, ends, pltpu.roll(cells, 1, 1))
    east_cells = jnp.where(place == cx - 1, ends, pltpu.roll(cells, LANES - 1, 1))
    face_e = jnp.where(place == cx - 1, end_face, pltpu.roll(face_w, LANES - 1, 1))
    rise[0:levels, :] = advance_cells(
        cells, west_cells, east_cells, south_cells, north_cells, face_w, face_e, face_s, face_n
    )

    def level_of(ref, level):
        return jnp.broadcast_to(ref[level : level + 1, :], (8, LANES))

    climbed = []
    for level in range(levels):
        value = level_of(rise, level) * level_of(rim_inverse, level)
        climbed.append(value + level_of(rim_lower, level) * climbed[-1] if level else value)
    for level in range(levels - 2, -1, -1):
        climbed[level] = climbed[level] + level_of(rim_ratio, level) * climbed[level + 1]
    for level in range(levels):
        rise[level : level + 1, :] = climbed[level][0:1]
    high, low = halves(rise[0:levels, :])
    picks = rim_picks[...]
    picked = jnp.dot(high, picks, preferred_element_type=F32)
    picked = picked + jnp.dot(low, picks, preferred_element_type=F32)
    parcel[levels : 2 * levels, :] = picked


def advance_cells(cells, west, east, south, north, face_w, face_e, face_s, face_n):
    flux_w = jnp.maximum(face_w, 0.0) * west + jnp.minimum(face_w, 0.0) * cells
    flux_e = jnp.maximum(face_e, 0.0) * cells + jnp.minimum(face_e, 0.0) * east
    flux_s = jnp.maximum(face_s, 0.0) * south + jnp.minimum(face_s, 0.0) * cells
    flux_n = jnp.maximum(face_n, 0.0) * cells + jnp.minimum(face_n, 0.0) * north
    return cells + flux_w - flux_e + flux_s - flux_n


def scatter(force, in_row, in_lane):
    high, low = halves(in_row * force)
    dims = (((1,), (1,)), ((), ()))
    scattered = lax.dot_general(high, in_lane, dims, preferred_element_type=F32)
    return scattered + lax.dot_general(low, in_lane, dims, preferred_element_type=F32)


def force_kernel(plan, *refs):
    modeled, modeled_other, state, in_row, in_lane, base, base_other = refs[:7]
    near_out = refs[7]
    rim_outs = refs[8:]
    carried, cx, cy = base.shape
    misfit = modeled[...] + modeled_other[...] - state[1:2, :]
    force = state[0:1, :] * misfit
    scattered = scatter(force, in_row[...], in_lane[...])
    lane = iota((cx, cy), 1)
    even_y = is_even("facey")
    edges = []
    for number in range(len(rim_outs)):
        sends_last = even_y if number == 0 else jnp.logical_not(even_y)
        edges.append(jnp.where(sends_last, cy - 1, 0))
    rims = [jnp.zeros((cx, cy), F32) for _ in rim_outs]
    for t in range(2 * carried):
        values = scattered + (base[t] if t < carried else base_other[t - carried])
        near_out[t] = values
        for number, edge in enumerate(edges):
            moved = pltpu.roll(values, lax.rem(t + cy - edge, cy), 1)
            rims[number] = jnp.where(lane == t, moved, rims[number])
    for rim, out in zip(rims, rim_outs):
        out[...] = rim


def surface_kernel(sizes, plan, carried, levels, *refs):
    y_ops = plan["y_ops"]
    near = refs[0]
    rims = refs[6 + y_ops : 6 + 2 * y_ops]
    rim_values = [[rim[...] for rim in rims] for _ in range(near.shape[0])]
    values = [near[t] for t in range(near.shape[0])]
    spread_surface(
        sizes, plan, carried, levels, values, rim_values, refs[1:4], refs[4:6], refs[6 : 6 + y_ops], refs[6 + 2 * y_ops :]
    )


def weigh_kernel(sizes, plan, carried, levels, *refs):
    parcel, other, columns, live, rim_columns, rim_live, own, *refs = refs
    x_got, refs = refs[: len(plan["x_ops"])], refs[len(plan["x_ops"]) :]
    in_row, in_lane, base, base_other, rim_rows, rim_base = refs[:6]
    cx, cy = base.shape[1:]
    slots = live.shape[1]

    def force(blocks, start, weights, used):
        *groups, last = block_groups(blocks, slots // len(blocks))
        seen = jnp.zeros((8, slots), F32)
        sensitivity = jnp.zeros((8, slots), F32)
        for g, kernel in enumerate(groups):
            part = slice(start + 8 * g, start + 8 * g + 8)
            seen = seen + kernel * (parcel[part, :] + other[part, :])
            sensitivity = sensitivity + kernel * weights[8 * g : 8 * g + 8, :]
        modeled = jnp.sum(seen, axis=0, keepdims=True)
        gain = jnp.sum(sensitivity, axis=0, keepdims=True) * last[1:2] * used[...]
        return gain * (modeled - last[0:1])

    blocks, rim_blocks = relayed_blocks(plan, (carried + 1) * levels, cx, own, refs[11], refs[9:11], x_got)
    scattered = scatter(force(blocks, 0, columns, live), in_row[...], in_lane[...])
    on_rim = jnp.sum(rim_rows[...] * force(rim_blocks, levels, rim_columns, rim_live), axis=1, keepdims=True)
    near = [scattered + base[t] for t in range(carried)]
    near += [scattered + base_other[t] for t in range(carried)]
    rims = [[rim_base[0:cx, :] + on_rim] for _ in near]
    spread_surface(sizes, plan, carried, levels, near, rims, refs[6:9], refs[9:11], refs[11:12], refs[12:])


def spread_surface(sizes, plan, carried, levels, near, rim_values, fields, got, y_got, outs):
    west, south, scale = fields
    tracers = len(near)
    cx, cy = near[0].shape
    spot_v = plan["lane_v"]
    band = cy // sizes[0]
    per_tile = min(tracers, LANES // band)
    spot = carried * levels
    head = (carried + 1) * levels
    lane = iota((cx, cy), 1)
    row = iota((cx, cy), 0)
    even_y = is_even("facey")
    face_west = west[...]
    face_south = south[...]
    scales = scale[...]
    beyond_west, beyond_east = sides(plan, got[0][head : head + 1], got[1][head : head + 1])
    _, east_wind = sides(plan, got[0][spot : spot + 1], got[1][spot : spot + 1])
    face_east = jnp.where(row == cx - 1, east_wind, pltpu.roll(face_west, cx - 1, 0))
    face_north = left(face_south)
    norths = []
    for number in range(plan["y_ops"]):
        norths.append(even_y if number == 0 else jnp.logical_not(even_y))
        moved = pltpu.roll(y_got[number][0:cx, :], cy - 1 - spot_v, 1)
        keep = jnp.logical_and(lane == cy - 1, norths[number])
        face_north = jnp.where(keep, moved, face_north)
    to_middle = 1.0 + jnp.minimum(face_west, 0.0) - jnp.maximum(face_east, 0.0)
    to_middle = scales * (to_middle + jnp.minimum(face_south, 0.0) - jnp.maximum(face_north, 0.0))
    to_east = jnp.where(row == cx - 1, 0.0, scales * jnp.maximum(face_east, 0.0))
    to_west = jnp.where(row == 0, 0.0, scales * jnp.minimum(face_west, 0.0))
    to_north = scales * jnp.maximum(face_north, 0.0)
    to_south = scales * jnp.minimum(face_south, 0.0)
    west_gain = beyond_west * jnp.maximum(face_west[0:1], 0.0)
    east_gain = -beyond_east * jnp.minimum(face_east[cx - 1 : cx], 0.0)
    filler = jnp.zeros((6, cy), F32)
    grown = []
    for t in range(tracers):
        values = near[t]
        north_side = left(values)
        south_side = right(values)
        for number in range(plan["y_ops"]):
            rim = rim_values[t][number]
            at_north = jnp.logical_and(lane == cy - 1, norths[number])
            at_south = jnp.logical_and(lane == 0, jnp.logical_not(norths[number]))
            north_side = jnp.where(at_north, pltpu.roll(rim, (cy - 1 - t) % cy, 1), north_side)
            south_side = jnp.where(at_south, pltpu.roll(rim, (-t) % cy, 1), south_side)
        swept = to_middle * values + to_east * pltpu.roll(values, cx - 1, 0) - to_west * pltpu.roll(values, 1, 0)
        swept = swept + to_north * north_side - to_south * south_side
        grown.append(
            jnp.concatenate(
                [swept, west_gain * values[0:1], east_gain * values[cx - 1 : cx], filler], axis=0
            )
        )
    rows = cx + 8
    group_of_lane = lax.div(iota((rows, cy), 1), band)
    first_core = lax.axis_index("lev") == 0
    place = lax.axis_index("facex")
    for out, (for_first, for_second) in zip(outs, plan["bands"]):
        offset = for_first if for_first == for_second else jnp.where(first_core, for_first, for_second)
        target = jnp.bitwise_xor(place, offset)
        count = carried if for_first == for_second else tracers
        skip = carried if for_first == for_second != 0 and plan["cross"] else 0
        for start in range(0, count, per_tile):
            tile = jnp.zeros((rows, cy), F32)
            for a in range(min(per_tile, count - start)):
                moved = pltpu.roll(grown[skip + start + a], lax.rem(band * a + cy - band * target, cy), 1)
                tile = jnp.where(group_of_lane == a, moved, tile)
            out[start // per_tile * rows : (start // per_tile + 1) * rows, :] = tile


def regrid_kernel(sizes, plan, bands, carried, cx, band, *refs):
    index, weight = refs[:2]
    blocks, more, out = refs[2 : 2 + len(bands)], refs[2 + len(bands) : -1], refs[-1]
    taps, cells = index.shape
    rows = cx + 8
    per_tile = min(2 * carried, LANES // band)
    lane = iota((rows, LANES), 1)
    row = iota((rows, cells), 0)
    first_core = lax.axis_index("lev") == 0
    place = lax.axis_index("facex")
    around = sizes[0] * cx
    parts = []
    row_places = []
    for block, ((for_first, for_second), fetched, first) in zip(blocks, bands):
        if plan["cross"] != fetched:
            for_first, for_second = for_second, for_first
        offset = for_first if for_first == for_second else jnp.where(first_core, for_first, for_second)
        start = jnp.bitwise_xor(place, offset) * cx
        places = start + row
        places = jnp.where(row == cx, lax.rem(start + around - 1, around), places)
        places = jnp.where(row == cx + 1, lax.rem(start + cx, around), places)
        row_places.append(places)
        for t in range(first, first + carried):
            tile = block[t // per_tile * rows : (t // per_tile + 1) * rows, :]
            a = t % per_tile
            values = tile if a == 0 else pltpu.roll(tile, (-band * a) % LANES, 1)
            high = values.astype(BF16).astype(F32)
            low = pltpu.roll(values - high, band, 1)
            both = jnp.where(lane < band, high, jnp.where(lane < 2 * band, low, 0.0))
            parts.append(both.astype(BF16))
    left_side = jnp.concatenate(parts, axis=0)
    spread = iota((LANES, cells), 0)
    in_band = lax.rem(spread, band)
    used = spread < 2 * band
    totals = [jnp.zeros((rows, cells), F32) for _ in range(carried)]
    for tap in range(taps):
        place_of = index[tap : tap + 1, :]
        column = lax.div(place_of, band)
        in_lane = lax.rem(place_of, band)
        picks = jnp.where(jnp.logical_and(in_band == in_lane, used), 1.0, 0.0).astype(BF16)
        picked = jnp.dot(left_side, picks, preferred_element_type=F32)
        at = 0
        for places in row_places:
            chosen = jnp.where(places == column, weight[tap : tap + 1, :], 0.0)
            for t in range(carried):
                totals[t] = totals[t] + chosen * picked[at : at + rows]
                at += rows
    sums = jnp.concatenate([jnp.sum(total, axis=0, keepdims=True) for total in totals], axis=0)
    for ref in more:
        sums = sums + ref[...]
    out[...] = sums


def advance_kernel(plan, *refs):
    tracer, parts, lower, inverse, ratio = refs[:5]
    sent = refs[5:7]
    got = refs[7:9]
    y_ops = plan["y_ops"]
    y_sent, y_got, winds_sent, winds_got = (refs[9 + n * y_ops : 9 + (n + 1) * y_ops] for n in range(4))
    target, out, west_rows, east_rows, done = refs[-5:]
    carried, levels, cx, cy = tracer.shape
    head = (carried + 1) * levels
    spot = carried * levels
    beyond_west, beyond_east = sides(plan, got[0][0:head], got[1][0:head])
    at_west, at_east = own_sides(plan, sent[0][0:head], sent[1][0:head])
    face_west = at_west[spot:head]
    face_east = beyond_east[spot:head]
    for t in range(carried):
        part = slice(t * levels, (t + 1) * levels)
        west_rows[part, :] = jnp.maximum(face_west, 0.0) * beyond_west[part]
        east_rows[part, :] = -(
            jnp.maximum(face_east, 0.0) * at_east[part] + jnp.minimum(face_east, 0.0) * beyond_east[part]
        )
    lane = iota((cx, cy), 1)
    row = iota((cx, cy), 0)
    seams = [
        seam_lanes(
            n,
            plan,
            y_sent[n][0:cx, :],
            y_got[n][-cx:, :] if plan["relay"] else y_got[n][0:cx, :],
            winds_sent[n][0:cx, :],
            winds_got[n][0:cx, :],
            carried,
            levels,
        )
        for n in range(y_ops)
    ]
    stride = 4

    def forward(step, before):
        mixed = []
        for k in range(stride):
            level = step * stride + k
            weights = [parts[n, level] for n in range(5)]
            mixed.append([])
            for t in range(carried):
                value = mix(weights, tracer[t, level])
                value = value + jnp.where(row == 0, west_rows[pl.ds(t * levels + level, 1), :], 0.0)
                value = value + jnp.where(row == cx - 1, east_rows[pl.ds(t * levels + level, 1), :], 0.0)
                for packed, spot_y in seams:
                    moved = pltpu.roll(packed, lax.rem(spot_y - (t * levels + level) + 2 * cy, cy), 1)
                    value = value + jnp.where(lane == spot_y, moved, 0.0)
                mixed[k].append(value)
        for k in range(stride):
            level = step * stride + k
            from_below = lower[level]
            scaled = inverse[level]
            after = []
            for t in range(carried):
                value = mixed[k][t] * scaled + from_below * before[t]
                out[t, level] = value
                after.append(value)
            before = after
        return tuple(before)

    def copy(step):
        part = pl.ds(levels - (step + 1) * stride, stride)
        return pltpu.make_async_copy(out.at[:, part], target.at[:, part], done.at[step])

    start = tuple(jnp.zeros((cx, cy), F32) for _ in range(carried))
    lax.fori_loop(0, levels // stride, forward, start)
    above = list(start)
    for step in range(levels // stride):
        for k in range(stride):
            level = levels - 1 - step * stride - k
            factor = ratio[level]
            for t in range(carried):
                above[t] = out[t, level] + factor * above[t]
                out[t, level] = above[t]
        copy(step).start()
    for step in range(levels // stride):
        copy(step).wait()


GROUP = ("facex", "facey", "lev")


def exchange(values, sizes, rule):
    many_x, many_y, cores = sizes
    pairs = []
    for x in range(many_x):
        for y in range(many_y):
            for c in range(cores):
                to = rule(x, y, c)
                if to is not None:
                    pairs.append(((x * many_y + y) * cores + c, (to[0] * many_y + to[1]) * cores + to[2]))
    return lax.ppermute(values, GROUP, pairs)


def make_plan(sizes):
    many_x, many_y, _ = sizes
    tiles = many_x * many_y
    x_blocks = [many_y, (many_x - 1) * many_y if many_x == 4 else 0]
    relay = many_y == 2 and many_x == 4
    if relay:
        own_blocks = list(range(tiles))
        y_blocks = own_blocks
        x_ops = [offset for offset in own_blocks[2::2] if offset not in x_blocks]
        pairs = []
    else:
        own_blocks = [0] + [offset for offset in x_blocks if offset]
        y_blocks = [1]
        x_ops = []
        rest = [d for d in range(tiles) if d not in {1, *own_blocks}]
        rest.sort(key=lambda d: (d // many_y != many_x // 2, d))
        pairs = [(rest[n], rest[min(n + 1, len(rest) - 1)]) for n in range(0, len(rest), 2)]
    others = list(range(many_x - 1, 1, -1))
    bands = [(0, 0), (1, 1)] + [(others[n], others[n + 1]) for n in range(0, len(others), 2)]
    return {
        "relay": relay,
        "cross": 1 if relay else 0,
        "x_blocks": x_blocks,
        "x_ops": x_ops,
        "own_blocks": own_blocks,
        "y_blocks": y_blocks,
        "y_ops": 1 if many_y == 2 else 2,
        "y_tiles": 2 if relay else 1,
        "pairs": pairs,
        "bands": bands,
    }


def lane_plan(plan, carried, levels):
    starts = {"c": 0, "d": levels, "v": 2 * levels, "w": 3 * levels, "u": 4 * levels}
    if not plan["relay"]:
        starts = {"v": carried * levels}
    return {"lane_" + name: start for name, start in starts.items()}


def local(
    sizes,
    tracer,
    west_courant,
    south_courant,
    mixing,
    adjoint_later,
    emission_scale,
    send_cells,
    send_counts,
    kernels,
    observed,
    error_weight,
    regrid_index,
    regrid_weight,
):
    plan = make_plan(sizes)
    many_x, many_y, _ = sizes
    carried, levels, cx, cy = tracer.shape
    owners, cap = send_cells.shape[2:]
    slots = owners * cap
    taps, ll = regrid_index.shape[2:]
    plan.update(lane_plan(plan, carried, levels))
    head = (carried + 1) * levels
    y_ops = plan["y_ops"]
    band = cy // many_x

    def next_x(number):
        def rule(x, y, c):
            step = 1 if (plan["relay"] or x % 2 == 0) == (number == 0) else -1
            return ((x + step) % many_x, y, c)

        return rule

    def next_y(number, cross):
        def rule(x, y, c):
            to = y + (1 if (y % 2 == 0) == (number == 0) else -1)
            return (x, to, c ^ cross) if 0 <= to < many_y else None

        return rule

    def jump(for_first, for_second, cross=0):
        def rule(x, y, c):
            d = for_first if c == 0 else for_second
            return (x ^ (d // many_y), y ^ (d % many_y), c ^ cross)

        return rule

    def other_core(values):
        return exchange(values, sizes, lambda x, y, c: (x, y, 1 - c))

    strips = slots // LANES
    plan["parcel"] = -(-2 * strips // 8) * 8
    extra = 40 if plan["relay"] else 16
    row_shapes = [shape(head + extra, cy)] * 2
    y_rows = plan["y_tiles"] * cx + 8 * len(plan["y_blocks"]) + (plan["parcel"] if plan["relay"] else 0)
    lane_shapes = [shape(y_rows if n == 0 else cx, cy) for n in range(y_ops)]
    packed = call(
        functools.partial(pack_kernel, sizes, plan),
        lane_shapes
        + [shape(8 * len(plan["own_blocks"]), LANES)]
        + [shape(8, LANES)] * len(plan["pairs"])
        + [shape(1, slots, dtype=jnp.int32), shape(1, slots)]
        + [shape(*a.shape) for a in (tracer, west_courant, south_courant, emission_scale, mixing)],
        [
            tracer,
            west_courant,
            south_courant,
            emission_scale,
            kernels.reshape(owners, levels, cap),
            observed.reshape(owners, cap),
            error_weight.reshape(owners, cap),
            send_cells.reshape(owners, cap),
            send_counts.reshape(owners),
            mixing,
        ],
        "pack",
        100000,
        hbm=range(10),
        scratch=[
            pltpu.VMEM((owners, levels, cap), F32),
            pltpu.VMEM((owners, cap), F32),
            pltpu.VMEM((owners, cap), F32),
            pltpu.VMEM((owners, cap), jnp.int32),
            pltpu.SMEM((owners,), jnp.int32),
            pltpu.SemaphoreType.DMA((9 + carried,)),
        ],
    )
    lanes_sent = packed[:y_ops]
    own_blocks = packed[y_ops]
    pair_sent = packed[1 + y_ops : -7]
    cell, live, tracer, west_courant, south_courant, emission_scale, mixing = packed[-7:]
    lanes_got = [exchange(lanes_sent[n], sizes, next_y(n, plan["cross"])) for n in range(y_ops)]
    held, *_ = lax.optimization_barrier((tracer, *lanes_sent))
    inverse, lower, ratio, base, inner, parts, columns, in_row, in_lane = call(
        functools.partial(factor_kernel, sizes),
        [
            shape(levels, cx, cy),
            shape(levels, cx, cy),
            shape(levels, cx, cy),
            shape(carried, cx, cy),
            shape(levels, cx, cy),
            shape(5, levels, cx, cy),
            shape(levels, slots),
            shape(cx, slots),
            shape(cy, slots, dtype=BF16),
        ],
        [held, west_courant, south_courant, mixing, adjoint_later, cell],
        "factor",
        3000000,
    )
    rows_sent = list(
        call(
            functools.partial(rows_kernel, plan),
            row_shapes + ([shape(cx, cy)] if plan["relay"] else []),
            [tracer, west_courant, emission_scale, own_blocks],
            "rows",
            100000,
        )
    )
    per_tile = min(2 * carried, LANES // band)

    def band_shape(first, second):
        count = carried if first == second else 2 * carried
        return shape(-(-count // per_tile) * (cx + 8), cy)

    band_shapes = [band_shape(*b) for b in plan["bands"]]
    fields = [west_courant[0], south_courant[0], emission_scale]
    observe = functools.partial(
        call, functools.partial(observe_kernel, sizes, plan, carried), name="observe", flops=2000000
    )
    if plan["relay"]:
        base, *lanes_got = lax.optimization_barrier((base, *lanes_got))
        lanes_each = rows_sent.pop()
        base_other = other_core(base)

        def relay(number, *after):
            held, *_ = lax.optimization_barrier((rows_sent[number], *after))
            return call(
                functools.partial(relay_kernel, plan, head, cx, number),
                [row_shapes[number]],
                [held, own_blocks, lanes_got[0]],
                "relay",
                10000,
            )[0]

        rows_sent = [relay(0), relay(1)]
        x_sent = call(
            functools.partial(beyond_kernel, plan, cx),
            [shape(32, LANES)] * len(plan["x_ops"]),
            [own_blocks, lanes_got[0]],
            "beyond",
            10000,
        )
        x_got = [exchange(s, sizes, jump(d, d, 1)) for s, d in zip(x_sent, plan["x_ops"])]
        rows_got = [exchange(rows_sent[n], sizes, next_x(n)) for n in range(2)]
        held_y, *_ = lax.optimization_barrier((lanes_got[0], *rows_sent))
        rim = call(
            functools.partial(rim_kernel, plan, carried, levels, cx),
            [
                shape(levels, LANES),
                shape(levels, LANES),
                shape(levels, LANES),
                shape(6, levels, LANES),
                shape(levels, slots),
                shape(cx, slots),
                shape(LANES, slots, dtype=BF16),
                shape(1, slots),
                shape(2 * cx, cy),
            ],
            [lanes_sent[0], held_y, base, base_other, lanes_each],
            "rim",
            400000,
            scratch=[pltpu.VMEM((LANES, LANES), F32)],
        )
        *rim, rim_sent = rim
        rim_got = exchange(rim_sent, sizes, next_y(0, 0))
        (parcel,) = observe(
            [shape(2 * levels, slots)],
            [*rows_got, inner, lower, inverse, ratio, in_row, in_lane, *rows_sent, *lanes_sent, *lanes_got]
            + [*rim[:4], rim[6]],
            scratch=[pltpu.VMEM((LANES, LANES), F32), pltpu.VMEM((levels, LANES), F32)],
        )
        parcel_other = other_core(parcel)
        parcel_other, rim_got, *x_got = lax.optimization_barrier((parcel_other, rim_got, *x_got))
        band_sent = call(
            functools.partial(weigh_kernel, sizes, plan, carried, levels),
            band_shapes,
            [parcel, parcel_other, columns, live, rim[4], rim[7], own_blocks, *x_got, in_row, in_lane]
            + [base, base_other, rim[5], rim_got, *fields, *rows_got, *lanes_got],
            "weigh",
            500000,
        )
        lanes_own = [lanes_each, rim_got]
        held, *_ = lax.optimization_barrier((tracer, *band_sent))
    else:
        rows_got = [exchange(rows_sent[n], sizes, next_x(n)) for n in range(2)]
        pair_got = [exchange(s, sizes, jump(*p)) for s, p in zip(pair_sent, plan["pairs"])]
        base_other = other_core(base)
        modeled, state = observe(
            [shape(1, slots), shape(2, slots)],
            [*rows_got, inner, lower, inverse, ratio, in_row, in_lane, *rows_sent, *lanes_sent, *lanes_got]
            + [columns, live, own_blocks, *pair_got]
            + [other_core(jnp.concatenate(pair_got, axis=0))],
        )
        near, *rims_sent = call(
            functools.partial(force_kernel, plan),
            [shape(2 * carried, cx, cy)] + [shape(cx, cy)] * y_ops,
            [modeled, other_core(modeled), state, in_row, in_lane, base, base_other],
            "force",
            200000,
        )
        rims_got = [exchange(rims_sent[n], sizes, next_y(n, 0)) for n in range(y_ops)]
        band_sent = call(
            functools.partial(surface_kernel, sizes, plan, carried, levels),
            band_shapes,
            [near, *fields, *rows_got, *lanes_got, *rims_got],
            "surface",
            400000,
        )
        lanes_own = [*lanes_sent, *lanes_got]
        held = tracer
    (advanced,) = call(
        functools.partial(advance_kernel, plan),
        [shape(*tracer.shape)],
        [held, parts, lower, inverse, ratio]
        + list(rows_sent)
        + rows_got
        + lanes_own
        + list(lanes_sent)
        + lanes_got,
        "advance",
        6000000,
        scratch=[pltpu.VMEM(tracer.shape, F32)]
        + [pltpu.VMEM((carried * levels, cy), F32)] * 2
        + [pltpu.SemaphoreType.DMA((levels // 4,))],
        out_hbm=(0,),
    )
    band_got = [
        s
        if first == second == 0
        else exchange(s, sizes, jump(first * many_y, second * many_y, plan["cross"]))
        for s, (first, second) in zip(band_sent, plan["bands"])
    ]
    tables = [regrid_index.reshape(taps, ll), regrid_weight.reshape(taps, ll)]
    kinds = [first == second for first, second in plan["bands"]]

    def regridded(bands, blocks, *more):
        return call(
            functools.partial(regrid_kernel, sizes, plan, bands, carried, cx, band),
            [shape(carried, ll)],
            [*tables, *blocks, *more],
            "regrid",
            1000000,
        )[0]

    near = [(pair, 0, 0) for pair, kind in zip(plan["bands"], kinds) if kind]
    far = [pair for pair, kind in zip(plan["bands"], kinds) if not kind]
    near_got = [got for got, kind in zip(band_got, kinds) if kind]
    far_got = [got for got, kind in zip(band_got, kinds) if not kind]
    advanced, near_got, far_got = lax.optimization_barrier((advanced, near_got, far_got))
    far_fetched = [other_core(got) for got in far_got]
    mine = carried if plan["cross"] else 0
    partial = regridded(near + [(pair, 0, mine) for pair in far], near_got + far_got)
    latlon = regridded([(pair, 1, carried - mine) for pair in far], far_fetched, partial)
    return (advanced, latlon[:, None, None, :])


def solution(mesh):
    in_specs = (
        P("lev", "groups", "facex", "facey"),
        P("groups", "facex", "facey"),
        P("groups", "facex", "facey"),
        P("groups", "facex", "facey"),
        P("lev", "groups", "facex", "facey"),
        P("facex", "facey"),
        P("facex", "facey", "groups", None),
        P("facex", "facey", "groups"),
        P("facex", "facey", "groups", None, None),
        P("facex", "facey", "groups", None),
        P("facex", "facey", "groups", None),
        P("facex", "facey", None, None),
        P("facex", "facey", None, None),
    )
    out_specs = (P("lev", "groups", "facex", "facey"), P("lev", "facex", "facey", "groups"))
    sizes = tuple(mesh.shape[axis] for axis in GROUP)
    return jax.shard_map(
        functools.partial(local, sizes), mesh=mesh, in_specs=in_specs, out_specs=out_specs, check_vma=False
    )
```

```python
import functools

import jax
import jax.numpy as jnp
from jax import lax
from jax.experimental import pallas as pl
from jax.experimental.pallas import tpu as pltpu
from jax.sharding import PartitionSpec as P

F32 = jnp.float32
BF16 = jnp.bfloat16
LANES = 128


def call(body, outs, ins, name, flops, smem=(), hbm=(), scratch=(), out_hbm=()):
    moved = sum(4 * a.size for a in ins) + sum(4 * o.size for o in outs)
    ins = [pltpu.with_memory_space_constraint(a, pltpu.HBM) if i in hbm else a for i, a in enumerate(ins)]

    def space(number):
        return pltpu.SMEM if number in smem else pltpu.HBM if number in hbm else pltpu.VMEM

    return pl.pallas_call(
        body,
        out_shape=outs,
        in_specs=[pl.BlockSpec(memory_space=space(i)) for i in range(len(ins))],
        out_specs=[
            pl.BlockSpec(memory_space=pltpu.HBM if i in out_hbm else pltpu.VMEM) for i in range(len(outs))
        ],
        scratch_shapes=scratch,
        compiler_params=pltpu.CompilerParams(vmem_limit_bytes=40 << 20),
        cost_estimate=pl.CostEstimate(flops=flops, bytes_accessed=moved, transcendentals=0),
        name=name,
    )(*ins)


def shape(*dims, dtype=F32):
    return jax.ShapeDtypeStruct(dims, dtype)


def iota(dims, axis):
    return lax.broadcasted_iota(jnp.int32, dims, axis)


def halves(values):
    high = values.astype(BF16)
    return high, (values - high.astype(F32)).astype(BF16)


def tile_of(sizes):
    return lax.axis_index("facex") * sizes[1] + lax.axis_index("facey")


def is_even(axis):
    return lax.rem(lax.axis_index(axis), 2) == 0


def up(values):
    rows = values.shape[0]
    rolled = pltpu.roll(values, rows - 1, 0)
    return jnp.where(iota(values.shape, 0) == rows - 1, 0.0, rolled)


def right(values):
    rolled = pltpu.roll(values, 1, 1)
    return jnp.where(iota(values.shape, 1) == 0, 0.0, rolled)


def left(values):
    lanes = values.shape[1]
    rolled = pltpu.roll(values, lanes - 1, 1)
    return jnp.where(iota(values.shape, 1) == lanes - 1, 0.0, rolled)


def shares(west, south):
    east, north = up(west), left(south)
    middle = 1.0 + jnp.minimum(west, 0.0) - jnp.maximum(east, 0.0)
    middle = middle + jnp.minimum(south, 0.0) - jnp.maximum(north, 0.0)
    row, lane = iota(west.shape, 0), iota(west.shape, 1)
    return (
        middle,
        jnp.where(row == 0, 0.0, jnp.maximum(west, 0.0)),
        -jnp.minimum(east, 0.0),
        jnp.where(lane == 0, 0.0, jnp.maximum(south, 0.0)),
        -jnp.minimum(north, 0.0),
    )


def mix(parts, cells):
    rows, lanes = cells.shape
    middle, west, east, south, north = parts
    total = middle * cells + west * pltpu.roll(cells, 1, 0) + east * pltpu.roll(cells, rows - 1, 0)
    return total + south * pltpu.roll(cells, 1, 1) + north * pltpu.roll(cells, lanes - 1, 1)


def pack_kernel(sizes, plan, *refs):
    sources, refs = refs[:10], refs[10:]
    lanes_out, refs = refs[: plan["y_ops"]], refs[plan["y_ops"] :]
    own_out, refs = refs[0], refs[1:]
    block_outs, refs = refs[: len(plan["pairs"])], refs[len(plan["pairs"]) :]
    cell_out, live_out, tracer, west, south, scale, mixing, *refs = refs
    kernels, observed, weights, cells, counts, done = refs
    carried, levels, cx, cy = tracer.shape
    me = tile_of(sizes)
    copies = [
        pltpu.make_async_copy(source, target, done.at[number])
        for number, (source, target) in enumerate(
            zip(sources[1:], (west, south, scale, kernels, observed, weights, cells, counts, mixing))
        )
    ]
    copies += [
        pltpu.make_async_copy(sources[0].at[t], tracer.at[t], done.at[9 + t]) for t in range(carried)
    ]
    for number in (3, 4, 5, 6, 7, 1, 0, 8, *range(9, 9 + carried), 2):
        copies[number].start()

    def block(offset):
        where_to = jnp.bitwise_xor(me, offset)
        mine = kernels[where_to]
        last = jnp.concatenate(
            [
                observed[pl.ds(where_to, 1), :],
                weights[pl.ds(where_to, 1), :],
                jnp.zeros((6, mine.shape[1]), F32),
            ],
            axis=0,
        )
        return jnp.concatenate([mine[8 * g : 8 * g + 8] for g in range(levels // 8)] + [last], axis=1)

    for number in (3, 4, 5):
        copies[number].wait()
    for number, offset in enumerate(plan["y_blocks"]):
        at = plan["y_tiles"] * cx + 8 * number
        lanes_out[0][at : at + 8, :] = block(offset)
    for number, offset in enumerate(plan["own_blocks"]):
        own_out[8 * number : 8 * number + 8, :] = block(offset)
    first_core = lax.axis_index("lev") == 0
    for out, (for_first, for_second) in zip(block_outs, plan["pairs"]):
        out[...] = block(jnp.where(first_core, for_first, for_second))

    owners, cap = cells.shape
    slot = iota((1, cap), 1)
    copies[6].wait()
    copies[7].wait()
    cell_parts = []
    live_parts = []
    for offset in range(owners):
        owner = jnp.bitwise_xor(me, offset)
        cell_parts.append(cells[pl.ds(owner, 1), :])
        live_parts.append(jnp.where(slot < counts[owner], 1.0, 0.0))
    cell = jnp.concatenate(cell_parts, axis=1)
    live = jnp.concatenate(live_parts, axis=1)
    cell_out[...] = cell
    live_out[...] = live
    if plan["relay"]:
        at = plan["y_tiles"] * cx + 8 * len(plan["y_blocks"])
        strips = owners * cap // LANES
        for number in range(strips):
            part = slice(number * LANES, (number + 1) * LANES)
            lanes_out[0][at + number : at + number + 1, :] = cell[:, part].astype(F32)
            lanes_out[0][at + strips + number : at + strips + number + 1, :] = live[:, part]

    for number in (1, 0, 8):
        copies[number].wait()
    lane = iota((cx, cy), 1)
    if plan["relay"]:
        edge = edge_of(0, cy)
        inner = jnp.where(edge == 0, 1, cy - 2)
        tiles = {name: LanePacker(lane, at) for name, at in zip("cdvwuk", (edge, inner, edge, inner, edge, edge))}
        for level in range(levels):
            turned = pltpu.roll(south[level], level, 1) if level else south[level]
            tiles["v"].put(level, turned)
            tiles["w"].put(level, turned)
            tiles["u"].put(level, pltpu.roll(west[level], level, 1) if level else west[level])
            if level < levels - 1:
                tiles["k"].put(level, pltpu.roll(mixing[level], level, 1) if level else mixing[level])
        totals = None
        for t in range(carried):
            copies[9 + t].wait()
            totals = [tracer[t, level] + (totals[level] if t else 0.0) for level in range(levels)]
        for level in range(levels):
            turned = pltpu.roll(totals[level], level, 1) if level else totals[level]
            tiles["c"].put(level, turned)
            tiles["d"].put(level, turned)
        packed = jnp.zeros((cx, cy), F32)
        for name in "cdvwu":
            packed = packed + tiles[name].packed(plan["lane_" + name])
        lanes_out[0][0:cx, :] = packed
        lanes_out[0][cx : 2 * cx, :] = tiles["k"].packed(0)
    else:
        edges = [LanePacker(lane, edge_of(number, cy)) for number in range(len(lanes_out))]
        for t in range(carried):
            copies[9 + t].wait()
        for f in range(carried + 1):
            for level in range(levels):
                spot = f * levels + level
                values = tracer[f, level] if f < carried else south[level]
                for tile in edges:
                    tile.put(spot, pltpu.roll(values, spot, 1) if spot else values)
        for tile, out in zip(edges, lanes_out):
            out[0:cx, :] = tile.packed(0)
    copies[2].wait()


class LanePacker:
    def __init__(self, lane, edge):
        self.lanes = lane.shape[1]
        self.back = lax.rem(2 * self.lanes - edge, self.lanes)
        self.place = lax.rem(lane + self.back, self.lanes)
        self.tile = jnp.zeros(lane.shape, F32)

    def put(self, spot, turned):
        self.tile = jnp.where(self.place == spot, turned, self.tile)

    def packed(self, start):
        return pltpu.roll(self.tile, lax.rem(self.back + start, self.lanes), 1)


def edge_of(number, lanes):
    even_y = is_even("facey")
    return jnp.where(even_y if number == 0 else jnp.logical_not(even_y), lanes - 1, 0)


def rows_kernel(plan, tracer, west, scale, blocks, *outs):
    carried, levels, cx, cy = tracer.shape
    head = (carried + 1) * levels
    if plan["relay"]:
        tile = LanePacker(iota((cx, cy), 1), edge_of(0, cy))
        for t in range(carried):
            for level in range(levels):
                spot = t * levels + level
                tile.put(spot, pltpu.roll(tracer[t, level], spot, 1) if spot else tracer[t, level])
        outs[2][...] = tile.packed(0)
    for number, out in enumerate(outs[:2]):
        row = sent_row(plan, number, cx)
        for level in range(levels):
            for t in range(carried):
                spot = t * levels + level
                out[spot : spot + 1, :] = tracer[t, level, pl.ds(row, 1), :]
            spot = carried * levels + level
            out[spot : spot + 1, :] = west[level, pl.ds(row, 1), :]
        out[head : head + 8, :] = jnp.broadcast_to(scale[pl.ds(row, 1), :], (8, cy))
        if plan["x_blocks"][number] and not plan["relay"]:
            at = 8 * plan["own_blocks"].index(plan["x_blocks"][number])
            out[head + 8 : head + 16, :] = blocks[at : at + 8, :]


def relay_kernel(plan, head, cx, number, rows, blocks, y_got, out):
    out[0 : head + 8, :] = rows[0 : head + 8, :]
    row = sent_row(plan, number, cx)
    out[head + 1 : head + 2, :] = y_got[pl.ds(row, 1), :]
    near, far = plan["x_blocks"]
    even_x = is_even("facex")
    offset = jnp.where(even_x if number == 0 else jnp.logical_not(even_x), near, far)
    at = plan["y_tiles"] * cx + 8 * (offset - plan["y_blocks"][0])
    out[head + 8 : head + 24, :] = blocks[pl.ds(pl.multiple_of(8 * offset, 8), 16), :]
    out[head + 24 : head + 40, :] = y_got[pl.ds(pl.multiple_of(at, 8), 16), :]


def beyond_kernel(plan, cx, blocks, y_got, *outs):
    for out, offset in zip(outs, plan["x_ops"]):
        at = plan["y_tiles"] * cx + 8 * (offset - plan["y_blocks"][0])
        out[0:16, :] = blocks[8 * offset : 8 * offset + 16, :]
        out[16:32, :] = y_got[at : at + 16, :]


def rim_kernel(plan, carried, levels, cx, y_sent, y_got, base, base_other, lanes, own, *refs):
    inverse_out, ratio_out, lower_out, pieces_out, columns_out, rows_out, picks_out, live_out, base_out, square = refs
    cy = y_got.shape[1]
    slots = live_out.shape[1]

    def turned(values):
        square[...] = jnp.zeros((LANES, LANES), F32)
        square[0:cx, :] = values
        return jnp.transpose(square[...])

    def part(values, name):
        return values[plan["lane_" + name] : plan["lane_" + name] + levels]

    beyond = turned(y_got[0:cx, :])
    mine = turned(y_sent[0:cx, :])
    coupling = turned(y_got[cx : 2 * cx, :])
    north = is_even("facey")
    pieces_out[0] = part(beyond, "c")
    pieces_out[1] = part(beyond, "u")
    pieces_out[2] = part(beyond, "v")
    pieces_out[3] = jnp.where(north, part(beyond, "w"), part(mine, "v"))
    pieces_out[4] = jnp.where(north, part(mine, "c"), part(beyond, "d"))
    pieces_out[5] = jnp.where(north, part(beyond, "d"), part(mine, "c"))

    def level_of(ref, level):
        return jnp.broadcast_to(ref[level : level + 1, :], (8, LANES))

    square[...] = coupling
    first = []
    ratios = []
    before = None
    for level in range(levels):
        diagonal = jnp.ones((8, LANES), F32)
        if level > 0:
            below = level_of(square, level - 1)
            diagonal = diagonal + below
        if level < levels - 1:
            diagonal = diagonal + level_of(square, level)
        if level > 0:
            diagonal = diagonal - below * below * before
        inverse = 1.0 / diagonal
        ratios.append(level_of(square, level) * inverse if level < levels - 1 else jnp.zeros((8, LANES), F32))
        lower = below * inverse if level > 0 else jnp.zeros((8, LANES), F32)
        lower_out[level : level + 1, :] = lower[0:1]
        inverse_out[level : level + 1, :] = inverse[0:1]
        ratio_out[level : level + 1, :] = ratios[-1][0:1]
        first.append(inverse if level == 0 else lower * first[-1])
        before = inverse
    weight = first
    for level in range(levels - 2, -1, -1):
        weight[level] = first[level] + ratios[level] * weight[level + 1]
    for level in range(levels):
        square[level : level + 1, :] = weight[level][0:1]
    weights = square[0:levels, :]
    tile = LanePacker(iota((cx, cy), 1), edge_of(0, cy))
    for t in range(2 * carried):
        values = base[t] if t < carried else base_other[t - carried]
        tile.put(t, pltpu.roll(values, t, 1) if t else values)
    base_out[0:cx, :] = tile.packed(0)
    base_out[cx : 2 * cx, :] = lanes[...]
    base_out[2 * cx :, :] = own[0:16, :]
    at = plan["y_tiles"] * cx + 8 * len(plan["y_blocks"])
    strips = slots // LANES
    cell = jnp.concatenate([y_got[at + n : at + n + 1, :] for n in range(strips)], axis=1).astype(jnp.int32)
    live_out[...] = jnp.concatenate([y_got[at + strips + n : at + strips + n + 1, :] for n in range(strips)], axis=1)
    on_edge = lax.rem(cell, cy) == jnp.where(north, 0, cy - 1)
    x_of = jnp.where(on_edge, lax.div(cell, cy), LANES)
    picks = jnp.where(iota((LANES, slots), 0) == x_of, 1.0, 0.0)
    rows_out[...] = picks[0:cx]
    picks = picks.astype(BF16)
    picks_out[...] = picks
    high, low = halves(weights)
    columns_out[...] = jnp.dot(high, picks, preferred_element_type=F32) + jnp.dot(
        low, picks, preferred_element_type=F32
    )


def factor_kernel(sizes, *refs):
    (tracer, west, south, mixing, adjoint, cells) = refs[:6]
    inverse_out, lower_out, ratio_out, base_out, inner_out, shares_out, columns_out, rows_out, picks_out = refs[6:]
    carried, levels, cx, cy = tracer.shape
    slots = cells.shape[1]
    first = []
    before = None
    for level in range(levels):
        diagonal = jnp.ones((cx, cy), F32)
        if level > 0:
            diagonal = diagonal + mixing[level - 1]
        if level < levels - 1:
            diagonal = diagonal + mixing[level]
        if level > 0:
            diagonal = diagonal - mixing[level - 1] * mixing[level - 1] * before
        inverse = 1.0 / diagonal
        inverse_out[level] = inverse
        if level < levels - 1:
            ratio_out[level] = mixing[level] * inverse
        lower = mixing[level - 1] * inverse if level > 0 else jnp.zeros((cx, cy), F32)
        lower_out[level] = lower
        first.append(inverse if level == 0 else lower * first[-1])
        before = inverse
    ratio_out[levels - 1] = jnp.zeros((cx, cy), F32)
    weight = first
    for level in range(levels - 2, -1, -1):
        weight[level] = first[level] + ratio_out[level] * weight[level + 1]
    for t in range(carried):
        total = weight[0] * adjoint[t, 0]
        for level in range(1, levels):
            total = total + weight[level] * adjoint[t, level]
        base_out[t] = total
    for level in range(levels):
        total = tracer[0, level]
        for t in range(1, carried):
            total = total + tracer[t, level]
        parts = shares(west[level], south[level])
        for number, part in enumerate(parts):
            shares_out[number, level] = part
        inner_out[level] = mix(parts, total)
    cell = cells[...]
    x_of = lax.div(cell, cy)
    y_of = lax.rem(cell, cy)
    in_row = jnp.where(iota((cx, slots), 0) == x_of, 1.0, 0.0)
    in_lane = jnp.where(iota((cy, slots), 0) == y_of, 1.0, 0.0).astype(BF16)
    rows_out[...] = in_row
    picks_out[...] = in_lane
    high, low = halves(jnp.concatenate(weight, axis=0))
    picked = jnp.dot(high, in_lane, preferred_element_type=F32)
    picked = picked + jnp.dot(low, in_lane, preferred_element_type=F32)
    for level in range(levels):
        part = picked[level * cx : (level + 1) * cx] * in_row
        columns_out[level : level + 1, :] = jnp.sum(part, axis=0, keepdims=True)


def sides(plan, first, second):
    if plan["relay"]:
        return first, second
    even_x = is_even("facex")
    return jnp.where(even_x, second, first), jnp.where(even_x, first, second)


def own_sides(plan, first, second):
    return (second, first) if plan["relay"] else sides(plan, first, second)


def sent_row(plan, number, rows):
    if plan["relay"]:
        return rows - 1 if number == 0 else 0
    even_x = is_even("facex")
    return jnp.where(even_x if number == 0 else jnp.logical_not(even_x), rows - 1, 0)


def seam(number, sent, got, sent_face, got_face):
    even_y = is_even("facey")
    north = even_y if number == 0 else jnp.logical_not(even_y)
    to_north = -(jnp.maximum(got_face, 0.0) * sent + jnp.minimum(got_face, 0.0) * got)
    to_south = jnp.maximum(sent_face, 0.0) * got
    return jnp.where(north, to_north, to_south), jnp.where(north, sent.shape[1] - 1, 0)


def spread_wind(values, start, carried, levels):
    lane = iota(values.shape, 1)
    result = jnp.zeros_like(values)
    for t in range(carried):
        moved = pltpu.roll(values, (t * levels - start) % values.shape[1], 1)
        inside = jnp.logical_and(lane >= t * levels, lane < (t + 1) * levels)
        result = jnp.where(inside, moved, result)
    return result


def seam_lanes(number, plan, sent, got, sent_wind, got_wind, carried, levels):
    start = plan["lane_v"]
    faces = [spread_wind(wind, start, carried, levels) for wind in (sent_wind, got_wind)]
    return seam(number, sent, got, *faces)


def block_groups(blocks, cap):
    per_tile = LANES // cap
    group_of_lane = lax.div(iota((8, LANES), 1), cap)
    groups = []
    for group in range(per_tile):
        tiles = []
        for start in range(0, len(blocks), per_tile):
            tile = jnp.zeros((8, LANES), F32)
            for a in range(per_tile):
                moved = pltpu.roll(blocks[start + a], (cap * (a - group)) % LANES, 1)
                tile = jnp.where(group_of_lane == a, moved, tile)
            tiles.append(tile)
        groups.append(jnp.concatenate(tiles, axis=1))
    return groups


def relayed_blocks(plan, head, own, beyond, got, x_got):
    def block_at(ref, row):
        return ref[row : row + 8, :]

    blocks = {0: block_at(own, 0), 1: block_at(beyond, 8)}
    rim_blocks = {0: block_at(beyond, 0), 1: block_at(own, 8)}
    even_x = is_even("facex")
    from_west, from_east = (got[n][head + 8 : head + 40, :] for n in range(2))
    carriers = [
        (plan["x_blocks"][0], jnp.where(even_x, from_east, from_west)),
        (plan["x_blocks"][1], jnp.where(even_x, from_west, from_east)),
    ]
    carriers += [(offset, ref[...]) for offset, ref in zip(plan["x_ops"], x_got)]
    for offset, values in carriers:
        blocks[offset], rim_blocks[offset + 1] = block_at(values, 0), block_at(values, 8)
        rim_blocks[offset], blocks[offset + 1] = block_at(values, 16), block_at(values, 24)
    return blocks, rim_blocks


def observe_kernel(sizes, plan, carried, *refs):
    refs = list(refs)
    got = refs[0:2]
    inner, lower, inverse, ratio, in_row, in_lane = refs[2:8]
    sent = refs[8:10]
    refs = refs[10:]
    y_sent = refs[: plan["y_ops"]]
    y_got = refs[plan["y_ops"] : 2 * plan["y_ops"]]
    refs = refs[2 * plan["y_ops"] :]
    if plan["relay"]:
        rim_inverse, rim_ratio, rim_lower, pieces, rim_picks, parcel, turn, rise = refs
    else:
        columns, live, own, *refs = refs
        n_pairs = len(plan["pairs"])
        pair_got = refs[:n_pairs]
        swapped = refs[n_pairs] if n_pairs else None
        modeled_out, state_out = refs[-2:]
    levels, cx, cy = inner.shape
    slots = in_row.shape[1]
    head = (carried + 1) * levels

    def summed(rows):
        total = rows[0:levels]
        for t in range(1, carried):
            total = total + rows[t * levels : (t + 1) * levels]
        return total

    beyond_west, beyond_east = sides(plan, got[0][0:head], got[1][0:head])
    at_west, at_east = own_sides(plan, sent[0][0:head], sent[1][0:head])
    spot = carried * levels
    face_west = at_west[spot:head]
    face_east = beyond_east[spot:head]
    from_west = jnp.maximum(face_west, 0.0) * summed(beyond_west)
    from_east = -(
        jnp.maximum(face_east, 0.0) * summed(at_east) + jnp.minimum(face_east, 0.0) * summed(beyond_east)
    )
    lane_parts = []
    for number in range(plan["y_ops"]):
        mine, beyond = y_sent[number][0:cx, :], y_got[number][0:cx, :]
        if plan["relay"]:
            faces = [pltpu.roll(values, cy - plan["lane_v"], 1) for values in (mine, beyond)]
            total, spot_y = seam(number, mine, beyond, *faces)
        else:
            part, spot_y = seam_lanes(number, plan, mine, beyond, mine, beyond, carried, levels)
            total = part
            for t in range(1, carried):
                total = total + pltpu.roll(part, (-t * levels) % cy, 1)
        lane_parts.append((pltpu.roll(total, spot_y, 1), spot_y))
    lane = iota((cx, cy), 1)
    row = iota((cx, cy), 0)
    forward = []
    for level in range(levels):
        value = inner[level]
        value = value + jnp.where(row == 0, from_west[level : level + 1], 0.0)
        value = value + jnp.where(row == cx - 1, from_east[level : level + 1], 0.0)
        for total, spot_y in lane_parts:
            moved = pltpu.roll(total, cy - level, 1) if level else total
            value = value + jnp.where(lane == spot_y, moved, 0.0)
        value = value * inverse[level]
        forward.append(value + lower[level] * forward[-1] if level else value)
    result = forward
    for level in range(levels - 2, -1, -1):
        result[level] = forward[level] + ratio[level] * result[level + 1]
    high, low = halves(jnp.concatenate(result, axis=0))
    picks = in_lane[...]
    picked = jnp.dot(high, picks, preferred_element_type=F32)
    picked = picked + jnp.dot(low, picks, preferred_element_type=F32)

    if not plan["relay"]:
        start = plan["y_tiles"] * cx
        blocks = {0: own[0:8, :], plan["y_blocks"][0]: y_got[0][start : start + 8, :]}
        for number in range(2):
            offset = plan["x_blocks"][number]
            if offset:
                blocks[offset] = got[number][head + 8 : head + 16, :]
        first_core = lax.axis_index("lev") == 0
        for number, (for_first, for_second) in enumerate(plan["pairs"]):
            mine = pair_got[number][...]
            other = swapped[8 * number : 8 * number + 8, :]
            if for_first == for_second:
                blocks[for_first] = mine
            else:
                blocks[for_first] = jnp.where(first_core, mine, other)
                blocks[for_second] = jnp.where(first_core, other, mine)
        *groups, last = block_groups(blocks, slots // len(blocks))
        total = jnp.zeros((cx, slots), F32)
        sensitivity = jnp.zeros((8, slots), F32)
        for g, kernel in enumerate(groups):
            sensitivity = sensitivity + kernel * columns[8 * g : 8 * g + 8, :]
            for l in range(8):
                level = 8 * g + l
                total = total + kernel[l : l + 1] * picked[level * cx : (level + 1) * cx]
        modeled_out[...] = jnp.sum(total * in_row[...], axis=0, keepdims=True)
        gain = jnp.sum(sensitivity, axis=0, keepdims=True) * last[1:2] * live[...]
        state_out[...] = jnp.concatenate([gain, last[0:1]], axis=0)
        return

    chosen = in_row[...]
    for level in range(levels):
        part = picked[level * cx : (level + 1) * cx] * chosen
        parcel[level : level + 1, :] = jnp.sum(part, axis=0, keepdims=True)

    corners_west, corners_east = sides(plan, got[0][head + 1 : head + 2, :], got[1][head + 1 : head + 2, :])
    turn[...] = jnp.zeros((LANES, LANES), F32)
    turn[0:1, :] = corners_west
    turn[cx - 1 : cx, :] = corners_east
    turned = jnp.transpose(turn[...])
    ends = turned[plan["lane_c"] : plan["lane_c"] + levels]
    end_face = turned[plan["lane_u"] : plan["lane_u"] + levels]
    place = iota((levels, LANES), 1)
    cells, face_w, face_s, face_n, south_cells, north_cells = (pieces[n] for n in range(6))
    west_cells = jnp.where(place == 0, ends, pltpu.roll(cells, 1, 1))
    east_cells = jnp.where(place == cx - 1, ends, pltpu.roll(cells, LANES - 1, 1))
    face_e = jnp.where(place == cx - 1, end_face, pltpu.roll(face_w, LANES - 1, 1))
    rise[0:levels, :] = advance_cells(
        cells, west_cells, east_cells, south_cells, north_cells, face_w, face_e, face_s, face_n
    )

    def level_of(ref, level):
        return jnp.broadcast_to(ref[level : level + 1, :], (8, LANES))

    climbed = []
    for level in range(levels):
        value = level_of(rise, level) * level_of(rim_inverse, level)
        climbed.append(value + level_of(rim_lower, level) * climbed[-1] if level else value)
    for level in range(levels - 2, -1, -1):
        climbed[level] = climbed[level] + level_of(rim_ratio, level) * climbed[level + 1]
    for level in range(levels):
        rise[level : level + 1, :] = climbed[level][0:1]
    high, low = halves(rise[0:levels, :])
    picks = rim_picks[...]
    picked = jnp.dot(high, picks, preferred_element_type=F32)
    picked = picked + jnp.dot(low, picks, preferred_element_type=F32)
    parcel[levels : 2 * levels, :] = picked


def advance_cells(cells, west, east, south, north, face_w, face_e, face_s, face_n):
    flux_w = jnp.maximum(face_w, 0.0) * west + jnp.minimum(face_w, 0.0) * cells
    flux_e = jnp.maximum(face_e, 0.0) * cells + jnp.minimum(face_e, 0.0) * east
    flux_s = jnp.maximum(face_s, 0.0) * south + jnp.minimum(face_s, 0.0) * cells
    flux_n = jnp.maximum(face_n, 0.0) * cells + jnp.minimum(face_n, 0.0) * north
    return cells + flux_w - flux_e + flux_s - flux_n


def scatter(force, in_row, in_lane):
    high, low = halves(in_row * force)
    dims = (((1,), (1,)), ((), ()))
    scattered = lax.dot_general(high, in_lane, dims, preferred_element_type=F32)
    return scattered + lax.dot_general(low, in_lane, dims, preferred_element_type=F32)


def force_kernel(plan, *refs):
    modeled, modeled_other, state, in_row, in_lane, base, base_other = refs[:7]
    near_out = refs[7]
    rim_outs = refs[8:]
    carried, cx, cy = base.shape
    misfit = modeled[...] + modeled_other[...] - state[1:2, :]
    force = state[0:1, :] * misfit
    scattered = scatter(force, in_row[...], in_lane[...])
    lane = iota((cx, cy), 1)
    even_y = is_even("facey")
    edges = []
    for number in range(len(rim_outs)):
        sends_last = even_y if number == 0 else jnp.logical_not(even_y)
        edges.append(jnp.where(sends_last, cy - 1, 0))
    rims = [jnp.zeros((cx, cy), F32) for _ in rim_outs]
    for t in range(2 * carried):
        values = scattered + (base[t] if t < carried else base_other[t - carried])
        near_out[t] = values
        for number, edge in enumerate(edges):
            moved = pltpu.roll(values, lax.rem(t + cy - edge, cy), 1)
            rims[number] = jnp.where(lane == t, moved, rims[number])
    for rim, out in zip(rims, rim_outs):
        out[...] = rim


def surface_kernel(sizes, plan, carried, levels, *refs):
    y_ops = plan["y_ops"]
    near = refs[0]
    rims = refs[6 + y_ops : 6 + 2 * y_ops]
    rim_values = [[rim[...] for rim in rims] for _ in range(near.shape[0])]
    values = [near[t] for t in range(near.shape[0])]
    spread_surface(
        sizes, plan, carried, levels, values, rim_values, refs[1:4], refs[4:6], refs[6 : 6 + y_ops], refs[6 + 2 * y_ops :]
    )


def weigh_kernel(sizes, plan, carried, levels, *refs):
    parcel, other, columns, live, rim_columns, rim_live, own, *refs = refs
    x_got, refs = refs[: len(plan["x_ops"])], refs[len(plan["x_ops"]) :]
    in_row, in_lane, base, base_other, rim_rows, rim_base = refs[:6]
    cx, cy = base.shape[1:]
    slots = live.shape[1]

    def force(blocks, start, weights, used):
        *groups, last = block_groups(blocks, slots // len(blocks))
        seen = jnp.zeros((8, slots), F32)
        sensitivity = jnp.zeros((8, slots), F32)
        for g, kernel in enumerate(groups):
            part = slice(start + 8 * g, start + 8 * g + 8)
            seen = seen + kernel * (parcel[part, :] + other[part, :])
            sensitivity = sensitivity + kernel * weights[8 * g : 8 * g + 8, :]
        modeled = jnp.sum(seen, axis=0, keepdims=True)
        gain = jnp.sum(sensitivity, axis=0, keepdims=True) * last[1:2] * used[...]
        return gain * (modeled - last[0:1])

    blocks, rim_blocks = relayed_blocks(
        plan, (carried + 1) * levels, own, rim_base[2 * cx :, :], refs[9:11], x_got
    )
    scattered = scatter(force(blocks, 0, columns, live), in_row[...], in_lane[...])
    on_rim = jnp.sum(rim_rows[...] * force(rim_blocks, levels, rim_columns, rim_live), axis=1, keepdims=True)
    near = [scattered + base[t] for t in range(carried)]
    near += [scattered + base_other[t] for t in range(carried)]
    rims = [[rim_base[0:cx, :] + on_rim] for _ in near]
    spread_surface(sizes, plan, carried, levels, near, rims, refs[6:9], refs[9:11], refs[11:12], refs[12:])


def spread_surface(sizes, plan, carried, levels, near, rim_values, fields, got, y_got, outs):
    west, south, scale = fields
    tracers = len(near)
    cx, cy = near[0].shape
    spot_v = plan["lane_v"]
    band = cy // sizes[0]
    per_tile = min(tracers, LANES // band)
    spot = carried * levels
    head = (carried + 1) * levels
    lane = iota((cx, cy), 1)
    row = iota((cx, cy), 0)
    even_y = is_even("facey")
    face_west = west[...]
    face_south = south[...]
    scales = scale[...]
    beyond_west, beyond_east = sides(plan, got[0][head : head + 1], got[1][head : head + 1])
    _, east_wind = sides(plan, got[0][spot : spot + 1], got[1][spot : spot + 1])
    face_east = jnp.where(row == cx - 1, east_wind, pltpu.roll(face_west, cx - 1, 0))
    face_north = left(face_south)
    norths = []
    for number in range(plan["y_ops"]):
        norths.append(even_y if number == 0 else jnp.logical_not(even_y))
        moved = pltpu.roll(y_got[number][0:cx, :], cy - 1 - spot_v, 1)
        keep = jnp.logical_and(lane == cy - 1, norths[number])
        face_north = jnp.where(keep, moved, face_north)
    to_middle = 1.0 + jnp.minimum(face_west, 0.0) - jnp.maximum(face_east, 0.0)
    to_middle = scales * (to_middle + jnp.minimum(face_south, 0.0) - jnp.maximum(face_north, 0.0))
    to_east = jnp.where(row == cx - 1, 0.0, scales * jnp.maximum(face_east, 0.0))
    to_west = jnp.where(row == 0, 0.0, scales * jnp.minimum(face_west, 0.0))
    to_north = scales * jnp.maximum(face_north, 0.0)
    to_south = scales * jnp.minimum(face_south, 0.0)
    west_gain = beyond_west * jnp.maximum(face_west[0:1], 0.0)
    east_gain = -beyond_east * jnp.minimum(face_east[cx - 1 : cx], 0.0)
    filler = jnp.zeros((6, cy), F32)
    grown = []
    for t in range(tracers):
        values = near[t]
        north_side = left(values)
        south_side = right(values)
        for number in range(plan["y_ops"]):
            rim = rim_values[t][number]
            at_north = jnp.logical_and(lane == cy - 1, norths[number])
            at_south = jnp.logical_and(lane == 0, jnp.logical_not(norths[number]))
            north_side = jnp.where(at_north, pltpu.roll(rim, (cy - 1 - t) % cy, 1), north_side)
            south_side = jnp.where(at_south, pltpu.roll(rim, (-t) % cy, 1), south_side)
        swept = to_middle * values + to_east * pltpu.roll(values, cx - 1, 0) - to_west * pltpu.roll(values, 1, 0)
        swept = swept + to_north * north_side - to_south * south_side
        grown.append(
            jnp.concatenate(
                [swept, west_gain * values[0:1], east_gain * values[cx - 1 : cx], filler], axis=0
            )
        )
    rows = cx + 8
    group_of_lane = lax.div(iota((rows, cy), 1), band)
    first_core = lax.axis_index("lev") == 0
    place = lax.axis_index("facex")
    for out, (for_first, for_second) in zip(outs, plan["bands"]):
        offset = for_first if for_first == for_second else jnp.where(first_core, for_first, for_second)
        target = jnp.bitwise_xor(place, offset)
        count = carried if for_first == for_second else tracers
        skip = carried if for_first == for_second != 0 and plan["cross"] else 0
        for start in range(0, count, per_tile):
            tile = jnp.zeros((rows, cy), F32)
            for a in range(min(per_tile, count - start)):
                moved = pltpu.roll(grown[skip + start + a], lax.rem(band * a + cy - band * target, cy), 1)
                tile = jnp.where(group_of_lane == a, moved, tile)
            out[start // per_tile * rows : (start // per_tile + 1) * rows, :] = tile


def regrid_kernel(sizes, plan, bands, carried, cx, band, *refs):
    index, weight = refs[:2]
    blocks, more, out = refs[2 : 2 + len(bands)], refs[2 + len(bands) : -1], refs[-1]
    taps, cells = index.shape
    rows = cx + 8
    per_tile = min(2 * carried, LANES // band)
    lane = iota((rows, LANES), 1)
    row = iota((rows, cells), 0)
    first_core = lax.axis_index("lev") == 0
    place = lax.axis_index("facex")
    around = sizes[0] * cx
    parts = []
    row_places = []
    for block, ((for_first, for_second), fetched, first) in zip(blocks, bands):
        if plan["cross"] != fetched:
            for_first, for_second = for_second, for_first
        offset = for_first if for_first == for_second else jnp.where(first_core, for_first, for_second)
        start = jnp.bitwise_xor(place, offset) * cx
        places = start + row
        places = jnp.where(row == cx, lax.rem(start + around - 1, around), places)
        places = jnp.where(row == cx + 1, lax.rem(start + cx, around), places)
        row_places.append(places)
        for t in range(first, first + carried):
            tile = block[t // per_tile * rows : (t // per_tile + 1) * rows, :]
            a = t % per_tile
            values = tile if a == 0 else pltpu.roll(tile, (-band * a) % LANES, 1)
            high = values.astype(BF16).astype(F32)
            low = pltpu.roll(values - high, band, 1)
            both = jnp.where(lane < band, high, jnp.where(lane < 2 * band, low, 0.0))
            parts.append(both.astype(BF16))
    left_side = jnp.concatenate(parts, axis=0)
    spread = iota((LANES, cells), 0)
    in_band = lax.rem(spread, band)
    used = spread < 2 * band
    totals = [jnp.zeros((rows, cells), F32) for _ in range(carried)]
    for tap in range(taps):
        place_of = index[tap : tap + 1, :]
        column = lax.div(place_of, band)
        in_lane = lax.rem(place_of, band)
        picks = jnp.where(jnp.logical_and(in_band == in_lane, used), 1.0, 0.0).astype(BF16)
        picked = jnp.dot(left_side, picks, preferred_element_type=F32)
        at = 0
        for places in row_places:
            chosen = jnp.where(places == column, weight[tap : tap + 1, :], 0.0)
            for t in range(carried):
                totals[t] = totals[t] + chosen * picked[at : at + rows]
                at += rows
    sums = jnp.concatenate([jnp.sum(total, axis=0, keepdims=True) for total in totals], axis=0)
    for ref in more:
        sums = sums + ref[...]
    out[...] = sums


def advance_kernel(plan, *refs):
    tracer, parts, lower, inverse, ratio = refs[:5]
    sent = refs[5:7]
    got = refs[7:9]
    y_ops = plan["y_ops"]
    y_sent, y_got, winds_sent, winds_got = (refs[9 + n * y_ops : 9 + (n + 1) * y_ops] for n in range(4))
    target, out, west_rows, east_rows, done = refs[-5:]
    carried, levels, cx, cy = tracer.shape
    head = (carried + 1) * levels
    spot = carried * levels
    beyond_west, beyond_east = sides(plan, got[0][0:head], got[1][0:head])
    at_west, at_east = own_sides(plan, sent[0][0:head], sent[1][0:head])
    face_west = at_west[spot:head]
    face_east = beyond_east[spot:head]
    for t in range(carried):
        part = slice(t * levels, (t + 1) * levels)
        west_rows[part, :] = jnp.maximum(face_west, 0.0) * beyond_west[part]
        east_rows[part, :] = -(
            jnp.maximum(face_east, 0.0) * at_east[part] + jnp.minimum(face_east, 0.0) * beyond_east[part]
        )
    lane = iota((cx, cy), 1)
    row = iota((cx, cy), 0)
    seams = [
        seam_lanes(
            n,
            plan,
            y_sent[n][0:cx, :],
            y_got[n][cx : 2 * cx, :] if plan["relay"] else y_got[n][0:cx, :],
            winds_sent[n][0:cx, :],
            winds_got[n][0:cx, :],
            carried,
            levels,
        )
        for n in range(y_ops)
    ]
    stride = 4

    def forward(step, before):
        mixed = []
        for k in range(stride):
            level = step * stride + k
            weights = [parts[n, level] for n in range(5)]
            mixed.append([])
            for t in range(carried):
                value = mix(weights, tracer[t, level])
                value = value + jnp.where(row == 0, west_rows[pl.ds(t * levels + level, 1), :], 0.0)
                value = value + jnp.where(row == cx - 1, east_rows[pl.ds(t * levels + level, 1), :], 0.0)
                for packed, spot_y in seams:
                    moved = pltpu.roll(packed, lax.rem(spot_y - (t * levels + level) + 2 * cy, cy), 1)
                    value = value + jnp.where(lane == spot_y, moved, 0.0)
                mixed[k].append(value)
        for k in range(stride):
            level = step * stride + k
            from_below = lower[level]
            scaled = inverse[level]
            after = []
            for t in range(carried):
                value = mixed[k][t] * scaled + from_below * before[t]
                out[t, level] = value
                after.append(value)
            before = after
        return tuple(before)

    def copy(step):
        part = pl.ds(levels - (step + 1) * stride, stride)
        return pltpu.make_async_copy(out.at[:, part], target.at[:, part], done.at[step])

    start = tuple(jnp.zeros((cx, cy), F32) for _ in range(carried))
    lax.fori_loop(0, levels // stride, forward, start)
    above = list(start)
    for step in range(levels // stride):
        for k in range(stride):
            level = levels - 1 - step * stride - k
            factor = ratio[level]
            for t in range(carried):
                above[t] = out[t, level] + factor * above[t]
                out[t, level] = above[t]
        copy(step).start()
    for step in range(levels // stride):
        copy(step).wait()


GROUP = ("facex", "facey", "lev")


def exchange(values, sizes, rule):
    many_x, many_y, cores = sizes
    pairs = []
    for x in range(many_x):
        for y in range(many_y):
            for c in range(cores):
                to = rule(x, y, c)
                if to is not None:
                    pairs.append(((x * many_y + y) * cores + c, (to[0] * many_y + to[1]) * cores + to[2]))
    return lax.ppermute(values, GROUP, pairs)


def make_plan(sizes):
    many_x, many_y, _ = sizes
    tiles = many_x * many_y
    x_blocks = [many_y, (many_x - 1) * many_y if many_x == 4 else 0]
    relay = many_y == 2 and many_x == 4
    if relay:
        own_blocks = list(range(tiles))
        y_blocks = own_blocks[2:]
        x_ops = [offset for offset in own_blocks[2::2] if offset not in x_blocks]
        pairs = []
    else:
        own_blocks = [0] + [offset for offset in x_blocks if offset]
        y_blocks = [1]
        x_ops = []
        rest = [d for d in range(tiles) if d not in {1, *own_blocks}]
        rest.sort(key=lambda d: (d // many_y != many_x // 2, d))
        pairs = [(rest[n], rest[min(n + 1, len(rest) - 1)]) for n in range(0, len(rest), 2)]
    others = list(range(many_x - 1, 1, -1))
    bands = [(0, 0), (1, 1)] + [(others[n], others[n + 1]) for n in range(0, len(others), 2)]
    return {
        "relay": relay,
        "cross": 1 if relay else 0,
        "x_blocks": x_blocks,
        "x_ops": x_ops,
        "own_blocks": own_blocks,
        "y_blocks": y_blocks,
        "y_ops": 1 if many_y == 2 else 2,
        "y_tiles": 2 if relay else 1,
        "pairs": pairs,
        "bands": bands,
    }


def lane_plan(plan, carried, levels):
    starts = {"c": 0, "d": levels, "v": 2 * levels, "w": 3 * levels, "u": 4 * levels}
    if not plan["relay"]:
        starts = {"v": carried * levels}
    return {"lane_" + name: start for name, start in starts.items()}


def local(
    sizes,
    tracer,
    west_courant,
    south_courant,
    mixing,
    adjoint_later,
    emission_scale,
    send_cells,
    send_counts,
    kernels,
    observed,
    error_weight,
    regrid_index,
    regrid_weight,
):
    plan = make_plan(sizes)
    many_x, many_y, _ = sizes
    carried, levels, cx, cy = tracer.shape
    owners, cap = send_cells.shape[2:]
    slots = owners * cap
    taps, ll = regrid_index.shape[2:]
    plan.update(lane_plan(plan, carried, levels))
    head = (carried + 1) * levels
    y_ops = plan["y_ops"]
    band = cy // many_x

    def next_x(number):
        def rule(x, y, c):
            step = 1 if (plan["relay"] or x % 2 == 0) == (number == 0) else -1
            return ((x + step) % many_x, y, c)

        return rule

    def next_y(number, cross):
        def rule(x, y, c):
            to = y + (1 if (y % 2 == 0) == (number == 0) else -1)
            return (x, to, c ^ cross) if 0 <= to < many_y else None

        return rule

    def jump(for_first, for_second, cross=0):
        def rule(x, y, c):
            d = for_first if c == 0 else for_second
            return (x ^ (d // many_y), y ^ (d % many_y), c ^ cross)

        return rule

    def other_core(values):
        return exchange(values, sizes, lambda x, y, c: (x, y, 1 - c))

    strips = slots // LANES
    plan["parcel"] = -(-2 * strips // 8) * 8
    extra = 40 if plan["relay"] else 16
    row_shapes = [shape(head + extra, cy)] * 2
    y_rows = plan["y_tiles"] * cx + 8 * len(plan["y_blocks"]) + (plan["parcel"] if plan["relay"] else 0)
    lane_shapes = [shape(y_rows if n == 0 else cx, cy) for n in range(y_ops)]
    packed = call(
        functools.partial(pack_kernel, sizes, plan),
        lane_shapes
        + [shape(8 * len(plan["own_blocks"]), LANES)]
        + [shape(8, LANES)] * len(plan["pairs"])
        + [shape(1, slots, dtype=jnp.int32), shape(1, slots)]
        + [shape(*a.shape) for a in (tracer, west_courant, south_courant, emission_scale, mixing)],
        [
            tracer,
            west_courant,
            south_courant,
            emission_scale,
            kernels.reshape(owners, levels, cap),
            observed.reshape(owners, cap),
            error_weight.reshape(owners, cap),
            send_cells.reshape(owners, cap),
            send_counts.reshape(owners),
            mixing,
        ],
        "pack",
        100000,
        hbm=range(10),
        scratch=[
            pltpu.VMEM((owners, levels, cap), F32),
            pltpu.VMEM((owners, cap), F32),
            pltpu.VMEM((owners, cap), F32),
            pltpu.VMEM((owners, cap), jnp.int32),
            pltpu.SMEM((owners,), jnp.int32),
            pltpu.SemaphoreType.DMA((9 + carried,)),
        ],
    )
    lanes_sent = packed[:y_ops]
    own_blocks = packed[y_ops]
    pair_sent = packed[1 + y_ops : -7]
    cell, live, tracer, west_courant, south_courant, emission_scale, mixing = packed[-7:]
    lanes_got = [exchange(lanes_sent[n], sizes, next_y(n, plan["cross"])) for n in range(y_ops)]
    held, *_ = lax.optimization_barrier((tracer, *lanes_sent))
    inverse, lower, ratio, base, inner, parts, columns, in_row, in_lane = call(
        functools.partial(factor_kernel, sizes),
        [
            shape(levels, cx, cy),
            shape(levels, cx, cy),
            shape(levels, cx, cy),
            shape(carried, cx, cy),
            shape(levels, cx, cy),
            shape(5, levels, cx, cy),
            shape(levels, slots),
            shape(cx, slots),
            shape(cy, slots, dtype=BF16),
        ],
        [held, west_courant, south_courant, mixing, adjoint_later, cell],
        "factor",
        3000000,
    )
    rows_sent = list(
        call(
            functools.partial(rows_kernel, plan),
            row_shapes + ([shape(cx, cy)] if plan["relay"] else []),
            [tracer, west_courant, emission_scale, own_blocks],
            "rows",
            100000,
        )
    )
    per_tile = min(2 * carried, LANES // band)

    def band_shape(first, second):
        count = carried if first == second else 2 * carried
        return shape(-(-count // per_tile) * (cx + 8), cy)

    band_shapes = [band_shape(*b) for b in plan["bands"]]
    fields = [west_courant[0], south_courant[0], emission_scale]
    observe = functools.partial(
        call, functools.partial(observe_kernel, sizes, plan, carried), name="observe", flops=2000000
    )
    if plan["relay"]:
        base, *lanes_got = lax.optimization_barrier((base, *lanes_got))
        lanes_each = rows_sent.pop()
        base_other = other_core(base)

        def relay(number, *after):
            held, *_ = lax.optimization_barrier((rows_sent[number], *after))
            return call(
                functools.partial(relay_kernel, plan, head, cx, number),
                [row_shapes[number]],
                [held, own_blocks, lanes_got[0]],
                "relay",
                10000,
            )[0]

        rows_sent = [relay(0), relay(1)]
        x_sent = call(
            functools.partial(beyond_kernel, plan, cx),
            [shape(32, LANES)] * len(plan["x_ops"]),
            [own_blocks, lanes_got[0]],
            "beyond",
            10000,
        )
        x_got = [exchange(s, sizes, jump(d, d, 1)) for s, d in zip(x_sent, plan["x_ops"])]
        rows_got = [exchange(rows_sent[n], sizes, next_x(n)) for n in range(2)]
        held_y, *_ = lax.optimization_barrier((lanes_got[0], *rows_sent))
        rim = call(
            functools.partial(rim_kernel, plan, carried, levels, cx),
            [
                shape(levels, LANES),
                shape(levels, LANES),
                shape(levels, LANES),
                shape(6, levels, LANES),
                shape(levels, slots),
                shape(cx, slots),
                shape(LANES, slots, dtype=BF16),
                shape(1, slots),
                shape(2 * cx + 16, cy),
            ],
            [lanes_sent[0], held_y, base, base_other, lanes_each, own_blocks],
            "rim",
            400000,
            scratch=[pltpu.VMEM((LANES, LANES), F32)],
        )
        *rim, rim_sent = rim
        rim_got = exchange(rim_sent, sizes, next_y(0, 0))
        (parcel,) = observe(
            [shape(2 * levels, slots)],
            [*rows_got, inner, lower, inverse, ratio, in_row, in_lane, *rows_sent, *lanes_sent, *lanes_got]
            + [*rim[:4], rim[6]],
            scratch=[pltpu.VMEM((LANES, LANES), F32), pltpu.VMEM((levels, LANES), F32)],
        )
        parcel_other = other_core(parcel)
        parcel_other, rim_got, *x_got = lax.optimization_barrier((parcel_other, rim_got, *x_got))
        band_sent = call(
            functools.partial(weigh_kernel, sizes, plan, carried, levels),
            band_shapes,
            [parcel, parcel_other, columns, live, rim[4], rim[7], own_blocks, *x_got, in_row, in_lane]
            + [base, base_other, rim[5], rim_got, *fields, *rows_got, *lanes_got],
            "weigh",
            500000,
        )
        lanes_own = [lanes_each, rim_got]
        held, *_ = lax.optimization_barrier((tracer, *band_sent))
    else:
        rows_got = [exchange(rows_sent[n], sizes, next_x(n)) for n in range(2)]
        pair_got = [exchange(s, sizes, jump(*p)) for s, p in zip(pair_sent, plan["pairs"])]
        base_other = other_core(base)
        modeled, state = observe(
            [shape(1, slots), shape(2, slots)],
            [*rows_got, inner, lower, inverse, ratio, in_row, in_lane, *rows_sent, *lanes_sent, *lanes_got]
            + [columns, live, own_blocks, *pair_got]
            + [other_core(jnp.concatenate(pair_got, axis=0))],
        )
        near, *rims_sent = call(
            functools.partial(force_kernel, plan),
            [shape(2 * carried, cx, cy)] + [shape(cx, cy)] * y_ops,
            [modeled, other_core(modeled), state, in_row, in_lane, base, base_other],
            "force",
            200000,
        )
        rims_got = [exchange(rims_sent[n], sizes, next_y(n, 0)) for n in range(y_ops)]
        band_sent = call(
            functools.partial(surface_kernel, sizes, plan, carried, levels),
            band_shapes,
            [near, *fields, *rows_got, *lanes_got, *rims_got],
            "surface",
            400000,
        )
        lanes_own = [*lanes_sent, *lanes_got]
        held = tracer
    (advanced,) = call(
        functools.partial(advance_kernel, plan),
        [shape(*tracer.shape)],
        [held, parts, lower, inverse, ratio]
        + list(rows_sent)
        + rows_got
        + lanes_own
        + list(lanes_sent)
        + lanes_got,
        "advance",
        6000000,
        scratch=[pltpu.VMEM(tracer.shape, F32)]
        + [pltpu.VMEM((carried * levels, cy), F32)] * 2
        + [pltpu.SemaphoreType.DMA((levels // 4,))],
        out_hbm=(0,),
    )
    band_got = [
        s
        if first == second == 0
        else exchange(s, sizes, jump(first * many_y, second * many_y, plan["cross"]))
        for s, (first, second) in zip(band_sent, plan["bands"])
    ]
    tables = [regrid_index.reshape(taps, ll), regrid_weight.reshape(taps, ll)]
    kinds = [first == second for first, second in plan["bands"]]

    def regridded(bands, blocks, *more):
        return call(
            functools.partial(regrid_kernel, sizes, plan, bands, carried, cx, band),
            [shape(carried, ll)],
            [*tables, *blocks, *more],
            "regrid",
            1000000,
        )[0]

    near = [(pair, 0, 0) for pair, kind in zip(plan["bands"], kinds) if kind]
    far = [pair for pair, kind in zip(plan["bands"], kinds) if not kind]
    near_got = [got for got, kind in zip(band_got, kinds) if kind]
    far_got = [got for got, kind in zip(band_got, kinds) if not kind]
    advanced, near_got, far_got = lax.optimization_barrier((advanced, near_got, far_got))
    far_fetched = [other_core(got) for got in far_got]
    mine = carried if plan["cross"] else 0
    partial = regridded(near + [(pair, 0, mine) for pair in far], near_got + far_got)
    latlon = regridded([(pair, 1, carried - mine) for pair in far], far_fetched, partial)
    return (advanced, latlon[:, None, None, :])


def solution(mesh):
    in_specs = (
        P("lev", "groups", "facex", "facey"),
        P("groups", "facex", "facey"),
        P("groups", "facex", "facey"),
        P("groups", "facex", "facey"),
        P("lev", "groups", "facex", "facey"),
        P("facex", "facey"),
        P("facex", "facey", "groups", None),
        P("facex", "facey", "groups"),
        P("facex", "facey", "groups", None, None),
        P("facex", "facey", "groups", None),
        P("facex", "facey", "groups", None),
        P("facex", "facey", None, None),
        P("facex", "facey", None, None),
    )
    out_specs = (P("lev", "groups", "facex", "facey"), P("lev", "facex", "facey", "groups"))
    sizes = tuple(mesh.shape[axis] for axis in GROUP)
    return jax.shard_map(
        functools.partial(local, sizes), mesh=mesh, in_specs=in_specs, out_specs=out_specs, check_vma=False
    )
```

```python
import functools

import jax
import jax.numpy as jnp
from jax import lax
from jax.experimental import pallas as pl
from jax.experimental.pallas import tpu as pltpu
from jax.sharding import PartitionSpec as P

F32 = jnp.float32
BF16 = jnp.bfloat16
LANES = 128


def call(body, outs, ins, name, flops, smem=(), hbm=(), scratch=(), out_hbm=()):
    moved = sum(4 * a.size for a in ins) + sum(4 * o.size for o in outs)
    ins = [pltpu.with_memory_space_constraint(a, pltpu.HBM) if i in hbm else a for i, a in enumerate(ins)]

    def space(number):
        return pltpu.SMEM if number in smem else pltpu.HBM if number in hbm else pltpu.VMEM

    return pl.pallas_call(
        body,
        out_shape=outs,
        in_specs=[pl.BlockSpec(memory_space=space(i)) for i in range(len(ins))],
        out_specs=[
            pl.BlockSpec(memory_space=pltpu.HBM if i in out_hbm else pltpu.VMEM) for i in range(len(outs))
        ],
        scratch_shapes=scratch,
        compiler_params=pltpu.CompilerParams(vmem_limit_bytes=40 << 20),
        cost_estimate=pl.CostEstimate(flops=flops, bytes_accessed=moved, transcendentals=0),
        name=name,
    )(*ins)


def shape(*dims, dtype=F32):
    return jax.ShapeDtypeStruct(dims, dtype)


def iota(dims, axis):
    return lax.broadcasted_iota(jnp.int32, dims, axis)


def halves(values):
    high = values.astype(BF16)
    return high, (values - high.astype(F32)).astype(BF16)


def tile_of(sizes):
    return lax.axis_index("facex") * sizes[1] + lax.axis_index("facey")


def is_even(axis):
    return lax.rem(lax.axis_index(axis), 2) == 0


def up(values):
    rows = values.shape[0]
    rolled = pltpu.roll(values, rows - 1, 0)
    return jnp.where(iota(values.shape, 0) == rows - 1, 0.0, rolled)


def right(values):
    rolled = pltpu.roll(values, 1, 1)
    return jnp.where(iota(values.shape, 1) == 0, 0.0, rolled)


def left(values):
    lanes = values.shape[1]
    rolled = pltpu.roll(values, lanes - 1, 1)
    return jnp.where(iota(values.shape, 1) == lanes - 1, 0.0, rolled)


def shares(west, south):
    east, north = up(west), left(south)
    middle = 1.0 + jnp.minimum(west, 0.0) - jnp.maximum(east, 0.0)
    middle = middle + jnp.minimum(south, 0.0) - jnp.maximum(north, 0.0)
    row, lane = iota(west.shape, 0), iota(west.shape, 1)
    return (
        middle,
        jnp.where(row == 0, 0.0, jnp.maximum(west, 0.0)),
        -jnp.minimum(east, 0.0),
        jnp.where(lane == 0, 0.0, jnp.maximum(south, 0.0)),
        -jnp.minimum(north, 0.0),
    )


def mix(parts, cells):
    rows, lanes = cells.shape
    middle, west, east, south, north = parts
    total = middle * cells + west * pltpu.roll(cells, 1, 0) + east * pltpu.roll(cells, rows - 1, 0)
    return total + south * pltpu.roll(cells, 1, 1) + north * pltpu.roll(cells, lanes - 1, 1)


def pack_kernel(sizes, plan, *refs):
    sources, refs = refs[:10], refs[10:]
    lanes_out, refs = refs[: plan["y_ops"]], refs[plan["y_ops"] :]
    own_out, refs = refs[0], refs[1:]
    block_outs, refs = refs[: len(plan["pairs"])], refs[len(plan["pairs"]) :]
    cell_out, live_out, tracer, west, south, scale, mixing, *refs = refs
    kernels, observed, weights, cells, counts, done = refs
    carried, levels, cx, cy = tracer.shape
    me = tile_of(sizes)
    copies = [
        pltpu.make_async_copy(source, target, done.at[number])
        for number, (source, target) in enumerate(
            zip(sources[1:], (west, south, scale, kernels, observed, weights, cells, counts, mixing))
        )
    ]
    copies += [
        pltpu.make_async_copy(sources[0].at[t], tracer.at[t], done.at[9 + t]) for t in range(carried)
    ]
    for number in (3, 4, 5, 6, 7, 1, 0, 8, *range(9, 9 + carried), 2):
        copies[number].start()

    def block(offset):
        where_to = jnp.bitwise_xor(me, offset)
        mine = kernels[where_to]
        last = jnp.concatenate(
            [
                observed[pl.ds(where_to, 1), :],
                weights[pl.ds(where_to, 1), :],
                jnp.zeros((6, mine.shape[1]), F32),
            ],
            axis=0,
        )
        return jnp.concatenate([mine[8 * g : 8 * g + 8] for g in range(levels // 8)] + [last], axis=1)

    for number in (3, 4, 5):
        copies[number].wait()
    for number, offset in enumerate(plan["y_blocks"]):
        at = plan["y_tiles"] * cx + 8 * number
        lanes_out[0][at : at + 8, :] = block(offset)
    for number, offset in enumerate(plan["own_blocks"]):
        own_out[8 * number : 8 * number + 8, :] = block(offset)
    first_core = lax.axis_index("lev") == 0
    for out, (for_first, for_second) in zip(block_outs, plan["pairs"]):
        out[...] = block(jnp.where(first_core, for_first, for_second))

    owners, cap = cells.shape
    slot = iota((1, cap), 1)
    copies[6].wait()
    copies[7].wait()
    cell_parts = []
    live_parts = []
    for offset in range(owners):
        owner = jnp.bitwise_xor(me, offset)
        cell_parts.append(cells[pl.ds(owner, 1), :])
        live_parts.append(jnp.where(slot < counts[owner], 1.0, 0.0))
    cell = jnp.concatenate(cell_parts, axis=1)
    live = jnp.concatenate(live_parts, axis=1)
    cell_out[...] = cell
    live_out[...] = live
    if plan["relay"]:
        at = plan["y_tiles"] * cx + 8 * len(plan["y_blocks"])
        strips = owners * cap // LANES
        for number in range(strips):
            part = slice(number * LANES, (number + 1) * LANES)
            lanes_out[0][at + number : at + number + 1, :] = cell[:, part].astype(F32)
            lanes_out[0][at + strips + number : at + strips + number + 1, :] = live[:, part]

    for number in (1, 0, 8):
        copies[number].wait()
    lane = iota((cx, cy), 1)
    if plan["relay"]:
        edge = edge_of(0, cy)
        inner = jnp.where(edge == 0, 1, cy - 2)
        tiles = {name: LanePacker(lane, at) for name, at in zip("cdvwuk", (edge, inner, edge, inner, edge, edge))}
        for level in range(levels):
            turned = pltpu.roll(south[level], level, 1) if level else south[level]
            tiles["v"].put(level, turned)
            tiles["w"].put(level, turned)
            tiles["u"].put(level, pltpu.roll(west[level], level, 1) if level else west[level])
            if level < levels - 1:
                tiles["k"].put(level, pltpu.roll(mixing[level], level, 1) if level else mixing[level])
        totals = None
        for t in range(carried):
            copies[9 + t].wait()
            totals = [tracer[t, level] + (totals[level] if t else 0.0) for level in range(levels)]
        for level in range(levels):
            turned = pltpu.roll(totals[level], level, 1) if level else totals[level]
            tiles["c"].put(level, turned)
            tiles["d"].put(level, turned)
        packed = jnp.zeros((cx, cy), F32)
        for name in "cdvwu":
            packed = packed + tiles[name].packed(plan["lane_" + name])
        lanes_out[0][0:cx, :] = packed
        lanes_out[0][cx : 2 * cx, :] = tiles["k"].packed(0)
    else:
        edges = [LanePacker(lane, edge_of(number, cy)) for number in range(len(lanes_out))]
        for t in range(carried):
            copies[9 + t].wait()
        for f in range(carried + 1):
            for level in range(levels):
                spot = f * levels + level
                values = tracer[f, level] if f < carried else south[level]
                for tile in edges:
                    tile.put(spot, pltpu.roll(values, spot, 1) if spot else values)
        for tile, out in zip(edges, lanes_out):
            out[0:cx, :] = tile.packed(0)
    copies[2].wait()


class LanePacker:
    def __init__(self, lane, edge):
        self.lanes = lane.shape[1]
        self.back = lax.rem(2 * self.lanes - edge, self.lanes)
        self.place = lax.rem(lane + self.back, self.lanes)
        self.tile = jnp.zeros(lane.shape, F32)

    def put(self, spot, turned):
        self.tile = jnp.where(self.place == spot, turned, self.tile)

    def packed(self, start):
        return pltpu.roll(self.tile, lax.rem(self.back + start, self.lanes), 1)


def edge_of(number, lanes):
    even_y = is_even("facey")
    return jnp.where(even_y if number == 0 else jnp.logical_not(even_y), lanes - 1, 0)


def rows_kernel(plan, tracer, west, scale, blocks, *outs):
    carried, levels, cx, cy = tracer.shape
    head = (carried + 1) * levels
    if plan["relay"]:
        tile = LanePacker(iota((cx, cy), 1), edge_of(0, cy))
        for t in range(carried):
            for level in range(levels):
                spot = t * levels + level
                tile.put(spot, pltpu.roll(tracer[t, level], spot, 1) if spot else tracer[t, level])
        outs[2][...] = tile.packed(0)
    for number, out in enumerate(outs[:2]):
        row = sent_row(plan, number, cx)
        for level in range(levels):
            for t in range(carried):
                spot = t * levels + level
                out[spot : spot + 1, :] = tracer[t, level, pl.ds(row, 1), :]
            spot = carried * levels + level
            out[spot : spot + 1, :] = west[level, pl.ds(row, 1), :]
        out[head : head + 8, :] = jnp.broadcast_to(scale[pl.ds(row, 1), :], (8, cy))
        if plan["x_blocks"][number] and not plan["relay"]:
            at = 8 * plan["own_blocks"].index(plan["x_blocks"][number])
            out[head + 8 : head + 16, :] = blocks[at : at + 8, :]


def relay_kernel(plan, head, cx, number, rows, blocks, y_got, out):
    out[0 : head + 8, :] = rows[0 : head + 8, :]
    row = sent_row(plan, number, cx)
    out[head + 1 : head + 2, :] = y_got[pl.ds(row, 1), :]
    near, far = plan["x_blocks"]
    even_x = is_even("facex")
    offset = jnp.where(even_x if number == 0 else jnp.logical_not(even_x), near, far)
    at = plan["y_tiles"] * cx + 8 * (offset - plan["y_blocks"][0])
    out[head + 8 : head + 24, :] = blocks[pl.ds(pl.multiple_of(8 * offset, 8), 16), :]
    out[head + 24 : head + 40, :] = y_got[pl.ds(pl.multiple_of(at, 8), 16), :]


def beyond_kernel(plan, cx, blocks, y_got, *outs):
    for out, offset in zip(outs, plan["x_ops"]):
        at = plan["y_tiles"] * cx + 8 * (offset - plan["y_blocks"][0])
        out[0:16, :] = blocks[8 * offset : 8 * offset + 16, :]
        out[16:32, :] = y_got[at : at + 16, :]


def rim_kernel(plan, carried, levels, cx, y_sent, y_got, base, base_other, lanes, own, *refs):
    inverse_out, ratio_out, lower_out, pieces_out, columns_out, rows_out, picks_out, live_out, base_out, square = refs
    cy = y_got.shape[1]
    slots = live_out.shape[1]

    def turned(values):
        square[...] = jnp.zeros((LANES, LANES), F32)
        square[0:cx, :] = values
        return jnp.transpose(square[...])

    def part(values, name):
        return values[plan["lane_" + name] : plan["lane_" + name] + levels]

    beyond = turned(y_got[0:cx, :])
    mine = turned(y_sent[0:cx, :])
    coupling = turned(y_got[cx : 2 * cx, :])
    north = is_even("facey")
    pieces_out[0] = part(beyond, "c")
    pieces_out[1] = part(beyond, "u")
    pieces_out[2] = part(beyond, "v")
    pieces_out[3] = jnp.where(north, part(beyond, "w"), part(mine, "v"))
    pieces_out[4] = jnp.where(north, part(mine, "c"), part(beyond, "d"))
    pieces_out[5] = jnp.where(north, part(beyond, "d"), part(mine, "c"))

    def level_of(ref, level):
        return jnp.broadcast_to(ref[level : level + 1, :], (8, LANES))

    square[...] = coupling
    first = []
    ratios = []
    before = None
    for level in range(levels):
        diagonal = jnp.ones((8, LANES), F32)
        if level > 0:
            below = level_of(square, level - 1)
            diagonal = diagonal + below
        if level < levels - 1:
            diagonal = diagonal + level_of(square, level)
        if level > 0:
            diagonal = diagonal - below * below * before
        inverse = 1.0 / diagonal
        ratios.append(level_of(square, level) * inverse if level < levels - 1 else jnp.zeros((8, LANES), F32))
        lower = below * inverse if level > 0 else jnp.zeros((8, LANES), F32)
        lower_out[level : level + 1, :] = lower[0:1]
        inverse_out[level : level + 1, :] = inverse[0:1]
        ratio_out[level : level + 1, :] = ratios[-1][0:1]
        first.append(inverse if level == 0 else lower * first[-1])
        before = inverse
    weight = first
    for level in range(levels - 2, -1, -1):
        weight[level] = first[level] + ratios[level] * weight[level + 1]
    for level in range(levels):
        square[level : level + 1, :] = weight[level][0:1]
    weights = square[0:levels, :]
    tile = LanePacker(iota((cx, cy), 1), edge_of(0, cy))
    for t in range(2 * carried):
        values = base[t] if t < carried else base_other[t - carried]
        tile.put(t, pltpu.roll(values, t, 1) if t else values)
    base_out[0:cx, :] = tile.packed(0)
    base_out[cx : 2 * cx, :] = lanes[...]
    base_out[2 * cx :, :] = own[0:16, :]
    at = plan["y_tiles"] * cx + 8 * len(plan["y_blocks"])
    strips = slots // LANES
    cell = jnp.concatenate([y_got[at + n : at + n + 1, :] for n in range(strips)], axis=1).astype(jnp.int32)
    live_out[...] = jnp.concatenate([y_got[at + strips + n : at + strips + n + 1, :] for n in range(strips)], axis=1)
    on_edge = lax.rem(cell, cy) == jnp.where(north, 0, cy - 1)
    x_of = jnp.where(on_edge, lax.div(cell, cy), LANES)
    picks = jnp.where(iota((LANES, slots), 0) == x_of, 1.0, 0.0)
    rows_out[...] = picks[0:cx]
    picks = picks.astype(BF16)
    picks_out[...] = picks
    high, low = halves(weights)
    columns_out[...] = jnp.dot(high, picks, preferred_element_type=F32) + jnp.dot(
        low, picks, preferred_element_type=F32
    )


def factor_kernel(sizes, *refs):
    (tracer, west, south, mixing, adjoint, cells) = refs[:6]
    inverse_out, lower_out, ratio_out, base_out, inner_out, shares_out, columns_out, rows_out, picks_out = refs[6:]
    carried, levels, cx, cy = tracer.shape
    slots = cells.shape[1]
    first = []
    before = None
    for level in range(levels):
        diagonal = jnp.ones((cx, cy), F32)
        if level > 0:
            diagonal = diagonal + mixing[level - 1]
        if level < levels - 1:
            diagonal = diagonal + mixing[level]
        if level > 0:
            diagonal = diagonal - mixing[level - 1] * mixing[level - 1] * before
        inverse = 1.0 / diagonal
        inverse_out[level] = inverse
        if level < levels - 1:
            ratio_out[level] = mixing[level] * inverse
        lower = mixing[level - 1] * inverse if level > 0 else jnp.zeros((cx, cy), F32)
        lower_out[level] = lower
        first.append(inverse if level == 0 else lower * first[-1])
        before = inverse
    ratio_out[levels - 1] = jnp.zeros((cx, cy), F32)
    weight = first
    for level in range(levels - 2, -1, -1):
        weight[level] = first[level] + ratio_out[level] * weight[level + 1]
    for t in range(carried):
        total = weight[0] * adjoint[t, 0]
        for level in range(1, levels):
            total = total + weight[level] * adjoint[t, level]
        base_out[t] = total
    for level in range(levels):
        total = tracer[0, level]
        for t in range(1, carried):
            total = total + tracer[t, level]
        parts = shares(west[level], south[level])
        for number, part in enumerate(parts):
            shares_out[number, level] = part
        inner_out[level] = mix(parts, total)
    cell = cells[...]
    x_of = lax.div(cell, cy)
    y_of = lax.rem(cell, cy)
    in_row = jnp.where(iota((cx, slots), 0) == x_of, 1.0, 0.0)
    in_lane = jnp.where(iota((cy, slots), 0) == y_of, 1.0, 0.0).astype(BF16)
    rows_out[...] = in_row
    picks_out[...] = in_lane
    high, low = halves(jnp.concatenate(weight, axis=0))
    picked = jnp.dot(high, in_lane, preferred_element_type=F32)
    picked = picked + jnp.dot(low, in_lane, preferred_element_type=F32)
    for level in range(levels):
        part = picked[level * cx : (level + 1) * cx] * in_row
        columns_out[level : level + 1, :] = jnp.sum(part, axis=0, keepdims=True)


def sides(plan, first, second):
    if plan["relay"]:
        return first, second
    even_x = is_even("facex")
    return jnp.where(even_x, second, first), jnp.where(even_x, first, second)


def own_sides(plan, first, second):
    return (second, first) if plan["relay"] else sides(plan, first, second)


def sent_row(plan, number, rows):
    if plan["relay"]:
        return rows - 1 if number == 0 else 0
    even_x = is_even("facex")
    return jnp.where(even_x if number == 0 else jnp.logical_not(even_x), rows - 1, 0)


def seam(number, sent, got, sent_face, got_face):
    even_y = is_even("facey")
    north = even_y if number == 0 else jnp.logical_not(even_y)
    to_north = -(jnp.maximum(got_face, 0.0) * sent + jnp.minimum(got_face, 0.0) * got)
    to_south = jnp.maximum(sent_face, 0.0) * got
    return jnp.where(north, to_north, to_south), jnp.where(north, sent.shape[1] - 1, 0)


def spread_wind(values, start, carried, levels):
    lane = iota(values.shape, 1)
    result = jnp.zeros_like(values)
    for t in range(carried):
        moved = pltpu.roll(values, (t * levels - start) % values.shape[1], 1)
        inside = jnp.logical_and(lane >= t * levels, lane < (t + 1) * levels)
        result = jnp.where(inside, moved, result)
    return result


def seam_lanes(number, plan, sent, got, sent_wind, got_wind, carried, levels):
    start = plan["lane_v"]
    faces = [spread_wind(wind, start, carried, levels) for wind in (sent_wind, got_wind)]
    return seam(number, sent, got, *faces)


def block_groups(blocks, cap):
    per_tile = LANES // cap
    group_of_lane = lax.div(iota((8, LANES), 1), cap)
    groups = []
    for group in range(per_tile):
        tiles = []
        for start in range(0, len(blocks), per_tile):
            tile = jnp.zeros((8, LANES), F32)
            for a in range(per_tile):
                moved = pltpu.roll(blocks[start + a], (cap * (a - group)) % LANES, 1)
                tile = jnp.where(group_of_lane == a, moved, tile)
            tiles.append(tile)
        groups.append(jnp.concatenate(tiles, axis=1))
    return groups


def relayed_blocks(plan, head, own, beyond, got, x_got):
    def block_at(ref, row):
        return ref[row : row + 8, :]

    blocks = {0: block_at(own, 0), 1: block_at(beyond, 8)}
    rim_blocks = {0: block_at(beyond, 0), 1: block_at(own, 8)}
    even_x = is_even("facex")
    from_west, from_east = (got[n][head + 8 : head + 40, :] for n in range(2))
    carriers = [
        (plan["x_blocks"][0], jnp.where(even_x, from_east, from_west)),
        (plan["x_blocks"][1], jnp.where(even_x, from_west, from_east)),
    ]
    carriers += [(offset, ref[...]) for offset, ref in zip(plan["x_ops"], x_got)]
    for offset, values in carriers:
        blocks[offset], rim_blocks[offset + 1] = block_at(values, 0), block_at(values, 8)
        rim_blocks[offset], blocks[offset + 1] = block_at(values, 16), block_at(values, 24)
    return blocks, rim_blocks


def observe_kernel(sizes, plan, carried, *refs):
    refs = list(refs)
    got = refs[0:2]
    inner, lower, inverse, ratio, in_row, in_lane = refs[2:8]
    sent = refs[8:10]
    refs = refs[10:]
    y_sent = refs[: plan["y_ops"]]
    y_got = refs[plan["y_ops"] : 2 * plan["y_ops"]]
    refs = refs[2 * plan["y_ops"] :]
    if plan["relay"]:
        rim_inverse, rim_ratio, rim_lower, pieces, rim_picks, parcel, rows_out, turn, rise = refs
    else:
        columns, live, own, *refs = refs
        n_pairs = len(plan["pairs"])
        pair_got = refs[:n_pairs]
        swapped = refs[n_pairs] if n_pairs else None
        modeled_out, state_out = refs[-2:]
    levels, cx, cy = inner.shape
    slots = in_row.shape[1]
    head = (carried + 1) * levels

    def summed(rows):
        total = rows[0:levels]
        for t in range(1, carried):
            total = total + rows[t * levels : (t + 1) * levels]
        return total

    beyond_west, beyond_east = sides(plan, got[0][0:head], got[1][0:head])
    at_west, at_east = own_sides(plan, sent[0][0:head], sent[1][0:head])
    spot = carried * levels
    face_west = at_west[spot:head]
    face_east = beyond_east[spot:head]
    from_west = jnp.maximum(face_west, 0.0) * summed(beyond_west)
    from_east = -(
        jnp.maximum(face_east, 0.0) * summed(at_east) + jnp.minimum(face_east, 0.0) * summed(beyond_east)
    )
    lane_parts = []
    for number in range(plan["y_ops"]):
        mine, beyond = y_sent[number][0:cx, :], y_got[number][0:cx, :]
        if plan["relay"]:
            faces = [pltpu.roll(values, cy - plan["lane_v"], 1) for values in (mine, beyond)]
            total, spot_y = seam(number, mine, beyond, *faces)
        else:
            part, spot_y = seam_lanes(number, plan, mine, beyond, mine, beyond, carried, levels)
            total = part
            for t in range(1, carried):
                total = total + pltpu.roll(part, (-t * levels) % cy, 1)
        lane_parts.append((pltpu.roll(total, spot_y, 1), spot_y))
    lane = iota((cx, cy), 1)
    row = iota((cx, cy), 0)
    forward = []
    for level in range(levels):
        value = inner[level]
        value = value + jnp.where(row == 0, from_west[level : level + 1], 0.0)
        value = value + jnp.where(row == cx - 1, from_east[level : level + 1], 0.0)
        for total, spot_y in lane_parts:
            moved = pltpu.roll(total, cy - level, 1) if level else total
            value = value + jnp.where(lane == spot_y, moved, 0.0)
        value = value * inverse[level]
        forward.append(value + lower[level] * forward[-1] if level else value)
    result = forward
    for level in range(levels - 2, -1, -1):
        result[level] = forward[level] + ratio[level] * result[level + 1]
    high, low = halves(jnp.concatenate(result, axis=0))
    picks = in_lane[...]
    picked = jnp.dot(high, picks, preferred_element_type=F32)
    picked = picked + jnp.dot(low, picks, preferred_element_type=F32)

    if not plan["relay"]:
        start = plan["y_tiles"] * cx
        blocks = {0: own[0:8, :], plan["y_blocks"][0]: y_got[0][start : start + 8, :]}
        for number in range(2):
            offset = plan["x_blocks"][number]
            if offset:
                blocks[offset] = got[number][head + 8 : head + 16, :]
        first_core = lax.axis_index("lev") == 0
        for number, (for_first, for_second) in enumerate(plan["pairs"]):
            mine = pair_got[number][...]
            other = swapped[8 * number : 8 * number + 8, :]
            if for_first == for_second:
                blocks[for_first] = mine
            else:
                blocks[for_first] = jnp.where(first_core, mine, other)
                blocks[for_second] = jnp.where(first_core, other, mine)
        *groups, last = block_groups(blocks, slots // len(blocks))
        total = jnp.zeros((cx, slots), F32)
        sensitivity = jnp.zeros((8, slots), F32)
        for g, kernel in enumerate(groups):
            sensitivity = sensitivity + kernel * columns[8 * g : 8 * g + 8, :]
            for l in range(8):
                level = 8 * g + l
                total = total + kernel[l : l + 1] * picked[level * cx : (level + 1) * cx]
        modeled_out[...] = jnp.sum(total * in_row[...], axis=0, keepdims=True)
        gain = jnp.sum(sensitivity, axis=0, keepdims=True) * last[1:2] * live[...]
        state_out[...] = jnp.concatenate([gain, last[0:1]], axis=0)
        return

    chosen = in_row[...]
    for level in range(levels):
        part = picked[level * cx : (level + 1) * cx] * chosen
        parcel[level : level + 1, :] = jnp.sum(part, axis=0, keepdims=True)

    corners_west, corners_east = sides(plan, got[0][head + 1 : head + 2, :], got[1][head + 1 : head + 2, :])
    turn[...] = jnp.zeros((LANES, LANES), F32)
    turn[0:1, :] = corners_west
    turn[cx - 1 : cx, :] = corners_east
    turned = jnp.transpose(turn[...])
    ends = turned[plan["lane_c"] : plan["lane_c"] + levels]
    end_face = turned[plan["lane_u"] : plan["lane_u"] + levels]
    place = iota((levels, LANES), 1)
    cells, face_w, face_s, face_n, south_cells, north_cells = (pieces[n] for n in range(6))
    west_cells = jnp.where(place == 0, ends, pltpu.roll(cells, 1, 1))
    east_cells = jnp.where(place == cx - 1, ends, pltpu.roll(cells, LANES - 1, 1))
    face_e = jnp.where(place == cx - 1, end_face, pltpu.roll(face_w, LANES - 1, 1))
    rise[0:levels, :] = advance_cells(
        cells, west_cells, east_cells, south_cells, north_cells, face_w, face_e, face_s, face_n
    )

    def level_of(ref, level):
        return jnp.broadcast_to(ref[level : level + 1, :], (8, LANES))

    climbed = []
    for level in range(levels):
        value = level_of(rise, level) * level_of(rim_inverse, level)
        climbed.append(value + level_of(rim_lower, level) * climbed[-1] if level else value)
    for level in range(levels - 2, -1, -1):
        climbed[level] = climbed[level] + level_of(rim_ratio, level) * climbed[level + 1]
    for level in range(levels):
        rise[level : level + 1, :] = climbed[level][0:1]
    high, low = halves(rise[0:levels, :])
    picks = rim_picks[...]
    picked = jnp.dot(high, picks, preferred_element_type=F32)
    picked = picked + jnp.dot(low, picks, preferred_element_type=F32)
    parcel[levels : 2 * levels, :] = picked
    rows = carried * levels
    for number in range(2):
        rows_out[number * rows : (number + 1) * rows, :] = got[number][0:rows, :]


def advance_cells(cells, west, east, south, north, face_w, face_e, face_s, face_n):
    flux_w = jnp.maximum(face_w, 0.0) * west + jnp.minimum(face_w, 0.0) * cells
    flux_e = jnp.maximum(face_e, 0.0) * cells + jnp.minimum(face_e, 0.0) * east
    flux_s = jnp.maximum(face_s, 0.0) * south + jnp.minimum(face_s, 0.0) * cells
    flux_n = jnp.maximum(face_n, 0.0) * cells + jnp.minimum(face_n, 0.0) * north
    return cells + flux_w - flux_e + flux_s - flux_n


def scatter(force, in_row, in_lane):
    high, low = halves(in_row * force)
    dims = (((1,), (1,)), ((), ()))
    scattered = lax.dot_general(high, in_lane, dims, preferred_element_type=F32)
    return scattered + lax.dot_general(low, in_lane, dims, preferred_element_type=F32)


def force_kernel(plan, *refs):
    modeled, modeled_other, state, in_row, in_lane, base, base_other = refs[:7]
    near_out = refs[7]
    rim_outs = refs[8:]
    carried, cx, cy = base.shape
    misfit = modeled[...] + modeled_other[...] - state[1:2, :]
    force = state[0:1, :] * misfit
    scattered = scatter(force, in_row[...], in_lane[...])
    lane = iota((cx, cy), 1)
    even_y = is_even("facey")
    edges = []
    for number in range(len(rim_outs)):
        sends_last = even_y if number == 0 else jnp.logical_not(even_y)
        edges.append(jnp.where(sends_last, cy - 1, 0))
    rims = [jnp.zeros((cx, cy), F32) for _ in rim_outs]
    for t in range(2 * carried):
        values = scattered + (base[t] if t < carried else base_other[t - carried])
        near_out[t] = values
        for number, edge in enumerate(edges):
            moved = pltpu.roll(values, lax.rem(t + cy - edge, cy), 1)
            rims[number] = jnp.where(lane == t, moved, rims[number])
    for rim, out in zip(rims, rim_outs):
        out[...] = rim


def surface_kernel(sizes, plan, carried, levels, *refs):
    y_ops = plan["y_ops"]
    near = refs[0]
    rims = refs[6 + y_ops : 6 + 2 * y_ops]
    rim_values = [[rim[...] for rim in rims] for _ in range(near.shape[0])]
    values = [near[t] for t in range(near.shape[0])]
    spread_surface(
        sizes, plan, carried, levels, values, rim_values, refs[1:4], refs[4:6], refs[6 : 6 + y_ops], refs[6 + 2 * y_ops :]
    )


def weigh_kernel(sizes, plan, carried, levels, *refs):
    parcel, other, columns, live, rim_columns, rim_live, own, *refs = refs
    x_got, refs = refs[: len(plan["x_ops"])], refs[len(plan["x_ops"]) :]
    in_row, in_lane, base, base_other, rim_rows, rim_base = refs[:6]
    cx, cy = base.shape[1:]
    slots = live.shape[1]

    def force(blocks, start, weights, used):
        *groups, last = block_groups(blocks, slots // len(blocks))
        seen = jnp.zeros((8, slots), F32)
        sensitivity = jnp.zeros((8, slots), F32)
        for g, kernel in enumerate(groups):
            part = slice(start + 8 * g, start + 8 * g + 8)
            seen = seen + kernel * (parcel[part, :] + other[part, :])
            sensitivity = sensitivity + kernel * weights[8 * g : 8 * g + 8, :]
        modeled = jnp.sum(seen, axis=0, keepdims=True)
        gain = jnp.sum(sensitivity, axis=0, keepdims=True) * last[1:2] * used[...]
        return gain * (modeled - last[0:1])

    blocks, rim_blocks = relayed_blocks(
        plan, (carried + 1) * levels, own, rim_base[2 * cx :, :], refs[9:11], x_got
    )
    scattered = scatter(force(blocks, 0, columns, live), in_row[...], in_lane[...])
    on_rim = jnp.sum(rim_rows[...] * force(rim_blocks, levels, rim_columns, rim_live), axis=1, keepdims=True)
    near = [scattered + base[t] for t in range(carried)]
    near += [scattered + base_other[t] for t in range(carried)]
    rims = [[rim_base[0:cx, :] + on_rim] for _ in near]
    spread_surface(sizes, plan, carried, levels, near, rims, refs[6:9], refs[9:11], refs[11:12], refs[12:])


def spread_surface(sizes, plan, carried, levels, near, rim_values, fields, got, y_got, outs):
    west, south, scale = fields
    tracers = len(near)
    cx, cy = near[0].shape
    spot_v = plan["lane_v"]
    band = cy // sizes[0]
    per_tile = min(tracers, LANES // band)
    spot = carried * levels
    head = (carried + 1) * levels
    lane = iota((cx, cy), 1)
    row = iota((cx, cy), 0)
    even_y = is_even("facey")
    face_west = west[...]
    face_south = south[...]
    scales = scale[...]
    beyond_west, beyond_east = sides(plan, got[0][head : head + 1], got[1][head : head + 1])
    _, east_wind = sides(plan, got[0][spot : spot + 1], got[1][spot : spot + 1])
    face_east = jnp.where(row == cx - 1, east_wind, pltpu.roll(face_west, cx - 1, 0))
    face_north = left(face_south)
    norths = []
    for number in range(plan["y_ops"]):
        norths.append(even_y if number == 0 else jnp.logical_not(even_y))
        moved = pltpu.roll(y_got[number][0:cx, :], cy - 1 - spot_v, 1)
        keep = jnp.logical_and(lane == cy - 1, norths[number])
        face_north = jnp.where(keep, moved, face_north)
    to_middle = 1.0 + jnp.minimum(face_west, 0.0) - jnp.maximum(face_east, 0.0)
    to_middle = scales * (to_middle + jnp.minimum(face_south, 0.0) - jnp.maximum(face_north, 0.0))
    to_east = jnp.where(row == cx - 1, 0.0, scales * jnp.maximum(face_east, 0.0))
    to_west = jnp.where(row == 0, 0.0, scales * jnp.minimum(face_west, 0.0))
    to_north = scales * jnp.maximum(face_north, 0.0)
    to_south = scales * jnp.minimum(face_south, 0.0)
    west_gain = beyond_west * jnp.maximum(face_west[0:1], 0.0)
    east_gain = -beyond_east * jnp.minimum(face_east[cx - 1 : cx], 0.0)
    filler = jnp.zeros((6, cy), F32)
    grown = []
    for t in range(tracers):
        values = near[t]
        north_side = left(values)
        south_side = right(values)
        for number in range(plan["y_ops"]):
            rim = rim_values[t][number]
            at_north = jnp.logical_and(lane == cy - 1, norths[number])
            at_south = jnp.logical_and(lane == 0, jnp.logical_not(norths[number]))
            north_side = jnp.where(at_north, pltpu.roll(rim, (cy - 1 - t) % cy, 1), north_side)
            south_side = jnp.where(at_south, pltpu.roll(rim, (-t) % cy, 1), south_side)
        swept = to_middle * values + to_east * pltpu.roll(values, cx - 1, 0) - to_west * pltpu.roll(values, 1, 0)
        swept = swept + to_north * north_side - to_south * south_side
        grown.append(
            jnp.concatenate(
                [swept, west_gain * values[0:1], east_gain * values[cx - 1 : cx], filler], axis=0
            )
        )
    rows = cx + 8
    group_of_lane = lax.div(iota((rows, cy), 1), band)
    first_core = lax.axis_index("lev") == 0
    place = lax.axis_index("facex")
    for out, (for_first, for_second) in zip(outs, plan["bands"]):
        offset = for_first if for_first == for_second else jnp.where(first_core, for_first, for_second)
        target = jnp.bitwise_xor(place, offset)
        count = carried if for_first == for_second else tracers
        skip = carried if for_first == for_second != 0 and plan["cross"] else 0
        for start in range(0, count, per_tile):
            tile = jnp.zeros((rows, cy), F32)
            for a in range(min(per_tile, count - start)):
                moved = pltpu.roll(grown[skip + start + a], lax.rem(band * a + cy - band * target, cy), 1)
                tile = jnp.where(group_of_lane == a, moved, tile)
            out[start // per_tile * rows : (start // per_tile + 1) * rows, :] = tile


def regrid_kernel(sizes, plan, bands, carried, cx, band, *refs):
    index, weight = refs[:2]
    blocks, more, out = refs[2 : 2 + len(bands)], refs[2 + len(bands) : -1], refs[-1]
    taps, cells = index.shape
    rows = cx + 8
    per_tile = min(2 * carried, LANES // band)
    lane = iota((rows, LANES), 1)
    row = iota((rows, cells), 0)
    first_core = lax.axis_index("lev") == 0
    place = lax.axis_index("facex")
    around = sizes[0] * cx
    parts = []
    row_places = []
    for block, ((for_first, for_second), fetched, first) in zip(blocks, bands):
        if plan["cross"] != fetched:
            for_first, for_second = for_second, for_first
        offset = for_first if for_first == for_second else jnp.where(first_core, for_first, for_second)
        start = jnp.bitwise_xor(place, offset) * cx
        places = start + row
        places = jnp.where(row == cx, lax.rem(start + around - 1, around), places)
        places = jnp.where(row == cx + 1, lax.rem(start + cx, around), places)
        row_places.append(places)
        for t in range(first, first + carried):
            tile = block[t // per_tile * rows : (t // per_tile + 1) * rows, :]
            a = t % per_tile
            values = tile if a == 0 else pltpu.roll(tile, (-band * a) % LANES, 1)
            high = values.astype(BF16).astype(F32)
            low = pltpu.roll(values - high, band, 1)
            both = jnp.where(lane < band, high, jnp.where(lane < 2 * band, low, 0.0))
            parts.append(both.astype(BF16))
    left_side = jnp.concatenate(parts, axis=0)
    spread = iota((LANES, cells), 0)
    in_band = lax.rem(spread, band)
    used = spread < 2 * band
    totals = [jnp.zeros((rows, cells), F32) for _ in range(carried)]
    for tap in range(taps):
        place_of = index[tap : tap + 1, :]
        column = lax.div(place_of, band)
        in_lane = lax.rem(place_of, band)
        picks = jnp.where(jnp.logical_and(in_band == in_lane, used), 1.0, 0.0).astype(BF16)
        picked = jnp.dot(left_side, picks, preferred_element_type=F32)
        at = 0
        for places in row_places:
            chosen = jnp.where(places == column, weight[tap : tap + 1, :], 0.0)
            for t in range(carried):
                totals[t] = totals[t] + chosen * picked[at : at + rows]
                at += rows
    sums = jnp.concatenate([jnp.sum(total, axis=0, keepdims=True) for total in totals], axis=0)
    for ref in more:
        sums = sums + ref[...]
    out[...] = sums


def advance_kernel(plan, *refs):
    tracer, parts, lower, inverse, ratio = refs[:5]
    sent = refs[5:7]
    got = refs[7:9]
    swapped, *refs = refs[9:]
    y_ops = plan["y_ops"]
    y_sent, y_got, winds_sent, winds_got = (refs[n * y_ops : (n + 1) * y_ops] for n in range(4))
    target, out, west_rows, east_rows, done = refs[-5:]
    carried, levels, cx, cy = tracer.shape
    head = (carried + 1) * levels
    spot = carried * levels
    face_west, _ = own_sides(plan, sent[0][spot:head, :], sent[1][spot:head, :])
    _, face_east = sides(plan, got[0][spot:head, :], got[1][spot:head, :])
    each = [got[number][0:spot, :] for number in range(2)]
    if plan["cross"]:
        each = [swapped[number * spot : (number + 1) * spot, :] for number in range(2)]
    beyond_west, beyond_east = sides(plan, *each)
    _, at_east = own_sides(plan, sent[0][0:spot, :], sent[1][0:spot, :])
    for t in range(carried):
        part = slice(t * levels, (t + 1) * levels)
        west_rows[part, :] = jnp.maximum(face_west, 0.0) * beyond_west[part]
        east_rows[part, :] = -(
            jnp.maximum(face_east, 0.0) * at_east[part] + jnp.minimum(face_east, 0.0) * beyond_east[part]
        )
    lane = iota((cx, cy), 1)
    row = iota((cx, cy), 0)
    seams = [
        seam_lanes(
            n,
            plan,
            y_sent[n][0:cx, :],
            y_got[n][cx : 2 * cx, :] if plan["relay"] else y_got[n][0:cx, :],
            winds_sent[n][0:cx, :],
            winds_got[n][0:cx, :],
            carried,
            levels,
        )
        for n in range(y_ops)
    ]
    stride = 4

    def forward(step, before):
        mixed = []
        for k in range(stride):
            level = step * stride + k
            weights = [parts[n, level] for n in range(5)]
            mixed.append([])
            for t in range(carried):
                value = mix(weights, tracer[t, level])
                value = value + jnp.where(row == 0, west_rows[pl.ds(t * levels + level, 1), :], 0.0)
                value = value + jnp.where(row == cx - 1, east_rows[pl.ds(t * levels + level, 1), :], 0.0)
                for packed, spot_y in seams:
                    moved = pltpu.roll(packed, lax.rem(spot_y - (t * levels + level) + 2 * cy, cy), 1)
                    value = value + jnp.where(lane == spot_y, moved, 0.0)
                mixed[k].append(value)
        for k in range(stride):
            level = step * stride + k
            from_below = lower[level]
            scaled = inverse[level]
            after = []
            for t in range(carried):
                value = mixed[k][t] * scaled + from_below * before[t]
                out[t, level] = value
                after.append(value)
            before = after
        return tuple(before)

    def copy(step):
        part = pl.ds(levels - (step + 1) * stride, stride)
        return pltpu.make_async_copy(out.at[:, part], target.at[:, part], done.at[step])

    start = tuple(jnp.zeros((cx, cy), F32) for _ in range(carried))
    lax.fori_loop(0, levels // stride, forward, start)
    above = list(start)
    for step in range(levels // stride):
        for k in range(stride):
            level = levels - 1 - step * stride - k
            factor = ratio[level]
            for t in range(carried):
                above[t] = out[t, level] + factor * above[t]
                out[t, level] = above[t]
        copy(step).start()
    for step in range(levels // stride):
        copy(step).wait()


GROUP = ("facex", "facey", "lev")


def exchange(values, sizes, rule):
    many_x, many_y, cores = sizes
    pairs = []
    for x in range(many_x):
        for y in range(many_y):
            for c in range(cores):
                to = rule(x, y, c)
                if to is not None:
                    pairs.append(((x * many_y + y) * cores + c, (to[0] * many_y + to[1]) * cores + to[2]))
    return lax.ppermute(values, GROUP, pairs)


def make_plan(sizes):
    many_x, many_y, _ = sizes
    tiles = many_x * many_y
    x_blocks = [many_y, (many_x - 1) * many_y if many_x == 4 else 0]
    relay = many_y == 2 and many_x == 4
    if relay:
        own_blocks = list(range(tiles))
        y_blocks = own_blocks[2:]
        x_ops = [offset for offset in own_blocks[2::2] if offset not in x_blocks]
        pairs = []
    else:
        own_blocks = [0] + [offset for offset in x_blocks if offset]
        y_blocks = [1]
        x_ops = []
        rest = [d for d in range(tiles) if d not in {1, *own_blocks}]
        rest.sort(key=lambda d: (d // many_y != many_x // 2, d))
        pairs = [(rest[n], rest[min(n + 1, len(rest) - 1)]) for n in range(0, len(rest), 2)]
    others = list(range(many_x - 1, 1, -1))
    bands = [(0, 0), (1, 1)] + [(others[n + 1], others[n]) for n in range(0, len(others), 2)]
    return {
        "relay": relay,
        "cross": 1 if relay else 0,
        "x_blocks": x_blocks,
        "x_ops": x_ops,
        "own_blocks": own_blocks,
        "y_blocks": y_blocks,
        "y_ops": 1 if many_y == 2 else 2,
        "y_tiles": 2 if relay else 1,
        "pairs": pairs,
        "bands": bands,
    }


def lane_plan(plan, carried, levels):
    starts = {"c": 0, "d": levels, "v": 2 * levels, "w": 3 * levels, "u": 4 * levels}
    if not plan["relay"]:
        starts = {"v": carried * levels}
    return {"lane_" + name: start for name, start in starts.items()}


def local(
    sizes,
    tracer,
    west_courant,
    south_courant,
    mixing,
    adjoint_later,
    emission_scale,
    send_cells,
    send_counts,
    kernels,
    observed,
    error_weight,
    regrid_index,
    regrid_weight,
):
    plan = make_plan(sizes)
    many_x, many_y, _ = sizes
    carried, levels, cx, cy = tracer.shape
    owners, cap = send_cells.shape[2:]
    slots = owners * cap
    taps, ll = regrid_index.shape[2:]
    plan.update(lane_plan(plan, carried, levels))
    head = (carried + 1) * levels
    y_ops = plan["y_ops"]
    band = cy // many_x

    def next_x(number):
        def rule(x, y, c):
            step = 1 if (plan["relay"] or x % 2 == 0) == (number == 0) else -1
            return ((x + step) % many_x, y, c ^ plan["cross"])

        return rule

    def next_y(number, cross):
        def rule(x, y, c):
            to = y + (1 if (y % 2 == 0) == (number == 0) else -1)
            return (x, to, c ^ cross) if 0 <= to < many_y else None

        return rule

    def jump(for_first, for_second, cross=0):
        def rule(x, y, c):
            d = for_first if c == 0 else for_second
            return (x ^ (d // many_y), y ^ (d % many_y), c ^ cross)

        return rule

    def other_core(values):
        return exchange(values, sizes, lambda x, y, c: (x, y, 1 - c))

    strips = slots // LANES
    plan["parcel"] = -(-2 * strips // 8) * 8
    extra = 40 if plan["relay"] else 16
    row_shapes = [shape(head + extra, cy)] * 2
    y_rows = plan["y_tiles"] * cx + 8 * len(plan["y_blocks"]) + (plan["parcel"] if plan["relay"] else 0)
    lane_shapes = [shape(y_rows if n == 0 else cx, cy) for n in range(y_ops)]
    packed = call(
        functools.partial(pack_kernel, sizes, plan),
        lane_shapes
        + [shape(8 * len(plan["own_blocks"]), LANES)]
        + [shape(8, LANES)] * len(plan["pairs"])
        + [shape(1, slots, dtype=jnp.int32), shape(1, slots)]
        + [shape(*a.shape) for a in (tracer, west_courant, south_courant, emission_scale, mixing)],
        [
            tracer,
            west_courant,
            south_courant,
            emission_scale,
            kernels.reshape(owners, levels, cap),
            observed.reshape(owners, cap),
            error_weight.reshape(owners, cap),
            send_cells.reshape(owners, cap),
            send_counts.reshape(owners),
            mixing,
        ],
        "pack",
        100000,
        hbm=range(10),
        scratch=[
            pltpu.VMEM((owners, levels, cap), F32),
            pltpu.VMEM((owners, cap), F32),
            pltpu.VMEM((owners, cap), F32),
            pltpu.VMEM((owners, cap), jnp.int32),
            pltpu.SMEM((owners,), jnp.int32),
            pltpu.SemaphoreType.DMA((9 + carried,)),
        ],
    )
    lanes_sent = packed[:y_ops]
    own_blocks = packed[y_ops]
    pair_sent = packed[1 + y_ops : -7]
    cell, live, tracer, west_courant, south_courant, emission_scale, mixing = packed[-7:]
    lanes_got = [exchange(lanes_sent[n], sizes, next_y(n, plan["cross"])) for n in range(y_ops)]
    held, *_ = lax.optimization_barrier((tracer, *lanes_sent))
    inverse, lower, ratio, base, inner, parts, columns, in_row, in_lane = call(
        functools.partial(factor_kernel, sizes),
        [
            shape(levels, cx, cy),
            shape(levels, cx, cy),
            shape(levels, cx, cy),
            shape(carried, cx, cy),
            shape(levels, cx, cy),
            shape(5, levels, cx, cy),
            shape(levels, slots),
            shape(cx, slots),
            shape(cy, slots, dtype=BF16),
        ],
        [held, west_courant, south_courant, mixing, adjoint_later, cell],
        "factor",
        3000000,
    )
    rows_sent = list(
        call(
            functools.partial(rows_kernel, plan),
            row_shapes + ([shape(cx, cy)] if plan["relay"] else []),
            [tracer, west_courant, emission_scale, own_blocks],
            "rows",
            100000,
        )
    )
    per_tile = min(2 * carried, LANES // band)

    def band_shape(first, second):
        count = carried if first == second else 2 * carried
        return shape(-(-count // per_tile) * (cx + 8), cy)

    band_shapes = [band_shape(*b) for b in plan["bands"]]
    fields = [west_courant[0], south_courant[0], emission_scale]
    observe = functools.partial(
        call, functools.partial(observe_kernel, sizes, plan, carried), name="observe", flops=2000000
    )
    if plan["relay"]:
        base, *lanes_got = lax.optimization_barrier((base, *lanes_got))
        lanes_each = rows_sent.pop()
        base_other = other_core(base)

        def relay(number, *after):
            held, *_ = lax.optimization_barrier((rows_sent[number], *after))
            return call(
                functools.partial(relay_kernel, plan, head, cx, number),
                [row_shapes[number]],
                [held, own_blocks, lanes_got[0]],
                "relay",
                10000,
            )[0]

        rows_sent = [relay(0), relay(1)]
        x_sent = call(
            functools.partial(beyond_kernel, plan, cx),
            [shape(32, LANES)] * len(plan["x_ops"]),
            [own_blocks, lanes_got[0]],
            "beyond",
            10000,
        )
        x_got = [exchange(s, sizes, jump(d, d, 1)) for s, d in zip(x_sent, plan["x_ops"])]
        rows_got = [exchange(rows_sent[n], sizes, next_x(n)) for n in range(2)]
        held_y, *_ = lax.optimization_barrier((lanes_got[0], *rows_sent))
        rim = call(
            functools.partial(rim_kernel, plan, carried, levels, cx),
            [
                shape(levels, LANES),
                shape(levels, LANES),
                shape(levels, LANES),
                shape(6, levels, LANES),
                shape(levels, slots),
                shape(cx, slots),
                shape(LANES, slots, dtype=BF16),
                shape(1, slots),
                shape(2 * cx + 16, cy),
            ],
            [lanes_sent[0], held_y, base, base_other, lanes_each, own_blocks],
            "rim",
            400000,
            scratch=[pltpu.VMEM((LANES, LANES), F32)],
        )
        *rim, rim_sent = rim
        rim_got = exchange(rim_sent, sizes, next_y(0, 0))
        parcel, rows_crossed = observe(
            [shape(2 * levels, slots), shape(2 * carried * levels, cy)],
            [*rows_got, inner, lower, inverse, ratio, in_row, in_lane, *rows_sent, *lanes_sent, *lanes_got]
            + [*rim[:4], rim[6]],
            scratch=[pltpu.VMEM((LANES, LANES), F32), pltpu.VMEM((levels, LANES), F32)],
        )
        parcel_other = other_core(parcel)
        rows_swapped = other_core(rows_crossed)
        parcel_other, rim_got, *x_got = lax.optimization_barrier((parcel_other, rim_got, *x_got))
        band_sent = call(
            functools.partial(weigh_kernel, sizes, plan, carried, levels),
            band_shapes,
            [parcel, parcel_other, columns, live, rim[4], rim[7], own_blocks, *x_got, in_row, in_lane]
            + [base, base_other, rim[5], rim_got, *fields, *rows_got, *lanes_got],
            "weigh",
            500000,
        )
        lanes_own = [lanes_each, rim_got]
        held, *_ = lax.optimization_barrier((tracer, *band_sent))
    else:
        rows_got = [exchange(rows_sent[n], sizes, next_x(n)) for n in range(2)]
        pair_got = [exchange(s, sizes, jump(*p)) for s, p in zip(pair_sent, plan["pairs"])]
        base_other = other_core(base)
        modeled, state = observe(
            [shape(1, slots), shape(2, slots)],
            [*rows_got, inner, lower, inverse, ratio, in_row, in_lane, *rows_sent, *lanes_sent, *lanes_got]
            + [columns, live, own_blocks, *pair_got]
            + [other_core(jnp.concatenate(pair_got, axis=0))],
        )
        near, *rims_sent = call(
            functools.partial(force_kernel, plan),
            [shape(2 * carried, cx, cy)] + [shape(cx, cy)] * y_ops,
            [modeled, other_core(modeled), state, in_row, in_lane, base, base_other],
            "force",
            200000,
        )
        rims_got = [exchange(rims_sent[n], sizes, next_y(n, 0)) for n in range(y_ops)]
        band_sent = call(
            functools.partial(surface_kernel, sizes, plan, carried, levels),
            band_shapes,
            [near, *fields, *rows_got, *lanes_got, *rims_got],
            "surface",
            400000,
        )
        lanes_own = [*lanes_sent, *lanes_got]
        rows_swapped = rows_got[0]
        held = tracer
    (advanced,) = call(
        functools.partial(advance_kernel, plan),
        [shape(*tracer.shape)],
        [held, parts, lower, inverse, ratio]
        + list(rows_sent)
        + rows_got
        + [rows_swapped]
        + lanes_own
        + list(lanes_sent)
        + lanes_got,
        "advance",
        6000000,
        scratch=[pltpu.VMEM(tracer.shape, F32)]
        + [pltpu.VMEM((carried * levels, cy), F32)] * 2
        + [pltpu.SemaphoreType.DMA((levels // 4,))],
        out_hbm=(0,),
    )
    band_got = [
        s
        if first == second == 0
        else exchange(s, sizes, jump(first * many_y, second * many_y, plan["cross"]))
        for s, (first, second) in zip(band_sent, plan["bands"])
    ]
    tables = [regrid_index.reshape(taps, ll), regrid_weight.reshape(taps, ll)]
    kinds = [first == second for first, second in plan["bands"]]

    def regridded(bands, blocks, *more):
        return call(
            functools.partial(regrid_kernel, sizes, plan, bands, carried, cx, band),
            [shape(carried, ll)],
            [*tables, *blocks, *more],
            "regrid",
            1000000,
        )[0]

    near = [(pair, 0, 0) for pair, kind in zip(plan["bands"], kinds) if kind]
    far = [pair for pair, kind in zip(plan["bands"], kinds) if not kind]
    near_got = [got for got, kind in zip(band_got, kinds) if kind]
    far_got = [got for got, kind in zip(band_got, kinds) if not kind]
    advanced, near_got, far_got = lax.optimization_barrier((advanced, near_got, far_got))
    far_fetched = [other_core(got) for got in far_got]
    mine = carried if plan["cross"] else 0
    partial = regridded(near + [(pair, 0, mine) for pair in far], near_got + far_got)
    latlon = regridded([(pair, 1, carried - mine) for pair in far], far_fetched, partial) if far else partial
    return (advanced, latlon[:, None, None, :])


def solution(mesh):
    in_specs = (
        P("lev", "groups", "facex", "facey"),
        P("groups", "facex", "facey"),
        P("groups", "facex", "facey"),
        P("groups", "facex", "facey"),
        P("lev", "groups", "facex", "facey"),
        P("facex", "facey"),
        P("facex", "facey", "groups", None),
        P("facex", "facey", "groups"),
        P("facex", "facey", "groups", None, None),
        P("facex", "facey", "groups", None),
        P("facex", "facey", "groups", None),
        P("facex", "facey", None, None),
        P("facex", "facey", None, None),
    )
    out_specs = (P("lev", "groups", "facex", "facey"), P("lev", "facex", "facey", "groups"))
    sizes = tuple(mesh.shape[axis] for axis in GROUP)
    return jax.shard_map(
        functools.partial(local, sizes), mesh=mesh, in_specs=in_specs, out_specs=out_specs, check_vma=False
    )
```

```python
import functools

import jax
import jax.numpy as jnp
from jax import lax
from jax.experimental import pallas as pl
from jax.experimental.pallas import tpu as pltpu
from jax.sharding import PartitionSpec as P

F32 = jnp.float32
BF16 = jnp.bfloat16
LANES = 128


def call(body, outs, ins, name, flops, smem=(), hbm=(), scratch=(), out_hbm=()):
    moved = sum(4 * a.size for a in ins) + sum(4 * o.size for o in outs)
    ins = [pltpu.with_memory_space_constraint(a, pltpu.HBM) if i in hbm else a for i, a in enumerate(ins)]

    def space(number):
        return pltpu.SMEM if number in smem else pltpu.HBM if number in hbm else pltpu.VMEM

    return pl.pallas_call(
        body,
        out_shape=outs,
        in_specs=[pl.BlockSpec(memory_space=space(i)) for i in range(len(ins))],
        out_specs=[
            pl.BlockSpec(memory_space=pltpu.HBM if i in out_hbm else pltpu.VMEM) for i in range(len(outs))
        ],
        scratch_shapes=scratch,
        compiler_params=pltpu.CompilerParams(vmem_limit_bytes=40 << 20),
        cost_estimate=pl.CostEstimate(flops=flops, bytes_accessed=moved, transcendentals=0),
        name=name,
    )(*ins)


def shape(*dims, dtype=F32):
    return jax.ShapeDtypeStruct(dims, dtype)


def iota(dims, axis):
    return lax.broadcasted_iota(jnp.int32, dims, axis)


def halves(values):
    high = values.astype(BF16)
    return high, (values - high.astype(F32)).astype(BF16)


def tile_of(sizes):
    return lax.axis_index("facex") * sizes[1] + lax.axis_index("facey")


def is_even(axis):
    return lax.rem(lax.axis_index(axis), 2) == 0


def up(values):
    rows = values.shape[0]
    rolled = pltpu.roll(values, rows - 1, 0)
    return jnp.where(iota(values.shape, 0) == rows - 1, 0.0, rolled)


def right(values):
    rolled = pltpu.roll(values, 1, 1)
    return jnp.where(iota(values.shape, 1) == 0, 0.0, rolled)


def left(values):
    lanes = values.shape[1]
    rolled = pltpu.roll(values, lanes - 1, 1)
    return jnp.where(iota(values.shape, 1) == lanes - 1, 0.0, rolled)


def shares(west, south):
    east, north = up(west), left(south)
    middle = 1.0 + jnp.minimum(west, 0.0) - jnp.maximum(east, 0.0)
    middle = middle + jnp.minimum(south, 0.0) - jnp.maximum(north, 0.0)
    row, lane = iota(west.shape, 0), iota(west.shape, 1)
    return (
        middle,
        jnp.where(row == 0, 0.0, jnp.maximum(west, 0.0)),
        -jnp.minimum(east, 0.0),
        jnp.where(lane == 0, 0.0, jnp.maximum(south, 0.0)),
        -jnp.minimum(north, 0.0),
    )


def mix(parts, cells):
    rows, lanes = cells.shape
    middle, west, east, south, north = parts
    total = middle * cells + west * pltpu.roll(cells, 1, 0) + east * pltpu.roll(cells, rows - 1, 0)
    return total + south * pltpu.roll(cells, 1, 1) + north * pltpu.roll(cells, lanes - 1, 1)


def pack_kernel(sizes, plan, *refs):
    sources, refs = refs[:10], refs[10:]
    lanes_out, refs = refs[: plan["y_ops"]], refs[plan["y_ops"] :]
    own_out, refs = refs[0], refs[1:]
    block_outs, refs = refs[: len(plan["pairs"])], refs[len(plan["pairs"]) :]
    cell_out, live_out, tracer, west, south, scale, mixing, *refs = refs
    kernels, observed, weights, cells, counts, done = refs
    carried, levels, cx, cy = tracer.shape
    me = tile_of(sizes)
    copies = [
        pltpu.make_async_copy(source, target, done.at[number])
        for number, (source, target) in enumerate(
            zip(sources[1:], (west, south, scale, kernels, observed, weights, cells, counts, mixing))
        )
    ]
    copies += [
        pltpu.make_async_copy(sources[0].at[t], tracer.at[t], done.at[9 + t]) for t in range(carried)
    ]
    for number in (3, 4, 5, 6, 7, 1, 0, 8, *range(9, 9 + carried), 2):
        copies[number].start()

    def block(offset):
        where_to = jnp.bitwise_xor(me, offset)
        mine = kernels[where_to]
        last = jnp.concatenate(
            [
                observed[pl.ds(where_to, 1), :],
                weights[pl.ds(where_to, 1), :],
                jnp.zeros((6, mine.shape[1]), F32),
            ],
            axis=0,
        )
        return jnp.concatenate([mine[8 * g : 8 * g + 8] for g in range(levels // 8)] + [last], axis=1)

    for number in (3, 4, 5):
        copies[number].wait()
    for number, offset in enumerate(plan["y_blocks"]):
        at = plan["y_tiles"] * cx + 8 * number
        lanes_out[0][at : at + 8, :] = block(offset)
    for number, offset in enumerate(plan["own_blocks"]):
        own_out[8 * number : 8 * number + 8, :] = block(offset)
    first_core = lax.axis_index("lev") == 0
    for out, (for_first, for_second) in zip(block_outs, plan["pairs"]):
        out[...] = block(jnp.where(first_core, for_first, for_second))

    owners, cap = cells.shape
    slot = iota((1, cap), 1)
    copies[6].wait()
    copies[7].wait()
    cell_parts = []
    live_parts = []
    for offset in range(owners):
        owner = jnp.bitwise_xor(me, offset)
        cell_parts.append(cells[pl.ds(owner, 1), :])
        live_parts.append(jnp.where(slot < counts[owner], 1.0, 0.0))
    cell = jnp.concatenate(cell_parts, axis=1)
    live = jnp.concatenate(live_parts, axis=1)
    cell_out[...] = cell
    live_out[...] = live
    if plan["relay"]:
        at = plan["y_tiles"] * cx + 8 * len(plan["y_blocks"])
        strips = owners * cap // LANES
        for number in range(strips):
            part = slice(number * LANES, (number + 1) * LANES)
            lanes_out[0][at + number : at + number + 1, :] = cell[:, part].astype(F32)
            lanes_out[0][at + strips + number : at + strips + number + 1, :] = live[:, part]

    for number in (1, 0, 8):
        copies[number].wait()
    lane = iota((cx, cy), 1)
    if plan["relay"]:
        edge = edge_of(0, cy)
        inner = jnp.where(edge == 0, 1, cy - 2)
        tiles = {name: LanePacker(lane, at) for name, at in zip("cdvwuk", (edge, inner, edge, inner, edge, edge))}
        for level in range(levels):
            turned = pltpu.roll(south[level], level, 1) if level else south[level]
            tiles["v"].put(level, turned)
            tiles["w"].put(level, turned)
            tiles["u"].put(level, pltpu.roll(west[level], level, 1) if level else west[level])
            if level < levels - 1:
                tiles["k"].put(level, pltpu.roll(mixing[level], level, 1) if level else mixing[level])
        totals = None
        for t in range(carried):
            copies[9 + t].wait()
            totals = [tracer[t, level] + (totals[level] if t else 0.0) for level in range(levels)]
        for level in range(levels):
            turned = pltpu.roll(totals[level], level, 1) if level else totals[level]
            tiles["c"].put(level, turned)
            tiles["d"].put(level, turned)
        packed = jnp.zeros((cx, cy), F32)
        for name in "cdvwu":
            packed = packed + tiles[name].packed(plan["lane_" + name])
        lanes_out[0][0:cx, :] = packed
        lanes_out[0][cx : 2 * cx, :] = tiles["k"].packed(0)
    else:
        edges = [LanePacker(lane, edge_of(number, cy)) for number in range(len(lanes_out))]
        for t in range(carried):
            copies[9 + t].wait()
        for f in range(carried + 1):
            for level in range(levels):
                spot = f * levels + level
                values = tracer[f, level] if f < carried else south[level]
                for tile in edges:
                    tile.put(spot, pltpu.roll(values, spot, 1) if spot else values)
        for tile, out in zip(edges, lanes_out):
            out[0:cx, :] = tile.packed(0)
    copies[2].wait()


class LanePacker:
    def __init__(self, lane, edge):
        self.lanes = lane.shape[1]
        self.back = lax.rem(2 * self.lanes - edge, self.lanes)
        self.place = lax.rem(lane + self.back, self.lanes)
        self.tile = jnp.zeros(lane.shape, F32)

    def put(self, spot, turned):
        self.tile = jnp.where(self.place == spot, turned, self.tile)

    def packed(self, start):
        return pltpu.roll(self.tile, lax.rem(self.back + start, self.lanes), 1)


def edge_of(number, lanes):
    even_y = is_even("facey")
    return jnp.where(even_y if number == 0 else jnp.logical_not(even_y), lanes - 1, 0)


def rows_kernel(plan, tracer, west, scale, blocks, *outs):
    carried, levels, cx, cy = tracer.shape
    head = (carried + 1) * levels
    if plan["relay"]:
        tile = LanePacker(iota((cx, cy), 1), edge_of(0, cy))
        for t in range(carried):
            for level in range(levels):
                spot = t * levels + level
                tile.put(spot, pltpu.roll(tracer[t, level], spot, 1) if spot else tracer[t, level])
        outs[2][...] = tile.packed(0)
    for number, out in enumerate(outs[:2]):
        row = sent_row(plan, number, cx)
        for level in range(levels):
            for t in range(carried):
                spot = t * levels + level
                out[spot : spot + 1, :] = tracer[t, level, pl.ds(row, 1), :]
            spot = carried * levels + level
            out[spot : spot + 1, :] = west[level, pl.ds(row, 1), :]
        out[head : head + 8, :] = jnp.broadcast_to(scale[pl.ds(row, 1), :], (8, cy))
        if plan["x_blocks"][number] and not plan["relay"]:
            at = 8 * plan["own_blocks"].index(plan["x_blocks"][number])
            out[head + 8 : head + 16, :] = blocks[at : at + 8, :]


def relay_kernel(plan, head, cx, number, rows, blocks, y_got, out):
    out[0 : head + 8, :] = rows[0 : head + 8, :]
    row = sent_row(plan, number, cx)
    out[head + 1 : head + 2, :] = y_got[pl.ds(row, 1), :]
    near, far = plan["x_blocks"]
    even_x = is_even("facex")
    offset = jnp.where(even_x if number == 0 else jnp.logical_not(even_x), near, far)
    at = plan["y_tiles"] * cx + 8 * (offset - plan["y_blocks"][0])
    out[head + 8 : head + 24, :] = blocks[pl.ds(pl.multiple_of(8 * offset, 8), 16), :]
    out[head + 24 : head + 40, :] = y_got[pl.ds(pl.multiple_of(at, 8), 16), :]


def beyond_kernel(plan, cx, blocks, y_got, *outs):
    for out, offset in zip(outs, plan["x_ops"]):
        at = plan["y_tiles"] * cx + 8 * (offset - plan["y_blocks"][0])
        out[0:16, :] = blocks[8 * offset : 8 * offset + 16, :]
        out[16:32, :] = y_got[at : at + 16, :]


def rim_kernel(plan, carried, levels, cx, y_sent, y_got, base, base_other, lanes, own, *refs):
    inverse_out, ratio_out, lower_out, pieces_out, columns_out, rows_out, picks_out, live_out, base_out, square = refs
    cy = y_got.shape[1]
    slots = live_out.shape[1]

    def turned(values):
        square[...] = jnp.zeros((LANES, LANES), F32)
        square[0:cx, :] = values
        return jnp.transpose(square[...])

    def part(values, name):
        return values[plan["lane_" + name] : plan["lane_" + name] + levels]

    beyond = turned(y_got[0:cx, :])
    mine = turned(y_sent[0:cx, :])
    coupling = turned(y_got[cx : 2 * cx, :])
    north = is_even("facey")
    pieces_out[0] = part(beyond, "c")
    pieces_out[1] = part(beyond, "u")
    pieces_out[2] = part(beyond, "v")
    pieces_out[3] = jnp.where(north, part(beyond, "w"), part(mine, "v"))
    pieces_out[4] = jnp.where(north, part(mine, "c"), part(beyond, "d"))
    pieces_out[5] = jnp.where(north, part(beyond, "d"), part(mine, "c"))

    def level_of(ref, level):
        return jnp.broadcast_to(ref[level : level + 1, :], (8, LANES))

    square[...] = coupling
    first = []
    ratios = []
    before = None
    for level in range(levels):
        diagonal = jnp.ones((8, LANES), F32)
        if level > 0:
            below = level_of(square, level - 1)
            diagonal = diagonal + below
        if level < levels - 1:
            diagonal = diagonal + level_of(square, level)
        if level > 0:
            diagonal = diagonal - below * below * before
        inverse = 1.0 / diagonal
        ratios.append(level_of(square, level) * inverse if level < levels - 1 else jnp.zeros((8, LANES), F32))
        lower = below * inverse if level > 0 else jnp.zeros((8, LANES), F32)
        lower_out[level : level + 1, :] = lower[0:1]
        inverse_out[level : level + 1, :] = inverse[0:1]
        ratio_out[level : level + 1, :] = ratios[-1][0:1]
        first.append(inverse if level == 0 else lower * first[-1])
        before = inverse
    weight = first
    for level in range(levels - 2, -1, -1):
        weight[level] = first[level] + ratios[level] * weight[level + 1]
    for level in range(levels):
        square[level : level + 1, :] = weight[level][0:1]
    weights = square[0:levels, :]
    tile = LanePacker(iota((cx, cy), 1), edge_of(0, cy))
    for t in range(2 * carried):
        values = base[t] if t < carried else base_other[t - carried]
        tile.put(t, pltpu.roll(values, t, 1) if t else values)
    base_out[0:cx, :] = tile.packed(0)
    base_out[cx : 2 * cx, :] = lanes[...]
    base_out[2 * cx :, :] = own[0:16, :]
    at = plan["y_tiles"] * cx + 8 * len(plan["y_blocks"])
    strips = slots // LANES
    cell = jnp.concatenate([y_got[at + n : at + n + 1, :] for n in range(strips)], axis=1).astype(jnp.int32)
    live_out[...] = jnp.concatenate([y_got[at + strips + n : at + strips + n + 1, :] for n in range(strips)], axis=1)
    on_edge = lax.rem(cell, cy) == jnp.where(north, 0, cy - 1)
    x_of = jnp.where(on_edge, lax.div(cell, cy), LANES)
    picks = jnp.where(iota((LANES, slots), 0) == x_of, 1.0, 0.0)
    rows_out[...] = picks[0:cx]
    picks = picks.astype(BF16)
    picks_out[...] = picks
    high, low = halves(weights)
    columns_out[...] = jnp.dot(high, picks, preferred_element_type=F32) + jnp.dot(
        low, picks, preferred_element_type=F32
    )


def factor_kernel(sizes, *refs):
    (tracer, west, south, mixing, adjoint, cells) = refs[:6]
    inverse_out, lower_out, ratio_out, base_out, inner_out, shares_out, columns_out, rows_out, picks_out = refs[6:]
    carried, levels, cx, cy = tracer.shape
    slots = cells.shape[1]
    first = []
    before = None
    for level in range(levels):
        diagonal = jnp.ones((cx, cy), F32)
        if level > 0:
            diagonal = diagonal + mixing[level - 1]
        if level < levels - 1:
            diagonal = diagonal + mixing[level]
        if level > 0:
            diagonal = diagonal - mixing[level - 1] * mixing[level - 1] * before
        inverse = 1.0 / diagonal
        inverse_out[level] = inverse
        if level < levels - 1:
            ratio_out[level] = mixing[level] * inverse
        lower = mixing[level - 1] * inverse if level > 0 else jnp.zeros((cx, cy), F32)
        lower_out[level] = lower
        first.append(inverse if level == 0 else lower * first[-1])
        before = inverse
    ratio_out[levels - 1] = jnp.zeros((cx, cy), F32)
    weight = first
    for level in range(levels - 2, -1, -1):
        weight[level] = first[level] + ratio_out[level] * weight[level + 1]
    for t in range(carried):
        total = weight[0] * adjoint[t, 0]
        for level in range(1, levels):
            total = total + weight[level] * adjoint[t, level]
        base_out[t] = total
    for level in range(levels):
        total = tracer[0, level]
        for t in range(1, carried):
            total = total + tracer[t, level]
        parts = shares(west[level], south[level])
        for number, part in enumerate(parts):
            shares_out[number, level] = part
        inner_out[level] = mix(parts, total)
    cell = cells[...]
    x_of = lax.div(cell, cy)
    y_of = lax.rem(cell, cy)
    in_row = jnp.where(iota((cx, slots), 0) == x_of, 1.0, 0.0)
    in_lane = jnp.where(iota((cy, slots), 0) == y_of, 1.0, 0.0).astype(BF16)
    rows_out[...] = in_row
    picks_out[...] = in_lane
    high, low = halves(jnp.concatenate(weight, axis=0))
    picked = jnp.dot(high, in_lane, preferred_element_type=F32)
    picked = picked + jnp.dot(low, in_lane, preferred_element_type=F32)
    for level in range(levels):
        part = picked[level * cx : (level + 1) * cx] * in_row
        columns_out[level : level + 1, :] = jnp.sum(part, axis=0, keepdims=True)


def sides(plan, first, second):
    if plan["relay"]:
        return first, second
    even_x = is_even("facex")
    return jnp.where(even_x, second, first), jnp.where(even_x, first, second)


def own_sides(plan, first, second):
    return (second, first) if plan["relay"] else sides(plan, first, second)


def sent_row(plan, number, rows):
    if plan["relay"]:
        return rows - 1 if number == 0 else 0
    even_x = is_even("facex")
    return jnp.where(even_x if number == 0 else jnp.logical_not(even_x), rows - 1, 0)


def seam(number, sent, got, sent_face, got_face):
    even_y = is_even("facey")
    north = even_y if number == 0 else jnp.logical_not(even_y)
    to_north = -(jnp.maximum(got_face, 0.0) * sent + jnp.minimum(got_face, 0.0) * got)
    to_south = jnp.maximum(sent_face, 0.0) * got
    return jnp.where(north, to_north, to_south), jnp.where(north, sent.shape[1] - 1, 0)


def spread_wind(values, start, carried, levels):
    lane = iota(values.shape, 1)
    result = jnp.zeros_like(values)
    for t in range(carried):
        moved = pltpu.roll(values, (t * levels - start) % values.shape[1], 1)
        inside = jnp.logical_and(lane >= t * levels, lane < (t + 1) * levels)
        result = jnp.where(inside, moved, result)
    return result


def seam_lanes(number, plan, sent, got, sent_wind, got_wind, carried, levels):
    start = plan["lane_v"]
    faces = [spread_wind(wind, start, carried, levels) for wind in (sent_wind, got_wind)]
    return seam(number, sent, got, *faces)


def block_groups(blocks, cap):
    per_tile = LANES // cap
    group_of_lane = lax.div(iota((8, LANES), 1), cap)
    groups = []
    for group in range(per_tile):
        tiles = []
        for start in range(0, len(blocks), per_tile):
            tile = jnp.zeros((8, LANES), F32)
            for a in range(per_tile):
                moved = pltpu.roll(blocks[start + a], (cap * (a - group)) % LANES, 1)
                tile = jnp.where(group_of_lane == a, moved, tile)
            tiles.append(tile)
        groups.append(jnp.concatenate(tiles, axis=1))
    return groups


def relayed_blocks(plan, head, own, beyond, got, x_got):
    def block_at(ref, row):
        return ref[row : row + 8, :]

    blocks = {0: block_at(own, 0), 1: block_at(beyond, 8)}
    rim_blocks = {0: block_at(beyond, 0), 1: block_at(own, 8)}
    even_x = is_even("facex")
    from_west, from_east = (got[n][head + 8 : head + 40, :] for n in range(2))
    carriers = [
        (plan["x_blocks"][0], jnp.where(even_x, from_east, from_west)),
        (plan["x_blocks"][1], jnp.where(even_x, from_west, from_east)),
    ]
    carriers += [(offset, ref[...]) for offset, ref in zip(plan["x_ops"], x_got)]
    for offset, values in carriers:
        blocks[offset], rim_blocks[offset + 1] = block_at(values, 0), block_at(values, 8)
        rim_blocks[offset], blocks[offset + 1] = block_at(values, 16), block_at(values, 24)
    return blocks, rim_blocks


def observe_kernel(sizes, plan, carried, *refs):
    refs = list(refs)
    got = refs[0:2]
    inner, lower, inverse, ratio, in_row, in_lane = refs[2:8]
    sent = refs[8:10]
    refs = refs[10:]
    y_sent = refs[: plan["y_ops"]]
    y_got = refs[plan["y_ops"] : 2 * plan["y_ops"]]
    refs = refs[2 * plan["y_ops"] :]
    if plan["relay"]:
        rim_inverse, rim_ratio, rim_lower, pieces, rim_picks, parcel, rows_out, turn, rise = refs
    else:
        columns, live, own, *refs = refs
        n_pairs = len(plan["pairs"])
        pair_got = refs[:n_pairs]
        swapped = refs[n_pairs] if n_pairs else None
        modeled_out, state_out = refs[-2:]
    levels, cx, cy = inner.shape
    slots = in_row.shape[1]
    head = (carried + 1) * levels

    def summed(rows):
        total = rows[0:levels]
        for t in range(1, carried):
            total = total + rows[t * levels : (t + 1) * levels]
        return total

    beyond_west, beyond_east = sides(plan, got[0][0:head], got[1][0:head])
    at_west, at_east = own_sides(plan, sent[0][0:head], sent[1][0:head])
    spot = carried * levels
    face_west = at_west[spot:head]
    face_east = beyond_east[spot:head]
    from_west = jnp.maximum(face_west, 0.0) * summed(beyond_west)
    from_east = -(
        jnp.maximum(face_east, 0.0) * summed(at_east) + jnp.minimum(face_east, 0.0) * summed(beyond_east)
    )
    lane_parts = []
    for number in range(plan["y_ops"]):
        mine, beyond = y_sent[number][0:cx, :], y_got[number][0:cx, :]
        if plan["relay"]:
            faces = [pltpu.roll(values, cy - plan["lane_v"], 1) for values in (mine, beyond)]
            total, spot_y = seam(number, mine, beyond, *faces)
        else:
            part, spot_y = seam_lanes(number, plan, mine, beyond, mine, beyond, carried, levels)
            total = part
            for t in range(1, carried):
                total = total + pltpu.roll(part, (-t * levels) % cy, 1)
        lane_parts.append((pltpu.roll(total, spot_y, 1), spot_y))
    lane = iota((cx, cy), 1)
    row = iota((cx, cy), 0)
    forward = []
    for level in range(levels):
        value = inner[level]
        value = value + jnp.where(row == 0, from_west[level : level + 1], 0.0)
        value = value + jnp.where(row == cx - 1, from_east[level : level + 1], 0.0)
        for total, spot_y in lane_parts:
            moved = pltpu.roll(total, cy - level, 1) if level else total
            value = value + jnp.where(lane == spot_y, moved, 0.0)
        value = value * inverse[level]
        forward.append(value + lower[level] * forward[-1] if level else value)
    result = forward
    for level in range(levels - 2, -1, -1):
        result[level] = forward[level] + ratio[level] * result[level + 1]
    high, low = halves(jnp.concatenate(result, axis=0))
    picks = in_lane[...]
    picked = jnp.dot(high, picks, preferred_element_type=F32)
    picked = picked + jnp.dot(low, picks, preferred_element_type=F32)

    if not plan["relay"]:
        start = plan["y_tiles"] * cx
        blocks = {0: own[0:8, :], plan["y_blocks"][0]: y_got[0][start : start + 8, :]}
        for number in range(2):
            offset = plan["x_blocks"][number]
            if offset:
                blocks[offset] = got[number][head + 8 : head + 16, :]
        first_core = lax.axis_index("lev") == 0
        for number, (for_first, for_second) in enumerate(plan["pairs"]):
            mine = pair_got[number][...]
            other = swapped[8 * number : 8 * number + 8, :]
            if for_first == for_second:
                blocks[for_first] = mine
            else:
                blocks[for_first] = jnp.where(first_core, mine, other)
                blocks[for_second] = jnp.where(first_core, other, mine)
        *groups, last = block_groups(blocks, slots // len(blocks))
        total = jnp.zeros((cx, slots), F32)
        sensitivity = jnp.zeros((8, slots), F32)
        for g, kernel in enumerate(groups):
            sensitivity = sensitivity + kernel * columns[8 * g : 8 * g + 8, :]
            for l in range(8):
                level = 8 * g + l
                total = total + kernel[l : l + 1] * picked[level * cx : (level + 1) * cx]
        modeled_out[...] = jnp.sum(total * in_row[...], axis=0, keepdims=True)
        gain = jnp.sum(sensitivity, axis=0, keepdims=True) * last[1:2] * live[...]
        state_out[...] = jnp.concatenate([gain, last[0:1]], axis=0)
        return

    chosen = in_row[...]
    for level in range(levels):
        part = picked[level * cx : (level + 1) * cx] * chosen
        parcel[level : level + 1, :] = jnp.sum(part, axis=0, keepdims=True)

    corners_west, corners_east = sides(plan, got[0][head + 1 : head + 2, :], got[1][head + 1 : head + 2, :])
    turn[...] = jnp.zeros((LANES, LANES), F32)
    turn[0:1, :] = corners_west
    turn[cx - 1 : cx, :] = corners_east
    turned = jnp.transpose(turn[...])
    ends = turned[plan["lane_c"] : plan["lane_c"] + levels]
    end_face = turned[plan["lane_u"] : plan["lane_u"] + levels]
    place = iota((levels, LANES), 1)
    cells, face_w, face_s, face_n, south_cells, north_cells = (pieces[n] for n in range(6))
    west_cells = jnp.where(place == 0, ends, pltpu.roll(cells, 1, 1))
    east_cells = jnp.where(place == cx - 1, ends, pltpu.roll(cells, LANES - 1, 1))
    face_e = jnp.where(place == cx - 1, end_face, pltpu.roll(face_w, LANES - 1, 1))
    rise[0:levels, :] = advance_cells(
        cells, west_cells, east_cells, south_cells, north_cells, face_w, face_e, face_s, face_n
    )

    def level_of(ref, level):
        return jnp.broadcast_to(ref[level : level + 1, :], (8, LANES))

    climbed = []
    for level in range(levels):
        value = level_of(rise, level) * level_of(rim_inverse, level)
        climbed.append(value + level_of(rim_lower, level) * climbed[-1] if level else value)
    for level in range(levels - 2, -1, -1):
        climbed[level] = climbed[level] + level_of(rim_ratio, level) * climbed[level + 1]
    for level in range(levels):
        rise[level : level + 1, :] = climbed[level][0:1]
    high, low = halves(rise[0:levels, :])
    picks = rim_picks[...]
    picked = jnp.dot(high, picks, preferred_element_type=F32)
    picked = picked + jnp.dot(low, picks, preferred_element_type=F32)
    parcel[levels : 2 * levels, :] = picked
    rows = carried * levels
    for number in range(2):
        rows_out[number * rows : (number + 1) * rows, :] = got[number][0:rows, :]


def advance_cells(cells, west, east, south, north, face_w, face_e, face_s, face_n):
    flux_w = jnp.maximum(face_w, 0.0) * west + jnp.minimum(face_w, 0.0) * cells
    flux_e = jnp.maximum(face_e, 0.0) * cells + jnp.minimum(face_e, 0.0) * east
    flux_s = jnp.maximum(face_s, 0.0) * south + jnp.minimum(face_s, 0.0) * cells
    flux_n = jnp.maximum(face_n, 0.0) * cells + jnp.minimum(face_n, 0.0) * north
    return cells + flux_w - flux_e + flux_s - flux_n


def scatter(force, in_row, in_lane):
    high, low = halves(in_row * force)
    dims = (((1,), (1,)), ((), ()))
    scattered = lax.dot_general(high, in_lane, dims, preferred_element_type=F32)
    return scattered + lax.dot_general(low, in_lane, dims, preferred_element_type=F32)


def force_kernel(plan, *refs):
    modeled, modeled_other, state, in_row, in_lane, base, base_other = refs[:7]
    near_out = refs[7]
    rim_outs = refs[8:]
    carried, cx, cy = base.shape
    misfit = modeled[...] + modeled_other[...] - state[1:2, :]
    force = state[0:1, :] * misfit
    scattered = scatter(force, in_row[...], in_lane[...])
    lane = iota((cx, cy), 1)
    even_y = is_even("facey")
    edges = []
    for number in range(len(rim_outs)):
        sends_last = even_y if number == 0 else jnp.logical_not(even_y)
        edges.append(jnp.where(sends_last, cy - 1, 0))
    rims = [jnp.zeros((cx, cy), F32) for _ in rim_outs]
    for t in range(2 * carried):
        values = scattered + (base[t] if t < carried else base_other[t - carried])
        near_out[t] = values
        for number, edge in enumerate(edges):
            moved = pltpu.roll(values, lax.rem(t + cy - edge, cy), 1)
            rims[number] = jnp.where(lane == t, moved, rims[number])
    for rim, out in zip(rims, rim_outs):
        out[...] = rim


def surface_kernel(sizes, plan, carried, levels, *refs):
    y_ops = plan["y_ops"]
    near = refs[0]
    rims = refs[6 + y_ops : 6 + 2 * y_ops]
    rim_values = [[rim[...] for rim in rims] for _ in range(near.shape[0])]
    values = [near[t] for t in range(near.shape[0])]
    spread_surface(
        sizes, plan, carried, levels, values, rim_values, refs[1:4], refs[4:6], refs[6 : 6 + y_ops], refs[6 + 2 * y_ops :]
    )


def weigh_kernel(sizes, plan, carried, levels, *refs):
    parcel, other, columns, live, rim_columns, rim_live, own, *refs = refs
    x_got, refs = refs[: len(plan["x_ops"])], refs[len(plan["x_ops"]) :]
    in_row, in_lane, base, base_other, rim_rows, rim_base = refs[:6]
    cx, cy = base.shape[1:]
    slots = live.shape[1]

    def force(blocks, start, weights, used):
        *groups, last = block_groups(blocks, slots // len(blocks))
        seen = jnp.zeros((8, slots), F32)
        sensitivity = jnp.zeros((8, slots), F32)
        for g, kernel in enumerate(groups):
            part = slice(start + 8 * g, start + 8 * g + 8)
            seen = seen + kernel * (parcel[part, :] + other[part, :])
            sensitivity = sensitivity + kernel * weights[8 * g : 8 * g + 8, :]
        modeled = jnp.sum(seen, axis=0, keepdims=True)
        gain = jnp.sum(sensitivity, axis=0, keepdims=True) * last[1:2] * used[...]
        return gain * (modeled - last[0:1])

    blocks, rim_blocks = relayed_blocks(
        plan, (carried + 1) * levels, own, rim_base[2 * cx :, :], refs[9:11], x_got
    )
    scattered = scatter(force(blocks, 0, columns, live), in_row[...], in_lane[...])
    on_rim = jnp.sum(rim_rows[...] * force(rim_blocks, levels, rim_columns, rim_live), axis=1, keepdims=True)
    near = [scattered + base[t] for t in range(carried)]
    near += [scattered + base_other[t] for t in range(carried)]
    rims = [[rim_base[0:cx, :] + on_rim] for _ in near]
    spread_surface(sizes, plan, carried, levels, near, rims, refs[6:9], refs[9:11], refs[11:12], refs[12:])


def spread_surface(sizes, plan, carried, levels, near, rim_values, fields, got, y_got, outs):
    west, south, scale = fields
    tracers = len(near)
    cx, cy = near[0].shape
    spot_v = plan["lane_v"]
    band = cy // sizes[0]
    per_tile = min(tracers, LANES // band)
    spot = carried * levels
    head = (carried + 1) * levels
    lane = iota((cx, cy), 1)
    row = iota((cx, cy), 0)
    even_y = is_even("facey")
    face_west = west[...]
    face_south = south[...]
    scales = scale[...]
    beyond_west, beyond_east = sides(plan, got[0][head : head + 1], got[1][head : head + 1])
    _, east_wind = sides(plan, got[0][spot : spot + 1], got[1][spot : spot + 1])
    face_east = jnp.where(row == cx - 1, east_wind, pltpu.roll(face_west, cx - 1, 0))
    face_north = left(face_south)
    norths = []
    for number in range(plan["y_ops"]):
        norths.append(even_y if number == 0 else jnp.logical_not(even_y))
        moved = pltpu.roll(y_got[number][0:cx, :], cy - 1 - spot_v, 1)
        keep = jnp.logical_and(lane == cy - 1, norths[number])
        face_north = jnp.where(keep, moved, face_north)
    to_middle = 1.0 + jnp.minimum(face_west, 0.0) - jnp.maximum(face_east, 0.0)
    to_middle = scales * (to_middle + jnp.minimum(face_south, 0.0) - jnp.maximum(face_north, 0.0))
    to_east = jnp.where(row == cx - 1, 0.0, scales * jnp.maximum(face_east, 0.0))
    to_west = jnp.where(row == 0, 0.0, scales * jnp.minimum(face_west, 0.0))
    to_north = scales * jnp.maximum(face_north, 0.0)
    to_south = scales * jnp.minimum(face_south, 0.0)
    west_gain = beyond_west * jnp.maximum(face_west[0:1], 0.0)
    east_gain = -beyond_east * jnp.minimum(face_east[cx - 1 : cx], 0.0)
    filler = jnp.zeros((6, cy), F32)
    grown = []
    for t in range(tracers):
        values = near[t]
        north_side = left(values)
        south_side = right(values)
        for number in range(plan["y_ops"]):
            rim = rim_values[t][number]
            at_north = jnp.logical_and(lane == cy - 1, norths[number])
            at_south = jnp.logical_and(lane == 0, jnp.logical_not(norths[number]))
            north_side = jnp.where(at_north, pltpu.roll(rim, (cy - 1 - t) % cy, 1), north_side)
            south_side = jnp.where(at_south, pltpu.roll(rim, (-t) % cy, 1), south_side)
        swept = to_middle * values + to_east * pltpu.roll(values, cx - 1, 0) - to_west * pltpu.roll(values, 1, 0)
        swept = swept + to_north * north_side - to_south * south_side
        grown.append(
            jnp.concatenate(
                [swept, west_gain * values[0:1], east_gain * values[cx - 1 : cx], filler], axis=0
            )
        )
    rows = cx + 8
    group_of_lane = lax.div(iota((rows, cy), 1), band)
    first_core = lax.axis_index("lev") == 0
    place = lax.axis_index("facex")
    for out, (for_first, for_second) in zip(outs, plan["bands"]):
        offset = for_first if for_first == for_second else jnp.where(first_core, for_first, for_second)
        target = jnp.bitwise_xor(place, offset)
        count = carried if for_first == for_second else tracers
        skip = carried if for_first == for_second != 0 and plan["cross"] else 0
        for start in range(0, count, per_tile):
            tile = jnp.zeros((rows, cy), F32)
            for a in range(min(per_tile, count - start)):
                moved = pltpu.roll(grown[skip + start + a], lax.rem(band * a + cy - band * target, cy), 1)
                tile = jnp.where(group_of_lane == a, moved, tile)
            out[start // per_tile * rows : (start // per_tile + 1) * rows, :] = tile
        full = -(-count // per_tile) * rows
        if out.shape[0] > full:
            out[full:, :] = jnp.zeros((out.shape[0] - full, cy), F32)


def regrid_kernel(sizes, plan, bands, carried, cx, band, *refs):
    index, weight = refs[:2]
    blocks, more, out = refs[2 : 2 + len(bands)], refs[2 + len(bands) : -1], refs[-1]
    taps, cells = index.shape
    rows = cx + 8
    per_tile = min(2 * carried, LANES // band)
    lane = iota((rows, LANES), 1)
    row = iota((rows, cells), 0)
    first_core = lax.axis_index("lev") == 0
    place = lax.axis_index("facex")
    around = sizes[0] * cx
    parts = []
    row_places = []
    for block, ((for_first, for_second), fetched, first) in zip(blocks, bands):
        if plan["cross"] != fetched:
            for_first, for_second = for_second, for_first
        offset = for_first if for_first == for_second else jnp.where(first_core, for_first, for_second)
        start = jnp.bitwise_xor(place, offset) * cx
        places = start + row
        places = jnp.where(row == cx, lax.rem(start + around - 1, around), places)
        places = jnp.where(row == cx + 1, lax.rem(start + cx, around), places)
        row_places.append(places)
        for t in range(first, first + carried):
            tile = block[t // per_tile * rows : (t // per_tile + 1) * rows, :]
            a = t % per_tile
            values = tile if a == 0 else pltpu.roll(tile, (-band * a) % LANES, 1)
            high = values.astype(BF16).astype(F32)
            low = pltpu.roll(values - high, band, 1)
            both = jnp.where(lane < band, high, jnp.where(lane < 2 * band, low, 0.0))
            parts.append(both.astype(BF16))
    left_side = jnp.concatenate(parts, axis=0)
    spread = iota((LANES, cells), 0)
    in_band = lax.rem(spread, band)
    used = spread < 2 * band
    totals = [jnp.zeros((rows, cells), F32) for _ in range(carried)]
    for tap in range(taps):
        place_of = index[tap : tap + 1, :]
        column = lax.div(place_of, band)
        in_lane = lax.rem(place_of, band)
        picks = jnp.where(jnp.logical_and(in_band == in_lane, used), 1.0, 0.0).astype(BF16)
        picked = jnp.dot(left_side, picks, preferred_element_type=F32)
        at = 0
        for places in row_places:
            chosen = jnp.where(places == column, weight[tap : tap + 1, :], 0.0)
            for t in range(carried):
                totals[t] = totals[t] + chosen * picked[at : at + rows]
                at += rows
    sums = jnp.concatenate([jnp.sum(total, axis=0, keepdims=True) for total in totals], axis=0)
    for ref in more:
        sums = sums + ref[...]
    out[...] = sums


def advance_kernel(plan, *refs):
    tracer, parts, lower, inverse, ratio = refs[:5]
    sent = refs[5:7]
    got = refs[7:9]
    swapped, *refs = refs[9:]
    y_ops = plan["y_ops"]
    y_sent, y_got, winds_sent, winds_got = (refs[n * y_ops : (n + 1) * y_ops] for n in range(4))
    target, out, west_rows, east_rows, done = refs[-5:]
    carried, levels, cx, cy = tracer.shape
    head = (carried + 1) * levels
    spot = carried * levels
    face_west, _ = own_sides(plan, sent[0][spot:head, :], sent[1][spot:head, :])
    _, face_east = sides(plan, got[0][spot:head, :], got[1][spot:head, :])
    each = [got[number][0:spot, :] for number in range(2)]
    if plan["cross"]:
        each = [swapped[number * spot : (number + 1) * spot, :] for number in range(2)]
    beyond_west, beyond_east = sides(plan, *each)
    _, at_east = own_sides(plan, sent[0][0:spot, :], sent[1][0:spot, :])
    for t in range(carried):
        part = slice(t * levels, (t + 1) * levels)
        west_rows[part, :] = jnp.maximum(face_west, 0.0) * beyond_west[part]
        east_rows[part, :] = -(
            jnp.maximum(face_east, 0.0) * at_east[part] + jnp.minimum(face_east, 0.0) * beyond_east[part]
        )
    lane = iota((cx, cy), 1)
    row = iota((cx, cy), 0)
    seams = [
        seam_lanes(
            n,
            plan,
            y_sent[n][0:cx, :],
            y_got[n][cx : 2 * cx, :] if plan["relay"] else y_got[n][0:cx, :],
            winds_sent[n][0:cx, :],
            winds_got[n][0:cx, :],
            carried,
            levels,
        )
        for n in range(y_ops)
    ]
    stride = 4

    def forward(step, before):
        mixed = []
        for k in range(stride):
            level = step * stride + k
            weights = [parts[n, level] for n in range(5)]
            mixed.append([])
            for t in range(carried):
                value = mix(weights, tracer[t, level])
                value = value + jnp.where(row == 0, west_rows[pl.ds(t * levels + level, 1), :], 0.0)
                value = value + jnp.where(row == cx - 1, east_rows[pl.ds(t * levels + level, 1), :], 0.0)
                for packed, spot_y in seams:
                    moved = pltpu.roll(packed, lax.rem(spot_y - (t * levels + level) + 2 * cy, cy), 1)
                    value = value + jnp.where(lane == spot_y, moved, 0.0)
                mixed[k].append(value)
        for k in range(stride):
            level = step * stride + k
            from_below = lower[level]
            scaled = inverse[level]
            after = []
            for t in range(carried):
                value = mixed[k][t] * scaled + from_below * before[t]
                out[t, level] = value
                after.append(value)
            before = after
        return tuple(before)

    def copy(step):
        part = pl.ds(levels - (step + 1) * stride, stride)
        return pltpu.make_async_copy(out.at[:, part], target.at[:, part], done.at[step])

    start = tuple(jnp.zeros((cx, cy), F32) for _ in range(carried))
    lax.fori_loop(0, levels // stride, forward, start)
    above = list(start)
    for step in range(levels // stride):
        for k in range(stride):
            level = levels - 1 - step * stride - k
            factor = ratio[level]
            for t in range(carried):
                above[t] = out[t, level] + factor * above[t]
                out[t, level] = above[t]
        copy(step).start()
    for step in range(levels // stride):
        copy(step).wait()


GROUP = ("facex", "facey", "lev")


def exchange(values, sizes, rule):
    many_x, many_y, cores = sizes
    pairs = []
    for x in range(many_x):
        for y in range(many_y):
            for c in range(cores):
                to = rule(x, y, c)
                if to is not None:
                    pairs.append(((x * many_y + y) * cores + c, (to[0] * many_y + to[1]) * cores + to[2]))
    return lax.ppermute(values, GROUP, pairs)


def make_plan(sizes):
    many_x, many_y, _ = sizes
    tiles = many_x * many_y
    x_blocks = [many_y, (many_x - 1) * many_y if many_x == 4 else 0]
    relay = many_y == 2 and many_x == 4
    if relay:
        own_blocks = list(range(tiles))
        y_blocks = own_blocks[2:]
        x_ops = [offset for offset in own_blocks[2::2] if offset not in x_blocks]
        pairs = []
    else:
        own_blocks = [0] + [offset for offset in x_blocks if offset]
        y_blocks = [1]
        x_ops = []
        rest = [d for d in range(tiles) if d not in {1, *own_blocks}]
        rest.sort(key=lambda d: (d // many_y != many_x // 2, d))
        pairs = [(rest[n], rest[min(n + 1, len(rest) - 1)]) for n in range(0, len(rest), 2)]
    others = list(range(many_x - 1, 1, -1))
    bands = [(0, 0), (1, 1)] + [(others[n + 1], others[n]) for n in range(0, len(others), 2)]
    return {
        "relay": relay,
        "cross": 1 if relay else 0,
        "x_blocks": x_blocks,
        "x_ops": x_ops,
        "own_blocks": own_blocks,
        "y_blocks": y_blocks,
        "y_ops": 1 if many_y == 2 else 2,
        "y_tiles": 2 if relay else 1,
        "pairs": pairs,
        "bands": bands,
    }


def lane_plan(plan, carried, levels):
    starts = {"c": 0, "d": levels, "v": 2 * levels, "w": 3 * levels, "u": 4 * levels}
    if not plan["relay"]:
        starts = {"v": carried * levels}
    return {"lane_" + name: start for name, start in starts.items()}


def local(
    sizes,
    tracer,
    west_courant,
    south_courant,
    mixing,
    adjoint_later,
    emission_scale,
    send_cells,
    send_counts,
    kernels,
    observed,
    error_weight,
    regrid_index,
    regrid_weight,
):
    plan = make_plan(sizes)
    many_x, many_y, _ = sizes
    carried, levels, cx, cy = tracer.shape
    owners, cap = send_cells.shape[2:]
    slots = owners * cap
    taps, ll = regrid_index.shape[2:]
    plan.update(lane_plan(plan, carried, levels))
    head = (carried + 1) * levels
    y_ops = plan["y_ops"]
    band = cy // many_x

    def next_x(number):
        def rule(x, y, c):
            step = 1 if (plan["relay"] or x % 2 == 0) == (number == 0) else -1
            return ((x + step) % many_x, y, c ^ plan["cross"])

        return rule

    def next_y(number, cross):
        def rule(x, y, c):
            to = y + (1 if (y % 2 == 0) == (number == 0) else -1)
            return (x, to, c ^ cross) if 0 <= to < many_y else None

        return rule

    def jump(for_first, for_second, cross=0):
        def rule(x, y, c):
            d = for_first if c == 0 else for_second
            return (x ^ (d // many_y), y ^ (d % many_y), c ^ cross)

        return rule

    def other_core(values):
        return exchange(values, sizes, lambda x, y, c: (x, y, 1 - c))

    strips = slots // LANES
    plan["parcel"] = -(-2 * strips // 8) * 8
    extra = 40 if plan["relay"] else 16
    row_shapes = [shape(head + extra, cy)] * 2
    y_rows = plan["y_tiles"] * cx + 8 * len(plan["y_blocks"]) + (plan["parcel"] if plan["relay"] else 0)
    lane_shapes = [shape(y_rows if n == 0 else cx, cy) for n in range(y_ops)]
    packed = call(
        functools.partial(pack_kernel, sizes, plan),
        lane_shapes
        + [shape(8 * len(plan["own_blocks"]), LANES)]
        + [shape(8, LANES)] * len(plan["pairs"])
        + [shape(1, slots, dtype=jnp.int32), shape(1, slots)]
        + [shape(*a.shape) for a in (tracer, west_courant, south_courant, emission_scale, mixing)],
        [
            tracer,
            west_courant,
            south_courant,
            emission_scale,
            kernels.reshape(owners, levels, cap),
            observed.reshape(owners, cap),
            error_weight.reshape(owners, cap),
            send_cells.reshape(owners, cap),
            send_counts.reshape(owners),
            mixing,
        ],
        "pack",
        100000,
        hbm=range(10),
        scratch=[
            pltpu.VMEM((owners, levels, cap), F32),
            pltpu.VMEM((owners, cap), F32),
            pltpu.VMEM((owners, cap), F32),
            pltpu.VMEM((owners, cap), jnp.int32),
            pltpu.SMEM((owners,), jnp.int32),
            pltpu.SemaphoreType.DMA((9 + carried,)),
        ],
    )
    lanes_sent = packed[:y_ops]
    own_blocks = packed[y_ops]
    pair_sent = packed[1 + y_ops : -7]
    cell, live, tracer, west_courant, south_courant, emission_scale, mixing = packed[-7:]
    lanes_got = [exchange(lanes_sent[n], sizes, next_y(n, plan["cross"])) for n in range(y_ops)]
    held, *_ = lax.optimization_barrier((tracer, *lanes_sent))
    inverse, lower, ratio, base, inner, parts, columns, in_row, in_lane = call(
        functools.partial(factor_kernel, sizes),
        [
            shape(levels, cx, cy),
            shape(levels, cx, cy),
            shape(levels, cx, cy),
            shape(carried, cx, cy),
            shape(levels, cx, cy),
            shape(5, levels, cx, cy),
            shape(levels, slots),
            shape(cx, slots),
            shape(cy, slots, dtype=BF16),
        ],
        [held, west_courant, south_courant, mixing, adjoint_later, cell],
        "factor",
        3000000,
    )
    rows_sent = list(
        call(
            functools.partial(rows_kernel, plan),
            row_shapes + ([shape(cx, cy)] if plan["relay"] else []),
            [tracer, west_courant, emission_scale, own_blocks],
            "rows",
            100000,
        )
    )
    per_tile = min(2 * carried, LANES // band)

    def band_shape(first, second):
        count = carried if first == second else 2 * carried
        spare = 8 if plan["relay"] and first == second != 0 else 0
        return shape(-(-count // per_tile) * (cx + 8) + spare, cy)

    band_shapes = [band_shape(*b) for b in plan["bands"]]
    fields = [west_courant[0], south_courant[0], emission_scale]
    observe = functools.partial(
        call, functools.partial(observe_kernel, sizes, plan, carried), name="observe", flops=2000000
    )
    if plan["relay"]:
        base, *lanes_got = lax.optimization_barrier((base, *lanes_got))
        lanes_each = rows_sent.pop()
        base_other = other_core(base)

        def relay(number, *after):
            held, *_ = lax.optimization_barrier((rows_sent[number], *after))
            return call(
                functools.partial(relay_kernel, plan, head, cx, number),
                [row_shapes[number]],
                [held, own_blocks, lanes_got[0]],
                "relay",
                10000,
            )[0]

        rows_sent = [relay(0), relay(1)]
        x_sent = call(
            functools.partial(beyond_kernel, plan, cx),
            [shape(32, LANES)] * len(plan["x_ops"]),
            [own_blocks, lanes_got[0]],
            "beyond",
            10000,
        )
        x_got = [exchange(s, sizes, jump(d, d, 1)) for s, d in zip(x_sent, plan["x_ops"])]
        rows_got = [exchange(rows_sent[n], sizes, next_x(n)) for n in range(2)]
        held_y, *_ = lax.optimization_barrier((lanes_got[0], *rows_sent))
        rim = call(
            functools.partial(rim_kernel, plan, carried, levels, cx),
            [
                shape(levels, LANES),
                shape(levels, LANES),
                shape(levels, LANES),
                shape(6, levels, LANES),
                shape(levels, slots),
                shape(cx, slots),
                shape(LANES, slots, dtype=BF16),
                shape(1, slots),
                shape(2 * cx + 16, cy),
            ],
            [lanes_sent[0], held_y, base, base_other, lanes_each, own_blocks],
            "rim",
            400000,
            scratch=[pltpu.VMEM((LANES, LANES), F32)],
        )
        *rim, rim_sent = rim
        rim_got = exchange(rim_sent, sizes, next_y(0, 0))
        parcel, rows_crossed = observe(
            [shape(2 * levels, slots), shape(2 * carried * levels, cy)],
            [*rows_got, inner, lower, inverse, ratio, in_row, in_lane, *rows_sent, *lanes_sent, *lanes_got]
            + [*rim[:4], rim[6]],
            scratch=[pltpu.VMEM((LANES, LANES), F32), pltpu.VMEM((levels, LANES), F32)],
        )
        parcel_other = other_core(parcel)
        rows_swapped = other_core(rows_crossed)
        parcel_other, rim_got, *x_got = lax.optimization_barrier((parcel_other, rim_got, *x_got))
        band_sent = call(
            functools.partial(weigh_kernel, sizes, plan, carried, levels),
            band_shapes,
            [parcel, parcel_other, columns, live, rim[4], rim[7], own_blocks, *x_got, in_row, in_lane]
            + [base, base_other, rim[5], rim_got, *fields, *rows_got, *lanes_got],
            "weigh",
            500000,
        )
        lanes_own = [lanes_each, rim_got]
        held, *_ = lax.optimization_barrier((tracer, *band_sent))
    else:
        rows_got = [exchange(rows_sent[n], sizes, next_x(n)) for n in range(2)]
        pair_got = [exchange(s, sizes, jump(*p)) for s, p in zip(pair_sent, plan["pairs"])]
        base_other = other_core(base)
        modeled, state = observe(
            [shape(1, slots), shape(2, slots)],
            [*rows_got, inner, lower, inverse, ratio, in_row, in_lane, *rows_sent, *lanes_sent, *lanes_got]
            + [columns, live, own_blocks, *pair_got]
            + [other_core(jnp.concatenate(pair_got, axis=0))],
        )
        near, *rims_sent = call(
            functools.partial(force_kernel, plan),
            [shape(2 * carried, cx, cy)] + [shape(cx, cy)] * y_ops,
            [modeled, other_core(modeled), state, in_row, in_lane, base, base_other],
            "force",
            200000,
        )
        rims_got = [exchange(rims_sent[n], sizes, next_y(n, 0)) for n in range(y_ops)]
        band_sent = call(
            functools.partial(surface_kernel, sizes, plan, carried, levels),
            band_shapes,
            [near, *fields, *rows_got, *lanes_got, *rims_got],
            "surface",
            400000,
        )
        lanes_own = [*lanes_sent, *lanes_got]
        rows_swapped = rows_got[0]
        held = tracer
    (advanced,) = call(
        functools.partial(advance_kernel, plan),
        [shape(*tracer.shape)],
        [held, parts, lower, inverse, ratio]
        + list(rows_sent)
        + rows_got
        + [rows_swapped]
        + lanes_own
        + list(lanes_sent)
        + lanes_got,
        "advance",
        6000000,
        scratch=[pltpu.VMEM(tracer.shape, F32)]
        + [pltpu.VMEM((carried * levels, cy), F32)] * 2
        + [pltpu.SemaphoreType.DMA((levels // 4,))],
        out_hbm=(0,),
    )
    band_got = [
        s
        if first == second == 0
        else exchange(s, sizes, jump(first * many_y, second * many_y, plan["cross"]))
        for s, (first, second) in zip(band_sent, plan["bands"])
    ]
    tables = [regrid_index.reshape(taps, ll), regrid_weight.reshape(taps, ll)]
    kinds = [first == second for first, second in plan["bands"]]

    def regridded(bands, blocks, *more):
        return call(
            functools.partial(regrid_kernel, sizes, plan, bands, carried, cx, band),
            [shape(carried, ll)],
            [*tables, *blocks, *more],
            "regrid",
            1000000,
        )[0]

    near = [(pair, 0, 0) for pair, kind in zip(plan["bands"], kinds) if kind]
    far = [pair for pair, kind in zip(plan["bands"], kinds) if not kind]
    near_got = [got for got, kind in zip(band_got, kinds) if kind]
    far_got = [got for got, kind in zip(band_got, kinds) if not kind]
    advanced, far_got = lax.optimization_barrier((advanced, far_got))
    far_fetched = [other_core(got[: cx + 8] if plan["relay"] else got) for got in far_got]
    mine = carried if plan["cross"] else 0
    partial = [regridded([(pair, 0, mine) for pair in far], far_got)] if far else []
    near_got, partial = lax.optimization_barrier((near_got, partial))
    partial = regridded(near, near_got, *partial)
    latlon = regridded([(pair, 1, carried - mine) for pair in far], far_fetched, partial) if far else partial
    return (advanced, latlon[:, None, None, :])


def solution(mesh):
    in_specs = (
        P("lev", "groups", "facex", "facey"),
        P("groups", "facex", "facey"),
        P("groups", "facex", "facey"),
        P("groups", "facex", "facey"),
        P("lev", "groups", "facex", "facey"),
        P("facex", "facey"),
        P("facex", "facey", "groups", None),
        P("facex", "facey", "groups"),
        P("facex", "facey", "groups", None, None),
        P("facex", "facey", "groups", None),
        P("facex", "facey", "groups", None),
        P("facex", "facey", None, None),
        P("facex", "facey", None, None),
    )
    out_specs = (P("lev", "groups", "facex", "facey"), P("lev", "facex", "facey", "groups"))
    sizes = tuple(mesh.shape[axis] for axis in GROUP)
    return jax.shard_map(
        functools.partial(local, sizes), mesh=mesh, in_specs=in_specs, out_specs=out_specs, check_vma=False
    )
```

```python
import functools

import jax
import jax.numpy as jnp
from jax import lax
from jax.experimental import pallas as pl
from jax.experimental.pallas import tpu as pltpu
from jax.sharding import PartitionSpec as P

F32 = jnp.float32
BF16 = jnp.bfloat16
LANES = 128


def call(body, outs, ins, name, flops, smem=(), hbm=(), scratch=(), out_hbm=()):
    moved = sum(4 * a.size for a in ins) + sum(4 * o.size for o in outs)
    ins = [pltpu.with_memory_space_constraint(a, pltpu.HBM) if i in hbm else a for i, a in enumerate(ins)]

    def space(number):
        return pltpu.SMEM if number in smem else pltpu.HBM if number in hbm else pltpu.VMEM

    return pl.pallas_call(
        body,
        out_shape=outs,
        in_specs=[pl.BlockSpec(memory_space=space(i)) for i in range(len(ins))],
        out_specs=[
            pl.BlockSpec(memory_space=pltpu.HBM if i in out_hbm else pltpu.VMEM) for i in range(len(outs))
        ],
        scratch_shapes=scratch,
        compiler_params=pltpu.CompilerParams(vmem_limit_bytes=40 << 20),
        cost_estimate=pl.CostEstimate(flops=flops, bytes_accessed=moved, transcendentals=0),
        name=name,
    )(*ins)


def shape(*dims, dtype=F32):
    return jax.ShapeDtypeStruct(dims, dtype)


def iota(dims, axis):
    return lax.broadcasted_iota(jnp.int32, dims, axis)


def halves(values):
    high = values.astype(BF16)
    return high, (values - high.astype(F32)).astype(BF16)


def tile_of(sizes):
    return lax.axis_index("facex") * sizes[1] + lax.axis_index("facey")


def is_even(axis):
    return lax.rem(lax.axis_index(axis), 2) == 0


def up(values):
    rows = values.shape[0]
    rolled = pltpu.roll(values, rows - 1, 0)
    return jnp.where(iota(values.shape, 0) == rows - 1, 0.0, rolled)


def right(values):
    rolled = pltpu.roll(values, 1, 1)
    return jnp.where(iota(values.shape, 1) == 0, 0.0, rolled)


def left(values):
    lanes = values.shape[1]
    rolled = pltpu.roll(values, lanes - 1, 1)
    return jnp.where(iota(values.shape, 1) == lanes - 1, 0.0, rolled)


def shares(west, south):
    east, north = up(west), left(south)
    middle = 1.0 + jnp.minimum(west, 0.0) - jnp.maximum(east, 0.0)
    middle = middle + jnp.minimum(south, 0.0) - jnp.maximum(north, 0.0)
    row, lane = iota(west.shape, 0), iota(west.shape, 1)
    return (
        middle,
        jnp.where(row == 0, 0.0, jnp.maximum(west, 0.0)),
        -jnp.minimum(east, 0.0),
        jnp.where(lane == 0, 0.0, jnp.maximum(south, 0.0)),
        -jnp.minimum(north, 0.0),
    )


def mix(parts, cells):
    rows, lanes = cells.shape
    middle, west, east, south, north = parts
    total = middle * cells + west * pltpu.roll(cells, 1, 0) + east * pltpu.roll(cells, rows - 1, 0)
    return total + south * pltpu.roll(cells, 1, 1) + north * pltpu.roll(cells, lanes - 1, 1)


def pack_kernel(sizes, plan, *refs):
    sources, refs = refs[:10], refs[10:]
    lanes_out, refs = refs[: plan.y_ops], refs[plan.y_ops :]
    own_out, refs = refs[0], refs[1:]
    block_outs, refs = refs[: len(plan.pairs)], refs[len(plan.pairs) :]
    cell_out, live_out, tracer, west, south, scale, mixing, *refs = refs
    kernels, observed, weights, cells, counts, done = refs
    carried, levels, cx, cy = tracer.shape
    me = tile_of(sizes)
    copies = [
        pltpu.make_async_copy(source, target, done.at[number])
        for number, (source, target) in enumerate(
            zip(sources[1:], (west, south, scale, kernels, observed, weights, cells, counts, mixing))
        )
    ]
    copies += [
        pltpu.make_async_copy(sources[0].at[t], tracer.at[t], done.at[9 + t]) for t in range(carried)
    ]
    for number in (3, 4, 5, 6, 7, 1, 0, 8, *range(9, 9 + carried), 2):
        copies[number].start()

    def block(offset):
        where_to = jnp.bitwise_xor(me, offset)
        mine = kernels[where_to]
        last = jnp.concatenate(
            [
                observed[pl.ds(where_to, 1), :],
                weights[pl.ds(where_to, 1), :],
                jnp.zeros((6, mine.shape[1]), F32),
            ],
            axis=0,
        )
        return jnp.concatenate([mine[8 * g : 8 * g + 8] for g in range(levels // 8)] + [last], axis=1)

    for number in (3, 4, 5):
        copies[number].wait()
    for number, offset in enumerate(plan.y_blocks):
        at = plan.y_tiles * cx + 8 * number
        lanes_out[0][at : at + 8, :] = block(offset)
    for number, offset in enumerate(plan.own_blocks):
        own_out[8 * number : 8 * number + 8, :] = block(offset)
    first_core = lax.axis_index("lev") == 0
    for out, (for_first, for_second) in zip(block_outs, plan.pairs):
        out[...] = block(jnp.where(first_core, for_first, for_second))

    owners, cap = cells.shape
    slot = iota((1, cap), 1)
    copies[6].wait()
    copies[7].wait()
    cell_parts = []
    live_parts = []
    for offset in range(owners):
        owner = jnp.bitwise_xor(me, offset)
        cell_parts.append(cells[pl.ds(owner, 1), :])
        live_parts.append(jnp.where(slot < counts[owner], 1.0, 0.0))
    cell = jnp.concatenate(cell_parts, axis=1)
    live = jnp.concatenate(live_parts, axis=1)
    cell_out[...] = cell
    live_out[...] = live
    if plan.relay:
        at = plan.y_tiles * cx + 8 * len(plan.y_blocks)
        strips = owners * cap // LANES
        for number in range(strips):
            part = slice(number * LANES, (number + 1) * LANES)
            lanes_out[0][at + number : at + number + 1, :] = cell[:, part].astype(F32)
            lanes_out[0][at + strips + number : at + strips + number + 1, :] = live[:, part]

    for number in (1, 0, 8):
        copies[number].wait()
    lane = iota((cx, cy), 1)
    if plan.relay:
        edge = edge_of(0, cy)
        inner = jnp.where(edge == 0, 1, cy - 2)
        tiles = {name: LanePacker(lane, at) for name, at in zip("cdvwuk", (edge, inner, edge, inner, edge, edge))}
        for level in range(levels):
            turned = pltpu.roll(south[level], level, 1) if level else south[level]
            tiles["v"].put(level, turned)
            tiles["w"].put(level, turned)
            tiles["u"].put(level, pltpu.roll(west[level], level, 1) if level else west[level])
            if level < levels - 1:
                tiles["k"].put(level, pltpu.roll(mixing[level], level, 1) if level else mixing[level])
        totals = None
        for t in range(carried):
            copies[9 + t].wait()
            totals = [tracer[t, level] + (totals[level] if t else 0.0) for level in range(levels)]
        for level in range(levels):
            turned = pltpu.roll(totals[level], level, 1) if level else totals[level]
            tiles["c"].put(level, turned)
            tiles["d"].put(level, turned)
        packed = jnp.zeros((cx, cy), F32)
        for name in "cdvwu":
            packed = packed + tiles[name].packed(plan["lane_" + name])
        lanes_out[0][0:cx, :] = packed
        lanes_out[0][cx : 2 * cx, :] = tiles["k"].packed(0)
    else:
        edges = [LanePacker(lane, edge_of(number, cy)) for number in range(len(lanes_out))]
        for t in range(carried):
            copies[9 + t].wait()
        for f in range(carried + 1):
            for level in range(levels):
                spot = f * levels + level
                values = tracer[f, level] if f < carried else south[level]
                for tile in edges:
                    tile.put(spot, pltpu.roll(values, spot, 1) if spot else values)
        for tile, out in zip(edges, lanes_out):
            out[0:cx, :] = tile.packed(0)
    copies[2].wait()


class Plan(dict):
    __getattr__ = dict.__getitem__


class LanePacker:
    def __init__(self, lane, edge):
        self.lanes = lane.shape[1]
        self.back = lax.rem(2 * self.lanes - edge, self.lanes)
        self.place = lax.rem(lane + self.back, self.lanes)
        self.tile = jnp.zeros(lane.shape, F32)

    def put(self, spot, turned):
        self.tile = jnp.where(self.place == spot, turned, self.tile)

    def packed(self, start):
        return pltpu.roll(self.tile, lax.rem(self.back + start, self.lanes), 1)


def edge_of(number, lanes):
    even_y = is_even("facey")
    return jnp.where(even_y if number == 0 else jnp.logical_not(even_y), lanes - 1, 0)


def rows_kernel(plan, tracer, west, scale, blocks, *outs):
    carried, levels, cx, cy = tracer.shape
    head = (carried + 1) * levels
    if plan.relay:
        tile = LanePacker(iota((cx, cy), 1), edge_of(0, cy))
        for t in range(carried):
            for level in range(levels):
                spot = t * levels + level
                tile.put(spot, pltpu.roll(tracer[t, level], spot, 1) if spot else tracer[t, level])
        outs[2][...] = tile.packed(0)
    for number, out in enumerate(outs[:2]):
        row = sent_row(plan, number, cx)
        for level in range(levels):
            for t in range(carried):
                spot = t * levels + level
                out[spot : spot + 1, :] = tracer[t, level, pl.ds(row, 1), :]
            spot = carried * levels + level
            out[spot : spot + 1, :] = west[level, pl.ds(row, 1), :]
        out[head : head + 8, :] = jnp.broadcast_to(scale[pl.ds(row, 1), :], (8, cy))
        if plan.x_blocks[number] and not plan.relay:
            at = 8 * plan.own_blocks.index(plan.x_blocks[number])
            out[head + 8 : head + 16, :] = blocks[at : at + 8, :]


def relay_kernel(plan, head, cx, number, rows, blocks, y_got, out):
    out[0 : head + 8, :] = rows[0 : head + 8, :]
    row = sent_row(plan, number, cx)
    out[head + 1 : head + 2, :] = y_got[pl.ds(row, 1), :]
    near, far = plan.x_blocks
    even_x = is_even("facex")
    offset = jnp.where(even_x if number == 0 else jnp.logical_not(even_x), near, far)
    at = plan.y_tiles * cx + 8 * (offset - plan.y_blocks[0])
    out[head + 8 : head + 24, :] = blocks[pl.ds(pl.multiple_of(8 * offset, 8), 16), :]
    out[head + 24 : head + 40, :] = y_got[pl.ds(pl.multiple_of(at, 8), 16), :]


def beyond_kernel(plan, cx, blocks, y_got, *outs):
    for out, offset in zip(outs, plan.x_ops):
        at = plan.y_tiles * cx + 8 * (offset - plan.y_blocks[0])
        out[0:16, :] = blocks[8 * offset : 8 * offset + 16, :]
        out[16:32, :] = y_got[at : at + 16, :]


def rim_kernel(plan, carried, levels, cx, y_sent, y_got, base, base_other, lanes, own, *refs):
    inverse_out, ratio_out, lower_out, pieces_out, columns_out, rows_out, picks_out, live_out, base_out, square = refs
    cy = y_got.shape[1]
    slots = live_out.shape[1]

    def turned(values):
        square[...] = jnp.zeros((LANES, LANES), F32)
        square[0:cx, :] = values
        return jnp.transpose(square[...])

    def part(values, name):
        return values[plan["lane_" + name] : plan["lane_" + name] + levels]

    beyond = turned(y_got[0:cx, :])
    mine = turned(y_sent[0:cx, :])
    coupling = turned(y_got[cx : 2 * cx, :])
    north = is_even("facey")
    pieces_out[0] = part(beyond, "c")
    pieces_out[1] = part(beyond, "u")
    pieces_out[2] = part(beyond, "v")
    pieces_out[3] = jnp.where(north, part(beyond, "w"), part(mine, "v"))
    pieces_out[4] = jnp.where(north, part(mine, "c"), part(beyond, "d"))
    pieces_out[5] = jnp.where(north, part(beyond, "d"), part(mine, "c"))

    def level_of(ref, level):
        return jnp.broadcast_to(ref[level : level + 1, :], (8, LANES))

    square[...] = coupling
    first = []
    ratios = []
    before = None
    for level in range(levels):
        diagonal = jnp.ones((8, LANES), F32)
        if level > 0:
            below = level_of(square, level - 1)
            diagonal = diagonal + below
        if level < levels - 1:
            diagonal = diagonal + level_of(square, level)
        if level > 0:
            diagonal = diagonal - below * below * before
        inverse = 1.0 / diagonal
        ratios.append(level_of(square, level) * inverse if level < levels - 1 else jnp.zeros((8, LANES), F32))
        lower = below * inverse if level > 0 else jnp.zeros((8, LANES), F32)
        lower_out[level : level + 1, :] = lower[0:1]
        inverse_out[level : level + 1, :] = inverse[0:1]
        ratio_out[level : level + 1, :] = ratios[-1][0:1]
        first.append(inverse if level == 0 else lower * first[-1])
        before = inverse
    weight = first
    for level in range(levels - 2, -1, -1):
        weight[level] = first[level] + ratios[level] * weight[level + 1]
    for level in range(levels):
        square[level : level + 1, :] = weight[level][0:1]
    weights = square[0:levels, :]
    tile = LanePacker(iota((cx, cy), 1), edge_of(0, cy))
    for t in range(2 * carried):
        values = base[t] if t < carried else base_other[t - carried]
        tile.put(t, pltpu.roll(values, t, 1) if t else values)
    base_out[0:cx, :] = tile.packed(0)
    base_out[cx : 2 * cx, :] = lanes[...]
    base_out[2 * cx :, :] = own[0:16, :]
    at = plan.y_tiles * cx + 8 * len(plan.y_blocks)
    strips = slots // LANES
    cell = jnp.concatenate([y_got[at + n : at + n + 1, :] for n in range(strips)], axis=1).astype(jnp.int32)
    live_out[...] = jnp.concatenate([y_got[at + strips + n : at + strips + n + 1, :] for n in range(strips)], axis=1)
    on_edge = lax.rem(cell, cy) == jnp.where(north, 0, cy - 1)
    x_of = jnp.where(on_edge, lax.div(cell, cy), LANES)
    picks = jnp.where(iota((LANES, slots), 0) == x_of, 1.0, 0.0)
    rows_out[...] = picks[0:cx]
    picks = picks.astype(BF16)
    picks_out[...] = picks
    high, low = halves(weights)
    columns_out[...] = jnp.dot(high, picks, preferred_element_type=F32) + jnp.dot(
        low, picks, preferred_element_type=F32
    )


def factor_kernel(sizes, *refs):
    (tracer, west, south, mixing, adjoint, cells) = refs[:6]
    inverse_out, lower_out, ratio_out, base_out, inner_out, shares_out, columns_out, rows_out, picks_out = refs[6:]
    carried, levels, cx, cy = tracer.shape
    slots = cells.shape[1]
    first = []
    before = None
    for level in range(levels):
        diagonal = jnp.ones((cx, cy), F32)
        if level > 0:
            diagonal = diagonal + mixing[level - 1]
        if level < levels - 1:
            diagonal = diagonal + mixing[level]
        if level > 0:
            diagonal = diagonal - mixing[level - 1] * mixing[level - 1] * before
        inverse = 1.0 / diagonal
        inverse_out[level] = inverse
        if level < levels - 1:
            ratio_out[level] = mixing[level] * inverse
        lower = mixing[level - 1] * inverse if level > 0 else jnp.zeros((cx, cy), F32)
        lower_out[level] = lower
        first.append(inverse if level == 0 else lower * first[-1])
        before = inverse
    ratio_out[levels - 1] = jnp.zeros((cx, cy), F32)
    weight = first
    for level in range(levels - 2, -1, -1):
        weight[level] = first[level] + ratio_out[level] * weight[level + 1]
    for t in range(carried):
        total = weight[0] * adjoint[t, 0]
        for level in range(1, levels):
            total = total + weight[level] * adjoint[t, level]
        base_out[t] = total
    for level in range(levels):
        total = tracer[0, level]
        for t in range(1, carried):
            total = total + tracer[t, level]
        parts = shares(west[level], south[level])
        for number, part in enumerate(parts):
            shares_out[number, level] = part
        inner_out[level] = mix(parts, total)
    cell = cells[...]
    x_of = lax.div(cell, cy)
    y_of = lax.rem(cell, cy)
    in_row = jnp.where(iota((cx, slots), 0) == x_of, 1.0, 0.0)
    in_lane = jnp.where(iota((cy, slots), 0) == y_of, 1.0, 0.0).astype(BF16)
    rows_out[...] = in_row
    picks_out[...] = in_lane
    high, low = halves(jnp.concatenate(weight, axis=0))
    picked = jnp.dot(high, in_lane, preferred_element_type=F32)
    picked = picked + jnp.dot(low, in_lane, preferred_element_type=F32)
    for level in range(levels):
        part = picked[level * cx : (level + 1) * cx] * in_row
        columns_out[level : level + 1, :] = jnp.sum(part, axis=0, keepdims=True)


def sides(plan, first, second):
    if plan.relay:
        return first, second
    even_x = is_even("facex")
    return jnp.where(even_x, second, first), jnp.where(even_x, first, second)


def own_sides(plan, first, second):
    return (second, first) if plan.relay else sides(plan, first, second)


def sent_row(plan, number, rows):
    if plan.relay:
        return rows - 1 if number == 0 else 0
    even_x = is_even("facex")
    return jnp.where(even_x if number == 0 else jnp.logical_not(even_x), rows - 1, 0)


def seam(number, sent, got, sent_face, got_face):
    even_y = is_even("facey")
    north = even_y if number == 0 else jnp.logical_not(even_y)
    to_north = -(jnp.maximum(got_face, 0.0) * sent + jnp.minimum(got_face, 0.0) * got)
    to_south = jnp.maximum(sent_face, 0.0) * got
    return jnp.where(north, to_north, to_south), jnp.where(north, sent.shape[1] - 1, 0)


def spread_wind(values, start, carried, levels):
    lane = iota(values.shape, 1)
    result = jnp.zeros_like(values)
    for t in range(carried):
        moved = pltpu.roll(values, (t * levels - start) % values.shape[1], 1)
        inside = jnp.logical_and(lane >= t * levels, lane < (t + 1) * levels)
        result = jnp.where(inside, moved, result)
    return result


def seam_lanes(number, plan, sent, got, sent_wind, got_wind, carried, levels):
    start = plan.lane_v
    faces = [spread_wind(wind, start, carried, levels) for wind in (sent_wind, got_wind)]
    return seam(number, sent, got, *faces)


def block_groups(blocks, cap):
    per_tile = LANES // cap
    group_of_lane = lax.div(iota((8, LANES), 1), cap)
    groups = []
    for group in range(per_tile):
        tiles = []
        for start in range(0, len(blocks), per_tile):
            tile = jnp.zeros((8, LANES), F32)
            for a in range(per_tile):
                moved = pltpu.roll(blocks[start + a], (cap * (a - group)) % LANES, 1)
                tile = jnp.where(group_of_lane == a, moved, tile)
            tiles.append(tile)
        groups.append(jnp.concatenate(tiles, axis=1))
    return groups


def relayed_blocks(plan, head, own, beyond, got, x_got):
    def block_at(ref, row):
        return ref[row : row + 8, :]

    blocks = {0: block_at(own, 0), 1: block_at(beyond, 8)}
    rim_blocks = {0: block_at(beyond, 0), 1: block_at(own, 8)}
    even_x = is_even("facex")
    from_west, from_east = (got[n][head + 8 : head + 40, :] for n in range(2))
    carriers = [
        (plan.x_blocks[0], jnp.where(even_x, from_east, from_west)),
        (plan.x_blocks[1], jnp.where(even_x, from_west, from_east)),
    ]
    carriers += [(offset, ref[...]) for offset, ref in zip(plan.x_ops, x_got)]
    for offset, values in carriers:
        blocks[offset], rim_blocks[offset + 1] = block_at(values, 0), block_at(values, 8)
        rim_blocks[offset], blocks[offset + 1] = block_at(values, 16), block_at(values, 24)
    return blocks, rim_blocks


def observe_kernel(sizes, plan, carried, *refs):
    refs = list(refs)
    got = refs[0:2]
    inner, lower, inverse, ratio, in_row, in_lane = refs[2:8]
    sent = refs[8:10]
    refs = refs[10:]
    y_sent = refs[: plan.y_ops]
    y_got = refs[plan.y_ops : 2 * plan.y_ops]
    refs = refs[2 * plan.y_ops :]
    if plan.relay:
        rim_inverse, rim_ratio, rim_lower, pieces, rim_picks, parcel, rows_out, turn, rise = refs
    else:
        columns, live, own, *refs = refs
        n_pairs = len(plan.pairs)
        pair_got = refs[:n_pairs]
        swapped = refs[n_pairs] if n_pairs else None
        modeled_out, state_out = refs[-2:]
    levels, cx, cy = inner.shape
    slots = in_row.shape[1]
    head = (carried + 1) * levels

    def summed(rows):
        total = rows[0:levels]
        for t in range(1, carried):
            total = total + rows[t * levels : (t + 1) * levels]
        return total

    beyond_west, beyond_east = sides(plan, got[0][0:head], got[1][0:head])
    at_west, at_east = own_sides(plan, sent[0][0:head], sent[1][0:head])
    spot = carried * levels
    face_west = at_west[spot:head]
    face_east = beyond_east[spot:head]
    from_west = jnp.maximum(face_west, 0.0) * summed(beyond_west)
    from_east = -(
        jnp.maximum(face_east, 0.0) * summed(at_east) + jnp.minimum(face_east, 0.0) * summed(beyond_east)
    )
    lane_parts = []
    for number in range(plan.y_ops):
        mine, beyond = y_sent[number][0:cx, :], y_got[number][0:cx, :]
        if plan.relay:
            faces = [pltpu.roll(values, cy - plan.lane_v, 1) for values in (mine, beyond)]
            total, spot_y = seam(number, mine, beyond, *faces)
        else:
            part, spot_y = seam_lanes(number, plan, mine, beyond, mine, beyond, carried, levels)
            total = part
            for t in range(1, carried):
                total = total + pltpu.roll(part, (-t * levels) % cy, 1)
        lane_parts.append((pltpu.roll(total, spot_y, 1), spot_y))
    lane = iota((cx, cy), 1)
    row = iota((cx, cy), 0)
    forward = []
    for level in range(levels):
        value = inner[level]
        value = value + jnp.where(row == 0, from_west[level : level + 1], 0.0)
        value = value + jnp.where(row == cx - 1, from_east[level : level + 1], 0.0)
        for total, spot_y in lane_parts:
            moved = pltpu.roll(total, cy - level, 1) if level else total
            value = value + jnp.where(lane == spot_y, moved, 0.0)
        value = value * inverse[level]
        forward.append(value + lower[level] * forward[-1] if level else value)
    result = forward
    for level in range(levels - 2, -1, -1):
        result[level] = forward[level] + ratio[level] * result[level + 1]
    high, low = halves(jnp.concatenate(result, axis=0))
    picks = in_lane[...]
    picked = jnp.dot(high, picks, preferred_element_type=F32)
    picked = picked + jnp.dot(low, picks, preferred_element_type=F32)

    if not plan.relay:
        start = plan.y_tiles * cx
        blocks = {0: own[0:8, :], plan.y_blocks[0]: y_got[0][start : start + 8, :]}
        for number in range(2):
            offset = plan.x_blocks[number]
            if offset:
                blocks[offset] = got[number][head + 8 : head + 16, :]
        first_core = lax.axis_index("lev") == 0
        for number, (for_first, for_second) in enumerate(plan.pairs):
            mine = pair_got[number][...]
            other = swapped[8 * number : 8 * number + 8, :]
            if for_first == for_second:
                blocks[for_first] = mine
            else:
                blocks[for_first] = jnp.where(first_core, mine, other)
                blocks[for_second] = jnp.where(first_core, other, mine)
        *groups, last = block_groups(blocks, slots // len(blocks))
        total = jnp.zeros((cx, slots), F32)
        sensitivity = jnp.zeros((8, slots), F32)
        for g, kernel in enumerate(groups):
            sensitivity = sensitivity + kernel * columns[8 * g : 8 * g + 8, :]
            for l in range(8):
                level = 8 * g + l
                total = total + kernel[l : l + 1] * picked[level * cx : (level + 1) * cx]
        modeled_out[...] = jnp.sum(total * in_row[...], axis=0, keepdims=True)
        gain = jnp.sum(sensitivity, axis=0, keepdims=True) * last[1:2] * live[...]
        state_out[...] = jnp.concatenate([gain, last[0:1]], axis=0)
        return

    chosen = in_row[...]
    for level in range(levels):
        part = picked[level * cx : (level + 1) * cx] * chosen
        parcel[level : level + 1, :] = jnp.sum(part, axis=0, keepdims=True)

    corners_west, corners_east = sides(plan, got[0][head + 1 : head + 2, :], got[1][head + 1 : head + 2, :])
    turn[...] = jnp.zeros((LANES, LANES), F32)
    turn[0:1, :] = corners_west
    turn[cx - 1 : cx, :] = corners_east
    turned = jnp.transpose(turn[...])
    ends = turned[plan.lane_c : plan.lane_c + levels]
    end_face = turned[plan.lane_u : plan.lane_u + levels]
    place = iota((levels, LANES), 1)
    cells, face_w, face_s, face_n, south_cells, north_cells = (pieces[n] for n in range(6))
    west_cells = jnp.where(place == 0, ends, pltpu.roll(cells, 1, 1))
    east_cells = jnp.where(place == cx - 1, ends, pltpu.roll(cells, LANES - 1, 1))
    face_e = jnp.where(place == cx - 1, end_face, pltpu.roll(face_w, LANES - 1, 1))
    rise[0:levels, :] = advance_cells(
        cells, west_cells, east_cells, south_cells, north_cells, face_w, face_e, face_s, face_n
    )

    def level_of(ref, level):
        return jnp.broadcast_to(ref[level : level + 1, :], (8, LANES))

    climbed = []
    for level in range(levels):
        value = level_of(rise, level) * level_of(rim_inverse, level)
        climbed.append(value + level_of(rim_lower, level) * climbed[-1] if level else value)
    for level in range(levels - 2, -1, -1):
        climbed[level] = climbed[level] + level_of(rim_ratio, level) * climbed[level + 1]
    for level in range(levels):
        rise[level : level + 1, :] = climbed[level][0:1]
    high, low = halves(rise[0:levels, :])
    picks = rim_picks[...]
    picked = jnp.dot(high, picks, preferred_element_type=F32)
    picked = picked + jnp.dot(low, picks, preferred_element_type=F32)
    parcel[levels : 2 * levels, :] = picked
    rows = carried * levels
    for number in range(2):
        rows_out[number * rows : (number + 1) * rows, :] = got[number][0:rows, :]


def advance_cells(cells, west, east, south, north, face_w, face_e, face_s, face_n):
    flux_w = jnp.maximum(face_w, 0.0) * west + jnp.minimum(face_w, 0.0) * cells
    flux_e = jnp.maximum(face_e, 0.0) * cells + jnp.minimum(face_e, 0.0) * east
    flux_s = jnp.maximum(face_s, 0.0) * south + jnp.minimum(face_s, 0.0) * cells
    flux_n = jnp.maximum(face_n, 0.0) * cells + jnp.minimum(face_n, 0.0) * north
    return cells + flux_w - flux_e + flux_s - flux_n


def scatter(force, in_row, in_lane):
    high, low = halves(in_row * force)
    dims = (((1,), (1,)), ((), ()))
    scattered = lax.dot_general(high, in_lane, dims, preferred_element_type=F32)
    return scattered + lax.dot_general(low, in_lane, dims, preferred_element_type=F32)


def force_kernel(plan, *refs):
    modeled, modeled_other, state, in_row, in_lane, base, base_other = refs[:7]
    near_out = refs[7]
    rim_outs = refs[8:]
    carried, cx, cy = base.shape
    misfit = modeled[...] + modeled_other[...] - state[1:2, :]
    force = state[0:1, :] * misfit
    scattered = scatter(force, in_row[...], in_lane[...])
    lane = iota((cx, cy), 1)
    even_y = is_even("facey")
    edges = []
    for number in range(len(rim_outs)):
        sends_last = even_y if number == 0 else jnp.logical_not(even_y)
        edges.append(jnp.where(sends_last, cy - 1, 0))
    rims = [jnp.zeros((cx, cy), F32) for _ in rim_outs]
    for t in range(2 * carried):
        values = scattered + (base[t] if t < carried else base_other[t - carried])
        near_out[t] = values
        for number, edge in enumerate(edges):
            moved = pltpu.roll(values, lax.rem(t + cy - edge, cy), 1)
            rims[number] = jnp.where(lane == t, moved, rims[number])
    for rim, out in zip(rims, rim_outs):
        out[...] = rim


def surface_kernel(sizes, plan, carried, levels, *refs):
    y_ops = plan.y_ops
    near = refs[0]
    rims = refs[6 + y_ops : 6 + 2 * y_ops]
    rim_values = [[rim[...] for rim in rims] for _ in range(near.shape[0])]
    values = [near[t] for t in range(near.shape[0])]
    spread_surface(
        sizes, plan, carried, levels, values, rim_values, refs[1:4], refs[4:6], refs[6 : 6 + y_ops], refs[6 + 2 * y_ops :]
    )


def weigh_kernel(sizes, plan, carried, levels, *refs):
    parcel, other, columns, live, rim_columns, rim_live, own, *refs = refs
    x_got, refs = refs[: len(plan.x_ops)], refs[len(plan.x_ops) :]
    in_row, in_lane, base, base_other, rim_rows, rim_base = refs[:6]
    cx, cy = base.shape[1:]
    slots = live.shape[1]

    def force(blocks, start, weights, used):
        *groups, last = block_groups(blocks, slots // len(blocks))
        seen = jnp.zeros((8, slots), F32)
        sensitivity = jnp.zeros((8, slots), F32)
        for g, kernel in enumerate(groups):
            part = slice(start + 8 * g, start + 8 * g + 8)
            seen = seen + kernel * (parcel[part, :] + other[part, :])
            sensitivity = sensitivity + kernel * weights[8 * g : 8 * g + 8, :]
        modeled = jnp.sum(seen, axis=0, keepdims=True)
        gain = jnp.sum(sensitivity, axis=0, keepdims=True) * last[1:2] * used[...]
        return gain * (modeled - last[0:1])

    blocks, rim_blocks = relayed_blocks(
        plan, (carried + 1) * levels, own, rim_base[2 * cx :, :], refs[9:11], x_got
    )
    scattered = scatter(force(blocks, 0, columns, live), in_row[...], in_lane[...])
    on_rim = jnp.sum(rim_rows[...] * force(rim_blocks, levels, rim_columns, rim_live), axis=1, keepdims=True)
    near = [scattered + base[t] for t in range(carried)]
    near += [scattered + base_other[t] for t in range(carried)]
    rims = [[rim_base[0:cx, :] + on_rim] for _ in near]
    spread_surface(sizes, plan, carried, levels, near, rims, refs[6:9], refs[9:11], refs[11:12], refs[12:])


def spread_surface(sizes, plan, carried, levels, near, rim_values, fields, got, y_got, outs):
    west, south, scale = fields
    tracers = len(near)
    cx, cy = near[0].shape
    spot_v = plan.lane_v
    band = cy // sizes[0]
    per_tile = min(tracers, LANES // band)
    spot = carried * levels
    head = (carried + 1) * levels
    lane = iota((cx, cy), 1)
    row = iota((cx, cy), 0)
    even_y = is_even("facey")
    face_west = west[...]
    face_south = south[...]
    scales = scale[...]
    beyond_west, beyond_east = sides(plan, got[0][head : head + 1], got[1][head : head + 1])
    _, east_wind = sides(plan, got[0][spot : spot + 1], got[1][spot : spot + 1])
    face_east = jnp.where(row == cx - 1, east_wind, pltpu.roll(face_west, cx - 1, 0))
    face_north = left(face_south)
    norths = []
    for number in range(plan.y_ops):
        norths.append(even_y if number == 0 else jnp.logical_not(even_y))
        moved = pltpu.roll(y_got[number][0:cx, :], cy - 1 - spot_v, 1)
        keep = jnp.logical_and(lane == cy - 1, norths[number])
        face_north = jnp.where(keep, moved, face_north)
    to_middle = 1.0 + jnp.minimum(face_west, 0.0) - jnp.maximum(face_east, 0.0)
    to_middle = scales * (to_middle + jnp.minimum(face_south, 0.0) - jnp.maximum(face_north, 0.0))
    to_east = jnp.where(row == cx - 1, 0.0, scales * jnp.maximum(face_east, 0.0))
    to_west = jnp.where(row == 0, 0.0, scales * jnp.minimum(face_west, 0.0))
    to_north = scales * jnp.maximum(face_north, 0.0)
    to_south = scales * jnp.minimum(face_south, 0.0)
    west_gain = beyond_west * jnp.maximum(face_west[0:1], 0.0)
    east_gain = -beyond_east * jnp.minimum(face_east[cx - 1 : cx], 0.0)
    filler = jnp.zeros((6, cy), F32)
    grown = []
    for t in range(tracers):
        values = near[t]
        north_side = left(values)
        south_side = right(values)
        for number in range(plan.y_ops):
            rim = rim_values[t][number]
            at_north = jnp.logical_and(lane == cy - 1, norths[number])
            at_south = jnp.logical_and(lane == 0, jnp.logical_not(norths[number]))
            north_side = jnp.where(at_north, pltpu.roll(rim, (cy - 1 - t) % cy, 1), north_side)
            south_side = jnp.where(at_south, pltpu.roll(rim, (-t) % cy, 1), south_side)
        swept = to_middle * values + to_east * pltpu.roll(values, cx - 1, 0) - to_west * pltpu.roll(values, 1, 0)
        swept = swept + to_north * north_side - to_south * south_side
        grown.append(
            jnp.concatenate(
                [swept, west_gain * values[0:1], east_gain * values[cx - 1 : cx], filler], axis=0
            )
        )
    rows = cx + 8
    group_of_lane = lax.div(iota((rows, cy), 1), band)
    first_core = lax.axis_index("lev") == 0
    place = lax.axis_index("facex")
    for out, (for_first, for_second) in zip(outs, plan.bands):
        offset = for_first if for_first == for_second else jnp.where(first_core, for_first, for_second)
        target = jnp.bitwise_xor(place, offset)
        count = carried if for_first == for_second else tracers
        skip = carried if for_first == for_second != 0 and plan.cross else 0
        for start in range(0, count, per_tile):
            tile = jnp.zeros((rows, cy), F32)
            for a in range(min(per_tile, count - start)):
                moved = pltpu.roll(grown[skip + start + a], lax.rem(band * a + cy - band * target, cy), 1)
                tile = jnp.where(group_of_lane == a, moved, tile)
            out[start // per_tile * rows : (start // per_tile + 1) * rows, :] = tile
        full = -(-count // per_tile) * rows
        if out.shape[0] > full:
            out[full:, :] = jnp.zeros((out.shape[0] - full, cy), F32)


def regrid_kernel(sizes, plan, bands, carried, cx, band, *refs):
    index, weight = refs[:2]
    blocks, more, out = refs[2 : 2 + len(bands)], refs[2 + len(bands) : -1], refs[-1]
    taps, cells = index.shape
    rows = cx + 8
    per_tile = min(2 * carried, LANES // band)
    lane = iota((rows, LANES), 1)
    row = iota((rows, cells), 0)
    first_core = lax.axis_index("lev") == 0
    place = lax.axis_index("facex")
    around = sizes[0] * cx
    parts = []
    row_places = []
    for block, ((for_first, for_second), fetched, first) in zip(blocks, bands):
        if plan.cross != fetched:
            for_first, for_second = for_second, for_first
        offset = for_first if for_first == for_second else jnp.where(first_core, for_first, for_second)
        start = jnp.bitwise_xor(place, offset) * cx
        places = start + row
        places = jnp.where(row == cx, lax.rem(start + around - 1, around), places)
        places = jnp.where(row == cx + 1, lax.rem(start + cx, around), places)
        row_places.append(places)
        for t in range(first, first + carried):
            tile = block[t // per_tile * rows : (t // per_tile + 1) * rows, :]
            a = t % per_tile
            values = tile if a == 0 else pltpu.roll(tile, (-band * a) % LANES, 1)
            high = values.astype(BF16).astype(F32)
            low = pltpu.roll(values - high, band, 1)
            both = jnp.where(lane < band, high, jnp.where(lane < 2 * band, low, 0.0))
            parts.append(both.astype(BF16))
    left_side = jnp.concatenate(parts, axis=0)
    spread = iota((LANES, cells), 0)
    in_band = lax.rem(spread, band)
    used = spread < 2 * band
    totals = [jnp.zeros((rows, cells), F32) for _ in range(carried)]
    for tap in range(taps):
        place_of = index[tap : tap + 1, :]
        column = lax.div(place_of, band)
        in_lane = lax.rem(place_of, band)
        picks = jnp.where(jnp.logical_and(in_band == in_lane, used), 1.0, 0.0).astype(BF16)
        picked = jnp.dot(left_side, picks, preferred_element_type=F32)
        at = 0
        for places in row_places:
            chosen = jnp.where(places == column, weight[tap : tap + 1, :], 0.0)
            for t in range(carried):
                totals[t] = totals[t] + chosen * picked[at : at + rows]
                at += rows
    sums = jnp.concatenate([jnp.sum(total, axis=0, keepdims=True) for total in totals], axis=0)
    for ref in more:
        sums = sums + ref[...]
    out[...] = sums


def advance_kernel(plan, *refs):
    tracer, parts, lower, inverse, ratio = refs[:5]
    sent = refs[5:7]
    got = refs[7:9]
    swapped, *refs = refs[9:]
    y_ops = plan.y_ops
    y_sent, y_got, winds_sent, winds_got = (refs[n * y_ops : (n + 1) * y_ops] for n in range(4))
    target, out, west_rows, east_rows, done = refs[-5:]
    carried, levels, cx, cy = tracer.shape
    head = (carried + 1) * levels
    spot = carried * levels
    face_west, _ = own_sides(plan, sent[0][spot:head, :], sent[1][spot:head, :])
    _, face_east = sides(plan, got[0][spot:head, :], got[1][spot:head, :])
    each = [got[number][0:spot, :] for number in range(2)]
    if plan.cross:
        each = [swapped[number * spot : (number + 1) * spot, :] for number in range(2)]
    beyond_west, beyond_east = sides(plan, *each)
    _, at_east = own_sides(plan, sent[0][0:spot, :], sent[1][0:spot, :])
    for t in range(carried):
        part = slice(t * levels, (t + 1) * levels)
        west_rows[part, :] = jnp.maximum(face_west, 0.0) * beyond_west[part]
        east_rows[part, :] = -(
            jnp.maximum(face_east, 0.0) * at_east[part] + jnp.minimum(face_east, 0.0) * beyond_east[part]
        )
    lane = iota((cx, cy), 1)
    row = iota((cx, cy), 0)
    seams = [
        seam_lanes(
            n,
            plan,
            y_sent[n][0:cx, :],
            y_got[n][cx : 2 * cx, :] if plan.relay else y_got[n][0:cx, :],
            winds_sent[n][0:cx, :],
            winds_got[n][0:cx, :],
            carried,
            levels,
        )
        for n in range(y_ops)
    ]
    stride = 4

    def forward(step, before):
        mixed = []
        for k in range(stride):
            level = step * stride + k
            weights = [parts[n, level] for n in range(5)]
            mixed.append([])
            for t in range(carried):
                value = mix(weights, tracer[t, level])
                value = value + jnp.where(row == 0, west_rows[pl.ds(t * levels + level, 1), :], 0.0)
                value = value + jnp.where(row == cx - 1, east_rows[pl.ds(t * levels + level, 1), :], 0.0)
                for packed, spot_y in seams:
                    moved = pltpu.roll(packed, lax.rem(spot_y - (t * levels + level) + 2 * cy, cy), 1)
                    value = value + jnp.where(lane == spot_y, moved, 0.0)
                mixed[k].append(value)
        for k in range(stride):
            level = step * stride + k
            from_below = lower[level]
            scaled = inverse[level]
            after = []
            for t in range(carried):
                value = mixed[k][t] * scaled + from_below * before[t]
                out[t, level] = value
                after.append(value)
            before = after
        return tuple(before)

    def copy(step):
        part = pl.ds(levels - (step + 1) * stride, stride)
        return pltpu.make_async_copy(out.at[:, part], target.at[:, part], done.at[step])

    start = tuple(jnp.zeros((cx, cy), F32) for _ in range(carried))
    lax.fori_loop(0, levels // stride, forward, start)
    above = list(start)
    for step in range(levels // stride):
        for k in range(stride):
            level = levels - 1 - step * stride - k
            factor = ratio[level]
            for t in range(carried):
                above[t] = out[t, level] + factor * above[t]
                out[t, level] = above[t]
        copy(step).start()
    for step in range(levels // stride):
        copy(step).wait()


GROUP = ("facex", "facey", "lev")


def exchange(values, sizes, rule):
    many_x, many_y, cores = sizes
    pairs = []
    for x in range(many_x):
        for y in range(many_y):
            for c in range(cores):
                to = rule(x, y, c)
                if to is not None:
                    pairs.append(((x * many_y + y) * cores + c, (to[0] * many_y + to[1]) * cores + to[2]))
    return lax.ppermute(values, GROUP, pairs)


def make_plan(sizes):
    many_x, many_y, _ = sizes
    tiles = many_x * many_y
    x_blocks = [many_y, (many_x - 1) * many_y if many_x == 4 else 0]
    relay = many_y == 2 and many_x == 4
    if relay:
        own_blocks = list(range(tiles))
        y_blocks = own_blocks[2:]
        x_ops = [offset for offset in own_blocks[2::2] if offset not in x_blocks]
        pairs = []
    else:
        own_blocks = [0] + [offset for offset in x_blocks if offset]
        y_blocks = [1]
        x_ops = []
        rest = [d for d in range(tiles) if d not in {1, *own_blocks}]
        rest.sort(key=lambda d: (d // many_y != many_x // 2, d))
        pairs = [(rest[n], rest[min(n + 1, len(rest) - 1)]) for n in range(0, len(rest), 2)]
    others = list(range(many_x - 1, 1, -1))
    bands = [(0, 0), (1, 1)] + [(others[n + 1], others[n]) for n in range(0, len(others), 2)]
    return Plan({
        "relay": relay,
        "cross": 1 if relay else 0,
        "x_blocks": x_blocks,
        "x_ops": x_ops,
        "own_blocks": own_blocks,
        "y_blocks": y_blocks,
        "y_ops": 1 if many_y == 2 else 2,
        "y_tiles": 2 if relay else 1,
        "pairs": pairs,
        "bands": bands,
    })


def lane_plan(plan, carried, levels):
    starts = {"c": 0, "d": levels, "v": 2 * levels, "w": 3 * levels, "u": 4 * levels}
    if not plan.relay:
        starts = {"v": carried * levels}
    return {"lane_" + name: start for name, start in starts.items()}


def local(
    sizes,
    tracer,
    west_courant,
    south_courant,
    mixing,
    adjoint_later,
    emission_scale,
    send_cells,
    send_counts,
    kernels,
    observed,
    error_weight,
    regrid_index,
    regrid_weight,
):
    plan = make_plan(sizes)
    many_x, many_y, _ = sizes
    carried, levels, cx, cy = tracer.shape
    owners, cap = send_cells.shape[2:]
    slots = owners * cap
    taps, ll = regrid_index.shape[2:]
    plan.update(lane_plan(plan, carried, levels))
    head = (carried + 1) * levels
    y_ops = plan.y_ops
    band = cy // many_x

    def next_x(number):
        def rule(x, y, c):
            step = 1 if (plan.relay or x % 2 == 0) == (number == 0) else -1
            return ((x + step) % many_x, y, c ^ plan.cross)

        return rule

    def next_y(number, cross):
        def rule(x, y, c):
            to = y + (1 if (y % 2 == 0) == (number == 0) else -1)
            return (x, to, c ^ cross) if 0 <= to < many_y else None

        return rule

    def jump(for_first, for_second, cross=0):
        def rule(x, y, c):
            d = for_first if c == 0 else for_second
            return (x ^ (d // many_y), y ^ (d % many_y), c ^ cross)

        return rule

    def other_core(values):
        return exchange(values, sizes, lambda x, y, c: (x, y, 1 - c))

    strips = slots // LANES
    plan["parcel"] = -(-2 * strips // 8) * 8
    extra = 40 if plan.relay else 16
    row_shapes = [shape(head + extra, cy)] * 2
    y_rows = plan.y_tiles * cx + 8 * len(plan.y_blocks) + (plan.parcel if plan.relay else 0)
    lane_shapes = [shape(y_rows if n == 0 else cx, cy) for n in range(y_ops)]
    packed = call(
        functools.partial(pack_kernel, sizes, plan),
        lane_shapes
        + [shape(8 * len(plan.own_blocks), LANES)]
        + [shape(8, LANES)] * len(plan.pairs)
        + [shape(1, slots, dtype=jnp.int32), shape(1, slots)]
        + [shape(*a.shape) for a in (tracer, west_courant, south_courant, emission_scale, mixing)],
        [
            tracer,
            west_courant,
            south_courant,
            emission_scale,
            kernels.reshape(owners, levels, cap),
            observed.reshape(owners, cap),
            error_weight.reshape(owners, cap),
            send_cells.reshape(owners, cap),
            send_counts.reshape(owners),
            mixing,
        ],
        "pack",
        100000,
        hbm=range(10),
        scratch=[
            pltpu.VMEM((owners, levels, cap), F32),
            pltpu.VMEM((owners, cap), F32),
            pltpu.VMEM((owners, cap), F32),
            pltpu.VMEM((owners, cap), jnp.int32),
            pltpu.SMEM((owners,), jnp.int32),
            pltpu.SemaphoreType.DMA((9 + carried,)),
        ],
    )
    lanes_sent = packed[:y_ops]
    own_blocks = packed[y_ops]
    pair_sent = packed[1 + y_ops : -7]
    cell, live, tracer, west_courant, south_courant, emission_scale, mixing = packed[-7:]
    lanes_got = [exchange(lanes_sent[n], sizes, next_y(n, plan.cross)) for n in range(y_ops)]
    held, *_ = lax.optimization_barrier((tracer, *lanes_sent))
    inverse, lower, ratio, base, inner, parts, columns, in_row, in_lane = call(
        functools.partial(factor_kernel, sizes),
        [
            shape(levels, cx, cy),
            shape(levels, cx, cy),
            shape(levels, cx, cy),
            shape(carried, cx, cy),
            shape(levels, cx, cy),
            shape(5, levels, cx, cy),
            shape(levels, slots),
            shape(cx, slots),
            shape(cy, slots, dtype=BF16),
        ],
        [held, west_courant, south_courant, mixing, adjoint_later, cell],
        "factor",
        3000000,
    )
    rows_sent = list(
        call(
            functools.partial(rows_kernel, plan),
            row_shapes + ([shape(cx, cy)] if plan.relay else []),
            [tracer, west_courant, emission_scale, own_blocks],
            "rows",
            100000,
        )
    )
    per_tile = min(2 * carried, LANES // band)

    def band_shape(first, second):
        count = carried if first == second else 2 * carried
        spare = 8 if plan.relay and first == second != 0 else 0
        return shape(-(-count // per_tile) * (cx + 8) + spare, cy)

    band_shapes = [band_shape(*b) for b in plan.bands]
    fields = [west_courant[0], south_courant[0], emission_scale]
    observe = functools.partial(
        call, functools.partial(observe_kernel, sizes, plan, carried), name="observe", flops=2000000
    )
    if plan.relay:
        base, *lanes_got = lax.optimization_barrier((base, *lanes_got))
        lanes_each = rows_sent.pop()
        base_other = other_core(base)

        def relay(number, *after):
            held, *_ = lax.optimization_barrier((rows_sent[number], *after))
            return call(
                functools.partial(relay_kernel, plan, head, cx, number),
                [row_shapes[number]],
                [held, own_blocks, lanes_got[0]],
                "relay",
                10000,
            )[0]

        rows_sent = [relay(0), relay(1)]
        x_sent = call(
            functools.partial(beyond_kernel, plan, cx),
            [shape(32, LANES)] * len(plan.x_ops),
            [own_blocks, lanes_got[0]],
            "beyond",
            10000,
        )
        x_got = [exchange(s, sizes, jump(d, d, 1)) for s, d in zip(x_sent, plan.x_ops)]
        rows_got = [exchange(rows_sent[n], sizes, next_x(n)) for n in range(2)]
        held_y, *_ = lax.optimization_barrier((lanes_got[0], *rows_sent))
        rim = call(
            functools.partial(rim_kernel, plan, carried, levels, cx),
            [
                shape(levels, LANES),
                shape(levels, LANES),
                shape(levels, LANES),
                shape(6, levels, LANES),
                shape(levels, slots),
                shape(cx, slots),
                shape(LANES, slots, dtype=BF16),
                shape(1, slots),
                shape(2 * cx + 16, cy),
            ],
            [lanes_sent[0], held_y, base, base_other, lanes_each, own_blocks],
            "rim",
            400000,
            scratch=[pltpu.VMEM((LANES, LANES), F32)],
        )
        *rim, rim_sent = rim
        rim_got = exchange(rim_sent, sizes, next_y(0, 0))
        parcel, rows_crossed = observe(
            [shape(2 * levels, slots), shape(2 * carried * levels, cy)],
            [*rows_got, inner, lower, inverse, ratio, in_row, in_lane, *rows_sent, *lanes_sent, *lanes_got]
            + [*rim[:4], rim[6]],
            scratch=[pltpu.VMEM((LANES, LANES), F32), pltpu.VMEM((levels, LANES), F32)],
        )
        parcel_other = other_core(parcel)
        rows_swapped = other_core(rows_crossed)
        parcel_other, rim_got, *x_got = lax.optimization_barrier((parcel_other, rim_got, *x_got))
        band_sent = call(
            functools.partial(weigh_kernel, sizes, plan, carried, levels),
            band_shapes,
            [parcel, parcel_other, columns, live, rim[4], rim[7], own_blocks, *x_got, in_row, in_lane]
            + [base, base_other, rim[5], rim_got, *fields, *rows_got, *lanes_got],
            "weigh",
            500000,
        )
        lanes_own = [lanes_each, rim_got]
        held, *_ = lax.optimization_barrier((tracer, *band_sent))
    else:
        rows_got = [exchange(rows_sent[n], sizes, next_x(n)) for n in range(2)]
        pair_got = [exchange(s, sizes, jump(*p)) for s, p in zip(pair_sent, plan.pairs)]
        base_other = other_core(base)
        modeled, state = observe(
            [shape(1, slots), shape(2, slots)],
            [*rows_got, inner, lower, inverse, ratio, in_row, in_lane, *rows_sent, *lanes_sent, *lanes_got]
            + [columns, live, own_blocks, *pair_got]
            + [other_core(jnp.concatenate(pair_got, axis=0))],
        )
        near, *rims_sent = call(
            functools.partial(force_kernel, plan),
            [shape(2 * carried, cx, cy)] + [shape(cx, cy)] * y_ops,
            [modeled, other_core(modeled), state, in_row, in_lane, base, base_other],
            "force",
            200000,
        )
        rims_got = [exchange(rims_sent[n], sizes, next_y(n, 0)) for n in range(y_ops)]
        band_sent = call(
            functools.partial(surface_kernel, sizes, plan, carried, levels),
            band_shapes,
            [near, *fields, *rows_got, *lanes_got, *rims_got],
            "surface",
            400000,
        )
        lanes_own = [*lanes_sent, *lanes_got]
        rows_swapped = rows_got[0]
        held = tracer
    (advanced,) = call(
        functools.partial(advance_kernel, plan),
        [shape(*tracer.shape)],
        [held, parts, lower, inverse, ratio]
        + list(rows_sent)
        + rows_got
        + [rows_swapped]
        + lanes_own
        + list(lanes_sent)
        + lanes_got,
        "advance",
        6000000,
        scratch=[pltpu.VMEM(tracer.shape, F32)]
        + [pltpu.VMEM((carried * levels, cy), F32)] * 2
        + [pltpu.SemaphoreType.DMA((levels // 4,))],
        out_hbm=(0,),
    )
    band_got = [
        s
        if first == second == 0
        else exchange(s, sizes, jump(first * many_y, second * many_y, plan.cross))
        for s, (first, second) in zip(band_sent, plan.bands)
    ]
    tables = [regrid_index.reshape(taps, ll), regrid_weight.reshape(taps, ll)]
    kinds = [first == second for first, second in plan.bands]

    def regridded(bands, blocks, *more):
        return call(
            functools.partial(regrid_kernel, sizes, plan, bands, carried, cx, band),
            [shape(carried, ll)],
            [*tables, *blocks, *more],
            "regrid",
            1000000,
        )[0]

    near = [(pair, 0, 0) for pair, kind in zip(plan.bands, kinds) if kind]
    far = [pair for pair, kind in zip(plan.bands, kinds) if not kind]
    near_got = [got for got, kind in zip(band_got, kinds) if kind]
    far_got = [got for got, kind in zip(band_got, kinds) if not kind]
    advanced, far_got = lax.optimization_barrier((advanced, far_got))
    far_fetched = [other_core(got[: cx + 8] if plan.relay else got) for got in far_got]
    mine = carried if plan.cross else 0
    partial = [regridded([(pair, 0, mine) for pair in far], far_got)] if far else []
    near_got, partial = lax.optimization_barrier((near_got, partial))
    partial = regridded(near, near_got, *partial)
    latlon = regridded([(pair, 1, carried - mine) for pair in far], far_fetched, partial) if far else partial
    return (advanced, latlon[:, None, None, :])


def solution(mesh):
    in_specs = (
        P("lev", "groups", "facex", "facey"),
        P("groups", "facex", "facey"),
        P("groups", "facex", "facey"),
        P("groups", "facex", "facey"),
        P("lev", "groups", "facex", "facey"),
        P("facex", "facey"),
        P("facex", "facey", "groups", None),
        P("facex", "facey", "groups"),
        P("facex", "facey", "groups", None, None),
        P("facex", "facey", "groups", None),
        P("facex", "facey", "groups", None),
        P("facex", "facey", None, None),
        P("facex", "facey", None, None),
    )
    out_specs = (P("lev", "groups", "facex", "facey"), P("lev", "facex", "facey", "groups"))
    sizes = tuple(mesh.shape[axis] for axis in GROUP)
    return jax.shard_map(
        functools.partial(local, sizes), mesh=mesh, in_specs=in_specs, out_specs=out_specs, check_vma=False
    )
```
